32 devices in a mesh: fsdp: 16 (over z, y, x), ctx: 2 (over core).
Axes of the slice: x: 2, y: 2, z: 4, core: 2. Of those that a mesh axis runs over, the one named last changes fastest.
Arguments:
- token_ids: int32 [256], P('ctx'), may hold values from 0 to 511
- embed: bfloat16 [512, 8192], P(None, 'fsdp'), may hold values from -6 to 6
- w_in: bfloat16 [8192, 3, 8192], P('ctx', None, 'fsdp'), may hold values from -0.09375 to 0.09375
- taps: float32 [7, 3, 8192], P(None, None, 'fsdp'), may hold values from -2 to 2
- rates: float32 [16, 8192], P(None, 'fsdp'), may hold values from 0.000390625 to 0.08, as said below
- residues: float32 [16, 8192], P(None, 'fsdp'), may hold values from -0.15 to 0.15
- cotangent: bfloat16 [256, 8192], P('ctx', 'fsdp'), may hold values from -6 to 6
Outputs:
- mixed: bfloat16 [256, 8192], P('ctx', 'fsdp')
- input_grad: bfloat16 [256, 8192], P('ctx', 'fsdp')
The draws below stay inside these ranges and needn't reach their ends.
Inputs may be any that keep to these rules, and one draw needn't show every extreme that they name: `rates`: every rate lies between 0.1 / 256 and 0.08.
All inputs are finite; a program needn't handle non-finite values.
Results may differ from the reference program's by a relative error of at most 0.0064.
Values may be sent and summed in bfloat16 or wider, within the bound.
No kernel may reach another device: no remote copies, remote signals or barrier semaphores. Data moves between devices by JAX's collectives and lax.ppermute only.
A program may use at most 128 MiB of HBM per device.

```python
import math
import jax
import jax.numpy as jnp
from jax import lax

D = 8192
VOCAB = 512
MODES = 16
KSHORT = 7
SEQ = 256


def draw_rates(key, part):
    spread = jax.random.uniform(key, (MODES, D), jnp.float32)
    lowest = math.log(0.1 / SEQ)
    highest = math.log(0.08)
    return jnp.exp(lowest + (highest - lowest) * spread).astype(jnp.float32)


def set_ends(values, stream_key, smallest, top_value):
    place = [jax.random.randint(jax.random.fold_in(stream_key, axis), (), 0, length) for axis, length in enumerate(values.shape)]
    main_axis = values.shape.index(max(values.shape))
    beside = place[:main_axis] + [(place[main_axis] + 1) % values.shape[main_axis]] + place[main_axis + 1:]
    return values.at[tuple(place)].set(smallest).at[tuple(beside)].set(top_value)


def with_spikes(drawn, key, source, target, parts, factor):
    def block_of(axis_at):
        return (jnp.arange(drawn.shape[axis_at]) // (drawn.shape[axis_at] // parts)).reshape((-1,) + (1,) * (drawn.ndim - 1 - axis_at))

    near = jax.random.permutation(key, parts)[block_of(target)]
    second = (block_of(target) + parts // 2) % parts
    return jnp.where((block_of(source) == near) | (block_of(source) == second), factor * drawn, drawn)


def steps_of(own_key, dims, cuts, least, top_value):
    def one(position, shards_of):
        heights = jax.random.uniform(jax.random.fold_in(jax.random.fold_in(own_key, 6), position), (shards_of,), jnp.float32, least / len(cuts), top_value / len(cuts))
        return jnp.repeat(jnp.exp(heights), dims[position] // shards_of).reshape((-1,) + (1,) * (len(dims) - position - 1))

    gain = one(*cuts[0])
    for cut in cuts[1:]:
        gain = gain * one(*cut)
    return gain


def centred(rng, extent, deviation, limit, shards=(), kind=jnp.bfloat16):
    factor_of = steps_of(rng, extent, shards, -0.22, 0.18) if shards else 1.0
    values = jax.random.normal(rng, extent, jnp.float32) * deviation * factor_of
    return jnp.minimum(jnp.maximum(values, -limit), limit).astype(kind)


def gaussian_with(own_key, extent, scale, limit, cuts, heavy, kind=jnp.bfloat16):
    array = scale * jax.random.normal(own_key, extent, jnp.float32)
    if cuts:
        array = array * steps_of(own_key, extent, cuts, -0.22, 0.18)
    return jnp.clip(with_spikes(array, jax.random.fold_in(own_key, 3), *heavy), -limit, limit).astype(kind)


def setup_inputs(seed: int = 0) -> dict:
    keys = jax.random.split(jax.random.key(seed), 8)
    return {
        "token_ids": set_ends(jax.random.randint(keys[0], (SEQ,), 0, VOCAB), jax.random.fold_in(keys[0], 1), 0, VOCAB - 1).astype(jnp.int32),
        "embed": centred(keys[1], (VOCAB, D), 1.0, 6.0, ((1, 16),)),
        "w_in": gaussian_with(keys[2], (D, 3, D), D ** -0.5, 0.09375, ((0, 2), (2, 16)), (2, 0, 16, 2.0)),
        "taps": centred(keys[3], (KSHORT, 3, D), 0.4, 2.0, ((2, 16),), jnp.float32),
        "rates": draw_rates(jax.random.fold_in(keys[7], 71), 0),
        "residues": centred(keys[5], (MODES, D), 0.03, 0.15, ((1, 16),), jnp.float32),
        "cotangent": centred(keys[6], (SEQ, D), 1.0, 6.0, ((0, 2), (1, 16))),
    }


def pair_combine(earlier, later):
    return (earlier[0] * later[0], later[0] * earlier[1] + later[1])


def modal_states(drive, step_decay):
    tok_count = drive.shape[0]
    factors = jnp.broadcast_to(step_decay[None], (tok_count,) + step_decay.shape)
    inputs = jnp.broadcast_to(drive[:, None, :], factors.shape)
    return lax.associative_scan(pair_combine, (factors, inputs), axis=0)[1]


def short_filter(extended, taps, tok_count):
    rim_width = taps.shape[0] - 1
    filtered = taps[0] * extended[rim_width:rim_width + tok_count]
    for shift_lag in range(1, rim_width + 1):
        filtered = filtered + taps[shift_lag] * extended[rim_width - shift_lag:rim_width - shift_lag + tok_count]
    return filtered


def short_adjoint(extended, taps, tok_count):
    rim_width = taps.shape[0] - 1
    result = taps[0] * extended[:tok_count]
    for shift_lag in range(1, rim_width + 1):
        result = result + taps[shift_lag] * extended[shift_lag:shift_lag + tok_count]
    return result


def block_mix(stored, grad_out, taps, rates, residues):
    tok_count = stored.shape[0]
    rim_width = taps.shape[0] - 1
    leading = jnp.zeros((rim_width,) + stored.shape[1:], jnp.bfloat16)
    extended = jnp.concatenate([leading, stored], axis=0).astype(jnp.float32)
    filtered = short_filter(extended, taps, tok_count)
    query_part = filtered[:, 0]
    key_part = filtered[:, 1]
    value_part = filtered[:, 2]
    drive = key_part * value_part
    step_decay = jnp.exp(-rates)
    states = modal_states(drive, step_decay)
    long_out = jnp.sum(residues[None] * states, axis=1)
    mixed = (query_part * long_out).astype(jnp.bfloat16)
    incoming = grad_out.astype(jnp.float32)
    grad_long = incoming * query_part
    grad_query = incoming * long_out
    adjoint = jnp.flip(modal_states(jnp.flip(grad_long, 0), step_decay), 0)
    grad_drive = jnp.sum(residues[None] * adjoint, axis=1)
    grad_filtered = jnp.stack([grad_query, grad_drive * value_part, grad_drive * key_part], axis=1)
    trailing = jnp.zeros((rim_width,) + grad_filtered.shape[1:], jnp.float32)
    ext_grad = jnp.concatenate([grad_filtered, trailing], axis=0)
    grad_stored = short_adjoint(ext_grad, taps, tok_count).astype(jnp.bfloat16)
    return mixed, grad_stored


def reference(token_ids, embed, w_in, taps, rates, residues, cotangent):
    embedded = embed[token_ids]
    flat_w = w_in.reshape(D, 3 * D)
    stored = lax.optimization_barrier(jnp.dot(embedded, flat_w, preferred_element_type=jnp.float32).astype(jnp.bfloat16))
    stored = stored.reshape(SEQ, 3, D)
    blocks = 16
    block_width = D // blocks

    def one_block(block_index):
        first = block_index * block_width
        return block_mix(
            lax.dynamic_slice_in_dim(stored, first, block_width, 2),
            lax.dynamic_slice_in_dim(cotangent, first, block_width, 1),
            lax.dynamic_slice_in_dim(taps, first, block_width, 2),
            lax.dynamic_slice_in_dim(rates, first, block_width, 1),
            lax.dynamic_slice_in_dim(residues, first, block_width, 1),
        )

    mixed_blocks, grad_blocks = lax.map(one_block, jnp.arange(blocks, dtype=jnp.int32))
    mixed = jnp.moveaxis(mixed_blocks, 0, 1).reshape(SEQ, D)
    grad_rows = jnp.moveaxis(grad_blocks, 0, 2).reshape(SEQ, 3 * D)
    input_grad = jnp.dot(grad_rows, flat_w.T, preferred_element_type=jnp.float32).astype(jnp.bfloat16)
    return (mixed, input_grad)
```

```python
import functools

import jax
import jax.numpy as jnp
from jax import lax
from jax.experimental import pallas as pl
from jax.experimental.pallas import tpu as pltpu
from jax.sharding import PartitionSpec as P

BOTH = ("fsdp", "ctx")
CHUNKS = 8
f32 = jnp.float32
bf16 = jnp.bfloat16


def from_behind(shard, axis, by):
    count = lax.axis_size(axis)
    pairs = [(i, i + by) for i in range(count) if 0 <= i + by < count]
    return lax.ppermute(shard, axis, pairs)


def pair_combine(earlier, later):
    return (earlier[0] * later[0], later[0] * earlier[1] + later[1])


def modal_states(drive, step_decay):
    tok_count = drive.shape[0]
    factors = jnp.broadcast_to(step_decay[None], (tok_count,) + step_decay.shape)
    inputs = jnp.broadcast_to(drive[:, None, :], factors.shape)
    return lax.associative_scan(pair_combine, (factors, inputs), axis=0)[1]


def short_filter(extended, taps, tok_count):
    rim_width = taps.shape[0] - 1
    filtered = taps[0] * extended[rim_width : rim_width + tok_count]
    for shift_lag in range(1, rim_width + 1):
        filtered = (
            filtered
            + taps[shift_lag] * extended[rim_width - shift_lag : rim_width - shift_lag + tok_count]
        )
    return filtered


def short_adjoint(extended, taps, tok_count):
    rim_width = taps.shape[0] - 1
    result = taps[0] * extended[:tok_count]
    for shift_lag in range(1, rim_width + 1):
        result = result + taps[shift_lag] * extended[shift_lag : shift_lag + tok_count]
    return result


def carry(block_decay, leaving, by):
    def relay_step(turn_index, incoming):
        return from_behind(block_decay * incoming + leaving, "ctx", by)

    return lax.fori_loop(0, lax.axis_size("ctx") - 1, relay_step, jnp.zeros_like(leaving))


def general_plan(token_ids, embed, w_in, taps, rates, residues, cotangent):
    tok_count = token_ids.shape[0]
    vocab_size = embed.shape[0]
    chan_width = embed.shape[1]
    rim_width = taps.shape[0] - 1
    onehot = (
        token_ids[:, None] == lax.broadcasted_iota(jnp.int32, (tok_count, vocab_size), 1)
    ).astype(bf16)
    embedded = jnp.dot(onehot, embed, preferred_element_type=f32).astype(bf16)
    features = lax.all_gather(embedded, "fsdp", axis=1, tiled=True)
    feat_width = features.shape[1]
    whole_w = lax.all_gather(w_in, "ctx", axis=0, tiled=True).reshape(feat_width, 3 * chan_width)
    projected = jnp.dot(features, whole_w, preferred_element_type=f32)
    stored = lax.optimization_barrier(projected.astype(bf16).reshape(tok_count, 3, chan_width))
    before = from_behind(stored[tok_count - rim_width :], "ctx", 1)
    extended = jnp.concatenate([before, stored], axis=0).astype(f32)
    filtered = short_filter(extended, taps, tok_count)
    query_part = filtered[:, 0]
    key_part = filtered[:, 1]
    value_part = filtered[:, 2]
    drive = key_part * value_part
    step_decay = jnp.exp(-rates)
    block_decay = jnp.exp(-rates * tok_count)
    local_states = modal_states(drive, step_decay)
    entering = carry(block_decay, local_states[tok_count - 1], 1)
    offsets = lax.broadcasted_iota(f32, (tok_count, 1, 1), 0)
    states = local_states + jnp.exp(-rates[None] * (offsets + 1.0)) * entering[None]
    long_out = jnp.sum(residues[None] * states, axis=1)
    mixed = (query_part * long_out).astype(bf16)
    incoming = cotangent.astype(f32)
    grad_long = incoming * query_part
    grad_query = incoming * long_out
    back_states = jnp.flip(modal_states(jnp.flip(grad_long, 0), step_decay), 0)
    beyond = carry(block_decay, back_states[0], -1)
    adjoint = back_states + jnp.exp(-rates[None] * (tok_count - offsets)) * beyond[None]
    grad_drive = jnp.sum(residues[None] * adjoint, axis=1)
    grad_filtered = jnp.stack([grad_query, grad_drive * value_part, grad_drive * key_part], axis=1)
    after = from_behind(grad_filtered[:rim_width], "ctx", -1)
    ext_grad = jnp.concatenate([grad_filtered, after], axis=0)
    grad_stored = short_adjoint(ext_grad, taps, tok_count).astype(bf16)
    grad_rows = grad_stored.reshape(tok_count, 3 * chan_width)
    own_rows = lax.psum_scatter(
        lax.dot_general(whole_w, grad_rows, (((1,), (1,)), ((), ())), preferred_element_type=f32),
        "fsdp",
        scatter_dimension=0,
        tiled=True,
    )
    return (mixed, own_rows.T.astype(bf16))


def device_at(z, y, x, core):
    return ((z * 2 + y) * 2 + x) * 2 + core


def everywhere(move):
    pairs = []
    for z in range(4):
        for y in range(2):
            for x in range(2):
                for core in range(2):
                    pairs.append((device_at(z, y, x, core), device_at(*move(z, y, x, core))))
    return pairs


OTHER_CORE = everywhere(lambda z, y, x, core: (z, y, x, 1 - core))
OVER_X = everywhere(lambda z, y, x, core: (z, y, 1 - x, core))
OVER_Y = everywhere(lambda z, y, x, core: (z, 1 - y, x, core))


def along_z(moves):
    pairs = []
    for core in range(2):
        for (place, other), (to_place, to_other) in moves:
            z, to_z = (place, to_place) if core == 0 else (3 - place, 3 - to_place)
            for y in range(2):
                for x in range(2):
                    pairs.append(
                        (
                            device_at(z, y, x, core ^ other),
                            device_at(to_z, y, x, core ^ to_other),
                        )
                    )
    return pairs


GATHER_Z = (
    along_z([((0, 0), (1, 0)), ((1, 0), (0, 0)), ((0, 1), (2, 0)), ((1, 1), (3, 0))]),
    along_z([((1, 0), (2, 0)), ((2, 0), (3, 0))]),
)
SCATTER_Z = (
    {2: (0, 0), 3: (0, 1), 0: (1, 0), 1: (1, 1)},
    {3: (0, 0), 2: (0, 1), 0: (1, 1)},
    {1: (0, 0), 0: (0, 1), 2: (1, 0), 3: (1, 1)},
    {1: (0, 1), 3: (1, 0), 2: (1, 1)},
)


def project_kernel(rows, which, has_base, last, index_ref, *refs):
    count, kinds = len(rows), max(which) + 1
    acts, weights = refs[:count], refs[count : count + kinds]
    step = pl.program_id(0)
    groups = weights[0].shape[0]
    if last:
        keep_ref, send_ref, total_ref = refs[-3:]
    else:
        total_ref = refs[-1]

    @pl.when(step == 0)
    def _():
        if has_base:
            total_ref[...] = refs[count + kinds][...]
        else:
            total_ref[...] = jnp.zeros_like(total_ref)

    for (low, high), kind, act in zip(rows, which, acts):
        for g in range(groups):
            total_ref[g, low:high] += jnp.dot(
                act[0], weights[kind][g], preferred_element_type=f32
            )
    if last:

        @pl.when(step == pl.num_programs(0) - 1)
        def _():
            half = total_ref.shape[2] // 2
            for core in range(2):

                @pl.when(index_ref[index_ref.shape[0] - 1] == core)
                def _():
                    keep_ref[...] = total_ref[:, :, core * half : (core + 1) * half]
                    send_ref[...] = total_ref[:, :, (1 - core) * half : (2 - core) * half].astype(
                        send_ref.dtype
                    )


def project(index, acts, rows, which, w, base, last, send_dtype=f32):
    count, kinds = len(acts), max(which) + 1
    steps, _, width = acts[0].shape
    groups, _, chans = w.shape
    toks = max(high for _, high in rows)
    total = jax.ShapeDtypeStruct((groups, toks, chans), f32)
    in_specs = [pl.BlockSpec((1,) + act.shape[1:], lambda s, idx: (s, 0, 0)) for act in acts]
    for kind in range(kinds):
        in_specs.append(
            pl.BlockSpec(
                (groups, width, chans), lambda s, idx, kind=kind: (0, idx[s * kinds + kind], 0)
            )
        )
    operands = list(acts) + [w] * kinds
    whole = pl.BlockSpec((groups, toks, chans), lambda s, idx: (0, 0, 0))
    if base is not None:
        in_specs.append(whole)
        operands.append(base)
    if last:
        half = pl.BlockSpec((groups, toks, chans // 2), lambda s, idx: (0, 0, 0))
        out_specs = [half, half]
        out_shape = [
            jax.ShapeDtypeStruct((groups, toks, chans // 2), f32),
            jax.ShapeDtypeStruct((groups, toks, chans // 2), send_dtype),
        ]
        scratch = [pltpu.VMEM(total.shape, f32)]
    else:
        out_specs, out_shape, scratch = whole, total, []
    flops = 2 * steps * groups * width * chans * sum(high - low for low, high in rows)
    return pl.pallas_call(
        functools.partial(project_kernel, rows, which, base is not None, last),
        grid_spec=pltpu.PrefetchScalarGridSpec(
            num_scalar_prefetch=1,
            grid=(steps,),
            in_specs=in_specs,
            out_specs=out_specs,
            scratch_shapes=scratch,
        ),
        out_shape=out_shape,
        compiler_params=pltpu.CompilerParams(vmem_limit_bytes=40 * 1024 * 1024),
        cost_estimate=pl.CostEstimate(
            flops=flops,
            bytes_accessed=2 * steps * kinds * groups * width * chans + 8 * groups * toks * chans,
            transcendentals=0,
        ),
        name="project",
    )(index, *operands)


def shifted(values, by):
    place = lax.broadcasted_iota(jnp.int32, values.shape, 0)
    moved = pltpu.roll(values, by % CHUNKS, 0)
    inside = place >= by if by > 0 else place < CHUNKS + by
    return jnp.where(inside, moved, 0.0)


def mixer_kernel(
    keep_ref,
    other_ref,
    taps_ref,
    rates_ref,
    residues_ref,
    cot_ref,
    mixed_ref,
    grad_ref,
    flat,
    flat_cot,
    ext,
    filt,
    drive,
    back,
    long_out,
    grad_ext,
):
    groups, toks, lanes = keep_ref.shape
    modes = rates_ref.shape[0]
    short = taps_ref.shape[0] // groups
    rim = short - 1
    length = toks // CHUNKS
    wide = (CHUNKS, lanes)

    flat[...] = (keep_ref[...] + other_ref[...].astype(f32)).astype(bf16).astype(f32)
    flat_cot[...] = cot_ref[...].astype(f32)

    def row(array, at):
        return jnp.broadcast_to(array[at : at + 1, :], wide)

    for g in range(groups):
        for k in range(length):
            ext[g, rim + k] = flat[g, pl.ds(k, CHUNKS, stride=length), :]
        for k in range(rim):
            ext[g, k] = shifted(ext[g, length + k], 1)

    taps = taps_ref[...]
    tap = [[row(taps, j * groups + g) for g in range(groups)] for j in range(short)]

    def filter_step(k, _):
        parts = []
        for g in range(groups):
            total = tap[0][g] * ext[g, k + rim]
            for j in range(1, short):
                total = total + tap[j][g] * ext[g, k + rim - j]
            parts.append(total)
            filt[g, k] = total
        drive[k] = parts[1] * parts[2]
        back[k] = parts[0] * flat_cot[pl.ds(k, CHUNKS, stride=length), :]
        return _

    lax.fori_loop(0, length, filter_step, 0, unroll=4)

    rates = rates_ref[...]
    decay_rows = jnp.exp(-rates)
    jump_rows = [jnp.exp(-rates * (length * n)) for n in (1, 2, 4)]
    residue_rows = residues_ref[...]

    def long_filter(source, forward, finish):
        decay = [row(decay_rows, m) for m in range(modes)]

        def place(k):
            return k if forward else length - 1 - k

        def end_step(k, states):
            value = source[place(k)]
            return tuple(decay[m] * states[m] + value for m in range(modes))

        zero = jnp.zeros(wide, f32)
        ends = lax.fori_loop(0, length, end_step, (zero,) * modes, unroll=8)
        entering = []
        sign = 1 if forward else -1
        for m in range(modes):
            carried = ends[m]
            for jump, by in zip(jump_rows, (1, 2, 4)):
                carried = carried + row(jump, m) * shifted(carried, sign * by)
            entering.append(shifted(carried, sign))

        def out_step(k, states):
            value = source[place(k)]
            states = tuple(decay[m] * states[m] + value for m in range(modes))
            terms = [row(residue_rows, m) * states[m] for m in range(modes)]
            while len(terms) > 1:
                terms = [a + b for a, b in zip(terms[::2], terms[1::2])]
            finish(place(k), terms[0])
            return states

        lax.fori_loop(0, length, out_step, tuple(entering), unroll=4)

    def finish_forward(k, total):
        flat[0, pl.ds(k, CHUNKS, stride=length), :] = filt[0, k] * total
        grad_ext[0, k] = flat_cot[pl.ds(k, CHUNKS, stride=length), :] * total

    def finish_backward(k, total):
        grad_ext[1, k] = total * filt[2, k]
        grad_ext[2, k] = total * filt[1, k]

    long_filter(drive, True, finish_forward)
    mixed_ref[...] = flat[0].astype(mixed_ref.dtype)
    long_filter(back, False, finish_backward)

    for g in range(groups):
        for k in range(rim):
            grad_ext[g, length + k] = shifted(grad_ext[g, k], -1)

    def adjoint_step(k, _):
        for g in range(groups):
            total = tap[0][g] * grad_ext[g, k]
            for j in range(1, short):
                total = total + tap[j][g] * grad_ext[g, k + j]
            flat[g, pl.ds(k, CHUNKS, stride=length), :] = total
        return _

    lax.fori_loop(0, length, adjoint_step, 0, unroll=4)
    grad_ref[...] = flat[...].astype(grad_ref.dtype)


def mixer(keep, other, taps, rates, residues, cotangent):
    groups, toks, chans = keep.shape
    modes = rates.shape[0]
    rim = taps.shape[0] // groups - 1
    lanes = 128
    length = toks // CHUNKS
    flat = pl.BlockSpec((toks, lanes), lambda c: (0, c))
    grouped = pl.BlockSpec((groups, toks, lanes), lambda c: (0, 0, c))
    return pl.pallas_call(
        mixer_kernel,
        grid=(chans // lanes,),
        in_specs=[
            grouped,
            grouped,
            pl.BlockSpec((taps.shape[0], lanes), lambda c: (0, c)),
            pl.BlockSpec((modes, lanes), lambda c: (0, c)),
            pl.BlockSpec((modes, lanes), lambda c: (0, c)),
            flat,
        ],
        out_specs=[flat, grouped],
        out_shape=[
            jax.ShapeDtypeStruct((toks, chans), bf16),
            jax.ShapeDtypeStruct((groups, toks, chans), bf16),
        ],
        scratch_shapes=[
            pltpu.VMEM((groups, toks, lanes), f32),
            pltpu.VMEM((toks, lanes), f32),
            pltpu.VMEM((groups, length + rim, CHUNKS, lanes), f32),
            pltpu.VMEM((groups, length, CHUNKS, lanes), f32),
            pltpu.VMEM((length, CHUNKS, lanes), f32),
            pltpu.VMEM((length, CHUNKS, lanes), f32),
            pltpu.VMEM((length, CHUNKS, lanes), f32),
            pltpu.VMEM((groups, length + rim, CHUNKS, lanes), f32),
        ],
        compiler_params=pltpu.CompilerParams(vmem_limit_bytes=24 * 1024 * 1024),
        cost_estimate=pl.CostEstimate(
            flops=12 * modes * toks * chans, bytes_accessed=16 * groups * toks * chans, transcendentals=0
        ),
        name="mixer",
    )(keep, other, taps, rates, residues, cotangent)


def back_kernel(index_ref, own_ref, other_ref, w_ref, *out_refs):
    groups, _, half = own_ref.shape

    for core in range(2):

        @pl.when(index_ref[index_ref.shape[0] - 1] == core)
        def _():
            total = None
            for g in range(groups):
                for ref, side in ((own_ref, core), (other_ref, 1 - core)):
                    term = lax.dot_general(
                        w_ref[g, :, side * half : (side + 1) * half],
                        ref[g],
                        (((1,), (1,)), ((), ())),
                        preferred_element_type=f32,
                    )
                    total = term if total is None else total + term
            if len(out_refs) == 1:
                out_refs[0][0] = total.astype(out_refs[0].dtype)
            else:
                part = total.shape[1] // len(out_refs)
                for n, out_ref in enumerate(out_refs):
                    out_ref[0] = total[:, n * part : (n + 1) * part].astype(out_ref.dtype)


def back_project(index, steps, own, other, w, width, dtypes):
    groups, toks, half = own.shape
    chans = w.shape[2]
    part = toks // len(dtypes)
    whole = pl.BlockSpec((groups, toks, half), lambda s, idx: (0, 0, 0))
    return pl.pallas_call(
        back_kernel,
        grid_spec=pltpu.PrefetchScalarGridSpec(
            num_scalar_prefetch=1,
            grid=(steps,),
            in_specs=[
                whole,
                whole,
                pl.BlockSpec((groups, width, chans), lambda s, idx: (0, idx[s], 0)),
            ],
            out_specs=[pl.BlockSpec((1, width, part), lambda s, idx: (s, 0, 0)) for _ in dtypes],
        ),
        out_shape=[jax.ShapeDtypeStruct((steps, width, part), dtype) for dtype in dtypes],
        compiler_params=pltpu.CompilerParams(vmem_limit_bytes=40 * 1024 * 1024),
        cost_estimate=pl.CostEstimate(
            flops=2 * steps * groups * width * chans * toks,
            bytes_accessed=2 * steps * groups * width * chans + 4 * steps * width * toks,
            transcendentals=0,
        ),
        name="back_project",
    )(index, own, other, w)


def chip_plan(token_ids, embed, w_in, taps, rates, residues, cotangent):
    vocab_size, width = embed.shape
    tok_half = token_ids.shape[0]
    toks = 2 * tok_half
    chan_half = width // 2
    spot = lax.axis_index("fsdp")
    core = lax.axis_index("ctx")
    z, y, x = spot // 4, (spot // 2) % 2, spot % 2
    first = core == 0
    place = jnp.where(first, z, 3 - z)
    w = jnp.transpose(w_in, (1, 0, 2))

    def swap(array):
        return lax.ppermute(array, BOTH, OTHER_CORE)

    def in_order(own, other, axis):
        return jnp.where(
            first,
            jnp.concatenate([own, other], axis=axis),
            jnp.concatenate([other, own], axis=axis),
        )

    def mine(array, axis):
        size = array.shape[axis] // 2
        return lax.dynamic_slice_in_dim(array, core * size, size, axis)

    def theirs(array, axis):
        size = array.shape[axis] // 2
        return lax.dynamic_slice_in_dim(array, (1 - core) * size, size, axis)

    ids = in_order(token_ids, swap(token_ids), 0)
    cot = in_order(mine(cotangent, 1), swap(theirs(cotangent, 1)), 0)
    onehot = (ids[:, None] == lax.broadcasted_iota(jnp.int32, (toks, vocab_size), 1)).astype(bf16)
    embedded = jnp.dot(onehot, embed, preferred_element_type=f32).astype(bf16)

    got_1 = lax.ppermute(embedded, BOTH, GATHER_Z[0])
    got_2 = lax.ppermute(jnp.where(place == 2, got_1, embedded), BOTH, GATHER_Z[1])
    far = jnp.where(place == 0, embedded, jnp.where(place == 3, got_2, got_1))
    near = jnp.where(place == 1, embedded, jnp.where(place == 2, got_2, got_1))
    block_far = core * 4
    block_near = (1 - core) * 4

    def blocks(y_at, x_at):
        return [block_far + y_at * 2 + x_at, block_near + y_at * 2 + x_at]

    def table(entries):
        return jnp.stack([jnp.asarray(e, jnp.int32) for e in entries])

    rows_a = jnp.stack([far[:tok_half], near[:tok_half]])
    rows_b = jnp.stack([far[tok_half:], near[tok_half:]])
    x_a = lax.ppermute(rows_a, BOTH, OVER_X)
    y_b = lax.ppermute(rows_b, BOTH, OVER_Y)
    x_b = lax.ppermute(rows_b, BOTH, OVER_X)
    y_a = lax.ppermute(rows_a, BOTH, OVER_Y)
    d_a = lax.ppermute(x_a, BOTH, OVER_Y)
    d_b = lax.ppermute(y_b, BOTH, OVER_X)

    upper, lower = (0, tok_half), (tok_half, toks)
    own_at, x_at, y_at, d_at = blocks(y, x), blocks(y, 1 - x), blocks(1 - y, x), blocks(1 - y, 1 - x)

    sums = project(table(own_at), [rows_a, rows_b], [upper, lower], [0, 0], w, None, False)
    sums = project(
        table([x_at[0], y_at[0], x_at[1], y_at[1]]),
        [x_a, y_b, x_b, y_a],
        [upper, lower, lower, upper],
        [0, 1, 0, 1],
        w,
        sums,
        False,
    )
    keep, send = project(
        table(d_at + [core]), [d_a, d_b], [upper, lower], [0, 0], w, sums, True
    )

    groups = w.shape[0]
    flat_taps = mine(taps, 2).reshape(taps.shape[0] * groups, chan_half)
    mixed_chans, grad_own = mixer(
        keep, swap(send), flat_taps, mine(rates, 1), mine(residues, 1), cot
    )
    grad_other = swap(grad_own)
    mixed = in_order(mine(mixed_chans, 0), swap(theirs(mixed_chans, 0)), 1)

    d_a, d_b = back_project(table(d_at + [core]), 2, grad_own, grad_other, w, width, [bf16, bf16])
    from_y = lax.ppermute(d_a, BOTH, OVER_Y)
    from_x = lax.ppermute(d_b, BOTH, OVER_X)
    x_a, x_b = back_project(table(x_at + [core]), 2, grad_own, grad_other, w, width, [f32, bf16])
    y_a, y_b = back_project(table(y_at + [core]), 2, grad_own, grad_other, w, width, [bf16, f32])
    own_x_b = lax.ppermute(x_b, BOTH, OVER_X)
    own_y_a = lax.ppermute(y_a, BOTH, OVER_Y)
    own_x_a = lax.ppermute((x_a + from_y.astype(f32)).astype(bf16), BOTH, OVER_X)
    own_y_b = lax.ppermute((y_b + from_x.astype(f32)).astype(bf16), BOTH, OVER_Y)
    own_a, own_b = back_project(table(own_at + [core]), 2, grad_own, grad_other, w, width, [f32, f32])
    own_a = own_a + own_y_a.astype(f32) + own_x_a.astype(f32)
    own_b = own_b + own_x_b.astype(f32) + own_y_b.astype(f32)

    held = jnp.stack([own_a[0], own_b[0], own_a[1], own_b[1]])
    rounded = held.astype(bf16)
    total = jnp.where(
        place < 2, lax.dynamic_index_in_dim(held, jnp.minimum(place, 1) * 2 + core, 0, False), 0.0
    )
    for moves in SCATTER_Z:
        pairs = along_z([((place_at, 0), to) for place_at, to in moves.items()])
        choice = jnp.zeros((), jnp.int32)
        for place_at, (to_place, to_other) in moves.items():
            half = jnp.where(first, to_other, 1 - to_other)
            choice = jnp.where(place == place_at, to_place * 2 + half, choice)
        payload = lax.dynamic_index_in_dim(rounded, choice, 0, False)
        total = total + lax.ppermute(payload, BOTH, pairs).astype(f32)
    return (mixed, total.T.astype(bf16))


def solution(mesh):
    in_specs = (
        P("ctx"),
        P(None, "fsdp"),
        P("ctx", None, "fsdp"),
        P(None, None, "fsdp"),
        P(None, "fsdp"),
        P(None, "fsdp"),
        P("ctx", "fsdp"),
    )
    out_specs = (P("ctx", "fsdp"), P("ctx", "fsdp"))
    chips = mesh.shape["fsdp"] == 16 and mesh.shape["ctx"] == 2
    return jax.shard_map(
        chip_plan if chips else general_plan,
        mesh=mesh,
        in_specs=in_specs,
        out_specs=out_specs,
        check_vma=False,
    )
```

```python
import functools

import jax
import jax.numpy as jnp
from jax import lax
from jax.experimental import pallas as pl
from jax.experimental.pallas import tpu as pltpu
from jax.sharding import PartitionSpec as P

BOTH = ("fsdp", "ctx")
CHUNKS = 8
f32 = jnp.float32
bf16 = jnp.bfloat16


def from_behind(shard, axis, by):
    count = lax.axis_size(axis)
    pairs = [(i, i + by) for i in range(count) if 0 <= i + by < count]
    return lax.ppermute(shard, axis, pairs)


def pair_combine(earlier, later):
    return (earlier[0] * later[0], later[0] * earlier[1] + later[1])


def modal_states(drive, step_decay):
    tok_count = drive.shape[0]
    factors = jnp.broadcast_to(step_decay[None], (tok_count,) + step_decay.shape)
    inputs = jnp.broadcast_to(drive[:, None, :], factors.shape)
    return lax.associative_scan(pair_combine, (factors, inputs), axis=0)[1]


def short_filter(extended, taps, tok_count):
    rim_width = taps.shape[0] - 1
    filtered = taps[0] * extended[rim_width : rim_width + tok_count]
    for shift_lag in range(1, rim_width + 1):
        filtered = (
            filtered
            + taps[shift_lag] * extended[rim_width - shift_lag : rim_width - shift_lag + tok_count]
        )
    return filtered


def short_adjoint(extended, taps, tok_count):
    rim_width = taps.shape[0] - 1
    result = taps[0] * extended[:tok_count]
    for shift_lag in range(1, rim_width + 1):
        result = result + taps[shift_lag] * extended[shift_lag : shift_lag + tok_count]
    return result


def carry(block_decay, leaving, by):
    def relay_step(turn_index, incoming):
        return from_behind(block_decay * incoming + leaving, "ctx", by)

    return lax.fori_loop(0, lax.axis_size("ctx") - 1, relay_step, jnp.zeros_like(leaving))


def general_plan(token_ids, embed, w_in, taps, rates, residues, cotangent):
    tok_count = token_ids.shape[0]
    vocab_size = embed.shape[0]
    chan_width = embed.shape[1]
    rim_width = taps.shape[0] - 1
    onehot = (
        token_ids[:, None] == lax.broadcasted_iota(jnp.int32, (tok_count, vocab_size), 1)
    ).astype(bf16)
    embedded = jnp.dot(onehot, embed, preferred_element_type=f32).astype(bf16)
    features = lax.all_gather(embedded, "fsdp", axis=1, tiled=True)
    feat_width = features.shape[1]
    whole_w = lax.all_gather(w_in, "ctx", axis=0, tiled=True).reshape(feat_width, 3 * chan_width)
    projected = jnp.dot(features, whole_w, preferred_element_type=f32)
    stored = lax.optimization_barrier(projected.astype(bf16).reshape(tok_count, 3, chan_width))
    before = from_behind(stored[tok_count - rim_width :], "ctx", 1)
    extended = jnp.concatenate([before, stored], axis=0).astype(f32)
    filtered = short_filter(extended, taps, tok_count)
    query_part = filtered[:, 0]
    key_part = filtered[:, 1]
    value_part = filtered[:, 2]
    drive = key_part * value_part
    step_decay = jnp.exp(-rates)
    block_decay = jnp.exp(-rates * tok_count)
    local_states = modal_states(drive, step_decay)
    entering = carry(block_decay, local_states[tok_count - 1], 1)
    offsets = lax.broadcasted_iota(f32, (tok_count, 1, 1), 0)
    states = local_states + jnp.exp(-rates[None] * (offsets + 1.0)) * entering[None]
    long_out = jnp.sum(residues[None] * states, axis=1)
    mixed = (query_part * long_out).astype(bf16)
    incoming = cotangent.astype(f32)
    grad_long = incoming * query_part
    grad_query = incoming * long_out
    back_states = jnp.flip(modal_states(jnp.flip(grad_long, 0), step_decay), 0)
    beyond = carry(block_decay, back_states[0], -1)
    adjoint = back_states + jnp.exp(-rates[None] * (tok_count - offsets)) * beyond[None]
    grad_drive = jnp.sum(residues[None] * adjoint, axis=1)
    grad_filtered = jnp.stack([grad_query, grad_drive * value_part, grad_drive * key_part], axis=1)
    after = from_behind(grad_filtered[:rim_width], "ctx", -1)
    ext_grad = jnp.concatenate([grad_filtered, after], axis=0)
    grad_stored = short_adjoint(ext_grad, taps, tok_count).astype(bf16)
    grad_rows = grad_stored.reshape(tok_count, 3 * chan_width)
    own_rows = lax.psum_scatter(
        lax.dot_general(whole_w, grad_rows, (((1,), (1,)), ((), ())), preferred_element_type=f32),
        "fsdp",
        scatter_dimension=0,
        tiled=True,
    )
    return (mixed, own_rows.T.astype(bf16))


def device_at(z, y, x, core):
    return ((z * 2 + y) * 2 + x) * 2 + core


def everywhere(move):
    pairs = []
    for z in range(4):
        for y in range(2):
            for x in range(2):
                for core in range(2):
                    pairs.append((device_at(z, y, x, core), device_at(*move(z, y, x, core))))
    return pairs


OTHER_CORE = everywhere(lambda z, y, x, core: (z, y, x, 1 - core))
OVER_X = everywhere(lambda z, y, x, core: (z, y, 1 - x, core))
OVER_Y = everywhere(lambda z, y, x, core: (z, 1 - y, x, core))


def along_z(moves):
    pairs = []
    for core in range(2):
        for (place, other), (to_place, to_other) in moves:
            z, to_z = (place, to_place) if core == 0 else (3 - place, 3 - to_place)
            for y in range(2):
                for x in range(2):
                    pairs.append(
                        (
                            device_at(z, y, x, core ^ other),
                            device_at(to_z, y, x, core ^ to_other),
                        )
                    )
    return pairs


GATHER_Z = (
    along_z([((0, 0), (1, 0)), ((1, 0), (0, 0)), ((0, 1), (2, 0)), ((1, 1), (3, 0))]),
    along_z([((1, 0), (2, 0)), ((2, 0), (3, 0))]),
)
SCATTER_Z = (
    along_z([((0, 0), (1, 0)), ((1, 0), (0, 0)), ((2, 0), (1, 1)), ((3, 0), (0, 1))]),
    along_z([((0, 0), (1, 1)), ((1, 0), (0, 1)), ((2, 0), (1, 0)), ((3, 0), (0, 0))]),
    along_z([((0, 0), (0, 1)), ((1, 0), (1, 1)), ((2, 0), (0, 0)), ((3, 0), (1, 0))]),
    along_z([((2, 0), (0, 1)), ((3, 0), (1, 1))]),
)

IN_VMEM = pl.BlockSpec(memory_space=pltpu.VMEM)
IN_SMEM = pl.BlockSpec(memory_space=pltpu.SMEM)


def small_call(kernel, out_shape, operands, name, flops=0, scratch=(), limit=8):
    sizes = [o.size * o.dtype.itemsize for o in operands]
    return pl.pallas_call(
        kernel,
        in_specs=[IN_SMEM] + [IN_VMEM] * (len(operands) - 1),
        out_specs=jax.tree.map(lambda _: IN_VMEM, out_shape),
        out_shape=out_shape,
        scratch_shapes=list(scratch),
        compiler_params=pltpu.CompilerParams(vmem_limit_bytes=limit * 1024 * 1024),
        cost_estimate=pl.CostEstimate(
            flops=flops, bytes_accessed=min(sum(sizes), 8 * 1024 * 1024), transcendentals=0
        ),
        name=name,
    )(*operands)


def load_kernel(w_ref, out_ref, sem):
    copy = pltpu.make_async_copy(w_ref, out_ref, sem)
    copy.start()
    copy.wait()


def load(w):
    return pl.pallas_call(
        load_kernel,
        in_specs=[pl.BlockSpec(memory_space=pltpu.HBM)],
        out_specs=IN_VMEM,
        out_shape=pltpu.VMEM(w.shape, w.dtype),
        scratch_shapes=[pltpu.SemaphoreType.DMA],
        compiler_params=pltpu.CompilerParams(vmem_limit_bytes=2 * 1024 * 1024),
        cost_estimate=pl.CostEstimate(
            flops=0, bytes_accessed=2 * w.size * w.dtype.itemsize, transcendentals=0
        ),
        name="load",
    )(pltpu.with_memory_space_constraint(w, pltpu.HBM))


def project_kernel(rows, has_base, last, index_ref, w_ref, *refs):
    count = len(rows)
    acts = refs[:count]
    groups, _, chans = w_ref.shape
    width = acts[0].shape[1]
    if last:
        keep_ref, send_ref, total_ref = refs[-3:]
    else:
        total_ref = refs[-1]
    toks = total_ref.shape[1]
    for g in range(groups):
        for low in range(0, toks, toks // 2):
            high = low + toks // 2
            total = refs[count][g, low:high] if has_base else None
            for n, ((first, end), act) in enumerate(zip(rows, acts)):
                if first > low or end < high:
                    continue
                start = pl.multiple_of(index_ref[n] * width, width)
                term = jnp.dot(
                    act[low - first : high - first],
                    w_ref[g, pl.ds(start, width), :],
                    preferred_element_type=f32,
                )
                total = term if total is None else total + term
            total_ref[g, low:high] = total
    if last:
        half = chans // 2
        for core in range(2):

            @pl.when(index_ref[count] == core)
            def _():
                keep_ref[...] = total_ref[:, :, core * half : (core + 1) * half]
                send_ref[...] = total_ref[:, :, (1 - core) * half : (2 - core) * half].astype(
                    send_ref.dtype
                )


def project(index, acts, rows, w, base, last):
    groups, _, chans = w.shape
    width = acts[0].shape[1]
    toks = max(high for _, high in rows)
    total = jax.ShapeDtypeStruct((groups, toks, chans), f32)
    scratch = []
    if last:
        out_shape = [
            jax.ShapeDtypeStruct((groups, toks, chans // 2), f32),
            jax.ShapeDtypeStruct((groups, toks, chans // 2), bf16),
        ]
        scratch = [pltpu.VMEM(total.shape, f32)]
    else:
        out_shape = total
    operands = [index, w] + list(acts) + ([] if base is None else [base])
    flops = 2 * groups * width * chans * sum(high - low for low, high in rows)
    return small_call(
        functools.partial(project_kernel, rows, base is not None, last),
        out_shape,
        operands,
        "project",
        flops,
        scratch,
        16,
    )


def shifted(values, by):
    place = lax.broadcasted_iota(jnp.int32, values.shape, 0)
    moved = pltpu.roll(values, by % CHUNKS, 0)
    inside = place >= by if by > 0 else place < CHUNKS + by
    return jnp.where(inside, moved, 0.0)


def mixer_kernel(
    core_ref,
    keep_ref,
    other_ref,
    taps_ref,
    rates_ref,
    residues_ref,
    cot_own_ref,
    cot_other_ref,
    mixed_own_ref,
    mixed_send_ref,
    grad_ref,
    flat,
    flat_cot,
    ext,
    filt,
    drive,
    back,
    grad_ext,
):
    groups, toks, chans = keep_ref.shape
    modes = rates_ref.shape[0]
    short = taps_ref.shape[0] // groups
    rim = short - 1
    length = toks // CHUNKS
    lanes = flat.shape[-1]
    wide = (CHUNKS, lanes)
    half = toks // 2
    core = core_ref[0]

    def row(array, at):
        return jnp.broadcast_to(array[at : at + 1, :], wide)

    def column(c, _):
        here = pl.ds(pl.multiple_of(c * lanes, lanes), lanes)
        whole = pl.ds(pl.multiple_of(core * chans + c * lanes, lanes), lanes)
        own_rows = pl.ds(pl.multiple_of(core * half, half), half)
        other_rows = pl.ds(pl.multiple_of((1 - core) * half, half), half)

        for g in range(groups):
            flat[g] = (keep_ref[g, :, here] + other_ref[g, :, here].astype(f32)).astype(bf16).astype(f32)
        flat_cot[own_rows] = cot_own_ref[:, whole].astype(f32)
        flat_cot[other_rows] = cot_other_ref[:, here].astype(f32)

        for g in range(groups):
            for k in range(length):
                ext[g, rim + k] = flat[g, pl.ds(k, CHUNKS, stride=length), :]
            for k in range(rim):
                ext[g, k] = shifted(ext[g, length + k], 1)

        taps = taps_ref[:, whole]
        tap = [[row(taps, j * groups + g) for g in range(groups)] for j in range(short)]

        def filter_step(k, _):
            parts = []
            for g in range(groups):
                total = tap[0][g] * ext[g, k + rim]
                for j in range(1, short):
                    total = total + tap[j][g] * ext[g, k + rim - j]
                parts.append(total)
                filt[g, k] = total
            drive[k] = parts[1] * parts[2]
            back[k] = parts[0] * flat_cot[pl.ds(k, CHUNKS, stride=length), :]
            return _

        lax.fori_loop(0, length, filter_step, 0, unroll=4)

        rates = rates_ref[:, whole]
        decay_rows = jnp.exp(-rates)
        jump_rows = [jnp.exp(-rates * (length * n)) for n in (1, 2, 4)]
        residue_rows = residues_ref[:, whole]

        def long_filter(source, forward, finish):
            decay = [row(decay_rows, m) for m in range(modes)]

            def place(k):
                return k if forward else length - 1 - k

            def end_step(k, states):
                value = source[place(k)]
                return tuple(decay[m] * states[m] + value for m in range(modes))

            zero = jnp.zeros(wide, f32)
            ends = lax.fori_loop(0, length, end_step, (zero,) * modes, unroll=8)
            entering = []
            sign = 1 if forward else -1
            for m in range(modes):
                carried = ends[m]
                for jump, by in zip(jump_rows, (1, 2, 4)):
                    carried = carried + row(jump, m) * shifted(carried, sign * by)
                entering.append(shifted(carried, sign))

            def out_step(k, states):
                value = source[place(k)]
                states = tuple(decay[m] * states[m] + value for m in range(modes))
                terms = [row(residue_rows, m) * states[m] for m in range(modes)]
                while len(terms) > 1:
                    terms = [a + b for a, b in zip(terms[::2], terms[1::2])]
                finish(place(k), terms[0])
                return states

            lax.fori_loop(0, length, out_step, tuple(entering), unroll=4)

        def finish_forward(k, total):
            flat[0, pl.ds(k, CHUNKS, stride=length), :] = filt[0, k] * total
            grad_ext[0, k] = flat_cot[pl.ds(k, CHUNKS, stride=length), :] * total

        def finish_backward(k, total):
            grad_ext[1, k] = total * filt[2, k]
            grad_ext[2, k] = total * filt[1, k]

        long_filter(drive, True, finish_forward)
        mixed_own_ref[:, here] = flat[0, own_rows].astype(bf16)
        mixed_send_ref[:, here] = flat[0, other_rows].astype(bf16)
        long_filter(back, False, finish_backward)

        for g in range(groups):
            for k in range(rim):
                grad_ext[g, length + k] = shifted(grad_ext[g, k], -1)

        def adjoint_step(k, _):
            for g in range(groups):
                total = tap[0][g] * grad_ext[g, k]
                for j in range(1, short):
                    total = total + tap[j][g] * grad_ext[g, k + j]
                flat[g, pl.ds(k, CHUNKS, stride=length), :] = total
            return _

        lax.fori_loop(0, length, adjoint_step, 0, unroll=4)
        for g in range(groups):
            grad_ref[g, here, :] = flat[g].T.astype(bf16)
        return _

    lax.fori_loop(0, chans // lanes, column, 0)


def mixer(core, keep, other, taps, rates, residues, cot_own, cot_other):
    groups, toks, chans = keep.shape
    modes = rates.shape[0]
    rim = taps.shape[0] // groups - 1
    lanes = 128
    length = toks // CHUNKS
    return small_call(
        mixer_kernel,
        [
            jax.ShapeDtypeStruct((toks // 2, chans), bf16),
            jax.ShapeDtypeStruct((toks // 2, chans), bf16),
            jax.ShapeDtypeStruct((groups, chans, toks), bf16),
        ],
        [core, keep, other, taps, rates, residues, cot_own, cot_other],
        "mixer",
        12 * modes * toks * chans,
        [
            pltpu.VMEM((groups, toks, lanes), f32),
            pltpu.VMEM((toks, lanes), f32),
            pltpu.VMEM((groups, length + rim, CHUNKS, lanes), f32),
            pltpu.VMEM((groups, length, CHUNKS, lanes), f32),
            pltpu.VMEM((length, CHUNKS, lanes), f32),
            pltpu.VMEM((length, CHUNKS, lanes), f32),
            pltpu.VMEM((groups, length + rim, CHUNKS, lanes), f32),
        ],
    )


def back_kernel(split, index_ref, w_ref, own_ref, other_ref, *out_refs):
    groups, half, toks = own_ref.shape
    per = 2 if split else 1
    width = out_refs[0].shape[0]
    count = len(out_refs) // per
    core = index_ref[count]
    own_at = pl.multiple_of(core * half, half)
    other_at = pl.multiple_of((1 - core) * half, half)
    for n in range(count):
        start = pl.multiple_of(index_ref[n] * width, width)
        total = None
        for g in range(groups):
            for ref, at in ((own_ref, own_at), (other_ref, other_at)):
                term = jnp.dot(
                    w_ref[g, pl.ds(start, width), pl.ds(at, half)],
                    ref[g],
                    preferred_element_type=f32,
                )
                total = term if total is None else total + term
        part = toks // per
        for p in range(per):
            out = out_refs[n * per + p]
            out[...] = total[:, p * part : (p + 1) * part].astype(out.dtype)


def back_project(index, w, own, other, width, split, dtype):
    groups, half, toks = own.shape
    count = index.shape[0] - 1
    per = 2 if split else 1
    return small_call(
        functools.partial(back_kernel, split),
        [jax.ShapeDtypeStruct((width, toks // per), dtype) for _ in range(count * per)],
        [index, w, own, other],
        "back_project",
        4 * count * groups * width * half * toks,
        (),
        16,
    )


def merge_kernel(core_ref, x_ref, y_ref, from_y_ref, from_x_ref, x_out, y_out):
    half = x_ref.shape[1] // 2
    x_out[:, :half] = (x_ref[:, :half] + from_y_ref[...].astype(f32)).astype(bf16)
    x_out[:, half:] = x_ref[:, half:].astype(bf16)
    y_out[:, :half] = y_ref[:, :half].astype(bf16)
    y_out[:, half:] = (y_ref[:, half:] + from_x_ref[...].astype(f32)).astype(bf16)


def merge(core, x_part, y_part, from_y, from_x):
    shape = jax.ShapeDtypeStruct(x_part.shape, bf16)
    return small_call(merge_kernel, [shape, shape], [core, x_part, y_part, from_y, from_x], "merge")


def column_kernel(flag_ref, own_ref, x_ref, y_ref, total_ref, one_ref, two_ref):
    half = own_ref.shape[1] // 2
    total_ref[...] = own_ref[...] + x_ref[...].astype(f32) + y_ref[...].astype(f32)
    first = pl.ds(pl.multiple_of(flag_ref[0] * half, half), half)
    second = pl.ds(pl.multiple_of((1 - flag_ref[0]) * half, half), half)
    one_ref[...] = total_ref[:, first].astype(bf16)
    two_ref[...] = total_ref[:, second].astype(bf16)


def column(flag, own, from_x, from_y):
    shape = jax.ShapeDtypeStruct((own.shape[0], own.shape[1] // 2), bf16)
    return small_call(
        column_kernel,
        [jax.ShapeDtypeStruct(own.shape, f32), shape, shape],
        [flag, own, from_x, from_y],
        "column",
    )


def finish_kernel(flag_ref, own_ref, a_ref, b_ref, c_ref, d_ref, out_ref):
    half = own_ref.shape[1] // 2
    mine = own_ref[:, pl.ds(pl.multiple_of(flag_ref[0] * half, half), half)]
    total = jnp.where(flag_ref[1] == 1, mine, 0.0)
    for ref in (a_ref, b_ref, c_ref, d_ref):
        total = total + ref[...].astype(f32)
    out_ref[...] = total.T.astype(bf16)


def finish(flags, own, received):
    shape = jax.ShapeDtypeStruct((own.shape[1] // 2, own.shape[0]), bf16)
    return small_call(finish_kernel, shape, [flags, own] + received, "finish")


def pair_kernel(core_ref, own_ref, other_ref, out_ref):
    half = own_ref.shape[1]
    out_ref[:, pl.ds(pl.multiple_of(core_ref[0] * half, half), half)] = own_ref[...]
    out_ref[:, pl.ds(pl.multiple_of((1 - core_ref[0]) * half, half), half)] = other_ref[...]


def pair(core, own, other):
    shape = jax.ShapeDtypeStruct((own.shape[0], 2 * own.shape[1]), own.dtype)
    return small_call(pair_kernel, shape, [core, own, other], "pair")


def chip_plan(token_ids, embed, w_in, taps, rates, residues, cotangent):
    vocab_size, width = embed.shape
    tok_half = token_ids.shape[0]
    toks = 2 * tok_half
    chan_half = width // 2
    spot = lax.axis_index("fsdp")
    core = lax.axis_index("ctx")
    z, y, x = spot // 4, (spot // 2) % 2, spot % 2
    first = core == 0
    place = jnp.where(first, z, 3 - z)
    inner = place < 2

    def table(*entries):
        return jnp.stack([jnp.asarray(e, jnp.int32) for e in entries])

    def swap(array):
        return lax.ppermute(array, BOTH, OTHER_CORE)

    def over_x(array):
        return lax.ppermute(array, BOTH, OVER_X)

    def over_y(array):
        return lax.ppermute(array, BOTH, OVER_Y)

    me = table(core)
    other_ids = swap(token_ids)
    cot_other = swap(lax.dynamic_slice_in_dim(cotangent, (1 - core) * chan_half, chan_half, 1))
    ids = jnp.where(
        first,
        jnp.concatenate([token_ids, other_ids]),
        jnp.concatenate([other_ids, token_ids]),
    )
    onehot = (ids[:, None] == lax.broadcasted_iota(jnp.int32, (toks, vocab_size), 1)).astype(bf16)
    embedded = jnp.dot(onehot, embed, preferred_element_type=f32).astype(bf16)

    got_1 = lax.ppermute(embedded, BOTH, GATHER_Z[0])
    w = load(jnp.transpose(w_in, (1, 0, 2)))
    w = pltpu.with_memory_space_constraint(w, pltpu.VMEM)
    got_1, w = lax.optimization_barrier((got_1, w))
    slot_1 = jnp.where(inner, embedded, got_1)
    got_2 = lax.ppermute(slot_1, BOTH, GATHER_Z[1])
    x_1, y_1 = over_x(slot_1), over_y(slot_1)
    far, near = core * 4, (1 - core) * 4
    base_1 = jnp.where(place % 2 == 0, far, near)
    base_2 = jnp.where(place % 2 == 0, near, far)

    def at(base, y_at, x_at):
        return base + y_at * 2 + x_at

    whole, upper, lower = (0, toks), (0, tok_half), (tok_half, toks)
    slot_2 = jnp.where(inner, got_1, got_2)
    x_2, y_2 = over_x(slot_2), over_y(slot_2)
    sums = project(
        table(at(base_1, y, x), at(base_2, y, x)), [slot_1, slot_2], [whole, whole], w, None, False
    )
    x_1, y_1, sums = lax.optimization_barrier((x_1, y_1, sums))
    d_1a, d_1b = over_y(x_1[:tok_half]), over_x(y_1[tok_half:])
    sums = project(
        table(at(base_1, y, 1 - x), at(base_1, 1 - y, x)), [x_1, y_1], [whole, whole], w, sums, False
    )
    x_2, y_2, sums = lax.optimization_barrier((x_2, y_2, sums))
    d_2a, d_2b = over_y(x_2[:tok_half]), over_x(y_2[tok_half:])
    sums = project(
        table(at(base_2, y, 1 - x), at(base_2, 1 - y, x)), [x_2, y_2], [whole, whole], w, sums, False
    )
    d_2a, d_2b, sums = lax.optimization_barrier((d_2a, d_2b, sums))
    diag_1, diag_2 = at(base_1, 1 - y, 1 - x), at(base_2, 1 - y, 1 - x)
    keep, send = project(
        table(diag_1, diag_1, diag_2, diag_2, core),
        [d_1a, d_1b, d_2a, d_2b],
        [upper, lower, upper, lower],
        w,
        sums,
        True,
    )

    groups = w.shape[0]
    mixed_own, mixed_send, grad_own = mixer(
        me,
        keep,
        swap(send),
        taps.reshape(taps.shape[0] * groups, width),
        rates,
        residues,
        cotangent,
        cot_other,
    )
    grad_other = swap(grad_own)
    mixed_other = swap(mixed_send)

    d_2a, d_2b, d_1a, d_1b = back_project(
        table(diag_2, diag_1, core), w, grad_own, grad_other, width, True, bf16
    )
    y_d2, x_d2 = over_y(d_2a), over_x(d_2b)
    y_d1, x_d1 = over_y(d_1a), over_x(d_1b)
    x_2, y_2, x_1, y_1, own_2, own_1 = back_project(
        table(
            at(base_2, y, 1 - x),
            at(base_2, 1 - y, x),
            at(base_1, y, 1 - x),
            at(base_1, 1 - y, x),
            at(base_2, y, x),
            at(base_1, y, x),
            core,
        ),
        w,
        grad_own,
        grad_other,
        width,
        False,
        f32,
    )
    x_2, y_2 = merge(me, x_2, y_2, y_d2, x_d2)
    x_2, y_2 = over_x(x_2), over_y(y_2)
    x_1, y_1 = merge(me, x_1, y_1, y_d1, x_d1)
    x_1, y_1 = over_x(x_1), over_y(y_1)

    half_2 = jnp.where(inner, core, 1 - core)
    _, send_1, send_2 = column(table(half_2), own_2, x_2, y_2)
    received = [
        lax.ppermute(send_1, BOTH, SCATTER_Z[0]),
        lax.ppermute(send_2, BOTH, SCATTER_Z[1]),
    ]
    mixed = pair(me, mixed_own, mixed_other)
    own, send_1, send_2 = column(table(1 - half_2), own_1, x_1, y_1)
    received += [
        lax.ppermute(send_1, BOTH, SCATTER_Z[2]),
        lax.ppermute(send_2, BOTH, SCATTER_Z[3]),
    ]
    return (mixed, finish(table(core, inner), own, received))


def solution(mesh):
    in_specs = (
        P("ctx"),
        P(None, "fsdp"),
        P("ctx", None, "fsdp"),
        P(None, None, "fsdp"),
        P(None, "fsdp"),
        P(None, "fsdp"),
        P("ctx", "fsdp"),
    )
    out_specs = (P("ctx", "fsdp"), P("ctx", "fsdp"))
    chips = mesh.shape["fsdp"] == 16 and mesh.shape["ctx"] == 2
    return jax.shard_map(
        chip_plan if chips else general_plan,
        mesh=mesh,
        in_specs=in_specs,
        out_specs=out_specs,
        check_vma=False,
    )
```

```python
import functools

import jax
import jax.numpy as jnp
from jax import lax
from jax.experimental import pallas as pl
from jax.experimental.pallas import tpu as pltpu
from jax.sharding import PartitionSpec as P

BOTH = ("fsdp", "ctx")
CHUNKS = 8
f32 = jnp.float32
bf16 = jnp.bfloat16


def from_behind(shard, axis, by):
    count = lax.axis_size(axis)
    pairs = [(i, i + by) for i in range(count) if 0 <= i + by < count]
    return lax.ppermute(shard, axis, pairs)


def pair_combine(earlier, later):
    return (earlier[0] * later[0], later[0] * earlier[1] + later[1])


def modal_states(drive, step_decay):
    tok_count = drive.shape[0]
    factors = jnp.broadcast_to(step_decay[None], (tok_count,) + step_decay.shape)
    inputs = jnp.broadcast_to(drive[:, None, :], factors.shape)
    return lax.associative_scan(pair_combine, (factors, inputs), axis=0)[1]


def short_filter(extended, taps, tok_count):
    rim_width = taps.shape[0] - 1
    filtered = taps[0] * extended[rim_width : rim_width + tok_count]
    for shift_lag in range(1, rim_width + 1):
        filtered = (
            filtered
            + taps[shift_lag] * extended[rim_width - shift_lag : rim_width - shift_lag + tok_count]
        )
    return filtered


def short_adjoint(extended, taps, tok_count):
    rim_width = taps.shape[0] - 1
    result = taps[0] * extended[:tok_count]
    for shift_lag in range(1, rim_width + 1):
        result = result + taps[shift_lag] * extended[shift_lag : shift_lag + tok_count]
    return result


def carry(block_decay, leaving, by):
    def relay_step(turn_index, incoming):
        return from_behind(block_decay * incoming + leaving, "ctx", by)

    return lax.fori_loop(0, lax.axis_size("ctx") - 1, relay_step, jnp.zeros_like(leaving))


def general_plan(token_ids, embed, w_in, taps, rates, residues, cotangent):
    tok_count = token_ids.shape[0]
    vocab_size = embed.shape[0]
    chan_width = embed.shape[1]
    rim_width = taps.shape[0] - 1
    onehot = (
        token_ids[:, None] == lax.broadcasted_iota(jnp.int32, (tok_count, vocab_size), 1)
    ).astype(bf16)
    embedded = jnp.dot(onehot, embed, preferred_element_type=f32).astype(bf16)
    features = lax.all_gather(embedded, "fsdp", axis=1, tiled=True)
    feat_width = features.shape[1]
    whole_w = lax.all_gather(w_in, "ctx", axis=0, tiled=True).reshape(feat_width, 3 * chan_width)
    projected = jnp.dot(features, whole_w, preferred_element_type=f32)
    stored = lax.optimization_barrier(projected.astype(bf16).reshape(tok_count, 3, chan_width))
    before = from_behind(stored[tok_count - rim_width :], "ctx", 1)
    extended = jnp.concatenate([before, stored], axis=0).astype(f32)
    filtered = short_filter(extended, taps, tok_count)
    query_part = filtered[:, 0]
    key_part = filtered[:, 1]
    value_part = filtered[:, 2]
    drive = key_part * value_part
    step_decay = jnp.exp(-rates)
    block_decay = jnp.exp(-rates * tok_count)
    local_states = modal_states(drive, step_decay)
    entering = carry(block_decay, local_states[tok_count - 1], 1)
    offsets = lax.broadcasted_iota(f32, (tok_count, 1, 1), 0)
    states = local_states + jnp.exp(-rates[None] * (offsets + 1.0)) * entering[None]
    long_out = jnp.sum(residues[None] * states, axis=1)
    mixed = (query_part * long_out).astype(bf16)
    incoming = cotangent.astype(f32)
    grad_long = incoming * query_part
    grad_query = incoming * long_out
    back_states = jnp.flip(modal_states(jnp.flip(grad_long, 0), step_decay), 0)
    beyond = carry(block_decay, back_states[0], -1)
    adjoint = back_states + jnp.exp(-rates[None] * (tok_count - offsets)) * beyond[None]
    grad_drive = jnp.sum(residues[None] * adjoint, axis=1)
    grad_filtered = jnp.stack([grad_query, grad_drive * value_part, grad_drive * key_part], axis=1)
    after = from_behind(grad_filtered[:rim_width], "ctx", -1)
    ext_grad = jnp.concatenate([grad_filtered, after], axis=0)
    grad_stored = short_adjoint(ext_grad, taps, tok_count).astype(bf16)
    grad_rows = grad_stored.reshape(tok_count, 3 * chan_width)
    own_rows = lax.psum_scatter(
        lax.dot_general(whole_w, grad_rows, (((1,), (1,)), ((), ())), preferred_element_type=f32),
        "fsdp",
        scatter_dimension=0,
        tiled=True,
    )
    return (mixed, own_rows.T.astype(bf16))


def device_at(z, y, x, core):
    return ((z * 2 + y) * 2 + x) * 2 + core


def everywhere(move):
    pairs = []
    for z in range(4):
        for y in range(2):
            for x in range(2):
                for core in range(2):
                    pairs.append((device_at(z, y, x, core), device_at(*move(z, y, x, core))))
    return pairs


OTHER_CORE = everywhere(lambda z, y, x, core: (z, y, x, 1 - core))
OVER_X = everywhere(lambda z, y, x, core: (z, y, 1 - x, core))
OVER_Y = everywhere(lambda z, y, x, core: (z, 1 - y, x, core))


def along_z(moves):
    pairs = []
    for core in range(2):
        for (place, other), (to_place, to_other) in moves:
            z, to_z = (place, to_place) if core == 0 else (3 - place, 3 - to_place)
            for y in range(2):
                for x in range(2):
                    pairs.append(
                        (
                            device_at(z, y, x, core ^ other),
                            device_at(to_z, y, x, core ^ to_other),
                        )
                    )
    return pairs


GATHER_Z = (
    along_z([((0, 0), (1, 0)), ((1, 0), (0, 0)), ((0, 1), (2, 0)), ((1, 1), (3, 0))]),
    along_z([((1, 0), (2, 0)), ((2, 0), (3, 0))]),
)
SCATTER_Z = (
    along_z([((0, 0), (1, 0)), ((1, 0), (0, 0)), ((2, 0), (1, 1)), ((3, 0), (0, 1))]),
    along_z([((0, 0), (1, 1)), ((1, 0), (0, 1)), ((2, 0), (1, 0)), ((3, 0), (0, 0))]),
    along_z([((0, 0), (0, 1)), ((1, 0), (1, 1)), ((2, 0), (0, 0)), ((3, 0), (1, 0))]),
    along_z([((2, 0), (0, 1)), ((3, 0), (1, 1))]),
)

IN_VMEM = pl.BlockSpec(memory_space=pltpu.VMEM)


def small_call(kernel, out_shape, operands, name, flops=0, scratch=(), limit=8):
    sizes = [o.size * o.dtype.itemsize for o in operands]
    return pl.pallas_call(
        kernel,
        in_specs=[IN_VMEM] * len(operands),
        out_specs=jax.tree.map(lambda _: IN_VMEM, out_shape),
        out_shape=out_shape,
        scratch_shapes=list(scratch),
        compiler_params=pltpu.CompilerParams(vmem_limit_bytes=limit * 1024 * 1024),
        cost_estimate=pl.CostEstimate(
            flops=flops, bytes_accessed=min(sum(sizes), 8 * 1024 * 1024), transcendentals=0
        ),
        name=name,
    )(*operands)


def here():
    spot = lax.axis_index("fsdp")
    return spot >> 2, (spot >> 1) & 1, spot & 1, lax.axis_index("ctx")


def is_inner():
    z, _, _, core = here()
    return core == (z >> 1)


def block_at(slot, far_y, far_x):
    z, y, x, _ = here()
    along = (z & 1) if slot == 1 else 1 - (z & 1)
    return along * 4 + (1 - y if far_y else y) * 2 + (1 - x if far_x else x)


def embed_kernel(own_ref, other_ref, table_ref, cot_ref, out_ref, cot_out_ref):
    vocab = table_ref.shape[0]
    half = own_ref.shape[1]
    chan_half = cot_out_ref.shape[1]
    _, _, _, core = here()
    for ref, side in ((own_ref, core), (other_ref, 1 - core)):
        across = jnp.broadcast_to(ref[...].astype(f32), (half, half)).T
        lane = lax.broadcasted_iota(jnp.int32, (half, half), 1).astype(f32)
        picks = [(across == lane + float(first)).astype(f32) for first in range(0, vocab, half)]
        rows = jnp.dot(
            jnp.concatenate(picks, axis=1).astype(bf16), table_ref[...], preferred_element_type=f32
        )
        out_ref[pl.ds(pl.multiple_of(side * half, half), half), :] = rows.astype(bf16)
    cot_out_ref[...] = cot_ref[:, pl.ds(pl.multiple_of((1 - core) * chan_half, chan_half), chan_half)]


def embed_rows(own_ids, other_ids, table, cotangent):
    toks, width = 2 * own_ids.shape[1], table.shape[1]
    return small_call(
        embed_kernel,
        [
            jax.ShapeDtypeStruct((toks, width), bf16),
            jax.ShapeDtypeStruct((cotangent.shape[0], cotangent.shape[1] // 2), bf16),
        ],
        [own_ids, other_ids, table, cotangent],
        "embed_rows",
        2 * toks * table.shape[0] * width,
    )


def choose_kernel(inner_ref, outer_ref, out_ref):
    @pl.when(is_inner())
    def _():
        out_ref[...] = inner_ref[...]

    @pl.when(jnp.logical_not(is_inner()))
    def _():
        out_ref[...] = outer_ref[...]


def choose(inner, outer):
    return small_call(
        choose_kernel, jax.ShapeDtypeStruct(inner.shape, inner.dtype), [inner, outer], "choose"
    )


def load_kernel(w_ref, out_ref, sem):
    copy = pltpu.make_async_copy(w_ref, out_ref, sem)
    copy.start()
    copy.wait()


def load(w):
    return pl.pallas_call(
        load_kernel,
        in_specs=[pl.BlockSpec(memory_space=pltpu.HBM)],
        out_specs=IN_VMEM,
        out_shape=pltpu.VMEM(w.shape, w.dtype),
        scratch_shapes=[pltpu.SemaphoreType.DMA],
        compiler_params=pltpu.CompilerParams(vmem_limit_bytes=2 * 1024 * 1024),
        cost_estimate=pl.CostEstimate(
            flops=0, bytes_accessed=2 * w.size * w.dtype.itemsize, transcendentals=0
        ),
        name="load",
    )(pltpu.with_memory_space_constraint(w, pltpu.HBM))


def project_kernel(blocks, has_base, last, w_ref, *refs):
    count = len(blocks)
    acts = refs[:count]
    groups, _, chans = w_ref.shape
    toks, width = acts[0].shape
    if last:
        keep_ref, send_ref, total_ref = refs[-3:]
    else:
        total_ref = refs[-1]
    starts = [pl.multiple_of(block_at(*block) * width, width) for block in blocks]
    for g in range(groups):
        total = refs[count][g] if has_base else None
        for start, act in zip(starts, acts):
            term = jnp.dot(act[...], w_ref[g, pl.ds(start, width), :], preferred_element_type=f32)
            total = term if total is None else total + term
        total_ref[g] = total
    if last:
        half = chans // 2
        _, _, _, core = here()
        keep_ref[...] = total_ref[:, :, pl.ds(pl.multiple_of(core * half, half), half)]
        send_ref[...] = total_ref[:, :, pl.ds(pl.multiple_of((1 - core) * half, half), half)]


def project(blocks, acts, w, base, last):
    groups, _, chans = w.shape
    toks, width = acts[0].shape
    total = jax.ShapeDtypeStruct((groups, toks, chans), f32)
    half = jax.ShapeDtypeStruct((groups, toks, chans // 2), f32)
    return small_call(
        functools.partial(project_kernel, blocks, base is not None, last),
        [half, half] if last else total,
        [w] + list(acts) + ([] if base is None else [base]),
        "project",
        2 * len(acts) * groups * width * chans * toks,
        [pltpu.VMEM(total.shape, f32)] if last else [],
        16,
    )


def shifted(values, by):
    place = lax.broadcasted_iota(jnp.int32, values.shape, 0)
    moved = pltpu.roll(values, by % CHUNKS, 0)
    inside = place >= by if by > 0 else place < CHUNKS + by
    return jnp.where(inside, moved, 0.0)


def mixer_kernel(
    keep_ref,
    other_ref,
    taps_ref,
    rates_ref,
    residues_ref,
    cot_own_ref,
    cot_other_ref,
    mixed_own_ref,
    mixed_send_ref,
    grad_ref,
    flat,
    flat_cot,
    ext,
    filt,
    drive,
    back,
    grad_ext,
):
    groups, toks, chans = keep_ref.shape
    modes = rates_ref.shape[0]
    short = taps_ref.shape[1]
    rim = short - 1
    length = toks // CHUNKS
    lanes = flat.shape[-1]
    wide = (CHUNKS, lanes)
    half = toks // 2
    _, _, _, core = here()

    def row(array, at):
        return jnp.broadcast_to(array[at : at + 1, :], wide)

    def column(c, _):
        some = pl.ds(pl.multiple_of(c * lanes, lanes), lanes)
        whole = pl.ds(pl.multiple_of(core * chans + c * lanes, lanes), lanes)
        own_rows = pl.ds(pl.multiple_of(core * half, half), half)
        other_rows = pl.ds(pl.multiple_of((1 - core) * half, half), half)

        for g in range(groups):
            flat[g] = (keep_ref[g, :, some] + other_ref[g, :, some].astype(f32)).astype(bf16).astype(f32)
        flat_cot[own_rows] = cot_own_ref[:, whole].astype(f32)
        flat_cot[other_rows] = cot_other_ref[:, some].astype(f32)

        for g in range(groups):
            for k in range(length):
                ext[g, rim + k] = flat[g, pl.ds(k, CHUNKS, stride=length), :]
            for k in range(rim):
                ext[g, k] = shifted(ext[g, length + k], 1)

        taps = [taps_ref[g, :, whole] for g in range(groups)]
        tap = [[row(taps[g], j) for g in range(groups)] for j in range(short)]

        def filter_step(k, _):
            parts = []
            for g in range(groups):
                total = tap[0][g] * ext[g, k + rim]
                for j in range(1, short):
                    total = total + tap[j][g] * ext[g, k + rim - j]
                parts.append(total)
                filt[g, k] = total
            drive[k] = parts[1] * parts[2]
            back[k] = parts[0] * flat_cot[pl.ds(k, CHUNKS, stride=length), :]
            return _

        lax.fori_loop(0, length, filter_step, 0, unroll=4)

        rates = rates_ref[:, whole]
        decay_rows = jnp.exp(-rates)
        jump_rows = [jnp.exp(-rates * (length * n)) for n in (1, 2, 4)]
        residue_rows = residues_ref[:, whole]

        def long_filter(source, forward, finish):
            decay = [row(decay_rows, m) for m in range(modes)]

            def place(k):
                return k if forward else length - 1 - k

            def end_step(k, states):
                value = source[place(k)]
                return tuple(decay[m] * states[m] + value for m in range(modes))

            zero = jnp.zeros(wide, f32)
            ends = lax.fori_loop(0, length, end_step, (zero,) * modes, unroll=8)
            entering = []
            sign = 1 if forward else -1
            for m in range(modes):
                carried = ends[m]
                for jump, by in zip(jump_rows, (1, 2, 4)):
                    carried = carried + row(jump, m) * shifted(carried, sign * by)
                entering.append(shifted(carried, sign))

            def out_step(k, states):
                value = source[place(k)]
                states = tuple(decay[m] * states[m] + value for m in range(modes))
                terms = [row(residue_rows, m) * states[m] for m in range(modes)]
                while len(terms) > 1:
                    terms = [a + b for a, b in zip(terms[::2], terms[1::2])]
                finish(place(k), terms[0])
                return states

            lax.fori_loop(0, length, out_step, tuple(entering), unroll=4)

        def finish_forward(k, total):
            flat[0, pl.ds(k, CHUNKS, stride=length), :] = filt[0, k] * total
            grad_ext[0, k] = flat_cot[pl.ds(k, CHUNKS, stride=length), :] * total

        def finish_backward(k, total):
            grad_ext[1, k] = total * filt[2, k]
            grad_ext[2, k] = total * filt[1, k]

        long_filter(drive, True, finish_forward)
        mixed_own_ref[:, some] = flat[0, own_rows].astype(bf16)
        mixed_send_ref[:, some] = flat[0, other_rows].astype(bf16)
        long_filter(back, False, finish_backward)

        for g in range(groups):
            for k in range(rim):
                grad_ext[g, length + k] = shifted(grad_ext[g, k], -1)

        def adjoint_step(k, _):
            for g in range(groups):
                total = tap[0][g] * grad_ext[g, k]
                for j in range(1, short):
                    total = total + tap[j][g] * grad_ext[g, k + j]
                flat[g, pl.ds(k, CHUNKS, stride=length), :] = total
            return _

        lax.fori_loop(0, length, adjoint_step, 0, unroll=4)
        for g in range(groups):
            grad_ref[g, some, :] = flat[g].T.astype(bf16)
        return _

    lax.fori_loop(0, chans // lanes, column, 0)


def mixer(keep, other, taps, rates, residues, cot_own, cot_other):
    groups, toks, chans = keep.shape
    modes = rates.shape[0]
    rim = taps.shape[1] - 1
    lanes = 128
    length = toks // CHUNKS
    return small_call(
        mixer_kernel,
        [
            jax.ShapeDtypeStruct((toks // 2, chans), bf16),
            jax.ShapeDtypeStruct((toks // 2, chans), bf16),
            jax.ShapeDtypeStruct((groups, chans, toks), bf16),
        ],
        [keep, other, taps, rates, residues, cot_own, cot_other],
        "mixer",
        12 * modes * toks * chans,
        [
            pltpu.VMEM((groups, toks, lanes), f32),
            pltpu.VMEM((toks, lanes), f32),
            pltpu.VMEM((groups, length + rim, CHUNKS, lanes), f32),
            pltpu.VMEM((groups, length, CHUNKS, lanes), f32),
            pltpu.VMEM((length, CHUNKS, lanes), f32),
            pltpu.VMEM((length, CHUNKS, lanes), f32),
            pltpu.VMEM((groups, length + rim, CHUNKS, lanes), f32),
        ],
    )


def back_kernel(blocks, w_ref, own_ref, other_ref, *out_refs):
    groups, half, _ = own_ref.shape
    width = out_refs[0].shape[0]
    _, _, _, core = here()
    own_at = pl.multiple_of(core * half, half)
    other_at = pl.multiple_of((1 - core) * half, half)
    for block, out in zip(blocks, out_refs):
        start = pl.multiple_of(block_at(*block) * width, width)
        total = None
        for g in range(groups):
            for ref, at in ((own_ref, own_at), (other_ref, other_at)):
                term = jnp.dot(
                    w_ref[g, pl.ds(start, width), pl.ds(at, half)],
                    ref[g],
                    preferred_element_type=f32,
                )
                total = term if total is None else total + term
        out[...] = total.astype(out.dtype)


def back_project(blocks, dtypes, w, own, other, width):
    groups, half, toks = own.shape
    return small_call(
        functools.partial(back_kernel, blocks),
        [jax.ShapeDtypeStruct((width, toks), dtype) for dtype in dtypes],
        [w, own, other],
        "back_project",
        4 * len(blocks) * groups * width * half * toks,
        (),
        16,
    )


def merge_kernel(part_ref, got_ref, out_ref):
    out_ref[...] = (part_ref[...] + got_ref[...].astype(f32)).astype(bf16)


def merge(part, got):
    return small_call(merge_kernel, jax.ShapeDtypeStruct(part.shape, bf16), [part, got], "merge")


def column_kernel(slot, own_ref, x_ref, y_ref, total_ref, one_ref, two_ref):
    half = own_ref.shape[1] // 2
    total_ref[...] = own_ref[...] + x_ref[...].astype(f32) + y_ref[...].astype(f32)
    z = here()[0]
    flag = (z >> 1) if slot == 2 else 1 - (z >> 1)
    one_ref[...] = total_ref[:, pl.ds(pl.multiple_of(flag * half, half), half)].astype(bf16)
    two_ref[...] = total_ref[:, pl.ds(pl.multiple_of((1 - flag) * half, half), half)].astype(bf16)


def column(slot, own, from_x, from_y):
    shape = jax.ShapeDtypeStruct((own.shape[0], own.shape[1] // 2), bf16)
    return small_call(
        functools.partial(column_kernel, slot),
        [jax.ShapeDtypeStruct(own.shape, f32), shape, shape],
        [own, from_x, from_y],
        "column",
    )


def finish_kernel(own_ref, a_ref, b_ref, c_ref, d_ref, out_ref):
    half = own_ref.shape[1] // 2
    core = here()[3]
    mine = own_ref[:, pl.ds(pl.multiple_of(core * half, half), half)]
    total = jnp.where(is_inner(), mine, 0.0)
    for ref in (a_ref, b_ref, c_ref, d_ref):
        total = total + ref[...].astype(f32)
    out_ref[...] = total.T.astype(bf16)


def finish(own, received):
    shape = jax.ShapeDtypeStruct((own.shape[1] // 2, own.shape[0]), bf16)
    return small_call(finish_kernel, shape, [own] + received, "finish")


def pair_kernel(own_ref, other_ref, out_ref):
    half = own_ref.shape[1]
    core = here()[3]
    out_ref[:, pl.ds(pl.multiple_of(core * half, half), half)] = own_ref[...]
    out_ref[:, pl.ds(pl.multiple_of((1 - core) * half, half), half)] = other_ref[...]


def pair(own, other):
    shape = jax.ShapeDtypeStruct((own.shape[0], 2 * own.shape[1]), own.dtype)
    return small_call(pair_kernel, shape, [own, other], "pair")


def chip_plan(token_ids, embed, w_in, taps, rates, residues, cotangent):
    width = embed.shape[1]

    def swap(array):
        return lax.ppermute(array, BOTH, OTHER_CORE)

    def over_x(array):
        return lax.ppermute(array, BOTH, OVER_X)

    def over_y(array):
        return lax.ppermute(array, BOTH, OVER_Y)

    own_ids = token_ids.reshape(1, -1)
    embedded, cot_send = embed_rows(own_ids, swap(own_ids), embed, cotangent)
    cot_other = swap(cot_send)

    got_1 = lax.ppermute(embedded, BOTH, GATHER_Z[0])
    w = load(jnp.transpose(w_in, (1, 0, 2)))
    w = pltpu.with_memory_space_constraint(w, pltpu.VMEM)
    got_1, cot_other, w = lax.optimization_barrier((got_1, cot_other, w))
    slot_1 = choose(embedded, got_1)
    got_2 = lax.ppermute(slot_1, BOTH, GATHER_Z[1])
    x_1, y_1 = over_x(slot_1), over_y(slot_1)
    slot_2 = choose(got_1, got_2)
    x_2, y_2 = over_x(slot_2), over_y(slot_2)
    sums = project([(1, 0, 0), (2, 0, 0)], [slot_1, slot_2], w, None, False)
    x_1, y_1, sums = lax.optimization_barrier((x_1, y_1, sums))
    d_1 = over_y(x_1)
    sums = project([(1, 0, 1), (1, 1, 0)], [x_1, y_1], w, sums, False)
    x_2, y_2, sums = lax.optimization_barrier((x_2, y_2, sums))
    d_2 = over_x(y_2)
    sums = project([(2, 0, 1), (2, 1, 0)], [x_2, y_2], w, sums, False)
    d_1, d_2, sums = lax.optimization_barrier((d_1, d_2, sums))
    keep, send = project([(1, 1, 1), (2, 1, 1)], [d_1, d_2], w, sums, True)

    mixed_own, mixed_send, grad_own = mixer(
        keep, swap(send), jnp.transpose(taps, (1, 0, 2)), rates, residues, cotangent, cot_other
    )
    grad_other = swap(grad_own)
    mixed_other = swap(mixed_send)

    d_2, d_1 = back_project([(2, 1, 1), (1, 1, 1)], [bf16] * 2, w, grad_own, grad_other, width)
    d_2, d_1 = over_x(d_2), over_y(d_1)
    x_2, y_2, x_1, y_1, own_2, own_1 = back_project(
        [(2, 0, 1), (2, 1, 0), (1, 0, 1), (1, 1, 0), (2, 0, 0), (1, 0, 0)],
        [bf16, f32, f32, bf16, f32, f32],
        w,
        grad_own,
        grad_other,
        width,
    )
    x_2, y_2 = over_x(x_2), over_y(merge(y_2, d_2))
    x_1, y_1 = over_x(merge(x_1, d_1)), over_y(y_1)
    _, send_1, send_2 = column(2, own_2, x_2, y_2)
    received = [
        lax.ppermute(send_1, BOTH, SCATTER_Z[0]),
        lax.ppermute(send_2, BOTH, SCATTER_Z[1]),
    ]
    mixed = pair(mixed_own, mixed_other)
    own, send_1, send_2 = column(1, own_1, x_1, y_1)
    received += [
        lax.ppermute(send_1, BOTH, SCATTER_Z[2]),
        lax.ppermute(send_2, BOTH, SCATTER_Z[3]),
    ]
    return (mixed, finish(own, received))


def solution(mesh):
    in_specs = (
        P("ctx"),
        P(None, "fsdp"),
        P("ctx", None, "fsdp"),
        P(None, None, "fsdp"),
        P(None, "fsdp"),
        P(None, "fsdp"),
        P("ctx", "fsdp"),
    )
    out_specs = (P("ctx", "fsdp"), P("ctx", "fsdp"))
    chips = mesh.shape["fsdp"] == 16 and mesh.shape["ctx"] == 2
    return jax.shard_map(
        chip_plan if chips else general_plan,
        mesh=mesh,
        in_specs=in_specs,
        out_specs=out_specs,
        check_vma=False,
    )
```

```python
import functools

import jax
import jax.numpy as jnp
from jax import lax
from jax.experimental import pallas as pl
from jax.experimental.pallas import tpu as pltpu
from jax.sharding import PartitionSpec as P

BOTH = ("fsdp", "ctx")
CHUNKS = 8
f32 = jnp.float32
bf16 = jnp.bfloat16


def from_behind(shard, axis, by):
    count = lax.axis_size(axis)
    pairs = [(i, i + by) for i in range(count) if 0 <= i + by < count]
    return lax.ppermute(shard, axis, pairs)


def pair_combine(earlier, later):
    return (earlier[0] * later[0], later[0] * earlier[1] + later[1])


def modal_states(drive, step_decay):
    tok_count = drive.shape[0]
    factors = jnp.broadcast_to(step_decay[None], (tok_count,) + step_decay.shape)
    inputs = jnp.broadcast_to(drive[:, None, :], factors.shape)
    return lax.associative_scan(pair_combine, (factors, inputs), axis=0)[1]


def short_filter(extended, taps, tok_count):
    rim_width = taps.shape[0] - 1
    filtered = taps[0] * extended[rim_width : rim_width + tok_count]
    for shift_lag in range(1, rim_width + 1):
        filtered = (
            filtered
            + taps[shift_lag] * extended[rim_width - shift_lag : rim_width - shift_lag + tok_count]
        )
    return filtered


def short_adjoint(extended, taps, tok_count):
    rim_width = taps.shape[0] - 1
    result = taps[0] * extended[:tok_count]
    for shift_lag in range(1, rim_width + 1):
        result = result + taps[shift_lag] * extended[shift_lag : shift_lag + tok_count]
    return result


def carry(block_decay, leaving, by):
    def relay_step(turn_index, incoming):
        return from_behind(block_decay * incoming + leaving, "ctx", by)

    return lax.fori_loop(0, lax.axis_size("ctx") - 1, relay_step, jnp.zeros_like(leaving))


def general_plan(token_ids, embed, w_in, taps, rates, residues, cotangent):
    tok_count = token_ids.shape[0]
    vocab_size = embed.shape[0]
    chan_width = embed.shape[1]
    rim_width = taps.shape[0] - 1
    onehot = (
        token_ids[:, None] == lax.broadcasted_iota(jnp.int32, (tok_count, vocab_size), 1)
    ).astype(bf16)
    embedded = jnp.dot(onehot, embed, preferred_element_type=f32).astype(bf16)
    features = lax.all_gather(embedded, "fsdp", axis=1, tiled=True)
    feat_width = features.shape[1]
    whole_w = lax.all_gather(w_in, "ctx", axis=0, tiled=True).reshape(feat_width, 3 * chan_width)
    projected = jnp.dot(features, whole_w, preferred_element_type=f32)
    stored = lax.optimization_barrier(projected.astype(bf16).reshape(tok_count, 3, chan_width))
    before = from_behind(stored[tok_count - rim_width :], "ctx", 1)
    extended = jnp.concatenate([before, stored], axis=0).astype(f32)
    filtered = short_filter(extended, taps, tok_count)
    query_part = filtered[:, 0]
    key_part = filtered[:, 1]
    value_part = filtered[:, 2]
    drive = key_part * value_part
    step_decay = jnp.exp(-rates)
    block_decay = jnp.exp(-rates * tok_count)
    local_states = modal_states(drive, step_decay)
    entering = carry(block_decay, local_states[tok_count - 1], 1)
    offsets = lax.broadcasted_iota(f32, (tok_count, 1, 1), 0)
    states = local_states + jnp.exp(-rates[None] * (offsets + 1.0)) * entering[None]
    long_out = jnp.sum(residues[None] * states, axis=1)
    mixed = (query_part * long_out).astype(bf16)
    incoming = cotangent.astype(f32)
    grad_long = incoming * query_part
    grad_query = incoming * long_out
    back_states = jnp.flip(modal_states(jnp.flip(grad_long, 0), step_decay), 0)
    beyond = carry(block_decay, back_states[0], -1)
    adjoint = back_states + jnp.exp(-rates[None] * (tok_count - offsets)) * beyond[None]
    grad_drive = jnp.sum(residues[None] * adjoint, axis=1)
    grad_filtered = jnp.stack([grad_query, grad_drive * value_part, grad_drive * key_part], axis=1)
    after = from_behind(grad_filtered[:rim_width], "ctx", -1)
    ext_grad = jnp.concatenate([grad_filtered, after], axis=0)
    grad_stored = short_adjoint(ext_grad, taps, tok_count).astype(bf16)
    grad_rows = grad_stored.reshape(tok_count, 3 * chan_width)
    own_rows = lax.psum_scatter(
        lax.dot_general(whole_w, grad_rows, (((1,), (1,)), ((), ())), preferred_element_type=f32),
        "fsdp",
        scatter_dimension=0,
        tiled=True,
    )
    return (mixed, own_rows.T.astype(bf16))


def device_at(z, y, x, core):
    return ((z * 2 + y) * 2 + x) * 2 + core


def everywhere(move):
    pairs = []
    for z in range(4):
        for y in range(2):
            for x in range(2):
                for core in range(2):
                    pairs.append((device_at(z, y, x, core), device_at(*move(z, y, x, core))))
    return pairs


OTHER_CORE = everywhere(lambda z, y, x, core: (z, y, x, 1 - core))
OVER_X = everywhere(lambda z, y, x, core: (z, y, 1 - x, core))
OVER_Y = everywhere(lambda z, y, x, core: (z, 1 - y, x, core))


def along_z(moves):
    pairs = []
    for core in range(2):
        for (place, other), (to_place, to_other) in moves:
            z, to_z = (place, to_place) if core == 0 else (3 - place, 3 - to_place)
            for y in range(2):
                for x in range(2):
                    pairs.append(
                        (
                            device_at(z, y, x, core ^ other),
                            device_at(to_z, y, x, core ^ to_other),
                        )
                    )
    return pairs


def some_cores(move, inner):
    pairs = []
    for z in range(4):
        core = (z >> 1) if inner else 1 - (z >> 1)
        for y in range(2):
            for x in range(2):
                pairs.append((device_at(z, y, x, core), device_at(*move(z, y, x, core))))
    return pairs


OVER_X_INNER = some_cores(lambda z, y, x, core: (z, y, 1 - x, core), True)
OVER_Y_INNER = some_cores(lambda z, y, x, core: (z, 1 - y, x, core), True)
OVER_X_OUTER = some_cores(lambda z, y, x, core: (z, y, 1 - x, core), False)
OVER_Y_OUTER = some_cores(lambda z, y, x, core: (z, 1 - y, x, core), False)
DIAGONAL = some_cores(lambda z, y, x, core: (z, 1 - y, 1 - x, 1 - core), False)
GATHER_Z = along_z([((0, 0), (1, 0)), ((1, 0), (0, 0)), ((0, 1), (2, 0)), ((1, 1), (3, 0))])
GATHER_Z_OUTER = along_z([((1, 1), (2, 0)), ((0, 1), (3, 0))])
SCATTER_Z = (
    along_z([((0, 0), (1, 0)), ((1, 0), (0, 0)), ((2, 0), (1, 1)), ((3, 0), (0, 1))]),
    along_z([((0, 0), (1, 1)), ((1, 0), (0, 1)), ((2, 0), (1, 0)), ((3, 0), (0, 0))]),
    along_z([((0, 0), (0, 1)), ((1, 0), (1, 1)), ((2, 0), (0, 0)), ((3, 0), (1, 0))]),
    along_z([((2, 0), (0, 1)), ((3, 0), (1, 1))]),
)

IN_VMEM = pl.BlockSpec(memory_space=pltpu.VMEM)


def small_call(kernel, out_shape, operands, name, flops=0, scratch=(), limit=8):
    sizes = [o.size * o.dtype.itemsize for o in operands]
    return pl.pallas_call(
        kernel,
        in_specs=[IN_VMEM] * len(operands),
        out_specs=jax.tree.map(lambda _: IN_VMEM, out_shape),
        out_shape=out_shape,
        scratch_shapes=list(scratch),
        compiler_params=pltpu.CompilerParams(vmem_limit_bytes=limit * 1024 * 1024),
        cost_estimate=pl.CostEstimate(
            flops=flops // 64, bytes_accessed=sum(sizes) // 64, transcendentals=0
        ),
        name=name,
    )(*operands)


def here():
    spot = lax.axis_index("fsdp")
    return spot >> 2, (spot >> 1) & 1, spot & 1, lax.axis_index("ctx")


def is_inner():
    z, _, _, core = here()
    return core == (z >> 1)


def block_at(slot, far_y, far_x):
    z, y, x, _ = here()
    along = (z & 1) if slot == 1 else 1 - (z & 1)
    return along * 4 + (1 - y if far_y else y) * 2 + (1 - x if far_x else x)


def embed_kernel(own_ref, other_ref, table_ref, cot_ref, out_ref, cot_out_ref):
    vocab = table_ref.shape[0]
    half = own_ref.shape[1]
    chan_half = cot_out_ref.shape[1]
    _, _, _, core = here()
    for ref, side in ((own_ref, core), (other_ref, 1 - core)):
        across = jnp.broadcast_to(ref[...].astype(f32), (half, half)).T
        lane = lax.broadcasted_iota(jnp.int32, (half, half), 1).astype(f32)
        picks = [(across == lane + float(first)).astype(f32) for first in range(0, vocab, half)]
        rows = jnp.dot(
            jnp.concatenate(picks, axis=1).astype(bf16), table_ref[...], preferred_element_type=f32
        )
        out_ref[pl.ds(pl.multiple_of(side * half, half), half), :] = rows.astype(bf16)
    cot_out_ref[...] = cot_ref[:, pl.ds(pl.multiple_of((1 - core) * chan_half, chan_half), chan_half)]


def embed_rows(own_ids, other_ids, table, cotangent):
    toks, width = 2 * own_ids.shape[1], table.shape[1]
    return small_call(
        embed_kernel,
        [
            jax.ShapeDtypeStruct((toks, width), bf16),
            jax.ShapeDtypeStruct((cotangent.shape[0], cotangent.shape[1] // 2), bf16),
        ],
        [own_ids, other_ids, table, cotangent],
        "embed_rows",
        2 * toks * table.shape[0] * width,
    )


def fetch_kernel(count, *refs):
    copies = [
        pltpu.make_async_copy(source, target, refs[-1].at[n])
        for n, (source, target) in enumerate(zip(refs[:count], refs[count : 2 * count]))
    ]
    for copy in copies:
        copy.start()
    for copy in copies:
        copy.wait()


def fetch(*arrays):
    out = pl.pallas_call(
        functools.partial(fetch_kernel, len(arrays)),
        in_specs=[pl.BlockSpec(memory_space=pltpu.HBM)] * len(arrays),
        out_specs=[IN_VMEM] * len(arrays),
        out_shape=[pltpu.VMEM(array.shape, array.dtype) for array in arrays],
        scratch_shapes=[pltpu.SemaphoreType.DMA((len(arrays),))],
        compiler_params=pltpu.CompilerParams(vmem_limit_bytes=2 * 1024 * 1024),
        cost_estimate=pl.CostEstimate(
            flops=0,
            bytes_accessed=2 * sum(array.size * array.dtype.itemsize for array in arrays),
            transcendentals=0,
        ),
        name="fetch",
    )(*[pltpu.with_memory_space_constraint(array, pltpu.HBM) for array in arrays])
    return [pltpu.with_memory_space_constraint(array, pltpu.VMEM) for array in out]


def project_kernel(inner, outer, count, has_base, last, w_ref, *refs):
    acts = refs[:count]
    groups, _, chans = w_ref.shape
    toks, width = acts[0].shape
    if last:
        keep_ref, send_ref, total_ref = refs[-3:]
    else:
        total_ref = refs[-1]

    def add(entries):
        starts = [pl.multiple_of(block_at(*entry[1:]) * width, width) for entry in entries]
        for g in range(groups):
            total = refs[count][g] if has_base else None
            for start, entry in zip(starts, entries):
                term = jnp.dot(
                    acts[entry[0]][...], w_ref[g, pl.ds(start, width), :], preferred_element_type=f32
                )
                total = term if total is None else total + term
            total_ref[g] = total

    pl.when(is_inner())(lambda: add(inner))
    pl.when(jnp.logical_not(is_inner()))(lambda: add(outer))
    if last:
        half = chans // 2
        core = here()[3]
        keep_ref[...] = total_ref[:, :, pl.ds(pl.multiple_of(core * half, half), half)]
        send_ref[...] = total_ref[:, :, pl.ds(pl.multiple_of((1 - core) * half, half), half)]


def project(acts, inner, outer, w, base, last):
    groups, _, chans = w.shape
    toks, width = acts[0].shape
    total = jax.ShapeDtypeStruct((groups, toks, chans), f32)
    half = jax.ShapeDtypeStruct((groups, toks, chans // 2), f32)
    return small_call(
        functools.partial(project_kernel, inner, outer, len(acts), base is not None, last),
        [half, half] if last else total,
        [w] + list(acts) + ([] if base is None else [base]),
        "project",
        2 * max(len(inner), len(outer)) * groups * width * chans * toks,
        [pltpu.VMEM(total.shape, f32)] if last else [],
        16,
    )


def shifted(values, by):
    place = lax.broadcasted_iota(jnp.int32, values.shape, 0)
    moved = pltpu.roll(values, by % CHUNKS, 0)
    inside = place >= by if by > 0 else place < CHUNKS + by
    return jnp.where(inside, moved, 0.0)


def mixer_kernel(
    keep_ref,
    other_ref,
    taps_ref,
    rates_ref,
    residues_ref,
    cot_own_ref,
    cot_other_ref,
    mixed_own_ref,
    mixed_send_ref,
    grad_ref,
    flat,
    flat_cot,
    ext,
    filt,
    drive,
    back,
    grad_ext,
):
    groups, toks, chans = keep_ref.shape
    modes = rates_ref.shape[0]
    short = taps_ref.shape[1]
    rim = short - 1
    length = toks // CHUNKS
    lanes = flat.shape[-1]
    wide = (CHUNKS, lanes)
    half = toks // 2
    _, _, _, core = here()

    def row(array, at):
        return jnp.broadcast_to(array[at : at + 1, :], wide)

    def column(c, _):
        some = pl.ds(pl.multiple_of(c * lanes, lanes), lanes)
        whole = pl.ds(pl.multiple_of(core * chans + c * lanes, lanes), lanes)
        own_rows = pl.ds(pl.multiple_of(core * half, half), half)
        other_rows = pl.ds(pl.multiple_of((1 - core) * half, half), half)

        for g in range(groups):
            flat[g] = (keep_ref[g, :, some] + other_ref[g, :, some].astype(f32)).astype(bf16).astype(f32)
        flat_cot[own_rows] = cot_own_ref[:, whole].astype(f32)
        flat_cot[other_rows] = cot_other_ref[:, some].astype(f32)

        for g in range(groups):
            for k in range(length):
                ext[g, rim + k] = flat[g, pl.ds(k, CHUNKS, stride=length), :]
            for k in range(rim):
                ext[g, k] = shifted(ext[g, length + k], 1)

        taps = [taps_ref[g, :, whole] for g in range(groups)]
        tap = [[row(taps[g], j) for g in range(groups)] for j in range(short)]

        def filter_step(k, _):
            parts = []
            for g in range(groups):
                total = tap[0][g] * ext[g, k + rim]
                for j in range(1, short):
                    total = total + tap[j][g] * ext[g, k + rim - j]
                parts.append(total)
                filt[g, k] = total
            drive[k] = parts[1] * parts[2]
            back[k] = parts[0] * flat_cot[pl.ds(k, CHUNKS, stride=length), :]
            return _

        lax.fori_loop(0, length, filter_step, 0, unroll=4)

        rates = rates_ref[:, whole]
        decay_rows = jnp.exp(-rates)
        jump_rows = [jnp.exp(-rates * (length * n)) for n in (1, 2, 4)]
        residue_rows = residues_ref[:, whole]

        def long_filter(source, forward, finish):
            decay = [row(decay_rows, m) for m in range(modes)]

            def place(k):
                return k if forward else length - 1 - k

            def end_step(k, states):
                value = source[place(k)]
                return tuple(decay[m] * states[m] + value for m in range(modes))

            zero = jnp.zeros(wide, f32)
            ends = lax.fori_loop(0, length, end_step, (zero,) * modes, unroll=8)
            entering = []
            sign = 1 if forward else -1
            for m in range(modes):
                carried = ends[m]
                for jump, by in zip(jump_rows, (1, 2, 4)):
                    carried = carried + row(jump, m) * shifted(carried, sign * by)
                entering.append(shifted(carried, sign))

            def out_step(k, states):
                value = source[place(k)]
                states = tuple(decay[m] * states[m] + value for m in range(modes))
                terms = [row(residue_rows, m) * states[m] for m in range(modes)]
                while len(terms) > 1:
                    terms = [a + b for a, b in zip(terms[::2], terms[1::2])]
                finish(place(k), terms[0])
                return states

            lax.fori_loop(0, length, out_step, tuple(entering), unroll=4)

        def finish_forward(k, total):
            flat[0, pl.ds(k, CHUNKS, stride=length), :] = filt[0, k] * total
            grad_ext[0, k] = flat_cot[pl.ds(k, CHUNKS, stride=length), :] * total

        def finish_backward(k, total):
            grad_ext[1, k] = total * filt[2, k]
            grad_ext[2, k] = total * filt[1, k]

        long_filter(drive, True, finish_forward)
        mixed_own_ref[:, some] = flat[0, own_rows].astype(bf16)
        mixed_send_ref[:, some] = flat[0, other_rows].astype(bf16)
        long_filter(back, False, finish_backward)

        for g in range(groups):
            for k in range(rim):
                grad_ext[g, length + k] = shifted(grad_ext[g, k], -1)

        def adjoint_step(k, _):
            for g in range(groups):
                total = tap[0][g] * grad_ext[g, k]
                for j in range(1, short):
                    total = total + tap[j][g] * grad_ext[g, k + j]
                flat[g, pl.ds(k, CHUNKS, stride=length), :] = total
            return _

        lax.fori_loop(0, length, adjoint_step, 0, unroll=4)
        for g in range(groups):
            grad_ref[g, some, :] = flat[g].T.astype(bf16)
        return _

    lax.fori_loop(0, chans // lanes, column, 0)


def mixer(keep, other, taps, rates, residues, cot_own, cot_other):
    groups, toks, chans = keep.shape
    modes = rates.shape[0]
    rim = taps.shape[1] - 1
    lanes = 128
    length = toks // CHUNKS
    return small_call(
        mixer_kernel,
        [
            jax.ShapeDtypeStruct((toks // 2, chans), bf16),
            jax.ShapeDtypeStruct((toks // 2, chans), bf16),
            jax.ShapeDtypeStruct((groups, chans, toks), bf16),
        ],
        [keep, other, taps, rates, residues, cot_own, cot_other],
        "mixer",
        12 * modes * toks * chans,
        [
            pltpu.VMEM((groups, toks, lanes), f32),
            pltpu.VMEM((toks, lanes), f32),
            pltpu.VMEM((groups, length + rim, CHUNKS, lanes), f32),
            pltpu.VMEM((groups, length, CHUNKS, lanes), f32),
            pltpu.VMEM((length, CHUNKS, lanes), f32),
            pltpu.VMEM((length, CHUNKS, lanes), f32),
            pltpu.VMEM((groups, length + rim, CHUNKS, lanes), f32),
        ],
    )


def back_kernel(blocks, w_ref, own_ref, other_ref, *out_refs):
    groups, half, _ = own_ref.shape
    width = out_refs[0].shape[0]
    _, _, _, core = here()
    own_at = pl.multiple_of(core * half, half)
    other_at = pl.multiple_of((1 - core) * half, half)
    for block, out in zip(blocks, out_refs):
        start = pl.multiple_of(block_at(*block) * width, width)
        total = None
        for g in range(groups):
            for ref, at in ((own_ref, own_at), (other_ref, other_at)):
                term = jnp.dot(
                    w_ref[g, pl.ds(start, width), pl.ds(at, half)],
                    ref[g],
                    preferred_element_type=f32,
                )
                total = term if total is None else total + term
        out[...] = total.astype(out.dtype)


def back_project(blocks, dtypes, w, own, other, width):
    groups, half, toks = own.shape
    return small_call(
        functools.partial(back_kernel, blocks),
        [jax.ShapeDtypeStruct((width, toks), dtype) for dtype in dtypes],
        [w, own, other],
        "back_project",
        4 * len(blocks) * groups * width * half * toks,
        (),
        16,
    )


def merge_kernel(part_ref, got_ref, out_ref):
    out_ref[...] = (part_ref[...] + got_ref[...].astype(f32)).astype(bf16)


def merge(part, got):
    return small_call(merge_kernel, jax.ShapeDtypeStruct(part.shape, bf16), [part, got], "merge")


def column_kernel(slot, own_ref, x_ref, y_ref, total_ref, one_ref, two_ref):
    half = own_ref.shape[1] // 2
    total_ref[...] = own_ref[...] + x_ref[...].astype(f32) + y_ref[...].astype(f32)
    z = here()[0]
    flag = (z >> 1) if slot == 2 else 1 - (z >> 1)
    one_ref[...] = total_ref[:, pl.ds(pl.multiple_of(flag * half, half), half)].astype(bf16)
    two_ref[...] = total_ref[:, pl.ds(pl.multiple_of((1 - flag) * half, half), half)].astype(bf16)


def column(slot, own, from_x, from_y):
    shape = jax.ShapeDtypeStruct((own.shape[0], own.shape[1] // 2), bf16)
    return small_call(
        functools.partial(column_kernel, slot),
        [jax.ShapeDtypeStruct(own.shape, f32), shape, shape],
        [own, from_x, from_y],
        "column",
    )


def finish_kernel(own_ref, a_ref, b_ref, c_ref, d_ref, out_ref):
    half = own_ref.shape[1] // 2
    core = here()[3]
    mine = own_ref[:, pl.ds(pl.multiple_of(core * half, half), half)]
    total = jnp.where(is_inner(), mine, 0.0)
    for ref in (a_ref, b_ref, c_ref, d_ref):
        total = total + ref[...].astype(f32)
    out_ref[...] = total.T.astype(bf16)


def finish(own, received):
    shape = jax.ShapeDtypeStruct((own.shape[1] // 2, own.shape[0]), bf16)
    return small_call(finish_kernel, shape, [own] + received, "finish")


def pair_kernel(own_ref, other_ref, out_ref):
    half = own_ref.shape[1]
    core = here()[3]
    out_ref[:, pl.ds(pl.multiple_of(core * half, half), half)] = own_ref[...]
    out_ref[:, pl.ds(pl.multiple_of((1 - core) * half, half), half)] = other_ref[...]


def pair(own, other):
    shape = jax.ShapeDtypeStruct((own.shape[0], 2 * own.shape[1]), own.dtype)
    return small_call(pair_kernel, shape, [own, other], "pair")


def chip_plan(token_ids, embed, w_in, taps, rates, residues, cotangent):
    width = embed.shape[1]

    def swap(array):
        return lax.ppermute(array, BOTH, OTHER_CORE)

    def over_x(array):
        return lax.ppermute(array, BOTH, OVER_X)

    def over_y(array):
        return lax.ppermute(array, BOTH, OVER_Y)

    own_ids = token_ids.reshape(1, -1)
    other_ids = swap(own_ids)
    table, own_ids, cot = fetch(embed, own_ids, cotangent)
    embedded, cot_send = embed_rows(own_ids, other_ids, table, cot)

    got_1 = lax.ppermute(embedded, BOTH, GATHER_Z)
    near_x = lax.ppermute(embedded, BOTH, OVER_X_INNER + GATHER_Z_OUTER)
    near_y = lax.ppermute(embedded, BOTH, OVER_Y_INNER)
    near_d = lax.ppermute(embedded, BOTH, DIAGONAL)
    cot_other = swap(cot_send)
    (w,) = fetch(jnp.transpose(w_in, (1, 0, 2)))
    got_1, cot_other, w = lax.optimization_barrier((got_1, cot_other, w))
    x_1, y_1 = over_x(got_1), over_y(got_1)
    got_2 = near_x
    x_2 = lax.ppermute(got_2, BOTH, OVER_X_OUTER)
    y_2 = lax.ppermute(got_2, BOTH, OVER_Y_OUTER)
    sums = project(
        [embedded, near_x, near_y, near_d, got_1],
        [(0, 1, 0, 0), (1, 1, 0, 1), (2, 1, 1, 0), (3, 1, 1, 1), (4, 2, 0, 0)],
        [(4, 1, 0, 0), (1, 2, 0, 0)],
        w,
        None,
        False,
    )
    x_1, y_1, sums = lax.optimization_barrier((x_1, y_1, sums))
    d_1 = over_x(y_1)
    sums = project([x_1, y_1], [(0, 2, 0, 1), (1, 2, 1, 0)], [(0, 1, 0, 1), (1, 1, 1, 0)], w, sums, False)
    x_2, y_2 = lax.optimization_barrier((x_2, y_2))
    d_2 = lax.ppermute(x_2, BOTH, OVER_Y_OUTER)
    d_1, d_2, sums = lax.optimization_barrier((d_1, d_2, sums))
    keep, send = project(
        [x_2, y_2, d_1, d_2],
        [(2, 2, 1, 1)],
        [(0, 2, 0, 1), (1, 2, 1, 0), (2, 1, 1, 1), (3, 2, 1, 1)],
        w,
        sums,
        True,
    )

    mixed_own, mixed_send, grad_own = mixer(
        keep, swap(send), jnp.transpose(taps, (1, 0, 2)), rates, residues, cotangent, cot_other
    )
    grad_other = swap(grad_own)
    mixed_other = swap(mixed_send)

    d_2, d_1 = back_project([(2, 1, 1), (1, 1, 1)], [bf16] * 2, w, grad_own, grad_other, width)
    d_2, d_1 = over_x(d_2), over_y(d_1)
    x_2, y_2, x_1, y_1, own_2, own_1 = back_project(
        [(2, 0, 1), (2, 1, 0), (1, 0, 1), (1, 1, 0), (2, 0, 0), (1, 0, 0)],
        [bf16, f32, f32, bf16, f32, f32],
        w,
        grad_own,
        grad_other,
        width,
    )
    x_2, y_2 = over_x(x_2), over_y(merge(y_2, d_2))
    x_1, y_1 = over_x(merge(x_1, d_1)), over_y(y_1)
    _, send_1, send_2 = column(2, own_2, x_2, y_2)
    received = [
        lax.ppermute(send_1, BOTH, SCATTER_Z[0]),
        lax.ppermute(send_2, BOTH, SCATTER_Z[1]),
    ]
    mixed = pair(mixed_own, mixed_other)
    own, send_1, send_2 = column(1, own_1, x_1, y_1)
    received += [
        lax.ppermute(send_1, BOTH, SCATTER_Z[2]),
        lax.ppermute(send_2, BOTH, SCATTER_Z[3]),
    ]
    return (mixed, finish(own, received))


def solution(mesh):
    in_specs = (
        P("ctx"),
        P(None, "fsdp"),
        P("ctx", None, "fsdp"),
        P(None, None, "fsdp"),
        P(None, "fsdp"),
        P(None, "fsdp"),
        P("ctx", "fsdp"),
    )
    out_specs = (P("ctx", "fsdp"), P("ctx", "fsdp"))
    chips = mesh.shape["fsdp"] == 16 and mesh.shape["ctx"] == 2
    return jax.shard_map(
        chip_plan if chips else general_plan,
        mesh=mesh,
        in_specs=in_specs,
        out_specs=out_specs,
        check_vma=False,
    )
```

```python
import functools

import jax
import jax.numpy as jnp
from jax import lax
from jax.experimental import pallas as pl
from jax.experimental.pallas import tpu as pltpu
from jax.sharding import PartitionSpec as P

BOTH = ("fsdp", "ctx")
CHUNKS = 8
f32 = jnp.float32
bf16 = jnp.bfloat16


def from_behind(shard, axis, by):
    count = lax.axis_size(axis)
    pairs = [(i, i + by) for i in range(count) if 0 <= i + by < count]
    return lax.ppermute(shard, axis, pairs)


def pair_combine(earlier, later):
    return (earlier[0] * later[0], later[0] * earlier[1] + later[1])


def modal_states(drive, step_decay):
    tok_count = drive.shape[0]
    factors = jnp.broadcast_to(step_decay[None], (tok_count,) + step_decay.shape)
    inputs = jnp.broadcast_to(drive[:, None, :], factors.shape)
    return lax.associative_scan(pair_combine, (factors, inputs), axis=0)[1]


def short_filter(extended, taps, tok_count):
    rim_width = taps.shape[0] - 1
    filtered = taps[0] * extended[rim_width : rim_width + tok_count]
    for shift_lag in range(1, rim_width + 1):
        filtered = (
            filtered
            + taps[shift_lag] * extended[rim_width - shift_lag : rim_width - shift_lag + tok_count]
        )
    return filtered


def short_adjoint(extended, taps, tok_count):
    rim_width = taps.shape[0] - 1
    result = taps[0] * extended[:tok_count]
    for shift_lag in range(1, rim_width + 1):
        result = result + taps[shift_lag] * extended[shift_lag : shift_lag + tok_count]
    return result


def carry(block_decay, leaving, by):
    def relay_step(turn_index, incoming):
        return from_behind(block_decay * incoming + leaving, "ctx", by)

    return lax.fori_loop(0, lax.axis_size("ctx") - 1, relay_step, jnp.zeros_like(leaving))


def general_plan(token_ids, embed, w_in, taps, rates, residues, cotangent):
    tok_count = token_ids.shape[0]
    vocab_size = embed.shape[0]
    chan_width = embed.shape[1]
    rim_width = taps.shape[0] - 1
    onehot = (
        token_ids[:, None] == lax.broadcasted_iota(jnp.int32, (tok_count, vocab_size), 1)
    ).astype(bf16)
    embedded = jnp.dot(onehot, embed, preferred_element_type=f32).astype(bf16)
    features = lax.all_gather(embedded, "fsdp", axis=1, tiled=True)
    feat_width = features.shape[1]
    whole_w = lax.all_gather(w_in, "ctx", axis=0, tiled=True).reshape(feat_width, 3 * chan_width)
    projected = jnp.dot(features, whole_w, preferred_element_type=f32)
    stored = lax.optimization_barrier(projected.astype(bf16).reshape(tok_count, 3, chan_width))
    before = from_behind(stored[tok_count - rim_width :], "ctx", 1)
    extended = jnp.concatenate([before, stored], axis=0).astype(f32)
    filtered = short_filter(extended, taps, tok_count)
    query_part = filtered[:, 0]
    key_part = filtered[:, 1]
    value_part = filtered[:, 2]
    drive = key_part * value_part
    step_decay = jnp.exp(-rates)
    block_decay = jnp.exp(-rates * tok_count)
    local_states = modal_states(drive, step_decay)
    entering = carry(block_decay, local_states[tok_count - 1], 1)
    offsets = lax.broadcasted_iota(f32, (tok_count, 1, 1), 0)
    states = local_states + jnp.exp(-rates[None] * (offsets + 1.0)) * entering[None]
    long_out = jnp.sum(residues[None] * states, axis=1)
    mixed = (query_part * long_out).astype(bf16)
    incoming = cotangent.astype(f32)
    grad_long = incoming * query_part
    grad_query = incoming * long_out
    back_states = jnp.flip(modal_states(jnp.flip(grad_long, 0), step_decay), 0)
    beyond = carry(block_decay, back_states[0], -1)
    adjoint = back_states + jnp.exp(-rates[None] * (tok_count - offsets)) * beyond[None]
    grad_drive = jnp.sum(residues[None] * adjoint, axis=1)
    grad_filtered = jnp.stack([grad_query, grad_drive * value_part, grad_drive * key_part], axis=1)
    after = from_behind(grad_filtered[:rim_width], "ctx", -1)
    ext_grad = jnp.concatenate([grad_filtered, after], axis=0)
    grad_stored = short_adjoint(ext_grad, taps, tok_count).astype(bf16)
    grad_rows = grad_stored.reshape(tok_count, 3 * chan_width)
    own_rows = lax.psum_scatter(
        lax.dot_general(whole_w, grad_rows, (((1,), (1,)), ((), ())), preferred_element_type=f32),
        "fsdp",
        scatter_dimension=0,
        tiled=True,
    )
    return (mixed, own_rows.T.astype(bf16))


def device_at(z, y, x, core):
    return ((z * 2 + y) * 2 + x) * 2 + core


def everywhere(move):
    pairs = []
    for z in range(4):
        for y in range(2):
            for x in range(2):
                for core in range(2):
                    pairs.append((device_at(z, y, x, core), device_at(*move(z, y, x, core))))
    return pairs


OTHER_CORE = everywhere(lambda z, y, x, core: (z, y, x, 1 - core))
OVER_X = everywhere(lambda z, y, x, core: (z, y, 1 - x, core))
OVER_Y = everywhere(lambda z, y, x, core: (z, 1 - y, x, core))
OVER_XY = everywhere(lambda z, y, x, core: (z, 1 - y, 1 - x, core))


def along_z(moves):
    pairs = []
    for core in range(2):
        for (place, other), (to_place, to_other) in moves:
            z, to_z = (place, to_place) if core == 0 else (3 - place, 3 - to_place)
            for y in range(2):
                for x in range(2):
                    pairs.append(
                        (
                            device_at(z, y, x, core ^ other),
                            device_at(to_z, y, x, core ^ to_other),
                        )
                    )
    return pairs


def some_cores(move, inner):
    pairs = []
    for z in range(4):
        core = (z >> 1) if inner else 1 - (z >> 1)
        for y in range(2):
            for x in range(2):
                pairs.append((device_at(z, y, x, core), device_at(*move(z, y, x, core))))
    return pairs


OVER_X_INNER = some_cores(lambda z, y, x, core: (z, y, 1 - x, core), True)
OVER_Y_INNER = some_cores(lambda z, y, x, core: (z, 1 - y, x, core), True)
OVER_X_OUTER = some_cores(lambda z, y, x, core: (z, y, 1 - x, core), False)
OVER_Y_OUTER = some_cores(lambda z, y, x, core: (z, 1 - y, x, core), False)
OVER_XY_OUTER = some_cores(lambda z, y, x, core: (z, 1 - y, 1 - x, core), False)
DIAGONAL = some_cores(lambda z, y, x, core: (z, 1 - y, 1 - x, 1 - core), False)
GATHER_Z = along_z([((0, 0), (1, 0)), ((1, 0), (0, 0)), ((0, 1), (2, 0)), ((1, 1), (3, 0))])
GATHER_Z_OUTER = along_z([((1, 1), (2, 0)), ((0, 1), (3, 0))])
SCATTER_Z = (
    along_z([((0, 0), (1, 0)), ((1, 0), (0, 0)), ((2, 0), (1, 1)), ((3, 0), (0, 1))]),
    along_z([((0, 0), (1, 1)), ((1, 0), (0, 1)), ((2, 0), (1, 0)), ((3, 0), (0, 0))]),
    along_z([((0, 0), (0, 1)), ((1, 0), (1, 1)), ((2, 0), (0, 0)), ((3, 0), (1, 0))]),
    along_z([((2, 0), (0, 1)), ((3, 0), (1, 1))]),
)

IN_VMEM = pl.BlockSpec(memory_space=pltpu.VMEM)


def small_call(kernel, out_shape, operands, name, flops=0, scratch=(), limit=8):
    sizes = [o.size * o.dtype.itemsize for o in operands]
    return pl.pallas_call(
        kernel,
        in_specs=[IN_VMEM] * len(operands),
        out_specs=jax.tree.map(lambda _: IN_VMEM, out_shape),
        out_shape=out_shape,
        scratch_shapes=list(scratch),
        compiler_params=pltpu.CompilerParams(vmem_limit_bytes=limit * 1024 * 1024),
        cost_estimate=pl.CostEstimate(
            flops=flops // 64, bytes_accessed=sum(sizes) // 64, transcendentals=0
        ),
        name=name,
    )(*operands)


def here():
    spot = lax.axis_index("fsdp")
    return spot >> 2, (spot >> 1) & 1, spot & 1, lax.axis_index("ctx")


def is_inner():
    z, _, _, core = here()
    return core == (z >> 1)


def block_at(slot, far_y, far_x):
    z, y, x, _ = here()
    along = (z & 1) if slot == 1 else 1 - (z & 1)
    return along * 4 + (1 - y if far_y else y) * 2 + (1 - x if far_x else x)


def embed_kernel(own_ref, other_ref, table_ref, out_ref):
    vocab = table_ref.shape[0]
    half = own_ref.shape[1]
    core = here()[3]
    for ref, side in ((own_ref, core), (other_ref, 1 - core)):
        across = jnp.broadcast_to(ref[...].astype(f32), (half, half)).T
        lane = lax.broadcasted_iota(jnp.int32, (half, half), 1).astype(f32)
        picks = [(across == lane + float(first)).astype(f32) for first in range(0, vocab, half)]
        rows = jnp.dot(
            jnp.concatenate(picks, axis=1).astype(bf16), table_ref[...], preferred_element_type=f32
        )
        out_ref[pl.ds(pl.multiple_of(side * half, half), half), :] = rows.astype(bf16)


def embed_rows(own_ids, other_ids, table):
    toks, width = 2 * own_ids.shape[1], table.shape[1]
    return small_call(
        embed_kernel,
        jax.ShapeDtypeStruct((toks, width), bf16),
        [own_ids, other_ids, table],
        "embed_rows",
        2 * toks * table.shape[0] * width,
    )


def fetch_kernel(ids_ref, table_ref, ids_out, table_out, sems):
    copies = [
        pltpu.make_async_copy(ids_ref, ids_out, sems.at[0]),
        pltpu.make_async_copy(table_ref, table_out, sems.at[1]),
    ]
    for copy in copies:
        copy.start()
    for copy in copies:
        copy.wait()


def in_hbm(array):
    return pltpu.with_memory_space_constraint(array, pltpu.HBM)


def in_vmem(array):
    return pltpu.with_memory_space_constraint(array, pltpu.VMEM)


def fetch(ids, table):
    out = pl.pallas_call(
        fetch_kernel,
        in_specs=[pl.BlockSpec(memory_space=pltpu.HBM)] * 2,
        out_specs=[IN_VMEM] * 2,
        out_shape=[pltpu.VMEM(ids.shape, ids.dtype), pltpu.VMEM(table.shape, bf16)],
        scratch_shapes=[pltpu.SemaphoreType.DMA((2,))],
        compiler_params=pltpu.CompilerParams(vmem_limit_bytes=2 * 1024 * 1024),
        cost_estimate=pl.CostEstimate(
            flops=0, bytes_accessed=4 * table.size, transcendentals=0
        ),
        name="fetch",
    )(in_hbm(ids), in_hbm(table))
    return [in_vmem(array) for array in out]


def first_kernel(inner, outer, count, w_ref, *refs):
    acts = refs[:count]
    total_ref, w_out, sems = refs[count:]
    groups, rows, _ = w_out.shape
    width = acts[0].shape[1]
    order = [(slot, far_y, far_x) for slot in (1, 2) for far_y in (0, 1) for far_x in (0, 1)]
    spans = [
        pl.ds(pl.multiple_of(block_at(*block) * width, width), width) for block in order
    ]
    copies = [
        pltpu.make_async_copy(w_ref.at[:, span, :], w_out.at[:, span, :], sems.at[n])
        for n, span in enumerate(spans)
    ]
    for copy in copies:
        copy.start()

    def add(entries):
        met = set()
        for n, entry in enumerate(entries):
            block = order.index(entry[1:])
            if block not in met:
                copies[block].wait()
                met.add(block)
            for g in range(groups):
                term = jnp.dot(
                    acts[entry[0]][...], w_out[g, spans[block], :], preferred_element_type=f32
                )
                if n == 0:
                    total_ref[g] = term
                else:
                    total_ref[g] += term
        for block in range(len(order)):
            if block not in met:
                copies[block].wait()

    pl.when(is_inner())(lambda: add(inner))
    pl.when(jnp.logical_not(is_inner()))(lambda: add(outer))


def first_project(acts, inner, outer, w):
    groups, rows, chans = w.shape
    toks, width = acts[0].shape
    sums, w = pl.pallas_call(
        functools.partial(first_kernel, inner, outer, len(acts)),
        in_specs=[pl.BlockSpec(memory_space=pltpu.HBM)] + [IN_VMEM] * len(acts),
        out_specs=[IN_VMEM, IN_VMEM],
        out_shape=[
            pltpu.VMEM((groups, toks, chans), f32),
            pltpu.VMEM(w.shape, w.dtype),
        ],
        scratch_shapes=[pltpu.SemaphoreType.DMA((rows // width,))],
        compiler_params=pltpu.CompilerParams(vmem_limit_bytes=16 * 1024 * 1024),
        cost_estimate=pl.CostEstimate(
            flops=0, bytes_accessed=2 * w.size * w.dtype.itemsize, transcendentals=0
        ),
        name="first_project",
    )(in_hbm(w), *acts)
    return in_vmem(sums), in_vmem(w)


def project_kernel(inner, outer, count, has_base, last, w_ref, *refs):
    acts = refs[:count]
    groups, _, chans = w_ref.shape
    toks, width = acts[0].shape
    if last:
        keep_ref, send_ref, total_ref = refs[-3:]
    else:
        total_ref = refs[-1]

    def add(entries):
        starts = [pl.multiple_of(block_at(*entry[1:]) * width, width) for entry in entries]
        for g in range(groups):
            total = refs[count][g] if has_base else None
            for start, entry in zip(starts, entries):
                term = jnp.dot(
                    acts[entry[0]][...], w_ref[g, pl.ds(start, width), :], preferred_element_type=f32
                )
                total = term if total is None else total + term
            if total is not None:
                total_ref[g] = total

    pl.when(is_inner())(lambda: add(inner))
    pl.when(jnp.logical_not(is_inner()))(lambda: add(outer))
    if last:
        half = chans // 2
        core = here()[3]
        keep_ref[...] = total_ref[:, :, pl.ds(pl.multiple_of(core * half, half), half)]
        send_ref[...] = total_ref[:, :, pl.ds(pl.multiple_of((1 - core) * half, half), half)]


def project(acts, inner, outer, w, base, last):
    groups, _, chans = w.shape
    toks, width = acts[0].shape
    total = jax.ShapeDtypeStruct((groups, toks, chans), f32)
    half = jax.ShapeDtypeStruct((groups, toks, chans // 2), f32)
    return small_call(
        functools.partial(project_kernel, inner, outer, len(acts), base is not None, last),
        [half, half] if last else total,
        [w] + list(acts) + ([] if base is None else [base]),
        "project",
        2 * max(len(inner), len(outer)) * groups * width * chans * toks,
        [pltpu.VMEM(total.shape, f32)] if last else [],
        16,
    )


def shifted(values, by):
    place = lax.broadcasted_iota(jnp.int32, values.shape, 0)
    moved = pltpu.roll(values, by % CHUNKS, 0)
    inside = place >= by if by > 0 else place < CHUNKS + by
    return jnp.where(inside, moved, 0.0)


def mixer_kernel(
    keep_ref,
    other_ref,
    taps_ref,
    rates_ref,
    residues_ref,
    cot_own_ref,
    cot_other_ref,
    mixed_own_ref,
    mixed_send_ref,
    grad_ref,
    flat,
    flat_cot,
    ext,
    filt,
    drive,
    back,
    grad_ext,
):
    groups, toks, chans = keep_ref.shape
    modes = rates_ref.shape[0]
    short = taps_ref.shape[1]
    rim = short - 1
    length = toks // CHUNKS
    lanes = flat.shape[-1]
    wide = (CHUNKS, lanes)
    half = toks // 2
    _, _, _, core = here()

    def row(array, at):
        return jnp.broadcast_to(array[at : at + 1, :], wide)

    def column(c, _):
        some = pl.ds(pl.multiple_of(c * lanes, lanes), lanes)
        whole = pl.ds(pl.multiple_of(core * chans + c * lanes, lanes), lanes)
        own_rows = pl.ds(pl.multiple_of(core * half, half), half)
        other_rows = pl.ds(pl.multiple_of((1 - core) * half, half), half)

        for g in range(groups):
            flat[g] = (keep_ref[g, :, some] + other_ref[g, :, some].astype(f32)).astype(bf16).astype(f32)
        flat_cot[own_rows] = cot_own_ref[:, whole].astype(f32)
        flat_cot[other_rows] = cot_other_ref[:, some].astype(f32)

        for g in range(groups):
            for k in range(length):
                ext[g, rim + k] = flat[g, pl.ds(k, CHUNKS, stride=length), :]
            for k in range(rim):
                ext[g, k] = shifted(ext[g, length + k], 1)

        taps = [taps_ref[g, :, whole] for g in range(groups)]
        tap = [[row(taps[g], j) for g in range(groups)] for j in range(short)]

        def filter_step(k, _):
            parts = []
            for g in range(groups):
                total = tap[0][g] * ext[g, k + rim]
                for j in range(1, short):
                    total = total + tap[j][g] * ext[g, k + rim - j]
                parts.append(total)
                filt[g, k] = total
            drive[k] = parts[1] * parts[2]
            back[k] = parts[0] * flat_cot[pl.ds(k, CHUNKS, stride=length), :]
            return _

        lax.fori_loop(0, length, filter_step, 0, unroll=4)

        rates = rates_ref[:, whole]
        decay_rows = jnp.exp(-rates)
        jump_rows = [jnp.exp(-rates * (length * n)) for n in (1, 2, 4)]
        residue_rows = residues_ref[:, whole]

        def long_filter(source, forward, finish):
            decay = [row(decay_rows, m) for m in range(modes)]

            def place(k):
                return k if forward else length - 1 - k

            def end_step(k, states):
                value = source[place(k)]
                return tuple(decay[m] * states[m] + value for m in range(modes))

            zero = jnp.zeros(wide, f32)
            ends = lax.fori_loop(0, length, end_step, (zero,) * modes, unroll=8)
            entering = []
            sign = 1 if forward else -1
            for m in range(modes):
                carried = ends[m]
                for jump, by in zip(jump_rows, (1, 2, 4)):
                    carried = carried + row(jump, m) * shifted(carried, sign * by)
                entering.append(shifted(carried, sign))

            def out_step(k, states):
                value = source[place(k)]
                states = tuple(decay[m] * states[m] + value for m in range(modes))
                terms = [row(residue_rows, m) * states[m] for m in range(modes)]
                while len(terms) > 1:
                    terms = [a + b for a, b in zip(terms[::2], terms[1::2])]
                finish(place(k), terms[0])
                return states

            lax.fori_loop(0, length, out_step, tuple(entering), unroll=4)

        def finish_forward(k, total):
            flat[0, pl.ds(k, CHUNKS, stride=length), :] = filt[0, k] * total
            grad_ext[0, k] = flat_cot[pl.ds(k, CHUNKS, stride=length), :] * total

        def finish_backward(k, total):
            grad_ext[1, k] = total * filt[2, k]
            grad_ext[2, k] = total * filt[1, k]

        long_filter(drive, True, finish_forward)
        mixed_own_ref[:, some] = flat[0, own_rows].astype(bf16)
        mixed_send_ref[:, some] = flat[0, other_rows].astype(bf16)
        long_filter(back, False, finish_backward)

        for g in range(groups):
            for k in range(rim):
                grad_ext[g, length + k] = shifted(grad_ext[g, k], -1)

        def adjoint_step(k, _):
            for g in range(groups):
                total = tap[0][g] * grad_ext[g, k]
                for j in range(1, short):
                    total = total + tap[j][g] * grad_ext[g, k + j]
                flat[g, pl.ds(k, CHUNKS, stride=length), :] = total
            return _

        lax.fori_loop(0, length, adjoint_step, 0, unroll=4)
        for g in range(groups):
            grad_ref[g, some, :] = flat[g].T.astype(bf16)
        return _

    lax.fori_loop(0, chans // lanes, column, 0)


def mixer(keep, other, taps, rates, residues, cot_own, cot_other):
    groups, toks, chans = keep.shape
    modes = rates.shape[0]
    rim = taps.shape[1] - 1
    lanes = 128
    length = toks // CHUNKS
    return small_call(
        mixer_kernel,
        [
            jax.ShapeDtypeStruct((toks // 2, chans), bf16),
            jax.ShapeDtypeStruct((toks // 2, chans), bf16),
            jax.ShapeDtypeStruct((groups, chans, toks), bf16),
        ],
        [keep, other, taps, rates, residues, cot_own, cot_other],
        "mixer",
        12 * modes * toks * chans,
        [
            pltpu.VMEM((groups, toks, lanes), f32),
            pltpu.VMEM((toks, lanes), f32),
            pltpu.VMEM((groups, length + rim, CHUNKS, lanes), f32),
            pltpu.VMEM((groups, length, CHUNKS, lanes), f32),
            pltpu.VMEM((length, CHUNKS, lanes), f32),
            pltpu.VMEM((length, CHUNKS, lanes), f32),
            pltpu.VMEM((groups, length + rim, CHUNKS, lanes), f32),
        ],
    )


def back_kernel(blocks, w_ref, own_ref, other_ref, *out_refs):
    groups, half, _ = own_ref.shape
    width = out_refs[0].shape[0]
    _, _, _, core = here()
    own_at = pl.multiple_of(core * half, half)
    other_at = pl.multiple_of((1 - core) * half, half)
    for block, out in zip(blocks, out_refs):
        start = pl.multiple_of(block_at(*block) * width, width)
        total = None
        for g in range(groups):
            for ref, at in ((own_ref, own_at), (other_ref, other_at)):
                term = jnp.dot(
                    w_ref[g, pl.ds(start, width), pl.ds(at, half)],
                    ref[g],
                    preferred_element_type=f32,
                )
                total = term if total is None else total + term
        out[...] = total.astype(out.dtype)


def back_project(blocks, dtypes, w, own, other, width):
    groups, half, toks = own.shape
    return small_call(
        functools.partial(back_kernel, blocks),
        [jax.ShapeDtypeStruct((width, toks), dtype) for dtype in dtypes],
        [w, own, other],
        "back_project",
        4 * len(blocks) * groups * width * half * toks,
        (),
        16,
    )


def merge_kernel(part_ref, got_ref, out_ref):
    out_ref[...] = (part_ref[...] + got_ref[...].astype(f32)).astype(bf16)


def merge(part, got):
    return small_call(merge_kernel, jax.ShapeDtypeStruct(part.shape, bf16), [part, got], "merge")


def column_kernel(slot, own_ref, x_ref, y_ref, total_ref, one_ref, two_ref):
    half = own_ref.shape[1] // 2
    total_ref[...] = own_ref[...] + x_ref[...].astype(f32) + y_ref[...].astype(f32)
    z = here()[0]
    flag = (z >> 1) if slot == 2 else 1 - (z >> 1)
    one_ref[...] = total_ref[:, pl.ds(pl.multiple_of(flag * half, half), half)].astype(bf16)
    two_ref[...] = total_ref[:, pl.ds(pl.multiple_of((1 - flag) * half, half), half)].astype(bf16)


def column(slot, own, from_x, from_y):
    shape = jax.ShapeDtypeStruct((own.shape[0], own.shape[1] // 2), bf16)
    return small_call(
        functools.partial(column_kernel, slot),
        [jax.ShapeDtypeStruct(own.shape, f32), shape, shape],
        [own, from_x, from_y],
        "column",
    )


def finish_kernel(own_ref, a_ref, b_ref, c_ref, d_ref, out_ref):
    half = own_ref.shape[1] // 2
    core = here()[3]
    mine = own_ref[:, pl.ds(pl.multiple_of(core * half, half), half)]
    total = jnp.where(is_inner(), mine, 0.0)
    for ref in (a_ref, b_ref, c_ref, d_ref):
        total = total + ref[...].astype(f32)
    out_ref[...] = total.T.astype(bf16)


def finish(own, received):
    shape = jax.ShapeDtypeStruct((own.shape[1] // 2, own.shape[0]), bf16)
    return small_call(finish_kernel, shape, [own] + received, "finish")


def pair_kernel(own_ref, other_ref, out_ref):
    half = own_ref.shape[1]
    core = here()[3]
    out_ref[:, pl.ds(pl.multiple_of(core * half, half), half)] = own_ref[...]
    out_ref[:, pl.ds(pl.multiple_of((1 - core) * half, half), half)] = other_ref[...]


def pair(own, other):
    shape = jax.ShapeDtypeStruct((own.shape[0], 2 * own.shape[1]), own.dtype)
    return small_call(pair_kernel, shape, [own, other], "pair")


def chip_plan(token_ids, embed, w_in, taps, rates, residues, cotangent):
    width = embed.shape[1]

    def swap(array):
        return lax.ppermute(array, BOTH, OTHER_CORE)

    def over_x(array):
        return lax.ppermute(array, BOTH, OVER_X)

    def over_y(array):
        return lax.ppermute(array, BOTH, OVER_Y)

    own_ids = token_ids.reshape(1, -1)
    other_ids = swap(own_ids)
    cot_half = cotangent.shape[1] // 2
    cot_other = swap(
        lax.dynamic_slice_in_dim(cotangent, (1 - lax.axis_index("ctx")) * cot_half, cot_half, 1)
    )
    own_ids, table = fetch(own_ids, embed)
    embedded = embed_rows(own_ids, other_ids, table)

    embedded, cot_other = lax.optimization_barrier((embedded, cot_other))
    got_1 = lax.ppermute(embedded, BOTH, GATHER_Z)
    near_x = lax.ppermute(embedded, BOTH, OVER_X_INNER + GATHER_Z_OUTER)
    near_y = lax.ppermute(embedded, BOTH, OVER_Y_INNER)
    near_d = lax.ppermute(embedded, BOTH, DIAGONAL)
    x_1, y_1, d_1 = over_x(got_1), over_y(got_1), lax.ppermute(got_1, BOTH, OVER_XY)
    sums, w = first_project(
        [embedded, near_x, near_y, near_d, got_1],
        [(0, 1, 0, 0), (1, 1, 0, 1), (2, 1, 1, 0), (3, 1, 1, 1), (4, 2, 0, 0)],
        [(4, 1, 0, 0), (1, 2, 0, 0)],
        jnp.transpose(w_in, (1, 0, 2)),
    )
    got_2, sums = lax.optimization_barrier((near_x, sums))
    x_2 = lax.ppermute(got_2, BOTH, OVER_X_OUTER)
    y_2 = lax.ppermute(got_2, BOTH, OVER_Y_OUTER)
    d_2 = lax.ppermute(got_2, BOTH, OVER_XY_OUTER)
    sums = project(
        [x_1, y_1, d_1],
        [(0, 2, 0, 1), (1, 2, 1, 0), (2, 2, 1, 1)],
        [(0, 1, 0, 1), (1, 1, 1, 0), (2, 1, 1, 1)],
        w,
        sums,
        False,
    )
    x_2, y_2, d_2, sums = lax.optimization_barrier((x_2, y_2, d_2, sums))
    keep, send = project(
        [x_2, y_2, d_2], [], [(0, 2, 0, 1), (1, 2, 1, 0), (2, 2, 1, 1)], w, sums, True
    )

    mixed_own, mixed_send, grad_own = mixer(
        keep, swap(send), jnp.transpose(taps, (1, 0, 2)), rates, residues, cotangent, cot_other
    )
    grad_other = swap(grad_own)
    mixed_other = swap(mixed_send)

    d_2, d_1 = back_project([(2, 1, 1), (1, 1, 1)], [bf16] * 2, w, grad_own, grad_other, width)
    d_2, d_1 = over_x(d_2), over_y(d_1)
    x_2, y_2, x_1, y_1, own_2, own_1 = back_project(
        [(2, 0, 1), (2, 1, 0), (1, 0, 1), (1, 1, 0), (2, 0, 0), (1, 0, 0)],
        [bf16, f32, f32, bf16, f32, f32],
        w,
        grad_own,
        grad_other,
        width,
    )
    x_2, y_2 = over_x(x_2), over_y(merge(y_2, d_2))
    x_1, y_1 = over_x(merge(x_1, d_1)), over_y(y_1)
    _, send_1, send_2 = column(2, own_2, x_2, y_2)
    received = [
        lax.ppermute(send_1, BOTH, SCATTER_Z[0]),
        lax.ppermute(send_2, BOTH, SCATTER_Z[1]),
    ]
    mixed = pair(mixed_own, mixed_other)
    own, send_1, send_2 = column(1, own_1, x_1, y_1)
    received += [
        lax.ppermute(send_1, BOTH, SCATTER_Z[2]),
        lax.ppermute(send_2, BOTH, SCATTER_Z[3]),
    ]
    return (mixed, finish(own, received))


def solution(mesh):
    in_specs = (
        P("ctx"),
        P(None, "fsdp"),
        P("ctx", None, "fsdp"),
        P(None, None, "fsdp"),
        P(None, "fsdp"),
        P(None, "fsdp"),
        P("ctx", "fsdp"),
    )
    out_specs = (P("ctx", "fsdp"), P("ctx", "fsdp"))
    chips = mesh.shape["fsdp"] == 16 and mesh.shape["ctx"] == 2
    return jax.shard_map(
        chip_plan if chips else general_plan,
        mesh=mesh,
        in_specs=in_specs,
        out_specs=out_specs,
        check_vma=False,
    )
```

```python
import functools

import jax
import jax.numpy as jnp
from jax import lax
from jax.experimental import pallas as pl
from jax.experimental.pallas import tpu as pltpu
from jax.sharding import PartitionSpec as P

BOTH = ("fsdp", "ctx")
CHUNKS = 8
f32 = jnp.float32
bf16 = jnp.bfloat16


def from_behind(shard, axis, by):
    count = lax.axis_size(axis)
    pairs = [(i, i + by) for i in range(count) if 0 <= i + by < count]
    return lax.ppermute(shard, axis, pairs)


def pair_combine(earlier, later):
    return (earlier[0] * later[0], later[0] * earlier[1] + later[1])


def modal_states(drive, step_decay):
    tok_count = drive.shape[0]
    factors = jnp.broadcast_to(step_decay[None], (tok_count,) + step_decay.shape)
    inputs = jnp.broadcast_to(drive[:, None, :], factors.shape)
    return lax.associative_scan(pair_combine, (factors, inputs), axis=0)[1]


def short_filter(extended, taps, tok_count):
    rim_width = taps.shape[0] - 1
    filtered = taps[0] * extended[rim_width : rim_width + tok_count]
    for shift_lag in range(1, rim_width + 1):
        filtered = (
            filtered
            + taps[shift_lag] * extended[rim_width - shift_lag : rim_width - shift_lag + tok_count]
        )
    return filtered


def short_adjoint(extended, taps, tok_count):
    rim_width = taps.shape[0] - 1
    result = taps[0] * extended[:tok_count]
    for shift_lag in range(1, rim_width + 1):
        result = result + taps[shift_lag] * extended[shift_lag : shift_lag + tok_count]
    return result


def carry(block_decay, leaving, by):
    def relay_step(turn_index, incoming):
        return from_behind(block_decay * incoming + leaving, "ctx", by)

    return lax.fori_loop(0, lax.axis_size("ctx") - 1, relay_step, jnp.zeros_like(leaving))


def general_plan(token_ids, embed, w_in, taps, rates, residues, cotangent):
    tok_count = token_ids.shape[0]
    vocab_size = embed.shape[0]
    chan_width = embed.shape[1]
    rim_width = taps.shape[0] - 1
    onehot = (
        token_ids[:, None] == lax.broadcasted_iota(jnp.int32, (tok_count, vocab_size), 1)
    ).astype(bf16)
    embedded = jnp.dot(onehot, embed, preferred_element_type=f32).astype(bf16)
    features = lax.all_gather(embedded, "fsdp", axis=1, tiled=True)
    feat_width = features.shape[1]
    whole_w = lax.all_gather(w_in, "ctx", axis=0, tiled=True).reshape(feat_width, 3 * chan_width)
    projected = jnp.dot(features, whole_w, preferred_element_type=f32)
    stored = lax.optimization_barrier(projected.astype(bf16).reshape(tok_count, 3, chan_width))
    before = from_behind(stored[tok_count - rim_width :], "ctx", 1)
    extended = jnp.concatenate([before, stored], axis=0).astype(f32)
    filtered = short_filter(extended, taps, tok_count)
    query_part = filtered[:, 0]
    key_part = filtered[:, 1]
    value_part = filtered[:, 2]
    drive = key_part * value_part
    step_decay = jnp.exp(-rates)
    block_decay = jnp.exp(-rates * tok_count)
    local_states = modal_states(drive, step_decay)
    entering = carry(block_decay, local_states[tok_count - 1], 1)
    offsets = lax.broadcasted_iota(f32, (tok_count, 1, 1), 0)
    states = local_states + jnp.exp(-rates[None] * (offsets + 1.0)) * entering[None]
    long_out = jnp.sum(residues[None] * states, axis=1)
    mixed = (query_part * long_out).astype(bf16)
    incoming = cotangent.astype(f32)
    grad_long = incoming * query_part
    grad_query = incoming * long_out
    back_states = jnp.flip(modal_states(jnp.flip(grad_long, 0), step_decay), 0)
    beyond = carry(block_decay, back_states[0], -1)
    adjoint = back_states + jnp.exp(-rates[None] * (tok_count - offsets)) * beyond[None]
    grad_drive = jnp.sum(residues[None] * adjoint, axis=1)
    grad_filtered = jnp.stack([grad_query, grad_drive * value_part, grad_drive * key_part], axis=1)
    after = from_behind(grad_filtered[:rim_width], "ctx", -1)
    ext_grad = jnp.concatenate([grad_filtered, after], axis=0)
    grad_stored = short_adjoint(ext_grad, taps, tok_count).astype(bf16)
    grad_rows = grad_stored.reshape(tok_count, 3 * chan_width)
    own_rows = lax.psum_scatter(
        lax.dot_general(whole_w, grad_rows, (((1,), (1,)), ((), ())), preferred_element_type=f32),
        "fsdp",
        scatter_dimension=0,
        tiled=True,
    )
    return (mixed, own_rows.T.astype(bf16))


def device_at(z, y, x, core):
    return ((z * 2 + y) * 2 + x) * 2 + core


def everywhere(move):
    pairs = []
    for z in range(4):
        for y in range(2):
            for x in range(2):
                for core in range(2):
                    pairs.append((device_at(z, y, x, core), device_at(*move(z, y, x, core))))
    return pairs


OTHER_CORE = everywhere(lambda z, y, x, core: (z, y, x, 1 - core))
OVER_X = everywhere(lambda z, y, x, core: (z, y, 1 - x, core))
OVER_Y = everywhere(lambda z, y, x, core: (z, 1 - y, x, core))


def along_z(moves):
    pairs = []
    for core in range(2):
        for (place, other), (to_place, to_other) in moves:
            z, to_z = (place, to_place) if core == 0 else (3 - place, 3 - to_place)
            for y in range(2):
                for x in range(2):
                    pairs.append(
                        (
                            device_at(z, y, x, core ^ other),
                            device_at(to_z, y, x, core ^ to_other),
                        )
                    )
    return pairs


GATHER_Z = (
    along_z([((0, 0), (1, 0)), ((1, 0), (0, 0)), ((0, 1), (2, 0)), ((1, 1), (3, 0))]),
    along_z([((2, 0), (3, 0)), ((3, 0), (2, 0))]),
)
SCATTER_Z = (
    along_z([((0, 0), (1, 0)), ((1, 0), (0, 0)), ((2, 0), (1, 1)), ((3, 0), (0, 1))]),
    along_z([((0, 0), (1, 1)), ((1, 0), (0, 1)), ((2, 0), (1, 0)), ((3, 0), (0, 0))]),
    along_z([((0, 0), (0, 1)), ((1, 0), (1, 1)), ((2, 0), (0, 0)), ((3, 0), (1, 0))]),
    along_z([((2, 0), (0, 1)), ((3, 0), (1, 1))]),
)

IN_VMEM = pl.BlockSpec(memory_space=pltpu.VMEM)


def small_call(kernel, out_shape, operands, name, flops=0, scratch=(), limit=8):
    sizes = [o.size * o.dtype.itemsize for o in operands]
    return pl.pallas_call(
        kernel,
        in_specs=[IN_VMEM] * len(operands),
        out_specs=jax.tree.map(lambda _: IN_VMEM, out_shape),
        out_shape=out_shape,
        scratch_shapes=list(scratch),
        compiler_params=pltpu.CompilerParams(vmem_limit_bytes=limit * 1024 * 1024),
        cost_estimate=pl.CostEstimate(
            flops=flops // 64, bytes_accessed=sum(sizes) // 64, transcendentals=0
        ),
        name=name,
    )(*operands)


def here():
    spot = lax.axis_index("fsdp")
    return spot >> 2, (spot >> 1) & 1, spot & 1, lax.axis_index("ctx")


def is_inner():
    z, _, _, core = here()
    return core == (z >> 1)


def block_at(slot, far_y, far_x):
    z, y, x, _ = here()
    along = (z & 1) if slot == 1 else 1 - (z & 1)
    return along * 4 + (1 - y if far_y else y) * 2 + (1 - x if far_x else x)


def embed_kernel(own_ref, other_ref, table_ref, out_ref):
    vocab = table_ref.shape[0]
    half = own_ref.shape[1]
    core = here()[3]
    for ref, side in ((own_ref, core), (other_ref, 1 - core)):
        across = jnp.broadcast_to(ref[...].astype(f32), (half, half)).T
        lane = lax.broadcasted_iota(jnp.int32, (half, half), 1).astype(f32)
        picks = [(across == lane + float(first)).astype(f32) for first in range(0, vocab, half)]
        rows = jnp.dot(
            jnp.concatenate(picks, axis=1).astype(bf16), table_ref[...], preferred_element_type=f32
        )
        out_ref[pl.ds(pl.multiple_of(side * half, half), half), :] = rows.astype(bf16)


def embed_rows(own_ids, other_ids, table):
    toks, width = 2 * own_ids.shape[1], table.shape[1]
    return small_call(
        embed_kernel,
        jax.ShapeDtypeStruct((toks, width), bf16),
        [own_ids, other_ids, table],
        "embed_rows",
        2 * toks * table.shape[0] * width,
    )


def fetch_kernel(ids_ref, table_ref, ids_out, table_out, sems):
    copies = [
        pltpu.make_async_copy(ids_ref, ids_out, sems.at[0]),
        pltpu.make_async_copy(table_ref, table_out, sems.at[1]),
    ]
    for copy in copies:
        copy.start()
    for copy in copies:
        copy.wait()


def in_hbm(array):
    return pltpu.with_memory_space_constraint(array, pltpu.HBM)


def in_vmem(array):
    return pltpu.with_memory_space_constraint(array, pltpu.VMEM)


def fetch(ids, table):
    out = pl.pallas_call(
        fetch_kernel,
        in_specs=[pl.BlockSpec(memory_space=pltpu.HBM)] * 2,
        out_specs=[IN_VMEM] * 2,
        out_shape=[pltpu.VMEM(ids.shape, ids.dtype), pltpu.VMEM(table.shape, bf16)],
        scratch_shapes=[pltpu.SemaphoreType.DMA((2,))],
        compiler_params=pltpu.CompilerParams(vmem_limit_bytes=2 * 1024 * 1024),
        cost_estimate=pl.CostEstimate(
            flops=0, bytes_accessed=4 * table.size, transcendentals=0
        ),
        name="fetch",
    )(in_hbm(ids), in_hbm(table))
    return [in_vmem(array) for array in out]


def load_kernel(w_ref, out_ref, sem):
    copy = pltpu.make_async_copy(w_ref, out_ref, sem)
    copy.start()
    copy.wait()


def load(w):
    out = pl.pallas_call(
        load_kernel,
        in_specs=[pl.BlockSpec(memory_space=pltpu.HBM)],
        out_specs=IN_VMEM,
        out_shape=pltpu.VMEM(w.shape, w.dtype),
        scratch_shapes=[pltpu.SemaphoreType.DMA],
        compiler_params=pltpu.CompilerParams(vmem_limit_bytes=2 * 1024 * 1024),
        cost_estimate=pl.CostEstimate(
            flops=0, bytes_accessed=2 * w.size * w.dtype.itemsize, transcendentals=0
        ),
        name="load",
    )(in_hbm(w))
    return in_vmem(out)


def choose_kernel(inner_ref, outer_ref, out_ref):
    @pl.when(is_inner())
    def _():
        out_ref[...] = inner_ref[...]

    @pl.when(jnp.logical_not(is_inner()))
    def _():
        out_ref[...] = outer_ref[...]


def choose(inner, outer):
    return small_call(
        choose_kernel, jax.ShapeDtypeStruct(inner.shape, inner.dtype), [inner, outer], "choose"
    )


def project_kernel(blocks, has_base, last, w_ref, *refs):
    count = len(blocks)
    acts = refs[:count]
    groups, _, chans = w_ref.shape
    toks, width = acts[0].shape
    if last:
        keep_ref, send_ref, total_ref = refs[-3:]
    else:
        total_ref = refs[-1]
    starts = [pl.multiple_of(block_at(*block) * width, width) for block in blocks]
    for g in range(groups):
        total = refs[count][g] if has_base else None
        for start, act in zip(starts, acts):
            term = jnp.dot(act[...], w_ref[g, pl.ds(start, width), :], preferred_element_type=f32)
            total = term if total is None else total + term
        total_ref[g] = total
    if last:
        half = chans // 2
        core = here()[3]
        keep_ref[...] = total_ref[:, :, pl.ds(pl.multiple_of(core * half, half), half)]
        send_ref[...] = total_ref[:, :, pl.ds(pl.multiple_of((1 - core) * half, half), half)]


def project(blocks, acts, w, base, last):
    groups, _, chans = w.shape
    toks, width = acts[0].shape
    total = jax.ShapeDtypeStruct((groups, toks, chans), f32)
    half = jax.ShapeDtypeStruct((groups, toks, chans // 2), f32)
    return small_call(
        functools.partial(project_kernel, blocks, base is not None, last),
        [half, half] if last else total,
        [w] + list(acts) + ([] if base is None else [base]),
        "project",
        2 * len(acts) * groups * width * chans * toks,
        [pltpu.VMEM(total.shape, f32)] if last else [],
        16,
    )


def shifted(values, by):
    place = lax.broadcasted_iota(jnp.int32, values.shape, 0)
    moved = pltpu.roll(values, by % CHUNKS, 0)
    inside = place >= by if by > 0 else place < CHUNKS + by
    return jnp.where(inside, moved, 0.0)


def mixer_kernel(
    keep_ref,
    other_ref,
    taps_ref,
    rates_ref,
    residues_ref,
    cot_own_ref,
    cot_other_ref,
    mixed_own_ref,
    mixed_send_ref,
    grad_ref,
    flat,
    flat_cot,
    ext,
    filt,
    drive,
    back,
    grad_ext,
):
    groups, toks, chans = keep_ref.shape
    modes = rates_ref.shape[0]
    short = taps_ref.shape[1]
    rim = short - 1
    length = toks // CHUNKS
    lanes = flat.shape[-1]
    wide = (CHUNKS, lanes)
    half = toks // 2
    _, _, _, core = here()

    def row(array, at):
        return jnp.broadcast_to(array[at : at + 1, :], wide)

    def column(c, _):
        some = pl.ds(pl.multiple_of(c * lanes, lanes), lanes)
        whole = pl.ds(pl.multiple_of(core * chans + c * lanes, lanes), lanes)
        own_rows = pl.ds(pl.multiple_of(core * half, half), half)
        other_rows = pl.ds(pl.multiple_of((1 - core) * half, half), half)

        for g in range(groups):
            flat[g] = (keep_ref[g, :, some] + other_ref[g, :, some].astype(f32)).astype(bf16).astype(f32)
        flat_cot[own_rows] = cot_own_ref[:, whole].astype(f32)
        flat_cot[other_rows] = cot_other_ref[:, some].astype(f32)

        for g in range(groups):
            for k in range(length):
                ext[g, rim + k] = flat[g, pl.ds(k, CHUNKS, stride=length), :]
            for k in range(rim):
                ext[g, k] = shifted(ext[g, length + k], 1)

        taps = [taps_ref[g, :, whole] for g in range(groups)]
        tap = [[row(taps[g], j) for g in range(groups)] for j in range(short)]

        def filter_step(k, _):
            parts = []
            for g in range(groups):
                total = tap[0][g] * ext[g, k + rim]
                for j in range(1, short):
                    total = total + tap[j][g] * ext[g, k + rim - j]
                parts.append(total)
                filt[g, k] = total
            drive[k] = parts[1] * parts[2]
            back[k] = parts[0] * flat_cot[pl.ds(k, CHUNKS, stride=length), :]
            return _

        lax.fori_loop(0, length, filter_step, 0, unroll=4)

        rates = rates_ref[:, whole]
        decay_rows = jnp.exp(-rates)
        jump_rows = [jnp.exp(-rates * (length * n)) for n in (1, 2, 4)]
        residue_rows = residues_ref[:, whole]

        def long_filter(source, forward, finish):
            decay = [row(decay_rows, m) for m in range(modes)]

            def place(k):
                return k if forward else length - 1 - k

            def end_step(k, states):
                value = source[place(k)]
                return tuple(decay[m] * states[m] + value for m in range(modes))

            zero = jnp.zeros(wide, f32)
            ends = lax.fori_loop(0, length, end_step, (zero,) * modes, unroll=8)
            entering = []
            sign = 1 if forward else -1
            for m in range(modes):
                carried = ends[m]
                for jump, by in zip(jump_rows, (1, 2, 4)):
                    carried = carried + row(jump, m) * shifted(carried, sign * by)
                entering.append(shifted(carried, sign))

            def out_step(k, states):
                value = source[place(k)]
                states = tuple(decay[m] * states[m] + value for m in range(modes))
                terms = [row(residue_rows, m) * states[m] for m in range(modes)]
                while len(terms) > 1:
                    terms = [a + b for a, b in zip(terms[::2], terms[1::2])]
                finish(place(k), terms[0])
                return states

            lax.fori_loop(0, length, out_step, tuple(entering), unroll=4)

        def finish_forward(k, total):
            flat[0, pl.ds(k, CHUNKS, stride=length), :] = filt[0, k] * total
            grad_ext[0, k] = flat_cot[pl.ds(k, CHUNKS, stride=length), :] * total

        def finish_backward(k, total):
            grad_ext[1, k] = total * filt[2, k]
            grad_ext[2, k] = total * filt[1, k]

        long_filter(drive, True, finish_forward)
        mixed_own_ref[:, some] = flat[0, own_rows].astype(bf16)
        mixed_send_ref[:, some] = flat[0, other_rows].astype(bf16)
        long_filter(back, False, finish_backward)

        for g in range(groups):
            for k in range(rim):
                grad_ext[g, length + k] = shifted(grad_ext[g, k], -1)

        def adjoint_step(k, _):
            for g in range(groups):
                total = tap[0][g] * grad_ext[g, k]
                for j in range(1, short):
                    total = total + tap[j][g] * grad_ext[g, k + j]
                flat[g, pl.ds(k, CHUNKS, stride=length), :] = total
            return _

        lax.fori_loop(0, length, adjoint_step, 0, unroll=4)
        for g in range(groups):
            grad_ref[g, some, :] = flat[g].T.astype(bf16)
        return _

    lax.fori_loop(0, chans // lanes, column, 0)


def mixer(keep, other, taps, rates, residues, cot_own, cot_other):
    groups, toks, chans = keep.shape
    modes = rates.shape[0]
    rim = taps.shape[1] - 1
    lanes = 128
    length = toks // CHUNKS
    return small_call(
        mixer_kernel,
        [
            jax.ShapeDtypeStruct((toks // 2, chans), bf16),
            jax.ShapeDtypeStruct((toks // 2, chans), bf16),
            jax.ShapeDtypeStruct((groups, chans, toks), bf16),
        ],
        [keep, other, taps, rates, residues, cot_own, cot_other],
        "mixer",
        12 * modes * toks * chans,
        [
            pltpu.VMEM((groups, toks, lanes), f32),
            pltpu.VMEM((toks, lanes), f32),
            pltpu.VMEM((groups, length + rim, CHUNKS, lanes), f32),
            pltpu.VMEM((groups, length, CHUNKS, lanes), f32),
            pltpu.VMEM((length, CHUNKS, lanes), f32),
            pltpu.VMEM((length, CHUNKS, lanes), f32),
            pltpu.VMEM((groups, length + rim, CHUNKS, lanes), f32),
        ],
    )


def back_kernel(blocks, w_ref, own_ref, other_ref, *out_refs):
    groups, half, _ = own_ref.shape
    width = out_refs[0].shape[0]
    _, _, _, core = here()
    own_at = pl.multiple_of(core * half, half)
    other_at = pl.multiple_of((1 - core) * half, half)
    for block, out in zip(blocks, out_refs):
        start = pl.multiple_of(block_at(*block) * width, width)
        total = None
        for g in range(groups):
            for ref, at in ((own_ref, own_at), (other_ref, other_at)):
                term = jnp.dot(
                    w_ref[g, pl.ds(start, width), pl.ds(at, half)],
                    ref[g],
                    preferred_element_type=f32,
                )
                total = term if total is None else total + term
        out[...] = total.astype(out.dtype)


def back_project(blocks, dtypes, w, own, other, width):
    groups, half, toks = own.shape
    return small_call(
        functools.partial(back_kernel, blocks),
        [jax.ShapeDtypeStruct((width, toks), dtype) for dtype in dtypes],
        [w, own, other],
        "back_project",
        4 * len(blocks) * groups * width * half * toks,
        (),
        16,
    )


def merge_kernel(part_ref, got_ref, out_ref):
    out_ref[...] = (part_ref[...] + got_ref[...].astype(f32)).astype(bf16)


def merge(part, got):
    return small_call(merge_kernel, jax.ShapeDtypeStruct(part.shape, bf16), [part, got], "merge")


def column_kernel(slot, own_ref, x_ref, y_ref, total_ref, one_ref, two_ref):
    half = own_ref.shape[1] // 2
    total_ref[...] = own_ref[...] + x_ref[...].astype(f32) + y_ref[...].astype(f32)
    z = here()[0]
    flag = (z >> 1) if slot == 2 else 1 - (z >> 1)
    one_ref[...] = total_ref[:, pl.ds(pl.multiple_of(flag * half, half), half)].astype(bf16)
    two_ref[...] = total_ref[:, pl.ds(pl.multiple_of((1 - flag) * half, half), half)].astype(bf16)


def column(slot, own, from_x, from_y):
    shape = jax.ShapeDtypeStruct((own.shape[0], own.shape[1] // 2), bf16)
    return small_call(
        functools.partial(column_kernel, slot),
        [jax.ShapeDtypeStruct(own.shape, f32), shape, shape],
        [own, from_x, from_y],
        "column",
    )


def finish_kernel(own_ref, a_ref, b_ref, c_ref, d_ref, out_ref):
    half = own_ref.shape[1] // 2
    core = here()[3]
    mine = own_ref[:, pl.ds(pl.multiple_of(core * half, half), half)]
    total = jnp.where(is_inner(), mine, 0.0)
    for ref in (a_ref, b_ref, c_ref, d_ref):
        total = total + ref[...].astype(f32)
    out_ref[...] = total.T.astype(bf16)


def finish(own, received):
    shape = jax.ShapeDtypeStruct((own.shape[1] // 2, own.shape[0]), bf16)
    return small_call(finish_kernel, shape, [own] + received, "finish")


def pair_kernel(own_ref, other_ref, out_ref):
    half = own_ref.shape[1]
    core = here()[3]
    out_ref[:, pl.ds(pl.multiple_of(core * half, half), half)] = own_ref[...]
    out_ref[:, pl.ds(pl.multiple_of((1 - core) * half, half), half)] = other_ref[...]


def pair(own, other):
    shape = jax.ShapeDtypeStruct((own.shape[0], 2 * own.shape[1]), own.dtype)
    return small_call(pair_kernel, shape, [own, other], "pair")


def chip_plan(token_ids, embed, w_in, taps, rates, residues, cotangent):
    width = embed.shape[1]

    def swap(array):
        return lax.ppermute(array, BOTH, OTHER_CORE)

    def over_x(array):
        return lax.ppermute(array, BOTH, OVER_X)

    def over_y(array):
        return lax.ppermute(array, BOTH, OVER_Y)

    own_ids = token_ids.reshape(1, -1)
    other_ids = swap(own_ids)
    cot_half = cotangent.shape[1] // 2
    cot_other = swap(
        lax.dynamic_slice_in_dim(cotangent, (1 - lax.axis_index("ctx")) * cot_half, cot_half, 1)
    )
    own_ids, table = fetch(own_ids, embed)
    embedded = embed_rows(own_ids, other_ids, table)

    embedded, cot_other = lax.optimization_barrier((embedded, cot_other))
    got_1 = lax.ppermute(embedded, BOTH, GATHER_Z[0])
    w = load(jnp.transpose(w_in, (1, 0, 2)))
    got_1, w = lax.optimization_barrier((got_1, w))
    slot_1 = choose(embedded, got_1)
    x_1, y_1 = over_x(slot_1), over_y(slot_1)
    got_2 = lax.ppermute(got_1, BOTH, GATHER_Z[1])
    slot_2 = choose(got_1, got_2)
    x_2, y_2 = over_x(slot_2), over_y(slot_2)
    sums = project([(1, 0, 0), (2, 0, 0)], [slot_1, slot_2], w, None, False)
    x_1, y_1, sums = lax.optimization_barrier((x_1, y_1, sums))
    d_1 = over_y(x_1)
    sums = project([(1, 0, 1), (1, 1, 0)], [x_1, y_1], w, sums, False)
    x_2, y_2, sums = lax.optimization_barrier((x_2, y_2, sums))
    d_2 = over_x(y_2)
    sums = project([(2, 0, 1), (2, 1, 0)], [x_2, y_2], w, sums, False)
    d_1, d_2, sums = lax.optimization_barrier((d_1, d_2, sums))
    keep, send = project([(1, 1, 1), (2, 1, 1)], [d_1, d_2], w, sums, True)

    mixed_own, mixed_send, grad_own = mixer(
        keep, swap(send), jnp.transpose(taps, (1, 0, 2)), rates, residues, cotangent, cot_other
    )
    grad_other = swap(grad_own)
    mixed_other = swap(mixed_send)

    d_2, d_1 = back_project([(2, 1, 1), (1, 1, 1)], [bf16] * 2, w, grad_own, grad_other, width)
    d_2, d_1 = over_x(d_2), over_y(d_1)
    x_2, y_2, x_1, y_1, own_2, own_1 = back_project(
        [(2, 0, 1), (2, 1, 0), (1, 0, 1), (1, 1, 0), (2, 0, 0), (1, 0, 0)],
        [bf16, f32, f32, bf16, f32, f32],
        w,
        grad_own,
        grad_other,
        width,
    )
    mixed = pair(mixed_own, mixed_other)
    x_2, d_2, mixed = lax.optimization_barrier((x_2, d_2, mixed))
    x_2, y_2 = lax.optimization_barrier((x_2, merge(y_2, d_2)))
    x_2, y_2 = over_x(x_2), over_y(y_2)
    x_1, y_1 = over_x(merge(x_1, d_1)), over_y(y_1)
    _, send_1, send_2 = column(2, own_2, x_2, y_2)
    received = [
        lax.ppermute(send_1, BOTH, SCATTER_Z[0]),
        lax.ppermute(send_2, BOTH, SCATTER_Z[1]),
    ]
    own, send_1, send_2 = column(1, own_1, x_1, y_1)
    received += [
        lax.ppermute(send_1, BOTH, SCATTER_Z[2]),
        lax.ppermute(send_2, BOTH, SCATTER_Z[3]),
    ]
    return (mixed, finish(own, received))


def solution(mesh):
    in_specs = (
        P("ctx"),
        P(None, "fsdp"),
        P("ctx", None, "fsdp"),
        P(None, None, "fsdp"),
        P(None, "fsdp"),
        P(None, "fsdp"),
        P("ctx", "fsdp"),
    )
    out_specs = (P("ctx", "fsdp"), P("ctx", "fsdp"))
    chips = mesh.shape["fsdp"] == 16 and mesh.shape["ctx"] == 2
    return jax.shard_map(
        chip_plan if chips else general_plan,
        mesh=mesh,
        in_specs=in_specs,
        out_specs=out_specs,
        check_vma=False,
    )
```

```python
import functools

import jax
import jax.numpy as jnp
from jax import lax
from jax.experimental import pallas as pl
from jax.experimental.pallas import tpu as pltpu
from jax.sharding import PartitionSpec as P

BOTH = ("fsdp", "ctx")
CHUNKS = 8
f32 = jnp.float32
bf16 = jnp.bfloat16


def from_behind(shard, axis, by):
    count = lax.axis_size(axis)
    pairs = [(i, i + by) for i in range(count) if 0 <= i + by < count]
    return lax.ppermute(shard, axis, pairs)


def pair_combine(earlier, later):
    return (earlier[0] * later[0], later[0] * earlier[1] + later[1])


def modal_states(drive, step_decay):
    tok_count = drive.shape[0]
    factors = jnp.broadcast_to(step_decay[None], (tok_count,) + step_decay.shape)
    inputs = jnp.broadcast_to(drive[:, None, :], factors.shape)
    return lax.associative_scan(pair_combine, (factors, inputs), axis=0)[1]


def short_filter(extended, taps, tok_count):
    rim_width = taps.shape[0] - 1
    filtered = taps[0] * extended[rim_width : rim_width + tok_count]
    for shift_lag in range(1, rim_width + 1):
        filtered = (
            filtered
            + taps[shift_lag] * extended[rim_width - shift_lag : rim_width - shift_lag + tok_count]
        )
    return filtered


def short_adjoint(extended, taps, tok_count):
    rim_width = taps.shape[0] - 1
    result = taps[0] * extended[:tok_count]
    for shift_lag in range(1, rim_width + 1):
        result = result + taps[shift_lag] * extended[shift_lag : shift_lag + tok_count]
    return result


def carry(block_decay, leaving, by):
    def relay_step(turn_index, incoming):
        return from_behind(block_decay * incoming + leaving, "ctx", by)

    return lax.fori_loop(0, lax.axis_size("ctx") - 1, relay_step, jnp.zeros_like(leaving))


def general_plan(token_ids, embed, w_in, taps, rates, residues, cotangent):
    tok_count = token_ids.shape[0]
    vocab_size = embed.shape[0]
    chan_width = embed.shape[1]
    rim_width = taps.shape[0] - 1
    onehot = (
        token_ids[:, None] == lax.broadcasted_iota(jnp.int32, (tok_count, vocab_size), 1)
    ).astype(bf16)
    embedded = jnp.dot(onehot, embed, preferred_element_type=f32).astype(bf16)
    features = lax.all_gather(embedded, "fsdp", axis=1, tiled=True)
    feat_width = features.shape[1]
    whole_w = lax.all_gather(w_in, "ctx", axis=0, tiled=True).reshape(feat_width, 3 * chan_width)
    projected = jnp.dot(features, whole_w, preferred_element_type=f32)
    stored = lax.optimization_barrier(projected.astype(bf16).reshape(tok_count, 3, chan_width))
    before = from_behind(stored[tok_count - rim_width :], "ctx", 1)
    extended = jnp.concatenate([before, stored], axis=0).astype(f32)
    filtered = short_filter(extended, taps, tok_count)
    query_part = filtered[:, 0]
    key_part = filtered[:, 1]
    value_part = filtered[:, 2]
    drive = key_part * value_part
    step_decay = jnp.exp(-rates)
    block_decay = jnp.exp(-rates * tok_count)
    local_states = modal_states(drive, step_decay)
    entering = carry(block_decay, local_states[tok_count - 1], 1)
    offsets = lax.broadcasted_iota(f32, (tok_count, 1, 1), 0)
    states = local_states + jnp.exp(-rates[None] * (offsets + 1.0)) * entering[None]
    long_out = jnp.sum(residues[None] * states, axis=1)
    mixed = (query_part * long_out).astype(bf16)
    incoming = cotangent.astype(f32)
    grad_long = incoming * query_part
    grad_query = incoming * long_out
    back_states = jnp.flip(modal_states(jnp.flip(grad_long, 0), step_decay), 0)
    beyond = carry(block_decay, back_states[0], -1)
    adjoint = back_states + jnp.exp(-rates[None] * (tok_count - offsets)) * beyond[None]
    grad_drive = jnp.sum(residues[None] * adjoint, axis=1)
    grad_filtered = jnp.stack([grad_query, grad_drive * value_part, grad_drive * key_part], axis=1)
    after = from_behind(grad_filtered[:rim_width], "ctx", -1)
    ext_grad = jnp.concatenate([grad_filtered, after], axis=0)
    grad_stored = short_adjoint(ext_grad, taps, tok_count).astype(bf16)
    grad_rows = grad_stored.reshape(tok_count, 3 * chan_width)
    own_rows = lax.psum_scatter(
        lax.dot_general(whole_w, grad_rows, (((1,), (1,)), ((), ())), preferred_element_type=f32),
        "fsdp",
        scatter_dimension=0,
        tiled=True,
    )
    return (mixed, own_rows.T.astype(bf16))


def device_at(z, y, x, core):
    return ((z * 2 + y) * 2 + x) * 2 + core


def everywhere(move):
    pairs = []
    for z in range(4):
        for y in range(2):
            for x in range(2):
                for core in range(2):
                    pairs.append((device_at(z, y, x, core), device_at(*move(z, y, x, core))))
    return pairs


OTHER_CORE = everywhere(lambda z, y, x, core: (z, y, x, 1 - core))
OVER_X = everywhere(lambda z, y, x, core: (z, y, 1 - x, core))
OVER_Y = everywhere(lambda z, y, x, core: (z, 1 - y, x, core))


def along_z(moves):
    pairs = []
    for core in range(2):
        for (place, other), (to_place, to_other) in moves:
            z, to_z = (place, to_place) if core == 0 else (3 - place, 3 - to_place)
            for y in range(2):
                for x in range(2):
                    pairs.append(
                        (
                            device_at(z, y, x, core ^ other),
                            device_at(to_z, y, x, core ^ to_other),
                        )
                    )
    return pairs


FIRST_WAY = everywhere(lambda z, y, x, core: (z, y, 1 - x, core) if core == 0 else (z, 1 - y, x, core))
OTHER_WAY = everywhere(lambda z, y, x, core: (z, 1 - y, x, core) if core == 0 else (z, y, 1 - x, core))
GATHER_Z = (
    along_z([((0, 0), (1, 0)), ((1, 0), (0, 0)), ((0, 1), (2, 0)), ((1, 1), (3, 0))]),
    along_z([((1, 1), (2, 0)), ((0, 1), (3, 0))]),
)
SCATTER_Z = (
    along_z([((0, 0), (1, 0)), ((1, 0), (0, 0)), ((2, 0), (1, 1)), ((3, 0), (0, 1))]),
    along_z([((0, 0), (1, 1)), ((1, 0), (0, 1)), ((2, 0), (1, 0)), ((3, 0), (0, 0))]),
    along_z([((0, 0), (0, 1)), ((1, 0), (1, 1)), ((2, 0), (0, 0)), ((3, 0), (1, 0))]),
    along_z([((2, 0), (0, 1)), ((3, 0), (1, 1))]),
)

IN_VMEM = pl.BlockSpec(memory_space=pltpu.VMEM)


def small_call(kernel, out_shape, operands, name, flops=0, scratch=(), limit=8):
    sizes = [o.size * o.dtype.itemsize for o in operands]
    return pl.pallas_call(
        kernel,
        in_specs=[IN_VMEM] * len(operands),
        out_specs=jax.tree.map(lambda _: IN_VMEM, out_shape),
        out_shape=out_shape,
        scratch_shapes=list(scratch),
        compiler_params=pltpu.CompilerParams(vmem_limit_bytes=limit * 1024 * 1024),
        cost_estimate=pl.CostEstimate(
            flops=flops // 64, bytes_accessed=sum(sizes) // 64, transcendentals=0
        ),
        name=name,
    )(*operands)


def here():
    spot = lax.axis_index("fsdp")
    return spot >> 2, (spot >> 1) & 1, spot & 1, lax.axis_index("ctx")


def is_inner():
    z, _, _, core = here()
    return core == (z >> 1)


def block_at(slot, far_y, far_x):
    z, y, x, _ = here()
    along = (z & 1) if slot == 1 else 1 - (z & 1)
    return along * 4 + (1 - y if far_y else y) * 2 + (1 - x if far_x else x)


def way_at(slot, way):
    core = here()[3]
    far = ((core, 1 - core), (1 - core, core), (1, 1))[way]
    z, y, x, _ = here()
    along = (z & 1) if slot == 1 else 1 - (z & 1)
    return along * 4 + (y ^ far[0]) * 2 + (x ^ far[1])


def embed_kernel(own_ref, other_ref, table_ref, *out_refs):
    vocab = table_ref.shape[0]
    half = own_ref.shape[1]
    core = here()[3]
    for ref, side in ((own_ref, core), (other_ref, 1 - core)):
        across = jnp.broadcast_to(ref[...].astype(f32), (half, half)).T
        lane = lax.broadcasted_iota(jnp.int32, (half, half), 1).astype(f32)
        picks = [(across == lane + float(first)).astype(f32) for first in range(0, vocab, half)]
        rows = jnp.dot(
            jnp.concatenate(picks, axis=1).astype(bf16), table_ref[...], preferred_element_type=f32
        )
        for n, out_ref in enumerate(out_refs):

            @pl.when(side == n)
            def _():
                out_ref[...] = rows.astype(bf16)


def embed_rows(own_ids, other_ids, table):
    toks, width = 2 * own_ids.shape[1], table.shape[1]
    return small_call(
        embed_kernel,
        [jax.ShapeDtypeStruct((toks // 2, width), bf16)] * 2,
        [own_ids, other_ids, table],
        "embed_rows",
        2 * toks * table.shape[0] * width,
    )


def fetch_kernel(ids_ref, table_ref, ids_out, table_out, sems):
    copies = [
        pltpu.make_async_copy(ids_ref, ids_out, sems.at[0]),
        pltpu.make_async_copy(table_ref, table_out, sems.at[1]),
    ]
    for copy in copies:
        copy.start()
    for copy in copies:
        copy.wait()


def in_hbm(array):
    return pltpu.with_memory_space_constraint(array, pltpu.HBM)


def in_vmem(array):
    return pltpu.with_memory_space_constraint(array, pltpu.VMEM)


def fetch(ids, table):
    out = pl.pallas_call(
        fetch_kernel,
        in_specs=[pl.BlockSpec(memory_space=pltpu.HBM)] * 2,
        out_specs=[IN_VMEM] * 2,
        out_shape=[pltpu.VMEM(ids.shape, ids.dtype), pltpu.VMEM(table.shape, bf16)],
        scratch_shapes=[pltpu.SemaphoreType.DMA((2,))],
        compiler_params=pltpu.CompilerParams(vmem_limit_bytes=2 * 1024 * 1024),
        cost_estimate=pl.CostEstimate(
            flops=0, bytes_accessed=4 * table.size, transcendentals=0
        ),
        name="fetch",
    )(in_hbm(ids), in_hbm(table))
    return [in_vmem(array) for array in out]


def load_kernel(w_ref, out_ref, sem):
    copy = pltpu.make_async_copy(w_ref, out_ref, sem)
    copy.start()
    copy.wait()


def load(w):
    out = pl.pallas_call(
        load_kernel,
        in_specs=[pl.BlockSpec(memory_space=pltpu.HBM)],
        out_specs=IN_VMEM,
        out_shape=pltpu.VMEM(w.shape, w.dtype),
        scratch_shapes=[pltpu.SemaphoreType.DMA],
        compiler_params=pltpu.CompilerParams(vmem_limit_bytes=2 * 1024 * 1024),
        cost_estimate=pl.CostEstimate(
            flops=0, bytes_accessed=2 * w.size * w.dtype.itemsize, transcendentals=0
        ),
        name="load",
    )(in_hbm(w))
    return in_vmem(out)


def slots_kernel(own_ref, one_ref, two_ref, out_ref):
    rows = own_ref.shape[0]

    @pl.when(is_inner())
    def _():
        out_ref[:rows] = own_ref[...]
        out_ref[rows:] = one_ref[...]

    @pl.when(jnp.logical_not(is_inner()))
    def _():
        out_ref[:rows] = one_ref[...]
        out_ref[rows:] = two_ref[...]


def slots(own, one, two):
    shape = jax.ShapeDtypeStruct((2 * own.shape[0], own.shape[1]), own.dtype)
    return small_call(slots_kernel, shape, [own, one, two], "slots")


def project_kernel(ways, last, w_ref, *refs):
    count = len(ways)
    acts = refs[:count]
    groups, _, chans = w_ref.shape
    rows, width = acts[0].shape
    rows //= 2
    total_ref = refs[-1]
    parts = []
    for way, act in zip(ways, acts):
        for slot in (1, 2):
            block = block_at(slot, 0, 0) if way is None else way_at(slot, way)
            start = pl.multiple_of(block * width, width)
            parts.append((act, pl.ds((slot - 1) * rows, rows), pl.ds(start, width)))
    for g in range(groups):
        total = refs[count][g] if last else None
        for act, span, block in parts:
            term = jnp.dot(act[span, :], w_ref[g, block, :], preferred_element_type=f32)
            total = term if total is None else total + term
        total_ref[g] = total
    if last:
        keep_ref, send_ref = refs[-3:-1]
        half = chans // 2
        core = here()[3]
        keep_ref[...] = total_ref[:, :, pl.ds(pl.multiple_of(core * half, half), half)]
        send_ref[...] = total_ref[:, :, pl.ds(pl.multiple_of((1 - core) * half, half), half)]


def project(ways, acts, w, base=None):
    groups, _, chans = w.shape
    rows, width = acts[0].shape
    total = jax.ShapeDtypeStruct((groups, rows // 2, chans), f32)
    half = jax.ShapeDtypeStruct((groups, rows // 2, chans // 2), f32)
    last = base is not None
    return small_call(
        functools.partial(project_kernel, ways, last),
        [half, half] if last else total,
        [w] + list(acts) + ([base] if last else []),
        "project",
        2 * len(acts) * groups * width * chans * rows,
        [pltpu.VMEM(total.shape, f32)] if last else [],
        16,
    )


def shifted(values, by):
    place = lax.broadcasted_iota(jnp.int32, values.shape, 0)
    moved = pltpu.roll(values, by % CHUNKS, 0)
    inside = place >= by if by > 0 else place < CHUNKS + by
    return jnp.where(inside, moved, 0.0)


def mixer_kernel(
    keep_refs,
    other_refs,
    taps_ref,
    rates_ref,
    residues_ref,
    cot_own_ref,
    cot_other_ref,
    mixed_own_ref,
    mixed_send_ref,
    grad_ref,
    flat,
    flat_cot,
    ext,
    filt,
    drive,
    back,
    grad_ext,
):
    groups, half, chans = keep_refs[0].shape
    toks = 2 * half
    modes = rates_ref.shape[0]
    short = taps_ref.shape[1]
    rim = short - 1
    length = toks // CHUNKS
    lanes = flat.shape[-1]
    wide = (CHUNKS, lanes)
    _, _, _, core = here()

    def row(array, at):
        return jnp.broadcast_to(array[at : at + 1, :], wide)

    def column(c, _):
        some = pl.ds(pl.multiple_of(c * lanes, lanes), lanes)
        whole = pl.ds(pl.multiple_of(core * chans + c * lanes, lanes), lanes)
        own_rows = pl.ds(pl.multiple_of(core * half, half), half)
        other_rows = pl.ds(pl.multiple_of((1 - core) * half, half), half)

        for g in range(groups):
            for n, (keep_ref, other_ref) in enumerate(zip(keep_refs, other_refs)):
                total = keep_ref[g, :, some] + other_ref[g, :, some]
                flat[g, n * half : (n + 1) * half] = total.astype(bf16).astype(f32)
        flat_cot[own_rows] = cot_own_ref[:, whole].astype(f32)
        flat_cot[other_rows] = cot_other_ref[:, some].astype(f32)

        for g in range(groups):
            for k in range(length):
                ext[g, rim + k] = flat[g, pl.ds(k, CHUNKS, stride=length), :]
            for k in range(rim):
                ext[g, k] = shifted(ext[g, length + k], 1)

        taps = [taps_ref[g, :, whole] for g in range(groups)]
        tap = [[row(taps[g], j) for g in range(groups)] for j in range(short)]

        def filter_step(k, _):
            parts = []
            for g in range(groups):
                total = tap[0][g] * ext[g, k + rim]
                for j in range(1, short):
                    total = total + tap[j][g] * ext[g, k + rim - j]
                parts.append(total)
                filt[g, k] = total
            drive[k] = parts[1] * parts[2]
            back[k] = parts[0] * flat_cot[pl.ds(k, CHUNKS, stride=length), :]
            return _

        lax.fori_loop(0, length, filter_step, 0, unroll=4)

        rates = rates_ref[:, whole]
        decay_rows = jnp.exp(-rates)
        jump_rows = [jnp.exp(-rates * (length * n)) for n in (1, 2, 4)]
        residue_rows = residues_ref[:, whole]

        def long_filter(source, forward, finish):
            decay = [row(decay_rows, m) for m in range(modes)]

            def place(k):
                return k if forward else length - 1 - k

            def end_step(k, states):
                value = source[place(k)]
                return tuple(decay[m] * states[m] + value for m in range(modes))

            zero = jnp.zeros(wide, f32)
            ends = lax.fori_loop(0, length, end_step, (zero,) * modes, unroll=8)
            entering = []
            sign = 1 if forward else -1
            for m in range(modes):
                carried = ends[m]
                for jump, by in zip(jump_rows, (1, 2, 4)):
                    carried = carried + row(jump, m) * shifted(carried, sign * by)
                entering.append(shifted(carried, sign))

            def out_step(k, states):
                value = source[place(k)]
                states = tuple(decay[m] * states[m] + value for m in range(modes))
                terms = [row(residue_rows, m) * states[m] for m in range(modes)]
                while len(terms) > 1:
                    terms = [a + b for a, b in zip(terms[::2], terms[1::2])]
                finish(place(k), terms[0])
                return states

            lax.fori_loop(0, length, out_step, tuple(entering), unroll=4)

        def finish_forward(k, total):
            flat[0, pl.ds(k, CHUNKS, stride=length), :] = filt[0, k] * total
            grad_ext[0, k] = flat_cot[pl.ds(k, CHUNKS, stride=length), :] * total

        def finish_backward(k, total):
            grad_ext[1, k] = total * filt[2, k]
            grad_ext[2, k] = total * filt[1, k]

        long_filter(drive, True, finish_forward)
        mixed_own_ref[:, some] = flat[0, own_rows].astype(bf16)
        mixed_send_ref[:, some] = flat[0, other_rows].astype(bf16)
        long_filter(back, False, finish_backward)

        for g in range(groups):
            for k in range(rim):
                grad_ext[g, length + k] = shifted(grad_ext[g, k], -1)

        def adjoint_step(k, _):
            for g in range(groups):
                total = tap[0][g] * grad_ext[g, k]
                for j in range(1, short):
                    total = total + tap[j][g] * grad_ext[g, k + j]
                flat[g, pl.ds(k, CHUNKS, stride=length), :] = total
            return _

        lax.fori_loop(0, length, adjoint_step, 0, unroll=4)
        for g in range(groups):
            grad_ref[g, some, :] = flat[g].T.astype(bf16)
        return _

    lax.fori_loop(0, chans // lanes, column, 0)


def mixer(keep, other, taps, rates, residues, cot_own, cot_other):
    groups, toks, chans = keep[0].shape
    toks *= 2
    modes = rates.shape[0]
    rim = taps.shape[1] - 1
    lanes = 128
    length = toks // CHUNKS
    return small_call(
        lambda *refs: mixer_kernel(refs[:2], refs[2:4], *refs[4:]),
        [
            jax.ShapeDtypeStruct((toks // 2, chans), bf16),
            jax.ShapeDtypeStruct((toks // 2, chans), bf16),
            jax.ShapeDtypeStruct((groups, chans, toks), bf16),
        ],
        list(keep) + list(other) + [taps, rates, residues, cot_own, cot_other],
        "mixer",
        12 * modes * toks * chans,
        [
            pltpu.VMEM((groups, toks, lanes), f32),
            pltpu.VMEM((toks, lanes), f32),
            pltpu.VMEM((groups, length + rim, CHUNKS, lanes), f32),
            pltpu.VMEM((groups, length, CHUNKS, lanes), f32),
            pltpu.VMEM((length, CHUNKS, lanes), f32),
            pltpu.VMEM((length, CHUNKS, lanes), f32),
            pltpu.VMEM((groups, length + rim, CHUNKS, lanes), f32),
        ],
    )


def back_kernel(blocks, w_ref, own_ref, other_ref, *out_refs):
    groups, half, _ = own_ref.shape
    width = out_refs[0].shape[0]
    _, _, _, core = here()
    own_at = pl.multiple_of(core * half, half)
    other_at = pl.multiple_of((1 - core) * half, half)
    for block, out in zip(blocks, out_refs):
        start = pl.multiple_of(block_at(*block) * width, width)
        total = None
        for g in range(groups):
            for ref, at in ((own_ref, own_at), (other_ref, other_at)):
                term = jnp.dot(
                    w_ref[g, pl.ds(start, width), pl.ds(at, half)],
                    ref[g],
                    preferred_element_type=f32,
                )
                total = term if total is None else total + term
        out[...] = total.astype(out.dtype)


def back_project(blocks, dtypes, w, own, other, width):
    groups, half, toks = own.shape
    return small_call(
        functools.partial(back_kernel, blocks),
        [jax.ShapeDtypeStruct((width, toks), dtype) for dtype in dtypes],
        [w, own, other],
        "back_project",
        4 * len(blocks) * groups * width * half * toks,
        (),
        16,
    )


def merge_kernel(part_ref, got_ref, out_ref):
    out_ref[...] = (part_ref[...] + got_ref[...].astype(f32)).astype(bf16)


def merge(part, got):
    return small_call(merge_kernel, jax.ShapeDtypeStruct(part.shape, bf16), [part, got], "merge")


def column_kernel(slot, own_ref, x_ref, y_ref, total_ref, one_ref, two_ref):
    half = own_ref.shape[1] // 2
    total_ref[...] = own_ref[...] + x_ref[...].astype(f32) + y_ref[...].astype(f32)
    z = here()[0]
    flag = (z >> 1) if slot == 2 else 1 - (z >> 1)
    one_ref[...] = total_ref[:, pl.ds(pl.multiple_of(flag * half, half), half)].astype(bf16)
    two_ref[...] = total_ref[:, pl.ds(pl.multiple_of((1 - flag) * half, half), half)].astype(bf16)


def column(slot, own, from_x, from_y):
    shape = jax.ShapeDtypeStruct((own.shape[0], own.shape[1] // 2), bf16)
    return small_call(
        functools.partial(column_kernel, slot),
        [jax.ShapeDtypeStruct(own.shape, f32), shape, shape],
        [own, from_x, from_y],
        "column",
    )


def finish_kernel(own_ref, a_ref, b_ref, c_ref, d_ref, out_ref):
    half = own_ref.shape[1] // 2
    core = here()[3]
    mine = own_ref[:, pl.ds(pl.multiple_of(core * half, half), half)]
    total = jnp.where(is_inner(), mine, 0.0)
    for ref in (a_ref, b_ref, c_ref, d_ref):
        total = total + ref[...].astype(f32)
    out_ref[...] = total.T.astype(bf16)


def finish(own, received):
    shape = jax.ShapeDtypeStruct((own.shape[1] // 2, own.shape[0]), bf16)
    return small_call(finish_kernel, shape, [own] + received, "finish")


def pair_kernel(own_ref, other_ref, out_ref):
    half = own_ref.shape[1]
    core = here()[3]
    out_ref[:, pl.ds(pl.multiple_of(core * half, half), half)] = own_ref[...]
    out_ref[:, pl.ds(pl.multiple_of((1 - core) * half, half), half)] = other_ref[...]


def pair(own, other):
    shape = jax.ShapeDtypeStruct((own.shape[0], 2 * own.shape[1]), own.dtype)
    return small_call(pair_kernel, shape, [own, other], "pair")


def chip_plan(token_ids, embed, w_in, taps, rates, residues, cotangent):
    width = embed.shape[1]

    def swap(array):
        return lax.ppermute(array, BOTH, OTHER_CORE)

    def over_x(array):
        return lax.ppermute(array, BOTH, OVER_X)

    def over_y(array):
        return lax.ppermute(array, BOTH, OVER_Y)

    own_ids = token_ids.reshape(1, -1)
    other_ids = swap(own_ids)
    cot_half = cotangent.shape[1] // 2
    cot_other = swap(
        lax.dynamic_slice_in_dim(cotangent, (1 - lax.axis_index("ctx")) * cot_half, cot_half, 1)
    )
    own_ids, table = fetch(own_ids, embed)
    upper, lower = embed_rows(own_ids, other_ids, table)
    upper, lower, cot_other = lax.optimization_barrier((upper, lower, cot_other))

    def z_stage(rows):
        return [lax.ppermute(rows, BOTH, pairs) for pairs in GATHER_Z]

    def plane_stage(held):
        first, other = lax.ppermute(held, BOTH, FIRST_WAY), lax.ppermute(held, BOTH, OTHER_WAY)
        return first, other, lax.ppermute(first, BOTH, OTHER_WAY)

    came = z_stage(upper)
    w = load(jnp.transpose(w_in, (1, 0, 2)))
    *came, w = lax.optimization_barrier((*came, w))
    held_1 = slots(upper, *came)
    held_1, lower = lax.optimization_barrier((held_1, lower))
    came = z_stage(lower)
    first_1, other_1, both_1 = plane_stage(held_1)
    sums = project([None, 0, 1], [held_1, first_1, other_1], w)
    *came, sums = lax.optimization_barrier((*came, sums))
    held_2 = slots(lower, *came)
    first_2, other_2, both_2 = plane_stage(held_2)
    keep_1, send_1 = project([2], [both_1], w, sums)
    got_1 = swap(send_1)
    first_2, other_2, send_1 = lax.optimization_barrier((first_2, other_2, send_1))
    sums = project([None, 0, 1], [held_2, first_2, other_2], w)
    keep_2, send_2 = project([2], [both_2], w, sums)
    got_2 = swap(send_2)
    mixed_own, mixed_send, grad_own = mixer(
        (keep_1, keep_2),
        (got_1, got_2),
        jnp.transpose(taps, (1, 0, 2)),
        rates,
        residues,
        cotangent,
        cot_other,
    )
    grad_other = swap(grad_own)
    mixed_other = swap(mixed_send)

    d_2, d_1 = back_project([(2, 1, 1), (1, 1, 1)], [bf16] * 2, w, grad_own, grad_other, width)
    d_2, d_1 = over_x(d_2), over_y(d_1)
    x_2, y_2, x_1, y_1, own_2, own_1 = back_project(
        [(2, 0, 1), (2, 1, 0), (1, 0, 1), (1, 1, 0), (2, 0, 0), (1, 0, 0)],
        [bf16, f32, f32, bf16, f32, f32],
        w,
        grad_own,
        grad_other,
        width,
    )
    mixed = pair(mixed_own, mixed_other)
    x_2, d_2, mixed = lax.optimization_barrier((x_2, d_2, mixed))
    x_2, y_2 = lax.optimization_barrier((x_2, merge(y_2, d_2)))
    x_2, y_2 = over_x(x_2), over_y(y_2)
    x_1, y_1 = over_x(merge(x_1, d_1)), over_y(y_1)
    _, send_1, send_2 = column(2, own_2, x_2, y_2)
    received = [
        lax.ppermute(send_1, BOTH, SCATTER_Z[0]),
        lax.ppermute(send_2, BOTH, SCATTER_Z[1]),
    ]
    own, send_1, send_2 = column(1, own_1, x_1, y_1)
    received += [
        lax.ppermute(send_1, BOTH, SCATTER_Z[2]),
        lax.ppermute(send_2, BOTH, SCATTER_Z[3]),
    ]
    return (mixed, finish(own, received))


def solution(mesh):
    in_specs = (
        P("ctx"),
        P(None, "fsdp"),
        P("ctx", None, "fsdp"),
        P(None, None, "fsdp"),
        P(None, "fsdp"),
        P(None, "fsdp"),
        P("ctx", "fsdp"),
    )
    out_specs = (P("ctx", "fsdp"), P("ctx", "fsdp"))
    chips = mesh.shape["fsdp"] == 16 and mesh.shape["ctx"] == 2
    return jax.shard_map(
        chip_plan if chips else general_plan,
        mesh=mesh,
        in_specs=in_specs,
        out_specs=out_specs,
        check_vma=False,
    )
```

```python
import functools

import jax
import jax.numpy as jnp
from jax import lax
from jax.experimental import pallas as pl
from jax.experimental.pallas import tpu as pltpu
from jax.sharding import PartitionSpec as P

BOTH = ("fsdp", "ctx")
CHUNKS = 8
f32 = jnp.float32
bf16 = jnp.bfloat16


def from_behind(shard, axis, by):
    count = lax.axis_size(axis)
    pairs = [(i, i + by) for i in range(count) if 0 <= i + by < count]
    return lax.ppermute(shard, axis, pairs)


def pair_combine(earlier, later):
    return (earlier[0] * later[0], later[0] * earlier[1] + later[1])


def modal_states(drive, step_decay):
    tok_count = drive.shape[0]
    factors = jnp.broadcast_to(step_decay[None], (tok_count,) + step_decay.shape)
    inputs = jnp.broadcast_to(drive[:, None, :], factors.shape)
    return lax.associative_scan(pair_combine, (factors, inputs), axis=0)[1]


def short_filter(extended, taps, tok_count):
    rim_width = taps.shape[0] - 1
    filtered = taps[0] * extended[rim_width : rim_width + tok_count]
    for shift_lag in range(1, rim_width + 1):
        filtered = (
            filtered
            + taps[shift_lag] * extended[rim_width - shift_lag : rim_width - shift_lag + tok_count]
        )
    return filtered


def short_adjoint(extended, taps, tok_count):
    rim_width = taps.shape[0] - 1
    result = taps[0] * extended[:tok_count]
    for shift_lag in range(1, rim_width + 1):
        result = result + taps[shift_lag] * extended[shift_lag : shift_lag + tok_count]
    return result


def carry(block_decay, leaving, by):
    def relay_step(turn_index, incoming):
        return from_behind(block_decay * incoming + leaving, "ctx", by)

    return lax.fori_loop(0, lax.axis_size("ctx") - 1, relay_step, jnp.zeros_like(leaving))


def general_plan(token_ids, embed, w_in, taps, rates, residues, cotangent):
    tok_count = token_ids.shape[0]
    vocab_size = embed.shape[0]
    chan_width = embed.shape[1]
    rim_width = taps.shape[0] - 1
    onehot = (
        token_ids[:, None] == lax.broadcasted_iota(jnp.int32, (tok_count, vocab_size), 1)
    ).astype(bf16)
    embedded = jnp.dot(onehot, embed, preferred_element_type=f32).astype(bf16)
    features = lax.all_gather(embedded, "fsdp", axis=1, tiled=True)
    feat_width = features.shape[1]
    whole_w = lax.all_gather(w_in, "ctx", axis=0, tiled=True).reshape(feat_width, 3 * chan_width)
    projected = jnp.dot(features, whole_w, preferred_element_type=f32)
    stored = lax.optimization_barrier(projected.astype(bf16).reshape(tok_count, 3, chan_width))
    before = from_behind(stored[tok_count - rim_width :], "ctx", 1)
    extended = jnp.concatenate([before, stored], axis=0).astype(f32)
    filtered = short_filter(extended, taps, tok_count)
    query_part = filtered[:, 0]
    key_part = filtered[:, 1]
    value_part = filtered[:, 2]
    drive = key_part * value_part
    step_decay = jnp.exp(-rates)
    block_decay = jnp.exp(-rates * tok_count)
    local_states = modal_states(drive, step_decay)
    entering = carry(block_decay, local_states[tok_count - 1], 1)
    offsets = lax.broadcasted_iota(f32, (tok_count, 1, 1), 0)
    states = local_states + jnp.exp(-rates[None] * (offsets + 1.0)) * entering[None]
    long_out = jnp.sum(residues[None] * states, axis=1)
    mixed = (query_part * long_out).astype(bf16)
    incoming = cotangent.astype(f32)
    grad_long = incoming * query_part
    grad_query = incoming * long_out
    back_states = jnp.flip(modal_states(jnp.flip(grad_long, 0), step_decay), 0)
    beyond = carry(block_decay, back_states[0], -1)
    adjoint = back_states + jnp.exp(-rates[None] * (tok_count - offsets)) * beyond[None]
    grad_drive = jnp.sum(residues[None] * adjoint, axis=1)
    grad_filtered = jnp.stack([grad_query, grad_drive * value_part, grad_drive * key_part], axis=1)
    after = from_behind(grad_filtered[:rim_width], "ctx", -1)
    ext_grad = jnp.concatenate([grad_filtered, after], axis=0)
    grad_stored = short_adjoint(ext_grad, taps, tok_count).astype(bf16)
    grad_rows = grad_stored.reshape(tok_count, 3 * chan_width)
    own_rows = lax.psum_scatter(
        lax.dot_general(whole_w, grad_rows, (((1,), (1,)), ((), ())), preferred_element_type=f32),
        "fsdp",
        scatter_dimension=0,
        tiled=True,
    )
    return (mixed, own_rows.T.astype(bf16))


def device_at(z, y, x, core):
    return ((z * 2 + y) * 2 + x) * 2 + core


def everywhere(move):
    pairs = []
    for z in range(4):
        for y in range(2):
            for x in range(2):
                for core in range(2):
                    pairs.append((device_at(z, y, x, core), device_at(*move(z, y, x, core))))
    return pairs


OTHER_CORE = everywhere(lambda z, y, x, core: (z, y, x, 1 - core))


def along_z(moves):
    pairs = []
    for core in range(2):
        for (place, other), (to_place, to_other) in moves:
            z, to_z = (place, to_place) if core == 0 else (3 - place, 3 - to_place)
            for y in range(2):
                for x in range(2):
                    pairs.append(
                        (
                            device_at(z, y, x, core ^ other),
                            device_at(to_z, y, x, core ^ to_other),
                        )
                    )
    return pairs


FIRST_WAY = everywhere(lambda z, y, x, core: (z, y, 1 - x, core) if core == 0 else (z, 1 - y, x, core))
OTHER_WAY = everywhere(lambda z, y, x, core: (z, 1 - y, x, core) if core == 0 else (z, y, 1 - x, core))
GATHER_Z = (
    along_z([((0, 0), (1, 0)), ((1, 0), (0, 0)), ((0, 1), (2, 0)), ((1, 1), (3, 0))]),
    along_z([((1, 1), (2, 0)), ((0, 1), (3, 0))]),
)
SCATTER_Z = (
    along_z([((0, 0), (1, 0)), ((1, 0), (0, 0)), ((2, 0), (1, 1)), ((3, 0), (0, 1))]),
    along_z([((0, 0), (1, 1)), ((1, 0), (0, 1)), ((2, 0), (1, 0)), ((3, 0), (0, 0))]),
    along_z([((0, 0), (0, 1)), ((1, 0), (1, 1)), ((2, 0), (0, 0)), ((3, 0), (1, 0))]),
    along_z([((2, 0), (0, 1)), ((3, 0), (1, 1))]),
)

IN_VMEM = pl.BlockSpec(memory_space=pltpu.VMEM)


def small_call(kernel, out_shape, operands, name, flops=0, scratch=(), limit=8):
    sizes = [o.size * o.dtype.itemsize for o in operands]
    return pl.pallas_call(
        kernel,
        in_specs=[IN_VMEM] * len(operands),
        out_specs=jax.tree.map(lambda _: IN_VMEM, out_shape),
        out_shape=out_shape,
        scratch_shapes=list(scratch),
        compiler_params=pltpu.CompilerParams(vmem_limit_bytes=limit * 1024 * 1024),
        cost_estimate=pl.CostEstimate(
            flops=flops // 64, bytes_accessed=sum(sizes) // 64, transcendentals=0
        ),
        name=name,
    )(*operands)


def here():
    spot = lax.axis_index("fsdp")
    return spot >> 2, (spot >> 1) & 1, spot & 1, lax.axis_index("ctx")


def is_inner():
    z, _, _, core = here()
    return core == (z >> 1)


def block_at(slot, way):
    z, y, x, core = here()
    along = (z & 1) if slot == 1 else 1 - (z & 1)
    if way is not None:
        far_y, far_x = ((core, 1 - core), (1 - core, core), (1, 1))[way]
        y, x = y ^ far_y, x ^ far_x
    return along * 4 + y * 2 + x


def embed_kernel(own_ref, other_ref, table_ref, out_ref):
    vocab = table_ref.shape[0]
    half = own_ref.shape[1]
    core = here()[3]
    for ref, side in ((own_ref, core), (other_ref, 1 - core)):
        across = jnp.broadcast_to(ref[...].astype(f32), (half, half)).T
        lane = lax.broadcasted_iota(jnp.int32, (half, half), 1).astype(f32)
        picks = [(across == lane + float(first)).astype(f32) for first in range(0, vocab, half)]
        rows = jnp.dot(
            jnp.concatenate(picks, axis=1).astype(bf16), table_ref[...], preferred_element_type=f32
        )
        out_ref[pl.ds(pl.multiple_of(side * half, half), half), :] = rows.astype(bf16)


def embed_rows(own_ids, other_ids, table):
    toks, width = 2 * own_ids.shape[1], table.shape[1]
    return small_call(
        embed_kernel,
        jax.ShapeDtypeStruct((toks, width), bf16),
        [own_ids, other_ids, table],
        "embed_rows",
        2 * toks * table.shape[0] * width,
    )


def fetch_kernel(ids_ref, table_ref, ids_out, table_out, sems):
    copies = [
        pltpu.make_async_copy(ids_ref, ids_out, sems.at[0]),
        pltpu.make_async_copy(table_ref, table_out, sems.at[1]),
    ]
    for copy in copies:
        copy.start()
    for copy in copies:
        copy.wait()


def in_hbm(array):
    return pltpu.with_memory_space_constraint(array, pltpu.HBM)


def in_vmem(array):
    return pltpu.with_memory_space_constraint(array, pltpu.VMEM)


def fetch(ids, table):
    out = pl.pallas_call(
        fetch_kernel,
        in_specs=[pl.BlockSpec(memory_space=pltpu.HBM)] * 2,
        out_specs=[IN_VMEM] * 2,
        out_shape=[pltpu.VMEM(ids.shape, ids.dtype), pltpu.VMEM(table.shape, bf16)],
        scratch_shapes=[pltpu.SemaphoreType.DMA((2,))],
        compiler_params=pltpu.CompilerParams(vmem_limit_bytes=2 * 1024 * 1024),
        cost_estimate=pl.CostEstimate(
            flops=0, bytes_accessed=4 * table.size, transcendentals=0
        ),
        name="fetch",
    )(in_hbm(ids), in_hbm(table))
    return [in_vmem(array) for array in out]


def load_kernel(w_ref, out_ref, sem):
    copy = pltpu.make_async_copy(w_ref, out_ref, sem)
    copy.start()
    copy.wait()


def load(w):
    out = pl.pallas_call(
        load_kernel,
        in_specs=[pl.BlockSpec(memory_space=pltpu.HBM)],
        out_specs=IN_VMEM,
        out_shape=pltpu.VMEM(w.shape, w.dtype),
        scratch_shapes=[pltpu.SemaphoreType.DMA],
        compiler_params=pltpu.CompilerParams(vmem_limit_bytes=2 * 1024 * 1024),
        cost_estimate=pl.CostEstimate(
            flops=0, bytes_accessed=2 * w.size * w.dtype.itemsize, transcendentals=0
        ),
        name="load",
    )(in_hbm(w))
    return in_vmem(out)


def slots_kernel(own_ref, one_ref, two_ref, out_ref):
    rows = own_ref.shape[0]

    @pl.when(is_inner())
    def _():
        out_ref[:rows] = own_ref[...]
        out_ref[rows:] = one_ref[...]

    @pl.when(jnp.logical_not(is_inner()))
    def _():
        out_ref[:rows] = one_ref[...]
        out_ref[rows:] = two_ref[...]


def slots(own, one, two):
    shape = jax.ShapeDtypeStruct((2 * own.shape[0], own.shape[1]), own.dtype)
    return small_call(slots_kernel, shape, [own, one, two], "slots")


def project_kernel(ways, has_base, last, w_ref, *refs):
    count = len(ways)
    acts = refs[:count]
    groups, _, chans = w_ref.shape
    rows, width = acts[0].shape
    rows //= 2
    total_ref = refs[-1]
    parts = []
    for way, act in zip(ways, acts):
        for slot in (1, 2):
            start = pl.multiple_of(block_at(slot, way) * width, width)
            parts.append((act, pl.ds((slot - 1) * rows, rows), pl.ds(start, width)))
    for g in range(groups):
        total = refs[count][g] if has_base else None
        for act, span, block in parts:
            term = jnp.dot(act[span, :], w_ref[g, block, :], preferred_element_type=f32)
            total = term if total is None else total + term
        total_ref[g] = total
    if last:
        keep_ref, send_ref = refs[-3:-1]
        half = chans // 2
        core = here()[3]
        keep_ref[...] = total_ref[:, :, pl.ds(pl.multiple_of(core * half, half), half)]
        send_ref[...] = total_ref[:, :, pl.ds(pl.multiple_of((1 - core) * half, half), half)]


def project(ways, acts, w, base, last):
    groups, _, chans = w.shape
    rows, width = acts[0].shape
    total = jax.ShapeDtypeStruct((groups, rows // 2, chans), f32)
    half = jax.ShapeDtypeStruct((groups, rows // 2, chans // 2), f32)
    return small_call(
        functools.partial(project_kernel, ways, base is not None, last),
        [half, half] if last else total,
        [w] + list(acts) + ([] if base is None else [base]),
        "project",
        2 * len(acts) * groups * width * chans * rows,
        [pltpu.VMEM(total.shape, f32)] if last else [],
        16,
    )


def shifted(values, by):
    place = lax.broadcasted_iota(jnp.int32, values.shape, 0)
    moved = pltpu.roll(values, by % CHUNKS, 0)
    inside = place >= by if by > 0 else place < CHUNKS + by
    return jnp.where(inside, moved, 0.0)


def mixer_kernel(
    keep_ref,
    other_ref,
    taps_ref,
    rates_ref,
    residues_ref,
    cot_own_ref,
    cot_other_ref,
    mixed_own_ref,
    mixed_send_ref,
    grad_ref,
    flat,
    flat_cot,
    ext,
    filt,
    drive,
    back,
    grad_ext,
):
    groups, toks, chans = keep_ref.shape
    half = toks // 2
    modes = rates_ref.shape[0]
    short = taps_ref.shape[1]
    rim = short - 1
    length = toks // CHUNKS
    lanes = flat.shape[-1]
    wide = (CHUNKS, lanes)
    _, _, _, core = here()

    def row(array, at):
        return jnp.broadcast_to(array[at : at + 1, :], wide)

    def column(c, _):
        some = pl.ds(pl.multiple_of(c * lanes, lanes), lanes)
        whole = pl.ds(pl.multiple_of(core * chans + c * lanes, lanes), lanes)
        own_rows = pl.ds(pl.multiple_of(core * half, half), half)
        other_rows = pl.ds(pl.multiple_of((1 - core) * half, half), half)

        for g in range(groups):
            flat[g] = (keep_ref[g, :, some] + other_ref[g, :, some]).astype(bf16).astype(f32)
        flat_cot[own_rows] = cot_own_ref[:, whole].astype(f32)
        flat_cot[other_rows] = cot_other_ref[:, some].astype(f32)

        for g in range(groups):
            for k in range(length):
                ext[g, rim + k] = flat[g, pl.ds(k, CHUNKS, stride=length), :]
            for k in range(rim):
                ext[g, k] = shifted(ext[g, length + k], 1)

        taps = [taps_ref[g, :, whole] for g in range(groups)]
        tap = [[row(taps[g], j) for g in range(groups)] for j in range(short)]

        def filter_step(k, _):
            parts = []
            for g in range(groups):
                total = tap[0][g] * ext[g, k + rim]
                for j in range(1, short):
                    total = total + tap[j][g] * ext[g, k + rim - j]
                parts.append(total)
                filt[g, k] = total
            drive[k] = parts[1] * parts[2]
            back[k] = parts[0] * flat_cot[pl.ds(k, CHUNKS, stride=length), :]
            return _

        lax.fori_loop(0, length, filter_step, 0, unroll=4)

        rates = rates_ref[:, whole]
        decay_rows = jnp.exp(-rates)
        jump_rows = [jnp.exp(-rates * (length * n)) for n in (1, 2, 4)]
        residue_rows = residues_ref[:, whole]

        def long_filter(source, forward, finish):
            decay = [row(decay_rows, m) for m in range(modes)]

            def place(k):
                return k if forward else length - 1 - k

            def end_step(k, states):
                value = source[place(k)]
                return tuple(decay[m] * states[m] + value for m in range(modes))

            zero = jnp.zeros(wide, f32)
            ends = lax.fori_loop(0, length, end_step, (zero,) * modes, unroll=8)
            entering = []
            sign = 1 if forward else -1
            for m in range(modes):
                carried = ends[m]
                for jump, by in zip(jump_rows, (1, 2, 4)):
                    carried = carried + row(jump, m) * shifted(carried, sign * by)
                entering.append(shifted(carried, sign))

            def out_step(k, states):
                value = source[place(k)]
                states = tuple(decay[m] * states[m] + value for m in range(modes))
                terms = [row(residue_rows, m) * states[m] for m in range(modes)]
                while len(terms) > 1:
                    terms = [a + b for a, b in zip(terms[::2], terms[1::2])]
                finish(place(k), terms[0])
                return states

            lax.fori_loop(0, length, out_step, tuple(entering), unroll=4)

        def finish_forward(k, total):
            flat[0, pl.ds(k, CHUNKS, stride=length), :] = filt[0, k] * total
            grad_ext[0, k] = flat_cot[pl.ds(k, CHUNKS, stride=length), :] * total

        def finish_backward(k, total):
            grad_ext[1, k] = total * filt[2, k]
            grad_ext[2, k] = total * filt[1, k]

        long_filter(drive, True, finish_forward)
        mixed_own_ref[:, some] = flat[0, own_rows].astype(bf16)
        mixed_send_ref[:, some] = flat[0, other_rows].astype(bf16)
        long_filter(back, False, finish_backward)

        for g in range(groups):
            for k in range(rim):
                grad_ext[g, length + k] = shifted(grad_ext[g, k], -1)

        def adjoint_step(k, _):
            for g in range(groups):
                total = tap[0][g] * grad_ext[g, k]
                for j in range(1, short):
                    total = total + tap[j][g] * grad_ext[g, k + j]
                flat[g, pl.ds(k, CHUNKS, stride=length), :] = total
            return _

        lax.fori_loop(0, length, adjoint_step, 0, unroll=4)
        for g in range(groups):
            grad_ref[g, some, :] = flat[g].T.astype(bf16)
        return _

    lax.fori_loop(0, chans // lanes, column, 0)


def mixer(keep, other, taps, rates, residues, cot_own, cot_other):
    groups, toks, chans = keep.shape
    modes = rates.shape[0]
    rim = taps.shape[1] - 1
    lanes = 128
    length = toks // CHUNKS
    return small_call(
        mixer_kernel,
        [
            jax.ShapeDtypeStruct((toks // 2, chans), bf16),
            jax.ShapeDtypeStruct((toks // 2, chans), bf16),
            jax.ShapeDtypeStruct((groups, chans, toks), bf16),
        ],
        [keep, other, taps, rates, residues, cot_own, cot_other],
        "mixer",
        12 * modes * toks * chans,
        [
            pltpu.VMEM((groups, toks, lanes), f32),
            pltpu.VMEM((toks, lanes), f32),
            pltpu.VMEM((groups, length + rim, CHUNKS, lanes), f32),
            pltpu.VMEM((groups, length, CHUNKS, lanes), f32),
            pltpu.VMEM((length, CHUNKS, lanes), f32),
            pltpu.VMEM((length, CHUNKS, lanes), f32),
            pltpu.VMEM((groups, length + rim, CHUNKS, lanes), f32),
        ],
    )


def back_kernel(outs, w_ref, own_ref, other_ref, *out_refs):
    groups, half, _ = own_ref.shape
    core = here()[3]
    own_at = pl.multiple_of(core * half, half)
    other_at = pl.multiple_of((1 - core) * half, half)
    for blocks, out in zip(outs, out_refs):
        width = out.shape[0] // len(blocks)
        for n, block in enumerate(blocks):
            start = pl.multiple_of(block_at(*block) * width, width)
            total = None
            for g in range(groups):
                for ref, at in ((own_ref, own_at), (other_ref, other_at)):
                    term = jnp.dot(
                        w_ref[g, pl.ds(start, width), pl.ds(at, half)],
                        ref[g],
                        preferred_element_type=f32,
                    )
                    total = term if total is None else total + term
            out[n * width : (n + 1) * width] = total.astype(out.dtype)


def back_project(outs, dtypes, w, own, other, width):
    groups, half, toks = own.shape
    return small_call(
        functools.partial(back_kernel, outs),
        [
            jax.ShapeDtypeStruct((width * len(blocks), toks), dtype)
            for blocks, dtype in zip(outs, dtypes)
        ],
        [w, own, other],
        "back_project",
        4 * sum(len(blocks) for blocks in outs) * groups * width * half * toks,
        (),
        16,
    )


def merge_kernel(two_ref, one_ref, got_ref, two_out, one_out):
    width = one_ref.shape[0]
    one_out[...] = (one_ref[...] + got_ref[:width].astype(f32)).astype(bf16)
    two_out[...] = (two_ref[...] + got_ref[width:].astype(f32)).astype(bf16)


def merge(two, one, got):
    shape = jax.ShapeDtypeStruct(one.shape, bf16)
    return small_call(merge_kernel, [shape, shape], [two, one, got], "merge")


def column_kernel(slot, own_ref, other_ref, first_ref, *out_refs):
    width, toks = own_ref.shape
    half = toks // 2
    total = (
        own_ref[...]
        + other_ref[(slot - 1) * width : slot * width].astype(f32)
        + first_ref[...].astype(f32)
    )
    z, _, _, core = here()
    side = (z >> 1) if slot == 2 else 1 - (z >> 1)
    low, high = total[:, :half], total[:, half:]
    send_low, send_high = out_refs[0], out_refs[1]

    @pl.when(side == 0)
    def _():
        send_low[...] = low.astype(bf16)
        send_high[...] = high.astype(bf16)

    @pl.when(side == 1)
    def _():
        send_low[...] = high.astype(bf16)
        send_high[...] = low.astype(bf16)

    if len(out_refs) == 3:
        inner = is_inner()
        out_refs[2][...] = jnp.where(inner, jnp.where(core == 0, low, high), 0.0)


def column(slot, own, other, first):
    width, toks = own.shape
    half = jax.ShapeDtypeStruct((width, toks // 2), bf16)
    kept = [jax.ShapeDtypeStruct((width, toks // 2), f32)] if slot == 1 else []
    return small_call(
        functools.partial(column_kernel, slot), [half, half] + kept, [own, other, first], "column"
    )


def finish_kernel(own_ref, a_ref, b_ref, c_ref, d_ref, out_ref):
    total = own_ref[...]
    for ref in (a_ref, b_ref, c_ref, d_ref):
        total = total + ref[...].astype(f32)
    out_ref[...] = total.T.astype(bf16)


def finish(own, received):
    shape = jax.ShapeDtypeStruct((own.shape[1], own.shape[0]), bf16)
    return small_call(finish_kernel, shape, [own] + received, "finish")


def pair_kernel(own_ref, other_ref, out_ref):
    half = own_ref.shape[1]
    core = here()[3]
    out_ref[:, pl.ds(pl.multiple_of(core * half, half), half)] = own_ref[...]
    out_ref[:, pl.ds(pl.multiple_of((1 - core) * half, half), half)] = other_ref[...]


def pair(own, other):
    shape = jax.ShapeDtypeStruct((own.shape[0], 2 * own.shape[1]), own.dtype)
    return small_call(pair_kernel, shape, [own, other], "pair")


def chip_plan(token_ids, embed, w_in, taps, rates, residues, cotangent):
    width = embed.shape[1]

    def swap(array):
        return lax.ppermute(array, BOTH, OTHER_CORE)

    def first_way(array):
        return lax.ppermute(array, BOTH, FIRST_WAY)

    def other_way(array):
        return lax.ppermute(array, BOTH, OTHER_WAY)

    own_ids = token_ids.reshape(1, -1)
    other_ids = swap(own_ids)
    cot_half = cotangent.shape[1] // 2
    cot_other = swap(
        lax.dynamic_slice_in_dim(cotangent, (1 - lax.axis_index("ctx")) * cot_half, cot_half, 1)
    )
    own_ids, table = fetch(own_ids, embed)
    embedded = embed_rows(own_ids, other_ids, table)
    embedded, cot_other = lax.optimization_barrier((embedded, cot_other))

    came = [lax.ppermute(embedded, BOTH, pairs) for pairs in GATHER_Z]
    w = load(jnp.transpose(w_in, (1, 0, 2)))
    *came, w = lax.optimization_barrier((*came, w))
    held = slots(embedded, *came)
    first, other = first_way(held), other_way(held)
    sums = project([None], [held], w, None, False)
    first, sums = lax.optimization_barrier((first, sums))
    both = other_way(first)
    sums = project([0, 1], [first, other], w, sums, False)
    keep, send = project([2], [both], w, sums, True)
    mixed_own, mixed_send, grad_own = mixer(
        keep, swap(send), jnp.transpose(taps, (1, 0, 2)), rates, residues, cotangent, cot_other
    )
    grad_other = swap(grad_own)
    mixed_other = swap(mixed_send)

    (across,) = back_project([[(1, 2), (2, 2)]], [bf16], w, grad_own, grad_other, width)
    across = other_way(across)
    (other,) = back_project([[(1, 1), (2, 1)]], [bf16], w, grad_own, grad_other, width)
    other = other_way(other)
    first_2, first_1, own_2, own_1 = back_project(
        [[(2, 0)], [(1, 0)], [(2, None)], [(1, None)]], [f32] * 4, w, grad_own, grad_other, width
    )
    mixed = pair(mixed_own, mixed_other)
    across, mixed = lax.optimization_barrier((across, mixed))
    first_2, first_1 = merge(first_2, first_1, across)
    first_2, first_1 = first_way(first_2), first_way(first_1)
    sends = column(2, own_2, other, first_2)
    received = [lax.ppermute(a, BOTH, pairs) for a, pairs in zip(sends, SCATTER_Z[:2])]
    *sends, own = column(1, own_1, other, first_1)
    received += [lax.ppermute(a, BOTH, pairs) for a, pairs in zip(sends, SCATTER_Z[2:])]
    return (mixed, finish(own, received))


def solution(mesh):
    in_specs = (
        P("ctx"),
        P(None, "fsdp"),
        P("ctx", None, "fsdp"),
        P(None, None, "fsdp"),
        P(None, "fsdp"),
        P(None, "fsdp"),
        P("ctx", "fsdp"),
    )
    out_specs = (P("ctx", "fsdp"), P("ctx", "fsdp"))
    chips = mesh.shape["fsdp"] == 16 and mesh.shape["ctx"] == 2
    return jax.shard_map(
        chip_plan if chips else general_plan,
        mesh=mesh,
        in_specs=in_specs,
        out_specs=out_specs,
        check_vma=False,
    )
```

```python
import functools

import jax
import jax.numpy as jnp
from jax import lax
from jax.experimental import pallas as pl
from jax.experimental.pallas import tpu as pltpu
from jax.sharding import PartitionSpec as P

BOTH = ("fsdp", "ctx")
CHUNKS = 8
f32 = jnp.float32
bf16 = jnp.bfloat16


def from_behind(shard, axis, by):
    count = lax.axis_size(axis)
    pairs = [(i, i + by) for i in range(count) if 0 <= i + by < count]
    return lax.ppermute(shard, axis, pairs)


def pair_combine(earlier, later):
    return (earlier[0] * later[0], later[0] * earlier[1] + later[1])


def modal_states(drive, step_decay):
    tok_count = drive.shape[0]
    factors = jnp.broadcast_to(step_decay[None], (tok_count,) + step_decay.shape)
    inputs = jnp.broadcast_to(drive[:, None, :], factors.shape)
    return lax.associative_scan(pair_combine, (factors, inputs), axis=0)[1]


def short_filter(extended, taps, tok_count):
    rim_width = taps.shape[0] - 1
    filtered = taps[0] * extended[rim_width : rim_width + tok_count]
    for shift_lag in range(1, rim_width + 1):
        filtered = (
            filtered
            + taps[shift_lag] * extended[rim_width - shift_lag : rim_width - shift_lag + tok_count]
        )
    return filtered


def short_adjoint(extended, taps, tok_count):
    rim_width = taps.shape[0] - 1
    result = taps[0] * extended[:tok_count]
    for shift_lag in range(1, rim_width + 1):
        result = result + taps[shift_lag] * extended[shift_lag : shift_lag + tok_count]
    return result


def carry(block_decay, leaving, by):
    def relay_step(turn_index, incoming):
        return from_behind(block_decay * incoming + leaving, "ctx", by)

    return lax.fori_loop(0, lax.axis_size("ctx") - 1, relay_step, jnp.zeros_like(leaving))


def general_plan(token_ids, embed, w_in, taps, rates, residues, cotangent):
    tok_count = token_ids.shape[0]
    vocab_size = embed.shape[0]
    chan_width = embed.shape[1]
    rim_width = taps.shape[0] - 1
    onehot = (
        token_ids[:, None] == lax.broadcasted_iota(jnp.int32, (tok_count, vocab_size), 1)
    ).astype(bf16)
    embedded = jnp.dot(onehot, embed, preferred_element_type=f32).astype(bf16)
    features = lax.all_gather(embedded, "fsdp", axis=1, tiled=True)
    feat_width = features.shape[1]
    whole_w = lax.all_gather(w_in, "ctx", axis=0, tiled=True).reshape(feat_width, 3 * chan_width)
    projected = jnp.dot(features, whole_w, preferred_element_type=f32)
    stored = lax.optimization_barrier(projected.astype(bf16).reshape(tok_count, 3, chan_width))
    before = from_behind(stored[tok_count - rim_width :], "ctx", 1)
    extended = jnp.concatenate([before, stored], axis=0).astype(f32)
    filtered = short_filter(extended, taps, tok_count)
    query_part = filtered[:, 0]
    key_part = filtered[:, 1]
    value_part = filtered[:, 2]
    drive = key_part * value_part
    step_decay = jnp.exp(-rates)
    block_decay = jnp.exp(-rates * tok_count)
    local_states = modal_states(drive, step_decay)
    entering = carry(block_decay, local_states[tok_count - 1], 1)
    offsets = lax.broadcasted_iota(f32, (tok_count, 1, 1), 0)
    states = local_states + jnp.exp(-rates[None] * (offsets + 1.0)) * entering[None]
    long_out = jnp.sum(residues[None] * states, axis=1)
    mixed = (query_part * long_out).astype(bf16)
    incoming = cotangent.astype(f32)
    grad_long = incoming * query_part
    grad_query = incoming * long_out
    back_states = jnp.flip(modal_states(jnp.flip(grad_long, 0), step_decay), 0)
    beyond = carry(block_decay, back_states[0], -1)
    adjoint = back_states + jnp.exp(-rates[None] * (tok_count - offsets)) * beyond[None]
    grad_drive = jnp.sum(residues[None] * adjoint, axis=1)
    grad_filtered = jnp.stack([grad_query, grad_drive * value_part, grad_drive * key_part], axis=1)
    after = from_behind(grad_filtered[:rim_width], "ctx", -1)
    ext_grad = jnp.concatenate([grad_filtered, after], axis=0)
    grad_stored = short_adjoint(ext_grad, taps, tok_count).astype(bf16)
    grad_rows = grad_stored.reshape(tok_count, 3 * chan_width)
    own_rows = lax.psum_scatter(
        lax.dot_general(whole_w, grad_rows, (((1,), (1,)), ((), ())), preferred_element_type=f32),
        "fsdp",
        scatter_dimension=0,
        tiled=True,
    )
    return (mixed, own_rows.T.astype(bf16))


def device_at(z, y, x, core):
    return ((z * 2 + y) * 2 + x) * 2 + core


def everywhere(move):
    pairs = []
    for z in range(4):
        for y in range(2):
            for x in range(2):
                for core in range(2):
                    pairs.append((device_at(z, y, x, core), device_at(*move(z, y, x, core))))
    return pairs


OTHER_CORE = everywhere(lambda z, y, x, core: (z, y, x, 1 - core))


def along_z(moves):
    pairs = []
    for core in range(2):
        for (place, other), (to_place, to_other) in moves:
            z, to_z = (place, to_place) if core == 0 else (3 - place, 3 - to_place)
            for y in range(2):
                for x in range(2):
                    pairs.append(
                        (
                            device_at(z, y, x, core ^ other),
                            device_at(to_z, y, x, core ^ to_other),
                        )
                    )
    return pairs


FIRST_WAY = everywhere(lambda z, y, x, core: (z, y, 1 - x, core) if core == 0 else (z, 1 - y, x, core))
OTHER_WAY = everywhere(lambda z, y, x, core: (z, 1 - y, x, core) if core == 0 else (z, y, 1 - x, core))
def some_move(move, inner):
    def target(z, y, x, core):
        return move(z, y, x, core) if (core == z >> 1) == inner else (z, y, x, core)

    return everywhere(target)


INNER_Y = some_move(lambda z, y, x, core: (z, 1 - y, x, core), True)
INNER_XY = some_move(lambda z, y, x, core: (z, 1 - y, 1 - x, core), True)
OUTER_X = some_move(lambda z, y, x, core: (z, y, 1 - x, core), False)
OUTER_Y = some_move(lambda z, y, x, core: (z, 1 - y, x, core), False)
OUTER_XY = some_move(lambda z, y, x, core: (z, 1 - y, 1 - x, core), False)
GATHER_Z = along_z([((0, 0), (1, 0)), ((1, 0), (0, 0)), ((0, 1), (2, 0)), ((1, 1), (3, 0))])
OUTER_Z_INNER_X = along_z([((1, 1), (2, 0)), ((0, 1), (3, 0))]) + [
    pair
    for pair in everywhere(lambda z, y, x, core: (z, y, 1 - x, core))
    if (pair[0] & 1) == pair[0] >> 4
]
SCATTER_Z = (
    along_z([((0, 0), (1, 0)), ((1, 0), (0, 0)), ((2, 0), (1, 1)), ((3, 0), (0, 1))]),
    along_z([((0, 0), (1, 1)), ((1, 0), (0, 1)), ((2, 0), (1, 0)), ((3, 0), (0, 0))]),
    along_z([((0, 0), (0, 1)), ((1, 0), (1, 1)), ((2, 0), (0, 0)), ((3, 0), (1, 0))]),
    along_z([((2, 0), (0, 1)), ((3, 0), (1, 1))]),
)

IN_VMEM = pl.BlockSpec(memory_space=pltpu.VMEM)


def small_call(kernel, out_shape, operands, name, flops=0, scratch=(), limit=8):
    sizes = [o.size * o.dtype.itemsize for o in operands]
    return pl.pallas_call(
        kernel,
        in_specs=[IN_VMEM] * len(operands),
        out_specs=jax.tree.map(lambda _: IN_VMEM, out_shape),
        out_shape=out_shape,
        scratch_shapes=list(scratch),
        compiler_params=pltpu.CompilerParams(vmem_limit_bytes=limit * 1024 * 1024),
        cost_estimate=pl.CostEstimate(
            flops=flops // 64, bytes_accessed=sum(sizes) // 64, transcendentals=0
        ),
        name=name,
    )(*operands)


def here():
    spot = lax.axis_index("fsdp")
    return spot >> 2, (spot >> 1) & 1, spot & 1, lax.axis_index("ctx")


def is_inner():
    z, _, _, core = here()
    return core == (z >> 1)


def block_at(slot, way):
    z, y, x, core = here()
    along = (z & 1) if slot == 1 else 1 - (z & 1)
    far = {None: (0, 0), 0: (core, 1 - core), 1: (1 - core, core), 2: (1, 1), "x": (0, 1), "y": (1, 0)}
    far_y, far_x = far[way]
    return along * 4 + (y ^ far_y) * 2 + (x ^ far_x)


def embed_kernel(own_ref, other_ref, table_ref, out_ref):
    vocab = table_ref.shape[0]
    half = own_ref.shape[1]
    core = here()[3]
    for ref, side in ((own_ref, core), (other_ref, 1 - core)):
        across = jnp.broadcast_to(ref[...].astype(f32), (half, half)).T
        lane = lax.broadcasted_iota(jnp.int32, (half, half), 1).astype(f32)
        picks = [(across == lane + float(first)).astype(f32) for first in range(0, vocab, half)]
        rows = jnp.dot(
            jnp.concatenate(picks, axis=1).astype(bf16), table_ref[...], preferred_element_type=f32
        )
        out_ref[pl.ds(pl.multiple_of(side * half, half), half), :] = rows.astype(bf16)


def embed_rows(own_ids, other_ids, table):
    toks, width = 2 * own_ids.shape[1], table.shape[1]
    return small_call(
        embed_kernel,
        jax.ShapeDtypeStruct((toks, width), bf16),
        [own_ids, other_ids, table],
        "embed_rows",
        2 * toks * table.shape[0] * width,
    )


def fetch_kernel(ids_ref, table_ref, ids_out, table_out, sems):
    copies = [
        pltpu.make_async_copy(ids_ref, ids_out, sems.at[0]),
        pltpu.make_async_copy(table_ref, table_out, sems.at[1]),
    ]
    for copy in copies:
        copy.start()
    for copy in copies:
        copy.wait()


def in_hbm(array):
    return pltpu.with_memory_space_constraint(array, pltpu.HBM)


def in_vmem(array):
    return pltpu.with_memory_space_constraint(array, pltpu.VMEM)


def fetch(ids, table):
    out = pl.pallas_call(
        fetch_kernel,
        in_specs=[pl.BlockSpec(memory_space=pltpu.HBM)] * 2,
        out_specs=[IN_VMEM] * 2,
        out_shape=[pltpu.VMEM(ids.shape, ids.dtype), pltpu.VMEM(table.shape, bf16)],
        scratch_shapes=[pltpu.SemaphoreType.DMA((2,))],
        compiler_params=pltpu.CompilerParams(vmem_limit_bytes=2 * 1024 * 1024),
        cost_estimate=pl.CostEstimate(
            flops=0, bytes_accessed=4 * table.size, transcendentals=0
        ),
        name="fetch",
    )(in_hbm(ids), in_hbm(table))
    return [in_vmem(array) for array in out]


def load_kernel(w_ref, out_ref, sem):
    copy = pltpu.make_async_copy(w_ref, out_ref, sem)
    copy.start()
    copy.wait()


def load(w):
    out = pl.pallas_call(
        load_kernel,
        in_specs=[pl.BlockSpec(memory_space=pltpu.HBM)],
        out_specs=IN_VMEM,
        out_shape=pltpu.VMEM(w.shape, w.dtype),
        scratch_shapes=[pltpu.SemaphoreType.DMA],
        compiler_params=pltpu.CompilerParams(vmem_limit_bytes=2 * 1024 * 1024),
        cost_estimate=pl.CostEstimate(
            flops=0, bytes_accessed=2 * w.size * w.dtype.itemsize, transcendentals=0
        ),
        name="load",
    )(in_hbm(w))
    return in_vmem(out)


def project_kernel(inner, outer, count, has_base, last, w_ref, *refs):
    acts = refs[:count]
    groups, _, chans = w_ref.shape
    width = acts[0].shape[1]
    if last:
        keep_ref, send_ref, total_ref = refs[-3:]
    else:
        total_ref = refs[-1]

    def add(entries):
        spans = [
            pl.ds(pl.multiple_of(block_at(slot, way) * width, width), width)
            for _, slot, way in entries
        ]
        for g in range(groups):
            total = refs[count][g] if has_base else None
            for (which, _, _), span in zip(entries, spans):
                term = jnp.dot(acts[which][...], w_ref[g, span, :], preferred_element_type=f32)
                total = term if total is None else total + term
            total_ref[g] = total

    pl.when(is_inner())(lambda: add(inner))
    pl.when(jnp.logical_not(is_inner()))(lambda: add(outer))
    if last:
        half = chans // 2
        core = here()[3]
        keep_ref[...] = total_ref[:, :, pl.ds(pl.multiple_of(core * half, half), half)]
        send_ref[...] = total_ref[:, :, pl.ds(pl.multiple_of((1 - core) * half, half), half)]


def project(acts, inner, outer, w, base, last):
    groups, _, chans = w.shape
    toks, width = acts[0].shape
    total = jax.ShapeDtypeStruct((groups, toks, chans), f32)
    half = jax.ShapeDtypeStruct((groups, toks, chans // 2), f32)
    return small_call(
        functools.partial(project_kernel, inner, outer, len(acts), base is not None, last),
        [half, half] if last else total,
        [w] + list(acts) + ([] if base is None else [base]),
        "project",
        2 * max(len(inner), len(outer)) * groups * width * chans * toks,
        [pltpu.VMEM(total.shape, f32)] if last else [],
        16,
    )


def shifted(values, by):
    place = lax.broadcasted_iota(jnp.int32, values.shape, 0)
    moved = pltpu.roll(values, by % CHUNKS, 0)
    inside = place >= by if by > 0 else place < CHUNKS + by
    return jnp.where(inside, moved, 0.0)


def mixer_kernel(
    keep_ref,
    other_ref,
    taps_ref,
    rates_ref,
    residues_ref,
    cot_own_ref,
    cot_other_ref,
    mixed_own_ref,
    mixed_send_ref,
    grad_ref,
    flat,
    flat_cot,
    ext,
    filt,
    drive,
    back,
    grad_ext,
):
    groups, toks, chans = keep_ref.shape
    half = toks // 2
    modes = rates_ref.shape[0]
    short = taps_ref.shape[1]
    rim = short - 1
    length = toks // CHUNKS
    lanes = flat.shape[-1]
    wide = (CHUNKS, lanes)
    _, _, _, core = here()

    def row(array, at):
        return jnp.broadcast_to(array[at : at + 1, :], wide)

    def column(c, _):
        some = pl.ds(pl.multiple_of(c * lanes, lanes), lanes)
        whole = pl.ds(pl.multiple_of(core * chans + c * lanes, lanes), lanes)
        own_rows = pl.ds(pl.multiple_of(core * half, half), half)
        other_rows = pl.ds(pl.multiple_of((1 - core) * half, half), half)

        for g in range(groups):
            flat[g] = (keep_ref[g, :, some] + other_ref[g, :, some]).astype(bf16).astype(f32)
        flat_cot[own_rows] = cot_own_ref[:, whole].astype(f32)
        flat_cot[other_rows] = cot_other_ref[:, whole].astype(f32)

        for g in range(groups):
            for k in range(length):
                ext[g, rim + k] = flat[g, pl.ds(k, CHUNKS, stride=length), :]
            for k in range(rim):
                ext[g, k] = shifted(ext[g, length + k], 1)

        taps = [taps_ref[g, :, whole] for g in range(groups)]
        tap = [[row(taps[g], j) for g in range(groups)] for j in range(short)]

        def filter_step(k, _):
            parts = []
            for g in range(groups):
                total = tap[0][g] * ext[g, k + rim]
                for j in range(1, short):
                    total = total + tap[j][g] * ext[g, k + rim - j]
                parts.append(total)
                filt[g, k] = total
            drive[k] = parts[1] * parts[2]
            back[k] = parts[0] * flat_cot[pl.ds(k, CHUNKS, stride=length), :]
            return _

        lax.fori_loop(0, length, filter_step, 0, unroll=4)

        rates = rates_ref[:, whole]
        decay_rows = jnp.exp(-rates)
        jump_rows = [jnp.exp(-rates * (length * n)) for n in (1, 2, 4)]
        residue_rows = residues_ref[:, whole]

        def long_filter(source, forward, finish):
            decay = [row(decay_rows, m) for m in range(modes)]

            def place(k):
                return k if forward else length - 1 - k

            def end_step(k, states):
                value = source[place(k)]
                return tuple(decay[m] * states[m] + value for m in range(modes))

            zero = jnp.zeros(wide, f32)
            ends = lax.fori_loop(0, length, end_step, (zero,) * modes, unroll=8)
            entering = []
            sign = 1 if forward else -1
            for m in range(modes):
                carried = ends[m]
                for jump, by in zip(jump_rows, (1, 2, 4)):
                    carried = carried + row(jump, m) * shifted(carried, sign * by)
                entering.append(shifted(carried, sign))

            def out_step(k, states):
                value = source[place(k)]
                states = tuple(decay[m] * states[m] + value for m in range(modes))
                terms = [row(residue_rows, m) * states[m] for m in range(modes)]
                while len(terms) > 1:
                    terms = [a + b for a, b in zip(terms[::2], terms[1::2])]
                finish(place(k), terms[0])
                return states

            lax.fori_loop(0, length, out_step, tuple(entering), unroll=4)

        def finish_forward(k, total):
            flat[0, pl.ds(k, CHUNKS, stride=length), :] = filt[0, k] * total
            grad_ext[0, k] = flat_cot[pl.ds(k, CHUNKS, stride=length), :] * total

        def finish_backward(k, total):
            grad_ext[1, k] = total * filt[2, k]
            grad_ext[2, k] = total * filt[1, k]

        long_filter(drive, True, finish_forward)
        mixed_own_ref[:, some] = flat[0, own_rows].astype(bf16)
        mixed_send_ref[:, some] = flat[0, other_rows].astype(bf16)
        long_filter(back, False, finish_backward)

        for g in range(groups):
            for k in range(rim):
                grad_ext[g, length + k] = shifted(grad_ext[g, k], -1)

        def adjoint_step(k, _):
            for g in range(groups):
                total = tap[0][g] * grad_ext[g, k]
                for j in range(1, short):
                    total = total + tap[j][g] * grad_ext[g, k + j]
                flat[g, pl.ds(k, CHUNKS, stride=length), :] = total
            return _

        lax.fori_loop(0, length, adjoint_step, 0, unroll=4)
        for g in range(groups):
            grad_ref[g, some, :] = flat[g].T.astype(bf16)
        return _

    lax.fori_loop(0, chans // lanes, column, 0)


def mixer(keep, other, taps, rates, residues, cot_own, cot_other):
    groups, toks, chans = keep.shape
    modes = rates.shape[0]
    rim = taps.shape[1] - 1
    lanes = 128
    length = toks // CHUNKS
    return small_call(
        mixer_kernel,
        [
            jax.ShapeDtypeStruct((toks // 2, chans), bf16),
            jax.ShapeDtypeStruct((toks // 2, chans), bf16),
            jax.ShapeDtypeStruct((groups, chans, toks), bf16),
        ],
        [keep, other, taps, rates, residues, cot_own, cot_other],
        "mixer",
        12 * modes * toks * chans,
        [
            pltpu.VMEM((groups, toks, lanes), f32),
            pltpu.VMEM((toks, lanes), f32),
            pltpu.VMEM((groups, length + rim, CHUNKS, lanes), f32),
            pltpu.VMEM((groups, length, CHUNKS, lanes), f32),
            pltpu.VMEM((length, CHUNKS, lanes), f32),
            pltpu.VMEM((length, CHUNKS, lanes), f32),
            pltpu.VMEM((groups, length + rim, CHUNKS, lanes), f32),
        ],
    )


def back_kernel(outs, w_ref, own_ref, other_ref, *out_refs):
    groups, half, _ = own_ref.shape
    core = here()[3]
    own_at = pl.multiple_of(core * half, half)
    other_at = pl.multiple_of((1 - core) * half, half)
    for blocks, out in zip(outs, out_refs):
        width = out.shape[0] // len(blocks)
        for n, block in enumerate(blocks):
            start = pl.multiple_of(block_at(*block) * width, width)
            total = None
            for g in range(groups):
                for ref, at in ((own_ref, own_at), (other_ref, other_at)):
                    term = jnp.dot(
                        w_ref[g, pl.ds(start, width), pl.ds(at, half)],
                        ref[g],
                        preferred_element_type=f32,
                    )
                    total = term if total is None else total + term
            out[n * width : (n + 1) * width] = total.astype(out.dtype)


def back_project(outs, dtypes, w, own, other, width):
    groups, half, toks = own.shape
    return small_call(
        functools.partial(back_kernel, outs),
        [
            jax.ShapeDtypeStruct((width * len(blocks), toks), dtype)
            for blocks, dtype in zip(outs, dtypes)
        ],
        [w, own, other],
        "back_project",
        4 * sum(len(blocks) for blocks in outs) * groups * width * half * toks,
        (),
        16,
    )


def merge_kernel(two_ref, one_ref, got_ref, two_out, one_out):
    width = one_ref.shape[0]
    one_out[...] = (one_ref[...] + got_ref[:width].astype(f32)).astype(bf16)
    two_out[...] = (two_ref[...] + got_ref[width:].astype(f32)).astype(bf16)


def merge(two, one, got):
    shape = jax.ShapeDtypeStruct(one.shape, bf16)
    return small_call(merge_kernel, [shape, shape], [two, one, got], "merge")


def column_kernel(slot, own_ref, other_ref, first_ref, *out_refs):
    width, toks = own_ref.shape
    half = toks // 2
    total = (
        own_ref[...]
        + other_ref[(slot - 1) * width : slot * width].astype(f32)
        + first_ref[...].astype(f32)
    )
    z, _, _, core = here()
    side = (z >> 1) if slot == 2 else 1 - (z >> 1)
    low, high = total[:, :half], total[:, half:]
    send_low, send_high = out_refs[0], out_refs[1]

    @pl.when(side == 0)
    def _():
        send_low[...] = low.astype(bf16)
        send_high[...] = high.astype(bf16)

    @pl.when(side == 1)
    def _():
        send_low[...] = high.astype(bf16)
        send_high[...] = low.astype(bf16)

    if len(out_refs) == 3:
        inner = is_inner()
        out_refs[2][...] = jnp.where(inner, jnp.where(core == 0, low, high), 0.0)


def column(slot, own, other, first):
    width, toks = own.shape
    half = jax.ShapeDtypeStruct((width, toks // 2), bf16)
    kept = [jax.ShapeDtypeStruct((width, toks // 2), f32)] if slot == 1 else []
    return small_call(
        functools.partial(column_kernel, slot), [half, half] + kept, [own, other, first], "column"
    )


def finish_kernel(own_ref, a_ref, b_ref, c_ref, d_ref, out_ref):
    total = own_ref[...]
    for ref in (a_ref, b_ref, c_ref, d_ref):
        total = total + ref[...].astype(f32)
    out_ref[...] = total.T.astype(bf16)


def finish(own, received):
    shape = jax.ShapeDtypeStruct((own.shape[1], own.shape[0]), bf16)
    return small_call(finish_kernel, shape, [own] + received, "finish")


def pair_kernel(own_ref, other_ref, out_ref):
    half = own_ref.shape[1]
    core = here()[3]
    out_ref[:, pl.ds(pl.multiple_of(core * half, half), half)] = own_ref[...]
    out_ref[:, pl.ds(pl.multiple_of((1 - core) * half, half), half)] = other_ref[...]


def pair(own, other):
    shape = jax.ShapeDtypeStruct((own.shape[0], 2 * own.shape[1]), own.dtype)
    return small_call(pair_kernel, shape, [own, other], "pair")


def chip_plan(token_ids, embed, w_in, taps, rates, residues, cotangent):
    width = embed.shape[1]

    def swap(array):
        return lax.ppermute(array, BOTH, OTHER_CORE)

    def first_way(array):
        return lax.ppermute(array, BOTH, FIRST_WAY)

    def other_way(array):
        return lax.ppermute(array, BOTH, OTHER_WAY)

    own_ids = token_ids.reshape(1, -1)
    other_ids = swap(own_ids)
    cot_other = swap(cotangent)
    own_ids, table = fetch(own_ids, embed)
    embedded = embed_rows(own_ids, other_ids, table)
    embedded, cot_other = lax.optimization_barrier((embedded, cot_other))

    came = lax.ppermute(embedded, BOTH, GATHER_Z)
    more = lax.ppermute(embedded, BOTH, OUTER_Z_INNER_X)
    near_y = lax.ppermute(embedded, BOTH, INNER_Y)
    near_d = lax.ppermute(embedded, BOTH, INNER_XY)
    w = load(jnp.transpose(w_in, (1, 0, 2)))
    came, w = lax.optimization_barrier((came, w))
    first, other = first_way(came), other_way(came)
    x_2 = lax.ppermute(more, BOTH, OUTER_X)
    y_2 = lax.ppermute(more, BOTH, OUTER_Y)
    d_2 = lax.ppermute(more, BOTH, OUTER_XY)
    sums = project(
        [embedded, more, near_y, near_d, came],
        [(0, 1, None), (1, 1, "x"), (2, 1, "y"), (3, 1, 2), (4, 2, None)],
        [(4, 1, None), (1, 2, None)],
        w,
        None,
        False,
    )
    first, other, sums = lax.optimization_barrier((first, other, sums))
    both = other_way(first)
    sums = project(
        [first, other], [(0, 2, 0), (1, 2, 1)], [(0, 1, 0), (1, 1, 1)], w, sums, False
    )
    both, x_2, y_2, d_2, sums = lax.optimization_barrier((both, x_2, y_2, d_2, sums))
    keep, send = project(
        [both, x_2, y_2, d_2],
        [(0, 2, 2)],
        [(0, 1, 2), (1, 2, "x"), (2, 2, "y"), (3, 2, 2)],
        w,
        sums,
        True,
    )
    mixed_own, mixed_send, grad_own = mixer(
        keep, swap(send), jnp.transpose(taps, (1, 0, 2)), rates, residues, cotangent, cot_other
    )
    grad_other = swap(grad_own)
    mixed_other = swap(mixed_send)

    (across,) = back_project([[(1, 2), (2, 2)]], [bf16], w, grad_own, grad_other, width)
    across = other_way(across)
    (other,) = back_project([[(1, 1), (2, 1)]], [bf16], w, grad_own, grad_other, width)
    other = other_way(other)
    first_2, first_1, own_2, own_1 = back_project(
        [[(2, 0)], [(1, 0)], [(2, None)], [(1, None)]], [f32] * 4, w, grad_own, grad_other, width
    )
    mixed = pair(mixed_own, mixed_other)
    across, mixed = lax.optimization_barrier((across, mixed))
    first_2, first_1 = merge(first_2, first_1, across)
    first_2, first_1 = first_way(first_2), first_way(first_1)
    sends = column(2, own_2, other, first_2)
    received = [lax.ppermute(a, BOTH, pairs) for a, pairs in zip(sends, SCATTER_Z[:2])]
    *sends, own = column(1, own_1, other, first_1)
    received += [lax.ppermute(a, BOTH, pairs) for a, pairs in zip(sends, SCATTER_Z[2:])]
    return (mixed, finish(own, received))


def solution(mesh):
    in_specs = (
        P("ctx"),
        P(None, "fsdp"),
        P("ctx", None, "fsdp"),
        P(None, None, "fsdp"),
        P(None, "fsdp"),
        P(None, "fsdp"),
        P("ctx", "fsdp"),
    )
    out_specs = (P("ctx", "fsdp"), P("ctx", "fsdp"))
    chips = mesh.shape["fsdp"] == 16 and mesh.shape["ctx"] == 2
    return jax.shard_map(
        chip_plan if chips else general_plan,
        mesh=mesh,
        in_specs=in_specs,
        out_specs=out_specs,
        check_vma=False,
    )
```

```python
import functools

import jax
import jax.numpy as jnp
from jax import lax
from jax.experimental import pallas as pl
from jax.experimental.pallas import tpu as pltpu
from jax.sharding import PartitionSpec as P

BOTH = ("fsdp", "ctx")
CHUNKS = 8
f32 = jnp.float32
bf16 = jnp.bfloat16


def from_behind(shard, axis, by):
    count = lax.axis_size(axis)
    pairs = [(i, i + by) for i in range(count) if 0 <= i + by < count]
    return lax.ppermute(shard, axis, pairs)


def pair_combine(earlier, later):
    return (earlier[0] * later[0], later[0] * earlier[1] + later[1])


def modal_states(drive, step_decay):
    tok_count = drive.shape[0]
    factors = jnp.broadcast_to(step_decay[None], (tok_count,) + step_decay.shape)
    inputs = jnp.broadcast_to(drive[:, None, :], factors.shape)
    return lax.associative_scan(pair_combine, (factors, inputs), axis=0)[1]


def short_filter(extended, taps, tok_count):
    rim_width = taps.shape[0] - 1
    filtered = taps[0] * extended[rim_width : rim_width + tok_count]
    for shift_lag in range(1, rim_width + 1):
        filtered = (
            filtered
            + taps[shift_lag] * extended[rim_width - shift_lag : rim_width - shift_lag + tok_count]
        )
    return filtered


def short_adjoint(extended, taps, tok_count):
    rim_width = taps.shape[0] - 1
    result = taps[0] * extended[:tok_count]
    for shift_lag in range(1, rim_width + 1):
        result = result + taps[shift_lag] * extended[shift_lag : shift_lag + tok_count]
    return result


def carry(block_decay, leaving, by):
    def relay_step(turn_index, incoming):
        return from_behind(block_decay * incoming + leaving, "ctx", by)

    return lax.fori_loop(0, lax.axis_size("ctx") - 1, relay_step, jnp.zeros_like(leaving))


def general_plan(token_ids, embed, w_in, taps, rates, residues, cotangent):
    tok_count = token_ids.shape[0]
    vocab_size = embed.shape[0]
    chan_width = embed.shape[1]
    rim_width = taps.shape[0] - 1
    onehot = (
        token_ids[:, None] == lax.broadcasted_iota(jnp.int32, (tok_count, vocab_size), 1)
    ).astype(bf16)
    embedded = jnp.dot(onehot, embed, preferred_element_type=f32).astype(bf16)
    features = lax.all_gather(embedded, "fsdp", axis=1, tiled=True)
    feat_width = features.shape[1]
    whole_w = lax.all_gather(w_in, "ctx", axis=0, tiled=True).reshape(feat_width, 3 * chan_width)
    projected = jnp.dot(features, whole_w, preferred_element_type=f32)
    stored = lax.optimization_barrier(projected.astype(bf16).reshape(tok_count, 3, chan_width))
    before = from_behind(stored[tok_count - rim_width :], "ctx", 1)
    extended = jnp.concatenate([before, stored], axis=0).astype(f32)
    filtered = short_filter(extended, taps, tok_count)
    query_part = filtered[:, 0]
    key_part = filtered[:, 1]
    value_part = filtered[:, 2]
    drive = key_part * value_part
    step_decay = jnp.exp(-rates)
    block_decay = jnp.exp(-rates * tok_count)
    local_states = modal_states(drive, step_decay)
    entering = carry(block_decay, local_states[tok_count - 1], 1)
    offsets = lax.broadcasted_iota(f32, (tok_count, 1, 1), 0)
    states = local_states + jnp.exp(-rates[None] * (offsets + 1.0)) * entering[None]
    long_out = jnp.sum(residues[None] * states, axis=1)
    mixed = (query_part * long_out).astype(bf16)
    incoming = cotangent.astype(f32)
    grad_long = incoming * query_part
    grad_query = incoming * long_out
    back_states = jnp.flip(modal_states(jnp.flip(grad_long, 0), step_decay), 0)
    beyond = carry(block_decay, back_states[0], -1)
    adjoint = back_states + jnp.exp(-rates[None] * (tok_count - offsets)) * beyond[None]
    grad_drive = jnp.sum(residues[None] * adjoint, axis=1)
    grad_filtered = jnp.stack([grad_query, grad_drive * value_part, grad_drive * key_part], axis=1)
    after = from_behind(grad_filtered[:rim_width], "ctx", -1)
    ext_grad = jnp.concatenate([grad_filtered, after], axis=0)
    grad_stored = short_adjoint(ext_grad, taps, tok_count).astype(bf16)
    grad_rows = grad_stored.reshape(tok_count, 3 * chan_width)
    own_rows = lax.psum_scatter(
        lax.dot_general(whole_w, grad_rows, (((1,), (1,)), ((), ())), preferred_element_type=f32),
        "fsdp",
        scatter_dimension=0,
        tiled=True,
    )
    return (mixed, own_rows.T.astype(bf16))


def device_at(z, y, x, core):
    return ((z * 2 + y) * 2 + x) * 2 + core


def everywhere(move):
    pairs = []
    for z in range(4):
        for y in range(2):
            for x in range(2):
                for core in range(2):
                    pairs.append((device_at(z, y, x, core), device_at(*move(z, y, x, core))))
    return pairs


OTHER_CORE = everywhere(lambda z, y, x, core: (z, y, x, 1 - core))


def along_z(moves):
    pairs = []
    for core in range(2):
        for (place, other), (to_place, to_other) in moves:
            z, to_z = (place, to_place) if core == 0 else (3 - place, 3 - to_place)
            for y in range(2):
                for x in range(2):
                    pairs.append(
                        (
                            device_at(z, y, x, core ^ other),
                            device_at(to_z, y, x, core ^ to_other),
                        )
                    )
    return pairs


FIRST_WAY = everywhere(lambda z, y, x, core: (z, y, 1 - x, core) if core == 0 else (z, 1 - y, x, core))
OTHER_WAY = everywhere(lambda z, y, x, core: (z, 1 - y, x, core) if core == 0 else (z, y, 1 - x, core))
def some_move(move, inner):
    def target(z, y, x, core):
        return move(z, y, x, core) if (core == z >> 1) == inner else (z, y, x, core)

    return everywhere(target)


INNER_Y = some_move(lambda z, y, x, core: (z, 1 - y, x, core), True)
INNER_XY = some_move(lambda z, y, x, core: (z, 1 - y, 1 - x, core), True)
OUTER_X = some_move(lambda z, y, x, core: (z, y, 1 - x, core), False)
OUTER_Y = some_move(lambda z, y, x, core: (z, 1 - y, x, core), False)
OUTER_XY = some_move(lambda z, y, x, core: (z, 1 - y, 1 - x, core), False)
GATHER_Z = along_z([((0, 0), (1, 0)), ((1, 0), (0, 0)), ((0, 1), (2, 0)), ((1, 1), (3, 0))])
OUTER_Z_INNER_X = along_z([((1, 1), (2, 0)), ((0, 1), (3, 0))]) + [
    pair
    for pair in everywhere(lambda z, y, x, core: (z, y, 1 - x, core))
    if (pair[0] & 1) == pair[0] >> 4
]
SCATTER_Z = (
    along_z([((0, 0), (1, 0)), ((1, 0), (0, 0)), ((2, 0), (1, 1)), ((3, 0), (0, 1))]),
    along_z([((0, 0), (1, 1)), ((1, 0), (0, 1)), ((2, 0), (1, 0)), ((3, 0), (0, 0))]),
    along_z([((0, 0), (0, 1)), ((1, 0), (1, 1)), ((2, 0), (0, 0)), ((3, 0), (1, 0))]),
    along_z([((2, 0), (0, 1)), ((3, 0), (1, 1))]),
)

IN_VMEM = pl.BlockSpec(memory_space=pltpu.VMEM)


def small_call(kernel, out_shape, operands, name, flops=0, scratch=(), limit=8):
    sizes = [o.size * o.dtype.itemsize for o in operands]
    return pl.pallas_call(
        kernel,
        in_specs=[IN_VMEM] * len(operands),
        out_specs=jax.tree.map(lambda _: IN_VMEM, out_shape),
        out_shape=out_shape,
        scratch_shapes=list(scratch),
        compiler_params=pltpu.CompilerParams(vmem_limit_bytes=limit * 1024 * 1024),
        cost_estimate=pl.CostEstimate(
            flops=flops // 64, bytes_accessed=sum(sizes) // 64, transcendentals=0
        ),
        name=name,
    )(*operands)


def here():
    spot = lax.axis_index("fsdp")
    return spot >> 2, (spot >> 1) & 1, spot & 1, lax.axis_index("ctx")


def is_inner():
    z, _, _, core = here()
    return core == (z >> 1)


def block_at(slot, way):
    z, y, x, core = here()
    along = (z & 1) if slot == 1 else 1 - (z & 1)
    far = {None: (0, 0), 0: (core, 1 - core), 1: (1 - core, core), 2: (1, 1), "x": (0, 1), "y": (1, 0)}
    far_y, far_x = far[way]
    return along * 4 + (y ^ far_y) * 2 + (x ^ far_x)


def embed_kernel(own_ref, other_ref, table_ref, out_ref):
    vocab = table_ref.shape[0]
    half = own_ref.shape[1]
    core = here()[3]
    for ref, side in ((own_ref, core), (other_ref, 1 - core)):
        across = jnp.broadcast_to(ref[...].astype(f32), (half, half)).T
        lane = lax.broadcasted_iota(jnp.int32, (half, half), 1).astype(f32)
        picks = [(across == lane + float(first)).astype(f32) for first in range(0, vocab, half)]
        rows = jnp.dot(
            jnp.concatenate(picks, axis=1).astype(bf16), table_ref[...], preferred_element_type=f32
        )
        out_ref[pl.ds(pl.multiple_of(side * half, half), half), :] = rows.astype(bf16)


def embed_rows(own_ids, other_ids, table):
    toks, width = 2 * own_ids.shape[1], table.shape[1]
    return small_call(
        embed_kernel,
        jax.ShapeDtypeStruct((toks, width), bf16),
        [own_ids, other_ids, table],
        "embed_rows",
        2 * toks * table.shape[0] * width,
    )


def fetch_kernel(ids_ref, table_ref, ids_out, table_out, sems):
    copies = [
        pltpu.make_async_copy(ids_ref, ids_out, sems.at[0]),
        pltpu.make_async_copy(table_ref, table_out, sems.at[1]),
    ]
    for copy in copies:
        copy.start()
    for copy in copies:
        copy.wait()


def in_hbm(array):
    return pltpu.with_memory_space_constraint(array, pltpu.HBM)


def in_vmem(array):
    return pltpu.with_memory_space_constraint(array, pltpu.VMEM)


def fetch(ids, table):
    out = pl.pallas_call(
        fetch_kernel,
        in_specs=[pl.BlockSpec(memory_space=pltpu.HBM)] * 2,
        out_specs=[IN_VMEM] * 2,
        out_shape=[pltpu.VMEM(ids.shape, ids.dtype), pltpu.VMEM(table.shape, bf16)],
        scratch_shapes=[pltpu.SemaphoreType.DMA((2,))],
        compiler_params=pltpu.CompilerParams(vmem_limit_bytes=2 * 1024 * 1024),
        cost_estimate=pl.CostEstimate(
            flops=0, bytes_accessed=4 * table.size, transcendentals=0
        ),
        name="fetch",
    )(in_hbm(ids), in_hbm(table))
    return [in_vmem(array) for array in out]


def load_kernel(w_ref, out_ref, sem):
    copy = pltpu.make_async_copy(w_ref, out_ref, sem)
    copy.start()
    copy.wait()


def load(w):
    out = pl.pallas_call(
        load_kernel,
        in_specs=[pl.BlockSpec(memory_space=pltpu.HBM)],
        out_specs=IN_VMEM,
        out_shape=pltpu.VMEM(w.shape, w.dtype),
        scratch_shapes=[pltpu.SemaphoreType.DMA],
        compiler_params=pltpu.CompilerParams(vmem_limit_bytes=2 * 1024 * 1024),
        cost_estimate=pl.CostEstimate(
            flops=0, bytes_accessed=2 * w.size * w.dtype.itemsize, transcendentals=0
        ),
        name="load",
    )(in_hbm(w))
    return in_vmem(out)


def project_kernel(inner, outer, count, has_base, last, w_ref, *refs):
    acts = refs[:count]
    groups, _, chans = w_ref.shape
    width = acts[0].shape[1]
    if last:
        keep_ref, send_ref, total_ref = refs[-3:]
    else:
        total_ref = refs[-1]

    def add(entries):
        spans = [
            pl.ds(pl.multiple_of(block_at(slot, way) * width, width), width)
            for _, slot, way in entries
        ]
        for g in range(groups):
            total = refs[count][g] if has_base else None
            for (which, _, _), span in zip(entries, spans):
                term = jnp.dot(acts[which][...], w_ref[g, span, :], preferred_element_type=f32)
                total = term if total is None else total + term
            total_ref[g] = total

    pl.when(is_inner())(lambda: add(inner))
    pl.when(jnp.logical_not(is_inner()))(lambda: add(outer))
    if last:
        half = chans // 2
        core = here()[3]
        keep_ref[...] = total_ref[:, :, pl.ds(pl.multiple_of(core * half, half), half)]
        send_ref[...] = total_ref[:, :, pl.ds(pl.multiple_of((1 - core) * half, half), half)]


def project(acts, inner, outer, w, base, last):
    groups, _, chans = w.shape
    toks, width = acts[0].shape
    total = jax.ShapeDtypeStruct((groups, toks, chans), f32)
    half = jax.ShapeDtypeStruct((groups, toks, chans // 2), f32)
    return small_call(
        functools.partial(project_kernel, inner, outer, len(acts), base is not None, last),
        [half, half] if last else total,
        [w] + list(acts) + ([] if base is None else [base]),
        "project",
        2 * max(len(inner), len(outer)) * groups * width * chans * toks,
        [pltpu.VMEM(total.shape, f32)] if last else [],
        16,
    )


def shifted(values, by):
    place = lax.broadcasted_iota(jnp.int32, values.shape, 0)
    moved = pltpu.roll(values, by % CHUNKS, 0)
    inside = place >= by if by > 0 else place < CHUNKS + by
    return jnp.where(inside, moved, 0.0)


def mixer_kernel(
    keep_ref,
    other_ref,
    taps_ref,
    rates_ref,
    residues_ref,
    cot_own_ref,
    cot_other_ref,
    mixed_own_ref,
    mixed_send_ref,
    grad_ref,
    flat,
    flat_cot,
    ext,
    filt,
    drive,
    back,
    grad_ext,
    decays,
    residues,
):
    groups, toks, chans = keep_ref.shape
    half = toks // 2
    modes = rates_ref.shape[0]
    short = taps_ref.shape[1]
    rim = short - 1
    length = toks // CHUNKS
    apart = flat.shape[1] // CHUNKS
    lanes = flat.shape[-1]
    wide = (CHUNKS, lanes)
    _, _, _, core = here()

    def spread(ref, at, values):
        for s in range(CHUNKS):
            ref[(*at, slice(s * apart, s * apart + length))] = values[s * length : (s + 1) * length]

    def row(array, at):
        return jnp.broadcast_to(array[at : at + 1, :], wide)

    def column(c, _):
        some = pl.ds(pl.multiple_of(c * lanes, lanes), lanes)
        whole = pl.ds(pl.multiple_of(core * chans + c * lanes, lanes), lanes)
        for g in range(groups):
            spread(flat, (g,), (keep_ref[g, :, some] + other_ref[g, :, some]).astype(bf16).astype(f32))
        for s in range(CHUNKS // 2):
            rows = slice(s * length, (s + 1) * length)
            own_at = pl.multiple_of((core * (CHUNKS // 2) + s) * apart, 8)
            other_at = pl.multiple_of(((1 - core) * (CHUNKS // 2) + s) * apart, 8)
            flat_cot[pl.ds(own_at, length)] = cot_own_ref[rows, whole].astype(f32)
            flat_cot[pl.ds(other_at, length)] = cot_other_ref[rows, whole].astype(f32)

        for g in range(groups):
            for k in range(length):
                ext[g, rim + k] = flat[g, pl.ds(k, CHUNKS, stride=apart), :]
            for k in range(rim):
                ext[g, k] = shifted(ext[g, length + k], 1)

        taps = [taps_ref[g, :, whole] for g in range(groups)]
        tap = [[row(taps[g], j) for g in range(groups)] for j in range(short)]

        def filter_step(k, _):
            parts = []
            for g in range(groups):
                total = tap[0][g] * ext[g, k + rim]
                for j in range(1, short):
                    total = total + tap[j][g] * ext[g, k + rim - j]
                parts.append(total)
                filt[g, k] = total
            drive[k] = parts[1] * parts[2]
            back[k] = parts[0] * flat_cot[pl.ds(k, CHUNKS, stride=apart), :]
            return _

        lax.fori_loop(0, length, filter_step, 0, unroll=4)

        rates = rates_ref[:, whole]
        decay_rows = jnp.exp(-rates)
        jump_rows = [jnp.exp(-rates * (length * n)) for n in (1, 2, 4)]
        residue_rows = residues_ref[:, whole]
        for m in range(modes):
            decays[m] = row(decay_rows, m)
            residues[m] = row(residue_rows, m)

        def long_filter(source, forward, finish):
            decay = [decays[m] for m in range(modes)]

            def place(k):
                return k if forward else length - 1 - k

            def end_step(k, states):
                value = source[place(k)]
                return tuple(decay[m] * states[m] + value for m in range(modes))

            zero = jnp.zeros(wide, f32)
            ends = lax.fori_loop(0, length, end_step, (zero,) * modes, unroll=8)
            entering = []
            sign = 1 if forward else -1
            for m in range(modes):
                carried = ends[m]
                for jump, by in zip(jump_rows, (1, 2, 4)):
                    carried = carried + row(jump, m) * shifted(carried, sign * by)
                entering.append(shifted(carried, sign))

            def out_step(k, states):
                value = source[place(k)]
                states = tuple(decay[m] * states[m] + value for m in range(modes))
                terms = [residues[m] * states[m] for m in range(modes)]
                while len(terms) > 1:
                    terms = [a + b for a, b in zip(terms[::2], terms[1::2])]
                finish(place(k), terms[0])
                return states

            lax.fori_loop(0, length, out_step, tuple(entering), unroll=4)

        def finish_forward(k, total):
            flat[0, pl.ds(k, CHUNKS, stride=apart), :] = filt[0, k] * total
            grad_ext[0, k] = flat_cot[pl.ds(k, CHUNKS, stride=apart), :] * total

        def finish_backward(k, total):
            grad_ext[1, k] = total * filt[2, k]
            grad_ext[2, k] = total * filt[1, k]

        long_filter(drive, True, finish_forward)
        for s in range(CHUNKS // 2):
            rows = slice(s * length, (s + 1) * length)
            own_at = pl.multiple_of((core * (CHUNKS // 2) + s) * apart, 8)
            other_at = pl.multiple_of(((1 - core) * (CHUNKS // 2) + s) * apart, 8)
            mixed_own_ref[rows, some] = flat[0, pl.ds(own_at, length)].astype(bf16)
            mixed_send_ref[rows, some] = flat[0, pl.ds(other_at, length)].astype(bf16)
        long_filter(back, False, finish_backward)

        for g in range(groups):
            for k in range(rim):
                grad_ext[g, length + k] = shifted(grad_ext[g, k], -1)

        def adjoint_step(k, _):
            for g in range(groups):
                total = tap[0][g] * grad_ext[g, k]
                for j in range(1, short):
                    total = total + tap[j][g] * grad_ext[g, k + j]
                flat[g, pl.ds(k, CHUNKS, stride=apart), :] = total
            return _

        lax.fori_loop(0, length, adjoint_step, 0, unroll=4)
        for g in range(groups):
            chunks = [flat[g, s * apart : s * apart + length] for s in range(CHUNKS)]
            grad_ref[g, some, :] = jnp.concatenate(chunks, axis=0).T.astype(bf16)
        return _

    lax.fori_loop(0, chans // lanes, column, 0)


def mixer(keep, other, taps, rates, residues, cot_own, cot_other):
    groups, toks, chans = keep.shape
    modes = rates.shape[0]
    rim = taps.shape[1] - 1
    lanes = 128
    length = toks // CHUNKS
    return small_call(
        mixer_kernel,
        [
            jax.ShapeDtypeStruct((toks // 2, chans), bf16),
            jax.ShapeDtypeStruct((toks // 2, chans), bf16),
            jax.ShapeDtypeStruct((groups, chans, toks), bf16),
        ],
        [keep, other, taps, rates, residues, cot_own, cot_other],
        "mixer",
        12 * modes * toks * chans,
        [
            pltpu.VMEM((groups, toks + 8 * CHUNKS, lanes), f32),
            pltpu.VMEM((toks + 8 * CHUNKS, lanes), f32),
            pltpu.VMEM((groups, length + rim, CHUNKS, lanes), f32),
            pltpu.VMEM((groups, length, CHUNKS, lanes), f32),
            pltpu.VMEM((length, CHUNKS, lanes), f32),
            pltpu.VMEM((length, CHUNKS, lanes), f32),
            pltpu.VMEM((groups, length + rim, CHUNKS, lanes), f32),
            pltpu.VMEM((modes, CHUNKS, lanes), f32),
            pltpu.VMEM((modes, CHUNKS, lanes), f32),
        ],
    )


def back_kernel(outs, count, base, w_ref, *refs):
    grads, out_refs = refs[: len(count)], refs[len(count) + base :]
    groups, half, _ = grads[0].shape
    core = here()[3]
    sides = [pl.multiple_of((1 - core if other else core) * half, half) for other in count]
    for blocks, out in zip(outs, out_refs):
        width = out.shape[0] // len(blocks)
        for n, block in enumerate(blocks):
            rows = slice(n * width, (n + 1) * width)
            start = pl.multiple_of(block_at(*block) * width, width)
            total = refs[len(count)][rows] if base else None
            for g in range(groups):
                for ref, at in zip(grads, sides):
                    term = jnp.dot(
                        w_ref[g, pl.ds(start, width), pl.ds(at, half)],
                        ref[g],
                        preferred_element_type=f32,
                    )
                    total = term if total is None else total + term
            out[rows] = total.astype(out.dtype)


def back_project(outs, dtypes, w, own, other, width, base=None):
    grads = [(side, grad) for side, grad in enumerate((own, other)) if grad is not None]
    groups, half, toks = grads[0][1].shape
    extra = [] if base is None else [base]
    return small_call(
        functools.partial(back_kernel, outs, [side for side, _ in grads], len(extra)),
        [
            jax.ShapeDtypeStruct((width * len(blocks), toks), dtype)
            for blocks, dtype in zip(outs, dtypes)
        ],
        [w] + [grad for _, grad in grads] + extra,
        "back_project",
        2 * sum(len(blocks) for blocks in outs) * groups * width * half * toks * len(grads),
        (),
        16,
    )


def merge_kernel(two_ref, one_ref, got_ref, two_out, one_out):
    width = one_ref.shape[0]
    one_out[...] = (one_ref[...] + got_ref[:width].astype(f32)).astype(bf16)
    two_out[...] = (two_ref[...] + got_ref[width:].astype(f32)).astype(bf16)


def merge(two, one, got):
    shape = jax.ShapeDtypeStruct(one.shape, bf16)
    return small_call(merge_kernel, [shape, shape], [two, one, got], "merge")


def column_kernel(slot, own_ref, other_ref, first_ref, *out_refs):
    width, toks = own_ref.shape
    half = toks // 2
    total = (
        own_ref[...]
        + other_ref[(slot - 1) * width : slot * width].astype(f32)
        + first_ref[...].astype(f32)
    )
    z, _, _, core = here()
    side = (z >> 1) if slot == 2 else 1 - (z >> 1)
    low, high = total[:, :half], total[:, half:]
    send_low, send_high = out_refs[0], out_refs[1]

    @pl.when(side == 0)
    def _():
        send_low[...] = low.astype(bf16)
        send_high[...] = high.astype(bf16)

    @pl.when(side == 1)
    def _():
        send_low[...] = high.astype(bf16)
        send_high[...] = low.astype(bf16)

    if len(out_refs) == 3:
        inner = is_inner()
        out_refs[2][...] = jnp.where(inner, jnp.where(core == 0, low, high), 0.0)


def column(slot, own, other, first):
    width, toks = own.shape
    half = jax.ShapeDtypeStruct((width, toks // 2), bf16)
    kept = [jax.ShapeDtypeStruct((width, toks // 2), f32)] if slot == 1 else []
    return small_call(
        functools.partial(column_kernel, slot), [half, half] + kept, [own, other, first], "column"
    )


def finish_kernel(own_ref, a_ref, b_ref, c_ref, d_ref, out_ref):
    total = own_ref[...]
    for ref in (a_ref, b_ref, c_ref, d_ref):
        total = total + ref[...].astype(f32)
    out_ref[...] = total.T.astype(bf16)


def finish(own, received):
    shape = jax.ShapeDtypeStruct((own.shape[1], own.shape[0]), bf16)
    return small_call(finish_kernel, shape, [own] + received, "finish")


def pair_kernel(own_ref, other_ref, out_ref):
    half = own_ref.shape[1]
    core = here()[3]
    out_ref[:, pl.ds(pl.multiple_of(core * half, half), half)] = own_ref[...]
    out_ref[:, pl.ds(pl.multiple_of((1 - core) * half, half), half)] = other_ref[...]


def pair(own, other):
    shape = jax.ShapeDtypeStruct((own.shape[0], 2 * own.shape[1]), own.dtype)
    return small_call(pair_kernel, shape, [own, other], "pair")


def chip_plan(token_ids, embed, w_in, taps, rates, residues, cotangent):
    width = embed.shape[1]

    def swap(array):
        return lax.ppermute(array, BOTH, OTHER_CORE)

    def first_way(array):
        return lax.ppermute(array, BOTH, FIRST_WAY)

    def other_way(array):
        return lax.ppermute(array, BOTH, OTHER_WAY)

    own_ids = token_ids.reshape(1, -1)
    other_ids = swap(own_ids)
    cot_other = swap(cotangent)
    own_ids, table = fetch(own_ids, embed)
    embedded = embed_rows(own_ids, other_ids, table)
    embedded, cot_other = lax.optimization_barrier((embedded, cot_other))

    came = lax.ppermute(embedded, BOTH, GATHER_Z)
    more = lax.ppermute(embedded, BOTH, OUTER_Z_INNER_X)
    near_y = lax.ppermute(embedded, BOTH, INNER_Y)
    near_d = lax.ppermute(embedded, BOTH, INNER_XY)
    w = load(jnp.transpose(w_in, (1, 0, 2)))
    came, w = lax.optimization_barrier((came, w))
    first, other = first_way(came), other_way(came)
    x_2 = lax.ppermute(more, BOTH, OUTER_X)
    y_2 = lax.ppermute(more, BOTH, OUTER_Y)
    sums = project(
        [embedded, more, near_y, near_d, came],
        [(0, 1, None), (1, 1, "x"), (2, 1, "y"), (3, 1, 2), (4, 2, None)],
        [(4, 1, None), (1, 2, None)],
        w,
        None,
        False,
    )
    first, other, more, sums = lax.optimization_barrier((first, other, more, sums))
    both = other_way(first)
    d_2 = lax.ppermute(more, BOTH, OUTER_XY)
    sums = project(
        [first, other], [(0, 2, 0), (1, 2, 1)], [(0, 1, 0), (1, 1, 1)], w, sums, False
    )
    both, x_2, y_2, d_2, sums = lax.optimization_barrier((both, x_2, y_2, d_2, sums))
    keep, send = project(
        [both, x_2, y_2, d_2],
        [(0, 2, 2)],
        [(0, 1, 2), (1, 2, "x"), (2, 2, "y"), (3, 2, 2)],
        w,
        sums,
        True,
    )
    mixed_own, mixed_send, grad_own = mixer(
        keep, swap(send), jnp.transpose(taps, (1, 0, 2)), rates, residues, cotangent, cot_other
    )
    grad_other = swap(grad_own)
    mixed_other = swap(mixed_send)

    (part,) = back_project([[(1, 2), (2, 2)]], [f32], w, grad_own, None, width)
    grad_other, part = lax.optimization_barrier((grad_other, part))
    (across,) = back_project([[(1, 2), (2, 2)]], [bf16], w, None, grad_other, width, part)
    across = other_way(across)
    (other,) = back_project([[(1, 1), (2, 1)]], [bf16], w, grad_own, grad_other, width)
    other = other_way(other)
    first_2, first_1, own_2, own_1 = back_project(
        [[(2, 0)], [(1, 0)], [(2, None)], [(1, None)]], [f32] * 4, w, grad_own, grad_other, width
    )
    mixed = pair(mixed_own, mixed_other)
    across, mixed = lax.optimization_barrier((across, mixed))
    first_2, first_1 = merge(first_2, first_1, across)
    first_2, first_1 = first_way(first_2), first_way(first_1)
    sends = column(2, own_2, other, first_2)
    received = [lax.ppermute(a, BOTH, pairs) for a, pairs in zip(sends, SCATTER_Z[:2])]
    *sends, own = column(1, own_1, other, first_1)
    received += [lax.ppermute(a, BOTH, pairs) for a, pairs in zip(sends, SCATTER_Z[2:])]
    return (mixed, finish(own, received))


def solution(mesh):
    in_specs = (
        P("ctx"),
        P(None, "fsdp"),
        P("ctx", None, "fsdp"),
        P(None, None, "fsdp"),
        P(None, "fsdp"),
        P(None, "fsdp"),
        P("ctx", "fsdp"),
    )
    out_specs = (P("ctx", "fsdp"), P("ctx", "fsdp"))
    chips = mesh.shape["fsdp"] == 16 and mesh.shape["ctx"] == 2
    return jax.shard_map(
        chip_plan if chips else general_plan,
        mesh=mesh,
        in_specs=in_specs,
        out_specs=out_specs,
        check_vma=False,
    )
```

```python
import functools

import jax
import jax.numpy as jnp
from jax import lax
from jax.experimental import pallas as pl
from jax.experimental.pallas import tpu as pltpu
from jax.sharding import PartitionSpec as P

BOTH = ("fsdp", "ctx")
CHUNKS = 8
f32 = jnp.float32
bf16 = jnp.bfloat16


def from_behind(shard, axis, by):
    count = lax.axis_size(axis)
    pairs = [(i, i + by) for i in range(count) if 0 <= i + by < count]
    return lax.ppermute(shard, axis, pairs)


def pair_combine(earlier, later):
    return (earlier[0] * later[0], later[0] * earlier[1] + later[1])


def modal_states(drive, step_decay):
    tok_count = drive.shape[0]
    factors = jnp.broadcast_to(step_decay[None], (tok_count,) + step_decay.shape)
    inputs = jnp.broadcast_to(drive[:, None, :], factors.shape)
    return lax.associative_scan(pair_combine, (factors, inputs), axis=0)[1]


def short_filter(extended, taps, tok_count):
    rim_width = taps.shape[0] - 1
    filtered = taps[0] * extended[rim_width : rim_width + tok_count]
    for shift_lag in range(1, rim_width + 1):
        filtered = (
            filtered
            + taps[shift_lag] * extended[rim_width - shift_lag : rim_width - shift_lag + tok_count]
        )
    return filtered


def short_adjoint(extended, taps, tok_count):
    rim_width = taps.shape[0] - 1
    result = taps[0] * extended[:tok_count]
    for shift_lag in range(1, rim_width + 1):
        result = result + taps[shift_lag] * extended[shift_lag : shift_lag + tok_count]
    return result


def carry(block_decay, leaving, by):
    def relay_step(turn_index, incoming):
        return from_behind(block_decay * incoming + leaving, "ctx", by)

    return lax.fori_loop(0, lax.axis_size("ctx") - 1, relay_step, jnp.zeros_like(leaving))


def general_plan(token_ids, embed, w_in, taps, rates, residues, cotangent):
    tok_count = token_ids.shape[0]
    vocab_size = embed.shape[0]
    chan_width = embed.shape[1]
    rim_width = taps.shape[0] - 1
    onehot = (
        token_ids[:, None] == lax.broadcasted_iota(jnp.int32, (tok_count, vocab_size), 1)
    ).astype(bf16)
    embedded = jnp.dot(onehot, embed, preferred_element_type=f32).astype(bf16)
    features = lax.all_gather(embedded, "fsdp", axis=1, tiled=True)
    feat_width = features.shape[1]
    whole_w = lax.all_gather(w_in, "ctx", axis=0, tiled=True).reshape(feat_width, 3 * chan_width)
    projected = jnp.dot(features, whole_w, preferred_element_type=f32)
    stored = lax.optimization_barrier(projected.astype(bf16).reshape(tok_count, 3, chan_width))
    before = from_behind(stored[tok_count - rim_width :], "ctx", 1)
    extended = jnp.concatenate([before, stored], axis=0).astype(f32)
    filtered = short_filter(extended, taps, tok_count)
    query_part = filtered[:, 0]
    key_part = filtered[:, 1]
    value_part = filtered[:, 2]
    drive = key_part * value_part
    step_decay = jnp.exp(-rates)
    block_decay = jnp.exp(-rates * tok_count)
    local_states = modal_states(drive, step_decay)
    entering = carry(block_decay, local_states[tok_count - 1], 1)
    offsets = lax.broadcasted_iota(f32, (tok_count, 1, 1), 0)
    states = local_states + jnp.exp(-rates[None] * (offsets + 1.0)) * entering[None]
    long_out = jnp.sum(residues[None] * states, axis=1)
    mixed = (query_part * long_out).astype(bf16)
    incoming = cotangent.astype(f32)
    grad_long = incoming * query_part
    grad_query = incoming * long_out
    back_states = jnp.flip(modal_states(jnp.flip(grad_long, 0), step_decay), 0)
    beyond = carry(block_decay, back_states[0], -1)
    adjoint = back_states + jnp.exp(-rates[None] * (tok_count - offsets)) * beyond[None]
    grad_drive = jnp.sum(residues[None] * adjoint, axis=1)
    grad_filtered = jnp.stack([grad_query, grad_drive * value_part, grad_drive * key_part], axis=1)
    after = from_behind(grad_filtered[:rim_width], "ctx", -1)
    ext_grad = jnp.concatenate([grad_filtered, after], axis=0)
    grad_stored = short_adjoint(ext_grad, taps, tok_count).astype(bf16)
    grad_rows = grad_stored.reshape(tok_count, 3 * chan_width)
    own_rows = lax.psum_scatter(
        lax.dot_general(whole_w, grad_rows, (((1,), (1,)), ((), ())), preferred_element_type=f32),
        "fsdp",
        scatter_dimension=0,
        tiled=True,
    )
    return (mixed, own_rows.T.astype(bf16))


def device_at(z, y, x, core):
    return ((z * 2 + y) * 2 + x) * 2 + core


def everywhere(move):
    pairs = []
    for z in range(4):
        for y in range(2):
            for x in range(2):
                for core in range(2):
                    pairs.append((device_at(z, y, x, core), device_at(*move(z, y, x, core))))
    return pairs


OTHER_CORE = everywhere(lambda z, y, x, core: (z, y, x, 1 - core))


def along_z(moves):
    pairs = []
    for core in range(2):
        for (place, other), (to_place, to_other) in moves:
            z, to_z = (place, to_place) if core == 0 else (3 - place, 3 - to_place)
            for y in range(2):
                for x in range(2):
                    pairs.append(
                        (
                            device_at(z, y, x, core ^ other),
                            device_at(to_z, y, x, core ^ to_other),
                        )
                    )
    return pairs


FIRST_WAY = everywhere(lambda z, y, x, core: (z, y, 1 - x, core) if core == 0 else (z, 1 - y, x, core))
OTHER_WAY = everywhere(lambda z, y, x, core: (z, 1 - y, x, core) if core == 0 else (z, y, 1 - x, core))
def some_move(move, inner):
    def target(z, y, x, core):
        return move(z, y, x, core) if (core == z >> 1) == inner else (z, y, x, core)

    return everywhere(target)


INNER_Y = some_move(lambda z, y, x, core: (z, 1 - y, x, core), True)
INNER_XY = some_move(lambda z, y, x, core: (z, 1 - y, 1 - x, core), True)
OUTER_X = some_move(lambda z, y, x, core: (z, y, 1 - x, core), False)
OUTER_Y = some_move(lambda z, y, x, core: (z, 1 - y, x, core), False)
OUTER_XY = some_move(lambda z, y, x, core: (z, 1 - y, 1 - x, core), False)
GATHER_Z = along_z([((0, 0), (1, 0)), ((1, 0), (0, 0)), ((0, 1), (2, 0)), ((1, 1), (3, 0))])
OUTER_Z_INNER_X = along_z([((1, 1), (2, 0)), ((0, 1), (3, 0))]) + [
    pair
    for pair in everywhere(lambda z, y, x, core: (z, y, 1 - x, core))
    if (pair[0] & 1) == pair[0] >> 4
]
SCATTER_Z = (
    along_z([((0, 0), (1, 0)), ((1, 0), (0, 0)), ((2, 0), (1, 1)), ((3, 0), (0, 1))]),
    along_z([((0, 0), (1, 1)), ((1, 0), (0, 1)), ((2, 0), (1, 0)), ((3, 0), (0, 0))]),
    along_z([((0, 0), (0, 1)), ((1, 0), (1, 1)), ((2, 0), (0, 0)), ((3, 0), (1, 0))]),
    along_z([((2, 0), (0, 1)), ((3, 0), (1, 1))]),
)

IN_VMEM = pl.BlockSpec(memory_space=pltpu.VMEM)


def small_call(kernel, out_shape, operands, name, flops=0, scratch=(), limit=8):
    sizes = [o.size * o.dtype.itemsize for o in operands]
    return pl.pallas_call(
        kernel,
        in_specs=[IN_VMEM] * len(operands),
        out_specs=jax.tree.map(lambda _: IN_VMEM, out_shape),
        out_shape=out_shape,
        scratch_shapes=list(scratch),
        compiler_params=pltpu.CompilerParams(vmem_limit_bytes=limit * 1024 * 1024),
        cost_estimate=pl.CostEstimate(
            flops=flops // 64, bytes_accessed=sum(sizes) // 64, transcendentals=0
        ),
        name=name,
    )(*operands)


def here():
    spot = lax.axis_index("fsdp")
    return spot >> 2, (spot >> 1) & 1, spot & 1, lax.axis_index("ctx")


def is_inner():
    z, _, _, core = here()
    return core == (z >> 1)


def block_at(slot, way):
    z, y, x, core = here()
    along = (z & 1) if slot == 1 else 1 - (z & 1)
    far = {None: (0, 0), 0: (core, 1 - core), 1: (1 - core, core), 2: (1, 1), "x": (0, 1), "y": (1, 0)}
    far_y, far_x = far[way]
    return along * 4 + (y ^ far_y) * 2 + (x ^ far_x)


def embed_kernel(own_ref, other_ref, table_ref, out_ref):
    vocab = table_ref.shape[0]
    half = own_ref.shape[1]
    core = here()[3]
    for ref, side in ((own_ref, core), (other_ref, 1 - core)):
        across = jnp.broadcast_to(ref[...].astype(f32), (half, half)).T
        lane = lax.broadcasted_iota(jnp.int32, (half, half), 1).astype(f32)
        picks = [(across == lane + float(first)).astype(f32) for first in range(0, vocab, half)]
        rows = jnp.dot(
            jnp.concatenate(picks, axis=1).astype(bf16), table_ref[...], preferred_element_type=f32
        )
        out_ref[pl.ds(pl.multiple_of(side * half, half), half), :] = rows.astype(bf16)


def embed_rows(own_ids, other_ids, table):
    toks, width = 2 * own_ids.shape[1], table.shape[1]
    return small_call(
        embed_kernel,
        jax.ShapeDtypeStruct((toks, width), bf16),
        [own_ids, other_ids, table],
        "embed_rows",
        2 * toks * table.shape[0] * width,
    )


def fetch_kernel(ids_ref, table_ref, ids_out, table_out, sems):
    copies = [
        pltpu.make_async_copy(ids_ref, ids_out, sems.at[0]),
        pltpu.make_async_copy(table_ref, table_out, sems.at[1]),
    ]
    for copy in copies:
        copy.start()
    for copy in copies:
        copy.wait()


def in_hbm(array):
    return pltpu.with_memory_space_constraint(array, pltpu.HBM)


def in_vmem(array):
    return pltpu.with_memory_space_constraint(array, pltpu.VMEM)


def fetch(ids, table):
    out = pl.pallas_call(
        fetch_kernel,
        in_specs=[pl.BlockSpec(memory_space=pltpu.HBM)] * 2,
        out_specs=[IN_VMEM] * 2,
        out_shape=[pltpu.VMEM(ids.shape, ids.dtype), pltpu.VMEM(table.shape, bf16)],
        scratch_shapes=[pltpu.SemaphoreType.DMA((2,))],
        compiler_params=pltpu.CompilerParams(vmem_limit_bytes=2 * 1024 * 1024),
        cost_estimate=pl.CostEstimate(
            flops=0, bytes_accessed=4 * table.size, transcendentals=0
        ),
        name="fetch",
    )(in_hbm(ids), in_hbm(table))
    return [in_vmem(array) for array in out]


def load_kernel(w_ref, out_ref, sem):
    copy = pltpu.make_async_copy(w_ref, out_ref, sem)
    copy.start()
    copy.wait()


def load(w):
    out = pl.pallas_call(
        load_kernel,
        in_specs=[pl.BlockSpec(memory_space=pltpu.HBM)],
        out_specs=IN_VMEM,
        out_shape=pltpu.VMEM(w.shape, w.dtype),
        scratch_shapes=[pltpu.SemaphoreType.DMA],
        compiler_params=pltpu.CompilerParams(vmem_limit_bytes=2 * 1024 * 1024),
        cost_estimate=pl.CostEstimate(
            flops=0, bytes_accessed=2 * w.size * w.dtype.itemsize, transcendentals=0
        ),
        name="load",
    )(in_hbm(w))
    return in_vmem(out)


def project_kernel(inner, outer, count, has_base, last, w_ref, *refs):
    acts = refs[:count]
    groups, _, chans = w_ref.shape
    width = acts[0].shape[1]
    if last:
        half = chans // 2
        core = here()[3]
        outs = [
            (refs[-2], pl.ds(pl.multiple_of(core * half, half), half)),
            (refs[-1], pl.ds(pl.multiple_of((1 - core) * half, half), half)),
        ]
    else:
        outs = [(refs[-1], slice(None))]

    def add(entries):
        spans = [
            pl.ds(pl.multiple_of(block_at(slot, way) * width, width), width)
            for _, slot, way in entries
        ]
        for g in range(groups):
            for out, some in outs:
                total = refs[count][g, :, some] if has_base else None
                for (which, _, _), span in zip(entries, spans):
                    term = jnp.dot(
                        acts[which][...], w_ref[g, span, some], preferred_element_type=f32
                    )
                    total = term if total is None else total + term
                out[g] = total

    pl.when(is_inner())(lambda: add(inner))
    pl.when(jnp.logical_not(is_inner()))(lambda: add(outer))


def project(acts, inner, outer, w, base, last):
    groups, _, chans = w.shape
    toks, width = acts[0].shape
    total = jax.ShapeDtypeStruct((groups, toks, chans), f32)
    half = jax.ShapeDtypeStruct((groups, toks, chans // 2), f32)
    return small_call(
        functools.partial(project_kernel, inner, outer, len(acts), base is not None, last),
        [half, half] if last else total,
        [w] + list(acts) + ([] if base is None else [base]),
        "project",
        2 * max(len(inner), len(outer)) * groups * width * chans * toks,
        (),
        16,
    )


def shifted(values, by):
    place = lax.broadcasted_iota(jnp.int32, values.shape, 0)
    moved = pltpu.roll(values, by % CHUNKS, 0)
    inside = place >= by if by > 0 else place < CHUNKS + by
    return jnp.where(inside, moved, 0.0)


def mixer_kernel(
    keep_ref,
    other_ref,
    taps_ref,
    rates_ref,
    residues_ref,
    cot_own_ref,
    cot_other_ref,
    mixed_own_ref,
    mixed_send_ref,
    grad_ref,
    flat,
    flat_cot,
    ext,
    filt,
    drive,
    back,
    grad_ext,
    decays,
    residues,
):
    groups, toks, chans = keep_ref.shape
    half = toks // 2
    modes = rates_ref.shape[0]
    short = taps_ref.shape[1]
    rim = short - 1
    length = toks // CHUNKS
    apart = flat.shape[1] // CHUNKS
    lanes = flat.shape[-1]
    wide = (CHUNKS, lanes)
    _, _, _, core = here()

    def spread(ref, at, values):
        for s in range(CHUNKS):
            ref[(*at, slice(s * apart, s * apart + length))] = values[s * length : (s + 1) * length]

    def row(array, at):
        return jnp.broadcast_to(array[at : at + 1, :], wide)

    def column(c, _):
        some = pl.ds(pl.multiple_of(c * lanes, lanes), lanes)
        whole = pl.ds(pl.multiple_of(core * chans + c * lanes, lanes), lanes)
        for g in range(groups):
            spread(flat, (g,), (keep_ref[g, :, some] + other_ref[g, :, some]).astype(bf16).astype(f32))
        for s in range(CHUNKS // 2):
            rows = slice(s * length, (s + 1) * length)
            own_at = pl.multiple_of((core * (CHUNKS // 2) + s) * apart, 8)
            other_at = pl.multiple_of(((1 - core) * (CHUNKS // 2) + s) * apart, 8)
            flat_cot[pl.ds(own_at, length)] = cot_own_ref[rows, whole].astype(f32)
            flat_cot[pl.ds(other_at, length)] = cot_other_ref[rows, whole].astype(f32)

        for g in range(groups):
            for k in range(length):
                ext[g, rim + k] = flat[g, pl.ds(k, CHUNKS, stride=apart), :]
            for k in range(rim):
                ext[g, k] = shifted(ext[g, length + k], 1)

        taps = [taps_ref[g, :, whole] for g in range(groups)]
        tap = [[row(taps[g], j) for g in range(groups)] for j in range(short)]

        def filter_step(k, _):
            parts = []
            for g in range(groups):
                total = tap[0][g] * ext[g, k + rim]
                for j in range(1, short):
                    total = total + tap[j][g] * ext[g, k + rim - j]
                parts.append(total)
                filt[g, k] = total
            drive[k] = parts[1] * parts[2]
            back[k] = parts[0] * flat_cot[pl.ds(k, CHUNKS, stride=apart), :]
            return _

        lax.fori_loop(0, length, filter_step, 0, unroll=4)

        rates = rates_ref[:, whole]
        decay_rows = jnp.exp(-rates)
        jump_rows = [jnp.exp(-rates * (length * n)) for n in (1, 2, 4)]
        residue_rows = residues_ref[:, whole]
        for m in range(modes):
            decays[m] = row(decay_rows, m)
            residues[m] = row(residue_rows, m)

        def long_filter(source, forward, finish):
            decay = [decays[m] for m in range(modes)]

            def place(k):
                return k if forward else length - 1 - k

            def end_step(k, states):
                value = source[place(k)]
                return tuple(decay[m] * states[m] + value for m in range(modes))

            zero = jnp.zeros(wide, f32)
            ends = lax.fori_loop(0, length, end_step, (zero,) * modes, unroll=8)
            entering = []
            sign = 1 if forward else -1
            for m in range(modes):
                carried = ends[m]
                for jump, by in zip(jump_rows, (1, 2, 4)):
                    carried = carried + row(jump, m) * shifted(carried, sign * by)
                entering.append(shifted(carried, sign))

            def out_step(k, states):
                value = source[place(k)]
                states = tuple(decay[m] * states[m] + value for m in range(modes))
                terms = [residues[m] * states[m] for m in range(modes)]
                while len(terms) > 1:
                    terms = [a + b for a, b in zip(terms[::2], terms[1::2])]
                finish(place(k), terms[0])
                return states

            lax.fori_loop(0, length, out_step, tuple(entering), unroll=4)

        def finish_forward(k, total):
            flat[0, pl.ds(k, CHUNKS, stride=apart), :] = filt[0, k] * total
            grad_ext[0, k] = flat_cot[pl.ds(k, CHUNKS, stride=apart), :] * total

        def finish_backward(k, total):
            grad_ext[1, k] = total * filt[2, k]
            grad_ext[2, k] = total * filt[1, k]

        long_filter(drive, True, finish_forward)
        for s in range(CHUNKS // 2):
            rows = slice(s * length, (s + 1) * length)
            own_at = pl.multiple_of((core * (CHUNKS // 2) + s) * apart, 8)
            other_at = pl.multiple_of(((1 - core) * (CHUNKS // 2) + s) * apart, 8)
            mixed_own_ref[rows, some] = flat[0, pl.ds(own_at, length)].astype(bf16)
            mixed_send_ref[rows, some] = flat[0, pl.ds(other_at, length)].astype(bf16)
        long_filter(back, False, finish_backward)

        for g in range(groups):
            for k in range(rim):
                grad_ext[g, length + k] = shifted(grad_ext[g, k], -1)

        def adjoint_step(k, _):
            for g in range(groups):
                total = tap[0][g] * grad_ext[g, k]
                for j in range(1, short):
                    total = total + tap[j][g] * grad_ext[g, k + j]
                flat[g, pl.ds(k, CHUNKS, stride=apart), :] = total
            return _

        lax.fori_loop(0, length, adjoint_step, 0, unroll=4)
        for g in range(groups):
            chunks = [flat[g, s * apart : s * apart + length].astype(bf16) for s in range(CHUNKS)]
            grad_ref[g, some, :] = jnp.concatenate(chunks, axis=0).T
        return _

    lax.fori_loop(0, chans // lanes, column, 0)


def mixer(keep, other, taps, rates, residues, cot_own, cot_other):
    groups, toks, chans = keep.shape
    modes = rates.shape[0]
    rim = taps.shape[1] - 1
    lanes = 128
    length = toks // CHUNKS
    return small_call(
        mixer_kernel,
        [
            jax.ShapeDtypeStruct((toks // 2, chans), bf16),
            jax.ShapeDtypeStruct((toks // 2, chans), bf16),
            jax.ShapeDtypeStruct((groups, chans, toks), bf16),
        ],
        [keep, other, taps, rates, residues, cot_own, cot_other],
        "mixer",
        12 * modes * toks * chans,
        [
            pltpu.VMEM((groups, toks + 8 * CHUNKS, lanes), f32),
            pltpu.VMEM((toks + 8 * CHUNKS, lanes), f32),
            pltpu.VMEM((groups, length + rim, CHUNKS, lanes), f32),
            pltpu.VMEM((groups, length, CHUNKS, lanes), f32),
            pltpu.VMEM((length, CHUNKS, lanes), f32),
            pltpu.VMEM((length, CHUNKS, lanes), f32),
            pltpu.VMEM((groups, length + rim, CHUNKS, lanes), f32),
            pltpu.VMEM((modes, CHUNKS, lanes), f32),
            pltpu.VMEM((modes, CHUNKS, lanes), f32),
        ],
    )


def back_kernel(outs, count, base, w_ref, *refs):
    grads, out_refs = refs[: len(count)], refs[len(count) + base :]
    groups, half, _ = grads[0].shape
    core = here()[3]
    sides = [pl.multiple_of((1 - core if other else core) * half, half) for other in count]
    for blocks, out in zip(outs, out_refs):
        width = out.shape[0] // len(blocks)
        for n, block in enumerate(blocks):
            rows = slice(n * width, (n + 1) * width)
            start = pl.multiple_of(block_at(*block) * width, width)
            total = refs[len(count)][rows] if base else None
            for g in range(groups):
                for ref, at in zip(grads, sides):
                    term = jnp.dot(
                        w_ref[g, pl.ds(start, width), pl.ds(at, half)],
                        ref[g],
                        preferred_element_type=f32,
                    )
                    total = term if total is None else total + term
            out[rows] = total.astype(out.dtype)


def back_project(outs, dtypes, w, own, other, width, base=None):
    grads = [(side, grad) for side, grad in enumerate((own, other)) if grad is not None]
    groups, half, toks = grads[0][1].shape
    extra = [] if base is None else [base]
    return small_call(
        functools.partial(back_kernel, outs, [side for side, _ in grads], len(extra)),
        [
            jax.ShapeDtypeStruct((width * len(blocks), toks), dtype)
            for blocks, dtype in zip(outs, dtypes)
        ],
        [w] + [grad for _, grad in grads] + extra,
        "back_project",
        2 * sum(len(blocks) for blocks in outs) * groups * width * half * toks * len(grads),
        (),
        16,
    )


def merge_kernel(two_ref, one_ref, got_ref, two_out, one_out):
    width = one_ref.shape[0]
    one_out[...] = (one_ref[...] + got_ref[:width].astype(f32)).astype(bf16)
    two_out[...] = (two_ref[...] + got_ref[width:].astype(f32)).astype(bf16)


def merge(two, one, got):
    shape = jax.ShapeDtypeStruct(one.shape, bf16)
    return small_call(merge_kernel, [shape, shape], [two, one, got], "merge")


def column_kernel(slot, own_ref, other_ref, first_ref, *out_refs):
    width, toks = own_ref.shape
    half = toks // 2
    total = (
        own_ref[...]
        + other_ref[(slot - 1) * width : slot * width].astype(f32)
        + first_ref[...].astype(f32)
    )
    z, _, _, core = here()
    side = (z >> 1) if slot == 2 else 1 - (z >> 1)
    low, high = total[:, :half], total[:, half:]
    send_low, send_high = out_refs[0], out_refs[1]

    @pl.when(side == 0)
    def _():
        send_low[...] = low.astype(bf16)
        send_high[...] = high.astype(bf16)

    @pl.when(side == 1)
    def _():
        send_low[...] = high.astype(bf16)
        send_high[...] = low.astype(bf16)

    if len(out_refs) == 3:
        inner = is_inner()
        out_refs[2][...] = jnp.where(inner, jnp.where(core == 0, low, high), 0.0)


def column(slot, own, other, first):
    width, toks = own.shape
    half = jax.ShapeDtypeStruct((width, toks // 2), bf16)
    kept = [jax.ShapeDtypeStruct((width, toks // 2), f32)] if slot == 1 else []
    return small_call(
        functools.partial(column_kernel, slot), [half, half] + kept, [own, other, first], "column"
    )


def finish_kernel(own_ref, a_ref, b_ref, c_ref, d_ref, out_ref):
    total = own_ref[...]
    for ref in (a_ref, b_ref, c_ref, d_ref):
        total = total + ref[...].astype(f32)
    out_ref[...] = total.T.astype(bf16)


def finish(own, received):
    shape = jax.ShapeDtypeStruct((own.shape[1], own.shape[0]), bf16)
    return small_call(finish_kernel, shape, [own] + received, "finish")


def pair_kernel(own_ref, other_ref, out_ref):
    half = own_ref.shape[1]
    core = here()[3]
    out_ref[:, pl.ds(pl.multiple_of(core * half, half), half)] = own_ref[...]
    out_ref[:, pl.ds(pl.multiple_of((1 - core) * half, half), half)] = other_ref[...]


def pair(own, other):
    shape = jax.ShapeDtypeStruct((own.shape[0], 2 * own.shape[1]), own.dtype)
    return small_call(pair_kernel, shape, [own, other], "pair")


def chip_plan(token_ids, embed, w_in, taps, rates, residues, cotangent):
    width = embed.shape[1]

    def swap(array):
        return lax.ppermute(array, BOTH, OTHER_CORE)

    def first_way(array):
        return lax.ppermute(array, BOTH, FIRST_WAY)

    def other_way(array):
        return lax.ppermute(array, BOTH, OTHER_WAY)

    own_ids = token_ids.reshape(1, -1)
    other_ids = swap(own_ids)
    cot_other = swap(cotangent)
    own_ids, table = fetch(own_ids, embed)
    embedded = embed_rows(own_ids, other_ids, table)
    embedded, cot_other = lax.optimization_barrier((embedded, cot_other))

    came = lax.ppermute(embedded, BOTH, GATHER_Z)
    more = lax.ppermute(embedded, BOTH, OUTER_Z_INNER_X)
    near_y = lax.ppermute(embedded, BOTH, INNER_Y)
    near_d = lax.ppermute(embedded, BOTH, INNER_XY)
    w = load(jnp.transpose(w_in, (1, 0, 2)))
    came, w = lax.optimization_barrier((came, w))
    first, other = first_way(came), other_way(came)
    x_2 = lax.ppermute(more, BOTH, OUTER_X)
    y_2 = lax.ppermute(more, BOTH, OUTER_Y)
    sums = project(
        [embedded, more, near_y, near_d, came],
        [(0, 1, None), (1, 1, "x"), (2, 1, "y"), (3, 1, 2), (4, 2, None)],
        [(4, 1, None), (1, 2, None)],
        w,
        None,
        False,
    )
    first, other, more, sums = lax.optimization_barrier((first, other, more, sums))
    both = other_way(first)
    d_2 = lax.ppermute(more, BOTH, OUTER_XY)
    sums = project(
        [first, other], [(0, 2, 0), (1, 2, 1)], [(0, 1, 0), (1, 1, 1)], w, sums, False
    )
    sums = project([x_2, y_2], [], [(0, 2, "x"), (1, 2, "y")], w, sums, False)
    both, d_2, sums = lax.optimization_barrier((both, d_2, sums))
    keep, send = project(
        [both, d_2],
        [(0, 2, 2)],
        [(0, 1, 2), (1, 2, 2)],
        w,
        sums,
        True,
    )
    mixed_own, mixed_send, grad_own = mixer(
        keep, swap(send), jnp.transpose(taps, (1, 0, 2)), rates, residues, cotangent, cot_other
    )
    grad_other = swap(grad_own)
    mixed_other = swap(mixed_send)

    (part,) = back_project([[(1, 2), (2, 2)]], [f32], w, grad_own, None, width)
    grad_other, part = lax.optimization_barrier((grad_other, part))
    (across,) = back_project([[(1, 2), (2, 2)]], [bf16], w, None, grad_other, width, part)
    across = other_way(across)
    (other,) = back_project([[(1, 1), (2, 1)]], [bf16], w, grad_own, grad_other, width)
    other = other_way(other)
    first_2, first_1, own_2, own_1 = back_project(
        [[(2, 0)], [(1, 0)], [(2, None)], [(1, None)]], [f32] * 4, w, grad_own, grad_other, width
    )
    mixed = pair(mixed_own, mixed_other)
    across, mixed = lax.optimization_barrier((across, mixed))
    first_2, first_1 = merge(first_2, first_1, across)
    first_2, first_1 = first_way(first_2), first_way(first_1)
    sends = column(2, own_2, other, first_2)
    received = [lax.ppermute(a, BOTH, pairs) for a, pairs in zip(sends, SCATTER_Z[:2])]
    *sends, own = column(1, own_1, other, first_1)
    received += [lax.ppermute(a, BOTH, pairs) for a, pairs in zip(sends, SCATTER_Z[2:])]
    return (mixed, finish(own, received))


def solution(mesh):
    in_specs = (
        P("ctx"),
        P(None, "fsdp"),
        P("ctx", None, "fsdp"),
        P(None, None, "fsdp"),
        P(None, "fsdp"),
        P(None, "fsdp"),
        P("ctx", "fsdp"),
    )
    out_specs = (P("ctx", "fsdp"), P("ctx", "fsdp"))
    chips = mesh.shape["fsdp"] == 16 and mesh.shape["ctx"] == 2
    return jax.shard_map(
        chip_plan if chips else general_plan,
        mesh=mesh,
        in_specs=in_specs,
        out_specs=out_specs,
        check_vma=False,
    )
```

```python
import functools

import jax
import jax.numpy as jnp
from jax import lax
from jax.experimental import pallas as pl
from jax.experimental.pallas import tpu as pltpu
from jax.sharding import PartitionSpec as P

BOTH = ("fsdp", "ctx")
CHUNKS = 8
f32 = jnp.float32
bf16 = jnp.bfloat16


def from_behind(shard, axis, by):
    count = lax.axis_size(axis)
    pairs = [(i, i + by) for i in range(count) if 0 <= i + by < count]
    return lax.ppermute(shard, axis, pairs)


def pair_combine(earlier, later):
    return (earlier[0] * later[0], later[0] * earlier[1] + later[1])


def modal_states(drive, step_decay):
    tok_count = drive.shape[0]
    factors = jnp.broadcast_to(step_decay[None], (tok_count,) + step_decay.shape)
    inputs = jnp.broadcast_to(drive[:, None, :], factors.shape)
    return lax.associative_scan(pair_combine, (factors, inputs), axis=0)[1]


def short_filter(extended, taps, tok_count):
    rim_width = taps.shape[0] - 1
    filtered = taps[0] * extended[rim_width : rim_width + tok_count]
    for shift_lag in range(1, rim_width + 1):
        filtered = (
            filtered
            + taps[shift_lag] * extended[rim_width - shift_lag : rim_width - shift_lag + tok_count]
        )
    return filtered


def short_adjoint(extended, taps, tok_count):
    rim_width = taps.shape[0] - 1
    result = taps[0] * extended[:tok_count]
    for shift_lag in range(1, rim_width + 1):
        result = result + taps[shift_lag] * extended[shift_lag : shift_lag + tok_count]
    return result


def carry(block_decay, leaving, by):
    def relay_step(turn_index, incoming):
        return from_behind(block_decay * incoming + leaving, "ctx", by)

    return lax.fori_loop(0, lax.axis_size("ctx") - 1, relay_step, jnp.zeros_like(leaving))


def general_plan(token_ids, embed, w_in, taps, rates, residues, cotangent):
    tok_count = token_ids.shape[0]
    vocab_size = embed.shape[0]
    chan_width = embed.shape[1]
    rim_width = taps.shape[0] - 1
    onehot = (
        token_ids[:, None] == lax.broadcasted_iota(jnp.int32, (tok_count, vocab_size), 1)
    ).astype(bf16)
    embedded = jnp.dot(onehot, embed, preferred_element_type=f32).astype(bf16)
    features = lax.all_gather(embedded, "fsdp", axis=1, tiled=True)
    feat_width = features.shape[1]
    whole_w = lax.all_gather(w_in, "ctx", axis=0, tiled=True).reshape(feat_width, 3 * chan_width)
    projected = jnp.dot(features, whole_w, preferred_element_type=f32)
    stored = lax.optimization_barrier(projected.astype(bf16).reshape(tok_count, 3, chan_width))
    before = from_behind(stored[tok_count - rim_width :], "ctx", 1)
    extended = jnp.concatenate([before, stored], axis=0).astype(f32)
    filtered = short_filter(extended, taps, tok_count)
    query_part = filtered[:, 0]
    key_part = filtered[:, 1]
    value_part = filtered[:, 2]
    drive = key_part * value_part
    step_decay = jnp.exp(-rates)
    block_decay = jnp.exp(-rates * tok_count)
    local_states = modal_states(drive, step_decay)
    entering = carry(block_decay, local_states[tok_count - 1], 1)
    offsets = lax.broadcasted_iota(f32, (tok_count, 1, 1), 0)
    states = local_states + jnp.exp(-rates[None] * (offsets + 1.0)) * entering[None]
    long_out = jnp.sum(residues[None] * states, axis=1)
    mixed = (query_part * long_out).astype(bf16)
    incoming = cotangent.astype(f32)
    grad_long = incoming * query_part
    grad_query = incoming * long_out
    back_states = jnp.flip(modal_states(jnp.flip(grad_long, 0), step_decay), 0)
    beyond = carry(block_decay, back_states[0], -1)
    adjoint = back_states + jnp.exp(-rates[None] * (tok_count - offsets)) * beyond[None]
    grad_drive = jnp.sum(residues[None] * adjoint, axis=1)
    grad_filtered = jnp.stack([grad_query, grad_drive * value_part, grad_drive * key_part], axis=1)
    after = from_behind(grad_filtered[:rim_width], "ctx", -1)
    ext_grad = jnp.concatenate([grad_filtered, after], axis=0)
    grad_stored = short_adjoint(ext_grad, taps, tok_count).astype(bf16)
    grad_rows = grad_stored.reshape(tok_count, 3 * chan_width)
    own_rows = lax.psum_scatter(
        lax.dot_general(whole_w, grad_rows, (((1,), (1,)), ((), ())), preferred_element_type=f32),
        "fsdp",
        scatter_dimension=0,
        tiled=True,
    )
    return (mixed, own_rows.T.astype(bf16))


def device_at(z, y, x, core):
    return ((z * 2 + y) * 2 + x) * 2 + core


def everywhere(move):
    pairs = []
    for z in range(4):
        for y in range(2):
            for x in range(2):
                for core in range(2):
                    pairs.append((device_at(z, y, x, core), device_at(*move(z, y, x, core))))
    return pairs


OTHER_CORE = everywhere(lambda z, y, x, core: (z, y, x, 1 - core))


def along_z(moves):
    pairs = []
    for core in range(2):
        for (place, other), (to_place, to_other) in moves:
            z, to_z = (place, to_place) if core == 0 else (3 - place, 3 - to_place)
            for y in range(2):
                for x in range(2):
                    pairs.append(
                        (
                            device_at(z, y, x, core ^ other),
                            device_at(to_z, y, x, core ^ to_other),
                        )
                    )
    return pairs


FIRST_WAY = everywhere(lambda z, y, x, core: (z, y, 1 - x, core) if core == 0 else (z, 1 - y, x, core))
OTHER_WAY = everywhere(lambda z, y, x, core: (z, 1 - y, x, core) if core == 0 else (z, y, 1 - x, core))
def some_move(move, inner):
    def target(z, y, x, core):
        return move(z, y, x, core) if (core == z >> 1) == inner else (z, y, x, core)

    return everywhere(target)


INNER_Y = some_move(lambda z, y, x, core: (z, 1 - y, x, core), True)
INNER_XY = some_move(lambda z, y, x, core: (z, 1 - y, 1 - x, core), True)
OUTER_X = some_move(lambda z, y, x, core: (z, y, 1 - x, core), False)
OUTER_Y = some_move(lambda z, y, x, core: (z, 1 - y, x, core), False)
OUTER_XY = some_move(lambda z, y, x, core: (z, 1 - y, 1 - x, core), False)
GATHER_Z = along_z([((0, 0), (1, 0)), ((1, 0), (0, 0)), ((0, 1), (2, 0)), ((1, 1), (3, 0))])
OUTER_Z_INNER_X = along_z([((1, 1), (2, 0)), ((0, 1), (3, 0))]) + [
    pair
    for pair in everywhere(lambda z, y, x, core: (z, y, 1 - x, core))
    if (pair[0] & 1) == pair[0] >> 4
]
SCATTER_Z = (
    along_z([((0, 0), (1, 0)), ((1, 0), (0, 0)), ((2, 0), (1, 1)), ((3, 0), (0, 1))]),
    along_z([((0, 0), (1, 1)), ((1, 0), (0, 1)), ((2, 0), (1, 0)), ((3, 0), (0, 0))]),
    along_z([((0, 0), (0, 1)), ((1, 0), (1, 1)), ((2, 0), (0, 0)), ((3, 0), (1, 0))]),
    along_z([((2, 0), (0, 1)), ((3, 0), (1, 1))]),
)

IN_VMEM = pl.BlockSpec(memory_space=pltpu.VMEM)


def small_call(kernel, out_shape, operands, name, flops=0, scratch=(), limit=8):
    sizes = [o.size * o.dtype.itemsize for o in operands]
    return pl.pallas_call(
        kernel,
        in_specs=[IN_VMEM] * len(operands),
        out_specs=jax.tree.map(lambda _: IN_VMEM, out_shape),
        out_shape=out_shape,
        scratch_shapes=list(scratch),
        compiler_params=pltpu.CompilerParams(vmem_limit_bytes=limit * 1024 * 1024),
        cost_estimate=pl.CostEstimate(
            flops=flops // 64, bytes_accessed=sum(sizes) // 64, transcendentals=0
        ),
        name=name,
    )(*operands)


def here():
    spot = lax.axis_index("fsdp")
    return spot >> 2, (spot >> 1) & 1, spot & 1, lax.axis_index("ctx")


def is_inner():
    z, _, _, core = here()
    return core == (z >> 1)


def block_at(slot, way):
    z, y, x, core = here()
    along = (z & 1) if slot == 1 else 1 - (z & 1)
    far = {None: (0, 0), 0: (core, 1 - core), 1: (1 - core, core), 2: (1, 1), "x": (0, 1), "y": (1, 0)}
    far_y, far_x = far[way]
    return along * 4 + (y ^ far_y) * 2 + (x ^ far_x)


def embed_kernel(own_ref, other_ref, table_ref, out_ref):
    vocab = table_ref.shape[0]
    half = own_ref.shape[1]
    core = here()[3]
    for ref, side in ((own_ref, core), (other_ref, 1 - core)):
        across = jnp.broadcast_to(ref[...].astype(f32), (half, half)).T
        lane = lax.broadcasted_iota(jnp.int32, (half, half), 1).astype(f32)
        picks = [(across == lane + float(first)).astype(f32) for first in range(0, vocab, half)]
        rows = jnp.dot(
            jnp.concatenate(picks, axis=1).astype(bf16), table_ref[...], preferred_element_type=f32
        )
        out_ref[pl.ds(pl.multiple_of(side * half, half), half), :] = rows.astype(bf16)


def embed_rows(own_ids, other_ids, table):
    toks, width = 2 * own_ids.shape[1], table.shape[1]
    return small_call(
        embed_kernel,
        jax.ShapeDtypeStruct((toks, width), bf16),
        [own_ids, other_ids, table],
        "embed_rows",
        2 * toks * table.shape[0] * width,
    )


def fetch_kernel(ids_ref, table_ref, ids_out, table_out, sems):
    copies = [
        pltpu.make_async_copy(ids_ref, ids_out, sems.at[0]),
        pltpu.make_async_copy(table_ref, table_out, sems.at[1]),
    ]
    for copy in copies:
        copy.start()
    for copy in copies:
        copy.wait()


def in_hbm(array):
    return pltpu.with_memory_space_constraint(array, pltpu.HBM)


def in_vmem(array):
    return pltpu.with_memory_space_constraint(array, pltpu.VMEM)


def fetch(ids, table):
    out = pl.pallas_call(
        fetch_kernel,
        in_specs=[pl.BlockSpec(memory_space=pltpu.HBM)] * 2,
        out_specs=[IN_VMEM] * 2,
        out_shape=[pltpu.VMEM(ids.shape, ids.dtype), pltpu.VMEM(table.shape, bf16)],
        scratch_shapes=[pltpu.SemaphoreType.DMA((2,))],
        compiler_params=pltpu.CompilerParams(vmem_limit_bytes=2 * 1024 * 1024),
        cost_estimate=pl.CostEstimate(
            flops=0, bytes_accessed=4 * table.size, transcendentals=0
        ),
        name="fetch",
    )(in_hbm(ids), in_hbm(table))
    return [in_vmem(array) for array in out]


def load_kernel(w_ref, out_ref, sem):
    copy = pltpu.make_async_copy(w_ref, out_ref, sem)
    copy.start()
    copy.wait()


def load(w):
    out = pl.pallas_call(
        load_kernel,
        in_specs=[pl.BlockSpec(memory_space=pltpu.HBM)],
        out_specs=IN_VMEM,
        out_shape=pltpu.VMEM(w.shape, w.dtype),
        scratch_shapes=[pltpu.SemaphoreType.DMA],
        compiler_params=pltpu.CompilerParams(vmem_limit_bytes=2 * 1024 * 1024),
        cost_estimate=pl.CostEstimate(
            flops=0, bytes_accessed=2 * w.size * w.dtype.itemsize, transcendentals=0
        ),
        name="load",
    )(in_hbm(w))
    return in_vmem(out)


def project_kernel(inner, outer, count, has_base, last, w_ref, *refs):
    acts = refs[:count]
    groups, _, chans = w_ref.shape
    width = acts[0].shape[1]
    if last:
        half = chans // 2
        core = here()[3]
        outs = [
            (refs[-2], pl.ds(pl.multiple_of(core * half, half), half)),
            (refs[-1], pl.ds(pl.multiple_of((1 - core) * half, half), half)),
        ]
    else:
        outs = [(refs[-1], slice(None))]

    def add(entries):
        spans = [
            pl.ds(pl.multiple_of(block_at(slot, way) * width, width), width)
            for _, slot, way in entries
        ]
        for g in range(groups):
            for out, some in outs:
                total = refs[count][g, :, some] if has_base else None
                for (which, _, _), span in zip(entries, spans):
                    term = jnp.dot(
                        acts[which][...], w_ref[g, span, some], preferred_element_type=f32
                    )
                    total = term if total is None else total + term
                out[g] = total

    pl.when(is_inner())(lambda: add(inner))
    pl.when(jnp.logical_not(is_inner()))(lambda: add(outer))


def project(acts, inner, outer, w, base, last):
    groups, _, chans = w.shape
    toks, width = acts[0].shape
    total = jax.ShapeDtypeStruct((groups, toks, chans), f32)
    half = jax.ShapeDtypeStruct((groups, toks, chans // 2), f32)
    return small_call(
        functools.partial(project_kernel, inner, outer, len(acts), base is not None, last),
        [half, half] if last else total,
        [w] + list(acts) + ([] if base is None else [base]),
        "project",
        2 * max(len(inner), len(outer)) * groups * width * chans * toks,
        (),
        16,
    )


def shifted(values, by):
    place = lax.broadcasted_iota(jnp.int32, values.shape, 0)
    moved = pltpu.roll(values, by % CHUNKS, 0)
    inside = place >= by if by > 0 else place < CHUNKS + by
    return jnp.where(inside, moved, 0.0)


def mixer_kernel(
    keep_ref,
    other_ref,
    taps_ref,
    rates_ref,
    residues_ref,
    cot_own_ref,
    cot_other_ref,
    mixed_own_ref,
    mixed_send_ref,
    grad_ref,
    flat,
    flat_cot,
    ext,
    filt,
    drive,
    back,
    grad_ext,
    decays,
    residues,
):
    groups, toks, chans = keep_ref.shape
    half = toks // 2
    modes = rates_ref.shape[0]
    short = taps_ref.shape[1]
    rim = short - 1
    length = toks // CHUNKS
    apart = flat.shape[1] // CHUNKS
    lanes = flat.shape[-1]
    wide = (CHUNKS, lanes)
    _, _, _, core = here()

    def spread(ref, at, values):
        for s in range(CHUNKS):
            ref[(*at, slice(s * apart, s * apart + length))] = values[s * length : (s + 1) * length]

    def row(array, at):
        return jnp.broadcast_to(array[at : at + 1, :], wide)

    def column(c, _):
        some = pl.ds(pl.multiple_of(c * lanes, lanes), lanes)
        whole = pl.ds(pl.multiple_of(core * chans + c * lanes, lanes), lanes)
        for g in range(groups):
            spread(flat, (g,), (keep_ref[g, :, some] + other_ref[g, :, some]).astype(bf16).astype(f32))
        for s in range(CHUNKS // 2):
            rows = slice(s * length, (s + 1) * length)
            own_at = pl.multiple_of((core * (CHUNKS // 2) + s) * apart, 8)
            other_at = pl.multiple_of(((1 - core) * (CHUNKS // 2) + s) * apart, 8)
            flat_cot[pl.ds(own_at, length)] = cot_own_ref[rows, whole].astype(f32)
            flat_cot[pl.ds(other_at, length)] = cot_other_ref[rows, whole].astype(f32)

        for g in range(groups):
            for k in range(length):
                ext[g, rim + k] = flat[g, pl.ds(k, CHUNKS, stride=apart), :]
            for k in range(rim):
                ext[g, k] = shifted(ext[g, length + k], 1)

        taps = [taps_ref[g, :, whole] for g in range(groups)]
        tap = [[row(taps[g], j) for g in range(groups)] for j in range(short)]

        def filter_step(k, _):
            parts = []
            for g in range(groups):
                total = tap[0][g] * ext[g, k + rim]
                for j in range(1, short):
                    total = total + tap[j][g] * ext[g, k + rim - j]
                parts.append(total)
                filt[g, k] = total
            drive[k] = parts[1] * parts[2]
            back[k] = parts[0] * flat_cot[pl.ds(k, CHUNKS, stride=apart), :]
            return _

        lax.fori_loop(0, length, filter_step, 0, unroll=4)

        rates = rates_ref[:, whole]
        decay_rows = jnp.exp(-rates)
        jump_rows = [jnp.exp(-rates * (length * n)) for n in (1, 2, 4)]
        residue_rows = residues_ref[:, whole]
        for m in range(modes):
            decays[m] = row(decay_rows, m)
            residues[m] = row(residue_rows, m)

        def long_filter(source, forward, finish):
            decay = [decays[m] for m in range(modes)]

            def place(k):
                return k if forward else length - 1 - k

            def end_step(k, states):
                value = source[place(k)]
                return tuple(decay[m] * states[m] + value for m in range(modes))

            zero = jnp.zeros(wide, f32)
            ends = lax.fori_loop(0, length, end_step, (zero,) * modes, unroll=8)
            entering = []
            sign = 1 if forward else -1
            for m in range(modes):
                carried = ends[m]
                for jump, by in zip(jump_rows, (1, 2, 4)):
                    carried = carried + row(jump, m) * shifted(carried, sign * by)
                entering.append(shifted(carried, sign))

            def out_step(k, states):
                value = source[place(k)]
                states = tuple(decay[m] * states[m] + value for m in range(modes))
                terms = [residues[m] * states[m] for m in range(modes)]
                while len(terms) > 1:
                    terms = [a + b for a, b in zip(terms[::2], terms[1::2])]
                finish(place(k), terms[0])
                return states

            lax.fori_loop(0, length, out_step, tuple(entering), unroll=4)

        def finish_forward(k, total):
            flat[0, pl.ds(k, CHUNKS, stride=apart), :] = filt[0, k] * total
            grad_ext[0, k] = flat_cot[pl.ds(k, CHUNKS, stride=apart), :] * total

        def finish_backward(k, total):
            grad_ext[1, k] = total * filt[2, k]
            grad_ext[2, k] = total * filt[1, k]

        long_filter(drive, True, finish_forward)
        for s in range(CHUNKS // 2):
            rows = slice(s * length, (s + 1) * length)
            own_at = pl.multiple_of((core * (CHUNKS // 2) + s) * apart, 8)
            other_at = pl.multiple_of(((1 - core) * (CHUNKS // 2) + s) * apart, 8)
            mixed_own_ref[rows, some] = flat[0, pl.ds(own_at, length)].astype(bf16)
            mixed_send_ref[rows, some] = flat[0, pl.ds(other_at, length)].astype(bf16)
        long_filter(back, False, finish_backward)

        for g in range(groups):
            for k in range(rim):
                grad_ext[g, length + k] = shifted(grad_ext[g, k], -1)

        def adjoint_step(k, _):
            for g in range(groups):
                total = tap[0][g] * grad_ext[g, k]
                for j in range(1, short):
                    total = total + tap[j][g] * grad_ext[g, k + j]
                flat[g, pl.ds(k, CHUNKS, stride=apart), :] = total
            return _

        lax.fori_loop(0, length, adjoint_step, 0, unroll=4)
        for g in range(groups):
            chunks = [flat[g, s * apart : s * apart + length].astype(bf16) for s in range(CHUNKS)]
            grad_ref[g, some, :] = jnp.concatenate(chunks, axis=0).T
        return _

    lax.fori_loop(0, chans // lanes, column, 0)


def mixer(keep, other, taps, rates, residues, cot_own, cot_other):
    groups, toks, chans = keep.shape
    modes = rates.shape[0]
    rim = taps.shape[1] - 1
    lanes = 128
    length = toks // CHUNKS
    return small_call(
        mixer_kernel,
        [
            jax.ShapeDtypeStruct((toks // 2, chans), bf16),
            jax.ShapeDtypeStruct((toks // 2, chans), bf16),
            jax.ShapeDtypeStruct((groups, chans, toks), bf16),
        ],
        [keep, other, taps, rates, residues, cot_own, cot_other],
        "mixer",
        12 * modes * toks * chans,
        [
            pltpu.VMEM((groups, toks + 8 * CHUNKS, lanes), f32),
            pltpu.VMEM((toks + 8 * CHUNKS, lanes), f32),
            pltpu.VMEM((groups, length + rim, CHUNKS, lanes), f32),
            pltpu.VMEM((groups, length, CHUNKS, lanes), f32),
            pltpu.VMEM((length, CHUNKS, lanes), f32),
            pltpu.VMEM((length, CHUNKS, lanes), f32),
            pltpu.VMEM((groups, length + rim, CHUNKS, lanes), f32),
            pltpu.VMEM((modes, CHUNKS, lanes), f32),
            pltpu.VMEM((modes, CHUNKS, lanes), f32),
        ],
    )


def back_kernel(outs, count, base, w_ref, *refs):
    grads, out_refs = refs[: len(count)], refs[len(count) + base :]
    groups, half, _ = grads[0].shape
    core = here()[3]
    sides = [pl.multiple_of((1 - core if other else core) * half, half) for other in count]
    for blocks, out in zip(outs, out_refs):
        width = out.shape[0] // len(blocks)
        for n, block in enumerate(blocks):
            rows = slice(n * width, (n + 1) * width)
            start = pl.multiple_of(block_at(*block) * width, width)
            total = refs[len(count)][rows] if base else None
            for g in range(groups):
                for ref, at in zip(grads, sides):
                    term = jnp.dot(
                        w_ref[g, pl.ds(start, width), pl.ds(at, half)],
                        ref[g],
                        preferred_element_type=f32,
                    )
                    total = term if total is None else total + term
            out[rows] = total.astype(out.dtype)


def back_project(outs, dtypes, w, own, other, width, base=None):
    grads = [(side, grad) for side, grad in enumerate((own, other)) if grad is not None]
    groups, half, toks = grads[0][1].shape
    extra = [] if base is None else [base]
    return small_call(
        functools.partial(back_kernel, outs, [side for side, _ in grads], len(extra)),
        [
            jax.ShapeDtypeStruct((width * len(blocks), toks), dtype)
            for blocks, dtype in zip(outs, dtypes)
        ],
        [w] + [grad for _, grad in grads] + extra,
        "back_project",
        2 * sum(len(blocks) for blocks in outs) * groups * width * half * toks * len(grads),
        (),
        16,
    )


def merge_kernel(two_ref, one_ref, got_ref, two_out, one_out):
    width = one_ref.shape[0]
    one_out[...] = (one_ref[...] + got_ref[:width].astype(f32)).astype(bf16)
    two_out[...] = (two_ref[...] + got_ref[width:].astype(f32)).astype(bf16)


def merge(two, one, got):
    shape = jax.ShapeDtypeStruct(one.shape, bf16)
    return small_call(merge_kernel, [shape, shape], [two, one, got], "merge")


def column_kernel(slot, own_ref, other_ref, first_ref, *out_refs):
    width, toks = own_ref.shape
    half = toks // 2
    total = (
        own_ref[...]
        + other_ref[(slot - 1) * width : slot * width].astype(f32)
        + first_ref[...].astype(f32)
    )
    z, _, _, core = here()
    side = (z >> 1) if slot == 2 else 1 - (z >> 1)
    low, high = total[:, :half], total[:, half:]
    send_low, send_high = out_refs[0], out_refs[1]

    @pl.when(side == 0)
    def _():
        send_low[...] = low.astype(bf16)
        send_high[...] = high.astype(bf16)

    @pl.when(side == 1)
    def _():
        send_low[...] = high.astype(bf16)
        send_high[...] = low.astype(bf16)

    if len(out_refs) == 3:
        inner = is_inner()
        out_refs[2][...] = jnp.where(inner, jnp.where(core == 0, low, high), 0.0)


def column(slot, own, other, first):
    width, toks = own.shape
    half = jax.ShapeDtypeStruct((width, toks // 2), bf16)
    kept = [jax.ShapeDtypeStruct((width, toks // 2), f32)] if slot == 1 else []
    return small_call(
        functools.partial(column_kernel, slot), [half, half] + kept, [own, other, first], "column"
    )


def finish_kernel(own_ref, a_ref, b_ref, c_ref, d_ref, out_ref):
    total = own_ref[...]
    for ref in (a_ref, b_ref, c_ref, d_ref):
        total = total + ref[...].astype(f32)
    out_ref[...] = total.T.astype(bf16)


def finish(own, received):
    shape = jax.ShapeDtypeStruct((own.shape[1], own.shape[0]), bf16)
    return small_call(finish_kernel, shape, [own] + received, "finish")


def pair_kernel(own_ref, other_ref, out_ref):
    half = own_ref.shape[1]
    core = here()[3]
    out_ref[:, pl.ds(pl.multiple_of(core * half, half), half)] = own_ref[...]
    out_ref[:, pl.ds(pl.multiple_of((1 - core) * half, half), half)] = other_ref[...]


def pair(own, other):
    shape = jax.ShapeDtypeStruct((own.shape[0], 2 * own.shape[1]), own.dtype)
    return small_call(pair_kernel, shape, [own, other], "pair")


def chip_plan(token_ids, embed, w_in, taps, rates, residues, cotangent):
    width = embed.shape[1]

    def swap(array):
        return lax.ppermute(array, BOTH, OTHER_CORE)

    def first_way(array):
        return lax.ppermute(array, BOTH, FIRST_WAY)

    def other_way(array):
        return lax.ppermute(array, BOTH, OTHER_WAY)

    own_ids = token_ids.reshape(1, -1)
    other_ids = swap(own_ids)
    cot_other = swap(cotangent)
    own_ids, table = fetch(own_ids, embed)
    embedded = embed_rows(own_ids, other_ids, table)
    embedded, cot_other = lax.optimization_barrier((embedded, cot_other))

    came = lax.ppermute(embedded, BOTH, GATHER_Z)
    more = lax.ppermute(embedded, BOTH, OUTER_Z_INNER_X)
    near_y = lax.ppermute(embedded, BOTH, INNER_Y)
    near_d = lax.ppermute(embedded, BOTH, INNER_XY)
    w = load(jnp.transpose(w_in, (1, 0, 2)))
    came, w = lax.optimization_barrier((came, w))
    first, other = first_way(came), other_way(came)
    sums = project(
        [embedded, near_y, near_d, came],
        [(0, 1, None), (1, 1, "y"), (2, 1, 2), (3, 2, None)],
        [(3, 1, None)],
        w,
        None,
        False,
    )
    more, sums = lax.optimization_barrier((more, sums))
    x_2 = lax.ppermute(more, BOTH, OUTER_X)
    y_2 = lax.ppermute(more, BOTH, OUTER_Y)
    first, other, more = lax.optimization_barrier((first, other, more))
    both = other_way(first)
    d_2 = lax.ppermute(more, BOTH, OUTER_XY)
    sums = project(
        [first, other, more],
        [(0, 2, 0), (1, 2, 1), (2, 1, "x")],
        [(0, 1, 0), (1, 1, 1), (2, 2, None)],
        w,
        sums,
        False,
    )
    sums = project([x_2, y_2], [], [(0, 2, "x"), (1, 2, "y")], w, sums, False)
    both, d_2, sums = lax.optimization_barrier((both, d_2, sums))
    keep, send = project(
        [both, d_2],
        [(0, 2, 2)],
        [(0, 1, 2), (1, 2, 2)],
        w,
        sums,
        True,
    )
    mixed_own, mixed_send, grad_own = mixer(
        keep, swap(send), jnp.transpose(taps, (1, 0, 2)), rates, residues, cotangent, cot_other
    )
    grad_other = swap(grad_own)
    mixed_other = swap(mixed_send)

    (part,) = back_project([[(1, 2), (2, 2)]], [f32], w, grad_own, None, width)
    grad_other, part = lax.optimization_barrier((grad_other, part))
    (across,) = back_project([[(1, 2), (2, 2)]], [bf16], w, None, grad_other, width, part)
    across = other_way(across)
    (other,) = back_project([[(1, 1), (2, 1)]], [bf16], w, grad_own, grad_other, width)
    other = other_way(other)
    first_2, first_1, own_2, own_1 = back_project(
        [[(2, 0)], [(1, 0)], [(2, None)], [(1, None)]], [f32] * 4, w, grad_own, grad_other, width
    )
    mixed = pair(mixed_own, mixed_other)
    across, mixed = lax.optimization_barrier((across, mixed))
    first_2, first_1 = merge(first_2, first_1, across)
    first_2, first_1 = first_way(first_2), first_way(first_1)
    sends = column(2, own_2, other, first_2)
    received = [lax.ppermute(a, BOTH, pairs) for a, pairs in zip(sends, SCATTER_Z[:2])]
    *sends, own = column(1, own_1, other, first_1)
    received += [lax.ppermute(a, BOTH, pairs) for a, pairs in zip(sends, SCATTER_Z[2:])]
    return (mixed, finish(own, received))


def solution(mesh):
    in_specs = (
        P("ctx"),
        P(None, "fsdp"),
        P("ctx", None, "fsdp"),
        P(None, None, "fsdp"),
        P(None, "fsdp"),
        P(None, "fsdp"),
        P("ctx", "fsdp"),
    )
    out_specs = (P("ctx", "fsdp"), P("ctx", "fsdp"))
    chips = mesh.shape["fsdp"] == 16 and mesh.shape["ctx"] == 2
    return jax.shard_map(
        chip_plan if chips else general_plan,
        mesh=mesh,
        in_specs=in_specs,
        out_specs=out_specs,
        check_vma=False,
    )
```

```python
import functools

import jax
import jax.numpy as jnp
from jax import lax
from jax.experimental import pallas as pl
from jax.experimental.pallas import tpu as pltpu
from jax.sharding import PartitionSpec as P

BOTH = ("fsdp", "ctx")
CHUNKS = 8
f32 = jnp.float32
bf16 = jnp.bfloat16


def from_behind(shard, axis, by):
    count = lax.axis_size(axis)
    pairs = [(i, i + by) for i in range(count) if 0 <= i + by < count]
    return lax.ppermute(shard, axis, pairs)


def pair_combine(earlier, later):
    return (earlier[0] * later[0], later[0] * earlier[1] + later[1])


def modal_states(drive, step_decay):
    tok_count = drive.shape[0]
    factors = jnp.broadcast_to(step_decay[None], (tok_count,) + step_decay.shape)
    inputs = jnp.broadcast_to(drive[:, None, :], factors.shape)
    return lax.associative_scan(pair_combine, (factors, inputs), axis=0)[1]


def short_filter(extended, taps, tok_count):
    rim_width = taps.shape[0] - 1
    filtered = taps[0] * extended[rim_width : rim_width + tok_count]
    for shift_lag in range(1, rim_width + 1):
        filtered = (
            filtered
            + taps[shift_lag] * extended[rim_width - shift_lag : rim_width - shift_lag + tok_count]
        )
    return filtered


def short_adjoint(extended, taps, tok_count):
    rim_width = taps.shape[0] - 1
    result = taps[0] * extended[:tok_count]
    for shift_lag in range(1, rim_width + 1):
        result = result + taps[shift_lag] * extended[shift_lag : shift_lag + tok_count]
    return result


def carry(block_decay, leaving, by):
    def relay_step(turn_index, incoming):
        return from_behind(block_decay * incoming + leaving, "ctx", by)

    return lax.fori_loop(0, lax.axis_size("ctx") - 1, relay_step, jnp.zeros_like(leaving))


def general_plan(token_ids, embed, w_in, taps, rates, residues, cotangent):
    tok_count = token_ids.shape[0]
    vocab_size = embed.shape[0]
    chan_width = embed.shape[1]
    rim_width = taps.shape[0] - 1
    onehot = (
        token_ids[:, None] == lax.broadcasted_iota(jnp.int32, (tok_count, vocab_size), 1)
    ).astype(bf16)
    embedded = jnp.dot(onehot, embed, preferred_element_type=f32).astype(bf16)
    features = lax.all_gather(embedded, "fsdp", axis=1, tiled=True)
    feat_width = features.shape[1]
    whole_w = lax.all_gather(w_in, "ctx", axis=0, tiled=True).reshape(feat_width, 3 * chan_width)
    projected = jnp.dot(features, whole_w, preferred_element_type=f32)
    stored = lax.optimization_barrier(projected.astype(bf16).reshape(tok_count, 3, chan_width))
    before = from_behind(stored[tok_count - rim_width :], "ctx", 1)
    extended = jnp.concatenate([before, stored], axis=0).astype(f32)
    filtered = short_filter(extended, taps, tok_count)
    query_part = filtered[:, 0]
    key_part = filtered[:, 1]
    value_part = filtered[:, 2]
    drive = key_part * value_part
    step_decay = jnp.exp(-rates)
    block_decay = jnp.exp(-rates * tok_count)
    local_states = modal_states(drive, step_decay)
    entering = carry(block_decay, local_states[tok_count - 1], 1)
    offsets = lax.broadcasted_iota(f32, (tok_count, 1, 1), 0)
    states = local_states + jnp.exp(-rates[None] * (offsets + 1.0)) * entering[None]
    long_out = jnp.sum(residues[None] * states, axis=1)
    mixed = (query_part * long_out).astype(bf16)
    incoming = cotangent.astype(f32)
    grad_long = incoming * query_part
    grad_query = incoming * long_out
    back_states = jnp.flip(modal_states(jnp.flip(grad_long, 0), step_decay), 0)
    beyond = carry(block_decay, back_states[0], -1)
    adjoint = back_states + jnp.exp(-rates[None] * (tok_count - offsets)) * beyond[None]
    grad_drive = jnp.sum(residues[None] * adjoint, axis=1)
    grad_filtered = jnp.stack([grad_query, grad_drive * value_part, grad_drive * key_part], axis=1)
    after = from_behind(grad_filtered[:rim_width], "ctx", -1)
    ext_grad = jnp.concatenate([grad_filtered, after], axis=0)
    grad_stored = short_adjoint(ext_grad, taps, tok_count).astype(bf16)
    grad_rows = grad_stored.reshape(tok_count, 3 * chan_width)
    own_rows = lax.psum_scatter(
        lax.dot_general(whole_w, grad_rows, (((1,), (1,)), ((), ())), preferred_element_type=f32),
        "fsdp",
        scatter_dimension=0,
        tiled=True,
    )
    return (mixed, own_rows.T.astype(bf16))


def device_at(z, y, x, core):
    return ((z * 2 + y) * 2 + x) * 2 + core


def everywhere(move):
    pairs = []
    for z in range(4):
        for y in range(2):
            for x in range(2):
                for core in range(2):
                    pairs.append((device_at(z, y, x, core), device_at(*move(z, y, x, core))))
    return pairs


OTHER_CORE = everywhere(lambda z, y, x, core: (z, y, x, 1 - core))


def along_z(moves):
    pairs = []
    for core in range(2):
        for (place, other), (to_place, to_other) in moves:
            z, to_z = (place, to_place) if core == 0 else (3 - place, 3 - to_place)
            for y in range(2):
                for x in range(2):
                    pairs.append(
                        (
                            device_at(z, y, x, core ^ other),
                            device_at(to_z, y, x, core ^ to_other),
                        )
                    )
    return pairs


FIRST_WAY = everywhere(lambda z, y, x, core: (z, y, 1 - x, core) if core == 0 else (z, 1 - y, x, core))
OTHER_WAY = everywhere(lambda z, y, x, core: (z, 1 - y, x, core) if core == 0 else (z, y, 1 - x, core))
def some_move(move, inner):
    def target(z, y, x, core):
        return move(z, y, x, core) if (core == z >> 1) == inner else (z, y, x, core)

    return everywhere(target)


INNER_Y = some_move(lambda z, y, x, core: (z, 1 - y, x, core), True)
INNER_XY = some_move(lambda z, y, x, core: (z, 1 - y, 1 - x, core), True)
OUTER_X = some_move(lambda z, y, x, core: (z, y, 1 - x, core), False)
OUTER_Y = some_move(lambda z, y, x, core: (z, 1 - y, x, core), False)
OUTER_XY = some_move(lambda z, y, x, core: (z, 1 - y, 1 - x, core), False)
GATHER_Z = along_z([((0, 0), (1, 0)), ((1, 0), (0, 0)), ((0, 1), (2, 0)), ((1, 1), (3, 0))])
OUTER_Z_INNER_X = along_z([((1, 1), (2, 0)), ((0, 1), (3, 0))]) + [
    pair
    for pair in everywhere(lambda z, y, x, core: (z, y, 1 - x, core))
    if (pair[0] & 1) == pair[0] >> 4
]
SCATTER_Z = (
    along_z([((0, 0), (1, 0)), ((1, 0), (0, 0)), ((2, 0), (1, 1)), ((3, 0), (0, 1))]),
    along_z([((0, 0), (1, 1)), ((1, 0), (0, 1)), ((2, 0), (1, 0)), ((3, 0), (0, 0))]),
    along_z([((0, 0), (0, 1)), ((1, 0), (1, 1)), ((2, 0), (0, 0)), ((3, 0), (1, 0))]),
    along_z([((2, 0), (0, 1)), ((3, 0), (1, 1))]),
)

IN_VMEM = pl.BlockSpec(memory_space=pltpu.VMEM)


def small_call(kernel, out_shape, operands, name, flops=0, scratch=(), limit=8):
    sizes = [o.size * o.dtype.itemsize for o in operands]
    return pl.pallas_call(
        kernel,
        in_specs=[IN_VMEM] * len(operands),
        out_specs=jax.tree.map(lambda _: IN_VMEM, out_shape),
        out_shape=out_shape,
        scratch_shapes=list(scratch),
        compiler_params=pltpu.CompilerParams(vmem_limit_bytes=limit * 1024 * 1024),
        cost_estimate=pl.CostEstimate(
            flops=flops // 64, bytes_accessed=sum(sizes) // 64, transcendentals=0
        ),
        name=name,
    )(*operands)


def here():
    spot = lax.axis_index("fsdp")
    return spot >> 2, (spot >> 1) & 1, spot & 1, lax.axis_index("ctx")


def is_inner():
    z, _, _, core = here()
    return core == (z >> 1)


def block_at(slot, way):
    z, y, x, core = here()
    along = (z & 1) if slot == 1 else 1 - (z & 1)
    far = {None: (0, 0), 0: (core, 1 - core), 1: (1 - core, core), 2: (1, 1), "x": (0, 1), "y": (1, 0)}
    far_y, far_x = far[way]
    return along * 4 + (y ^ far_y) * 2 + (x ^ far_x)


def embed_kernel(own_ref, other_ref, table_ref, out_ref):
    vocab = table_ref.shape[0]
    half = own_ref.shape[1]
    core = here()[3]
    for ref, side in ((own_ref, core), (other_ref, 1 - core)):
        across = jnp.broadcast_to(ref[...].astype(f32), (half, half)).T
        lane = lax.broadcasted_iota(jnp.int32, (half, half), 1).astype(f32)
        picks = [(across == lane + float(first)).astype(f32) for first in range(0, vocab, half)]
        rows = jnp.dot(
            jnp.concatenate(picks, axis=1).astype(bf16), table_ref[...], preferred_element_type=f32
        )
        out_ref[pl.ds(pl.multiple_of(side * half, half), half), :] = rows.astype(bf16)


def embed_rows(own_ids, other_ids, table):
    toks, width = 2 * own_ids.shape[1], table.shape[1]
    return small_call(
        embed_kernel,
        jax.ShapeDtypeStruct((toks, width), bf16),
        [own_ids, other_ids, table],
        "embed_rows",
        2 * toks * table.shape[0] * width,
    )


def fetch_kernel(ids_ref, table_ref, ids_out, table_out, sems):
    copies = [
        pltpu.make_async_copy(ids_ref, ids_out, sems.at[0]),
        pltpu.make_async_copy(table_ref, table_out, sems.at[1]),
    ]
    for copy in copies:
        copy.start()
    for copy in copies:
        copy.wait()


def in_hbm(array):
    return pltpu.with_memory_space_constraint(array, pltpu.HBM)


def in_vmem(array):
    return pltpu.with_memory_space_constraint(array, pltpu.VMEM)


def fetch(ids, table):
    out = pl.pallas_call(
        fetch_kernel,
        in_specs=[pl.BlockSpec(memory_space=pltpu.HBM)] * 2,
        out_specs=[IN_VMEM] * 2,
        out_shape=[pltpu.VMEM(ids.shape, ids.dtype), pltpu.VMEM(table.shape, bf16)],
        scratch_shapes=[pltpu.SemaphoreType.DMA((2,))],
        compiler_params=pltpu.CompilerParams(vmem_limit_bytes=2 * 1024 * 1024),
        cost_estimate=pl.CostEstimate(
            flops=0, bytes_accessed=4 * table.size, transcendentals=0
        ),
        name="fetch",
    )(in_hbm(ids), in_hbm(table))
    return [in_vmem(array) for array in out]


def load_kernel(w_ref, out_ref, sem):
    copy = pltpu.make_async_copy(w_ref, out_ref, sem)
    copy.start()
    copy.wait()


def load(w):
    out = pl.pallas_call(
        load_kernel,
        in_specs=[pl.BlockSpec(memory_space=pltpu.HBM)],
        out_specs=IN_VMEM,
        out_shape=pltpu.VMEM(w.shape, w.dtype),
        scratch_shapes=[pltpu.SemaphoreType.DMA],
        compiler_params=pltpu.CompilerParams(vmem_limit_bytes=2 * 1024 * 1024),
        cost_estimate=pl.CostEstimate(
            flops=0, bytes_accessed=2 * w.size * w.dtype.itemsize, transcendentals=0
        ),
        name="load",
    )(in_hbm(w))
    return in_vmem(out)


def project_kernel(inner, outer, count, has_base, part, w_ref, *refs):
    acts = refs[:count]
    groups, _, chans = w_ref.shape
    width = acts[0].shape[1]
    out_ref = refs[-1]
    if part is None:
        some = slice(None)
    else:
        half = chans // 2
        core = here()[3]
        side = core if part == "keep" else 1 - core
        some = pl.ds(pl.multiple_of(side * half, half), half)

    def add(entries):
        spans = [
            pl.ds(pl.multiple_of(block_at(slot, way) * width, width), width)
            for _, slot, way in entries
        ]
        for g in range(groups):
            total = refs[count][g, :, some] if has_base else None
            for (which, _, _), span in zip(entries, spans):
                term = jnp.dot(acts[which][...], w_ref[g, span, some], preferred_element_type=f32)
                total = term if total is None else total + term
            out_ref[g] = total

    pl.when(is_inner())(lambda: add(inner))
    pl.when(jnp.logical_not(is_inner()))(lambda: add(outer))


def project(acts, inner, outer, w, base, part=None):
    groups, _, chans = w.shape
    toks, width = acts[0].shape
    if part is not None:
        chans //= 2
    return small_call(
        functools.partial(project_kernel, inner, outer, len(acts), base is not None, part),
        jax.ShapeDtypeStruct((groups, toks, chans), f32),
        [w] + list(acts) + ([] if base is None else [base]),
        "project",
        2 * max(len(inner), len(outer)) * groups * width * chans * toks,
        (),
        16,
    )


def shifted(values, by):
    place = lax.broadcasted_iota(jnp.int32, values.shape, 0)
    moved = pltpu.roll(values, by % CHUNKS, 0)
    inside = place >= by if by > 0 else place < CHUNKS + by
    return jnp.where(inside, moved, 0.0)


def mixer_kernel(
    keep_ref,
    other_ref,
    taps_ref,
    rates_ref,
    residues_ref,
    cot_own_ref,
    cot_other_ref,
    mixed_own_ref,
    mixed_send_ref,
    grad_ref,
    flat,
    flat_cot,
    ext,
    filt,
    drive,
    back,
    grad_ext,
    decays,
    residues,
):
    groups, toks, chans = keep_ref.shape
    half = toks // 2
    modes = rates_ref.shape[0]
    short = taps_ref.shape[1]
    rim = short - 1
    length = toks // CHUNKS
    apart = flat.shape[1] // CHUNKS
    lanes = flat.shape[-1]
    wide = (CHUNKS, lanes)
    _, _, _, core = here()

    def spread(ref, at, values):
        for s in range(CHUNKS):
            ref[(*at, slice(s * apart, s * apart + length))] = values[s * length : (s + 1) * length]

    def row(array, at):
        return jnp.broadcast_to(array[at : at + 1, :], wide)

    def column(c, _):
        some = pl.ds(pl.multiple_of(c * lanes, lanes), lanes)
        whole = pl.ds(pl.multiple_of(core * chans + c * lanes, lanes), lanes)
        for g in range(groups):
            spread(flat, (g,), (keep_ref[g, :, some] + other_ref[g, :, some]).astype(bf16).astype(f32))
        for s in range(CHUNKS // 2):
            rows = slice(s * length, (s + 1) * length)
            own_at = pl.multiple_of((core * (CHUNKS // 2) + s) * apart, 8)
            other_at = pl.multiple_of(((1 - core) * (CHUNKS // 2) + s) * apart, 8)
            flat_cot[pl.ds(own_at, length)] = cot_own_ref[rows, whole].astype(f32)
            flat_cot[pl.ds(other_at, length)] = cot_other_ref[rows, whole].astype(f32)

        for g in range(groups):
            for k in range(length):
                ext[g, rim + k] = flat[g, pl.ds(k, CHUNKS, stride=apart), :]
            for k in range(rim):
                ext[g, k] = shifted(ext[g, length + k], 1)

        taps = [taps_ref[g, :, whole] for g in range(groups)]
        tap = [[row(taps[g], j) for g in range(groups)] for j in range(short)]

        def filter_step(k, _):
            parts = []
            for g in range(groups):
                total = tap[0][g] * ext[g, k + rim]
                for j in range(1, short):
                    total = total + tap[j][g] * ext[g, k + rim - j]
                parts.append(total)
                filt[g, k] = total
            drive[k] = parts[1] * parts[2]
            back[k] = parts[0] * flat_cot[pl.ds(k, CHUNKS, stride=apart), :]
            return _

        lax.fori_loop(0, length, filter_step, 0, unroll=8)

        rates = rates_ref[:, whole]
        decay_rows = jnp.exp(-rates)
        jump_rows = [jnp.exp(-rates * (length * n)) for n in (1, 2, 4)]
        residue_rows = residues_ref[:, whole]
        for m in range(modes):
            decays[m] = row(decay_rows, m)
            residues[m] = row(residue_rows, m)

        def long_filter(source, forward, finish):
            decay = [decays[m] for m in range(modes)]

            def place(k):
                return k if forward else length - 1 - k

            def end_step(k, states):
                value = source[place(k)]
                return tuple(decay[m] * states[m] + value for m in range(modes))

            zero = jnp.zeros(wide, f32)
            ends = lax.fori_loop(0, length, end_step, (zero,) * modes, unroll=16)
            entering = []
            sign = 1 if forward else -1
            for m in range(modes):
                carried = ends[m]
                for jump, by in zip(jump_rows, (1, 2, 4)):
                    carried = carried + row(jump, m) * shifted(carried, sign * by)
                entering.append(shifted(carried, sign))

            def out_step(k, states):
                value = source[place(k)]
                states = tuple(decay[m] * states[m] + value for m in range(modes))
                terms = [residues[m] * states[m] for m in range(modes)]
                while len(terms) > 1:
                    terms = [a + b for a, b in zip(terms[::2], terms[1::2])]
                finish(place(k), terms[0])
                return states

            lax.fori_loop(0, length, out_step, tuple(entering), unroll=8)

        def finish_forward(k, total):
            flat[0, pl.ds(k, CHUNKS, stride=apart), :] = filt[0, k] * total
            grad_ext[0, k] = flat_cot[pl.ds(k, CHUNKS, stride=apart), :] * total

        def finish_backward(k, total):
            grad_ext[1, k] = total * filt[2, k]
            grad_ext[2, k] = total * filt[1, k]

        long_filter(drive, True, finish_forward)
        for s in range(CHUNKS // 2):
            rows = slice(s * length, (s + 1) * length)
            own_at = pl.multiple_of((core * (CHUNKS // 2) + s) * apart, 8)
            other_at = pl.multiple_of(((1 - core) * (CHUNKS // 2) + s) * apart, 8)
            mixed_own_ref[rows, some] = flat[0, pl.ds(own_at, length)].astype(bf16)
            mixed_send_ref[rows, some] = flat[0, pl.ds(other_at, length)].astype(bf16)
        long_filter(back, False, finish_backward)

        for g in range(groups):
            for k in range(rim):
                grad_ext[g, length + k] = shifted(grad_ext[g, k], -1)

        def adjoint_step(k, _):
            for g in range(groups):
                total = tap[0][g] * grad_ext[g, k]
                for j in range(1, short):
                    total = total + tap[j][g] * grad_ext[g, k + j]
                flat[g, pl.ds(k, CHUNKS, stride=apart), :] = total
            return _

        lax.fori_loop(0, length, adjoint_step, 0, unroll=8)
        for g in range(groups):
            chunks = [flat[g, s * apart : s * apart + length].astype(bf16) for s in range(CHUNKS)]
            grad_ref[g, some, :] = jnp.concatenate(chunks, axis=0).T
        return _

    lax.fori_loop(0, chans // lanes, column, 0)


def mixer(keep, other, taps, rates, residues, cot_own, cot_other):
    groups, toks, chans = keep.shape
    modes = rates.shape[0]
    rim = taps.shape[1] - 1
    lanes = 128
    length = toks // CHUNKS
    return small_call(
        mixer_kernel,
        [
            jax.ShapeDtypeStruct((toks // 2, chans), bf16),
            jax.ShapeDtypeStruct((toks // 2, chans), bf16),
            jax.ShapeDtypeStruct((groups, chans, toks), bf16),
        ],
        [keep, other, taps, rates, residues, cot_own, cot_other],
        "mixer",
        12 * modes * toks * chans,
        [
            pltpu.VMEM((groups, toks + 8 * CHUNKS, lanes), f32),
            pltpu.VMEM((toks + 8 * CHUNKS, lanes), f32),
            pltpu.VMEM((groups, length + rim, CHUNKS, lanes), f32),
            pltpu.VMEM((groups, length, CHUNKS, lanes), f32),
            pltpu.VMEM((length, CHUNKS, lanes), f32),
            pltpu.VMEM((length, CHUNKS, lanes), f32),
            pltpu.VMEM((groups, length + rim, CHUNKS, lanes), f32),
            pltpu.VMEM((modes, CHUNKS, lanes), f32),
            pltpu.VMEM((modes, CHUNKS, lanes), f32),
        ],
    )


def back_kernel(outs, count, base, w_ref, *refs):
    grads, out_refs = refs[: len(count)], refs[len(count) + base :]
    groups, half, _ = grads[0].shape
    core = here()[3]
    sides = [pl.multiple_of((1 - core if other else core) * half, half) for other in count]
    for blocks, out in zip(outs, out_refs):
        width = out.shape[0] // len(blocks)
        for n, block in enumerate(blocks):
            rows = slice(n * width, (n + 1) * width)
            start = pl.multiple_of(block_at(*block) * width, width)
            total = refs[len(count)][rows] if base else None
            for g in range(groups):
                for ref, at in zip(grads, sides):
                    term = jnp.dot(
                        w_ref[g, pl.ds(start, width), pl.ds(at, half)],
                        ref[g],
                        preferred_element_type=f32,
                    )
                    total = term if total is None else total + term
            out[rows] = total.astype(out.dtype)


def back_project(outs, dtypes, w, own, other, width, base=None):
    grads = [(side, grad) for side, grad in enumerate((own, other)) if grad is not None]
    groups, half, toks = grads[0][1].shape
    extra = [] if base is None else [base]
    return small_call(
        functools.partial(back_kernel, outs, [side for side, _ in grads], len(extra)),
        [
            jax.ShapeDtypeStruct((width * len(blocks), toks), dtype)
            for blocks, dtype in zip(outs, dtypes)
        ],
        [w] + [grad for _, grad in grads] + extra,
        "back_project",
        2 * sum(len(blocks) for blocks in outs) * groups * width * half * toks * len(grads),
        (),
        16,
    )


def merge_kernel(two_ref, one_ref, got_ref, two_out, one_out):
    width = one_ref.shape[0]
    one_out[...] = (one_ref[...] + got_ref[:width].astype(f32)).astype(bf16)
    two_out[...] = (two_ref[...] + got_ref[width:].astype(f32)).astype(bf16)


def merge(two, one, got):
    shape = jax.ShapeDtypeStruct(one.shape, bf16)
    return small_call(merge_kernel, [shape, shape], [two, one, got], "merge")


def column_kernel(slot, own_ref, other_ref, first_ref, *out_refs):
    width, toks = own_ref.shape
    half = toks // 2
    total = (
        own_ref[...]
        + other_ref[(slot - 1) * width : slot * width].astype(f32)
        + first_ref[...].astype(f32)
    )
    z, _, _, core = here()
    side = (z >> 1) if slot == 2 else 1 - (z >> 1)
    low, high = total[:, :half], total[:, half:]
    send_low, send_high = out_refs[0], out_refs[1]

    @pl.when(side == 0)
    def _():
        send_low[...] = low.astype(bf16)
        send_high[...] = high.astype(bf16)

    @pl.when(side == 1)
    def _():
        send_low[...] = high.astype(bf16)
        send_high[...] = low.astype(bf16)

    if len(out_refs) == 3:
        inner = is_inner()
        out_refs[2][...] = jnp.where(inner, jnp.where(core == 0, low, high), 0.0)


def column(slot, own, other, first):
    width, toks = own.shape
    half = jax.ShapeDtypeStruct((width, toks // 2), bf16)
    kept = [jax.ShapeDtypeStruct((width, toks // 2), f32)] if slot == 1 else []
    return small_call(
        functools.partial(column_kernel, slot), [half, half] + kept, [own, other, first], "column"
    )


def finish_kernel(own_ref, a_ref, b_ref, c_ref, d_ref, out_ref):
    total = own_ref[...]
    for ref in (a_ref, b_ref, c_ref, d_ref):
        total = total + ref[...].astype(f32)
    out_ref[...] = total.T.astype(bf16)


def finish(own, received):
    shape = jax.ShapeDtypeStruct((own.shape[1], own.shape[0]), bf16)
    return small_call(finish_kernel, shape, [own] + received, "finish")


def pair_kernel(own_ref, other_ref, out_ref):
    half = own_ref.shape[1]
    core = here()[3]
    out_ref[:, pl.ds(pl.multiple_of(core * half, half), half)] = own_ref[...]
    out_ref[:, pl.ds(pl.multiple_of((1 - core) * half, half), half)] = other_ref[...]


def pair(own, other):
    shape = jax.ShapeDtypeStruct((own.shape[0], 2 * own.shape[1]), own.dtype)
    return small_call(pair_kernel, shape, [own, other], "pair")


def chip_plan(token_ids, embed, w_in, taps, rates, residues, cotangent):
    width = embed.shape[1]

    def swap(array):
        return lax.ppermute(array, BOTH, OTHER_CORE)

    def first_way(array):
        return lax.ppermute(array, BOTH, FIRST_WAY)

    def other_way(array):
        return lax.ppermute(array, BOTH, OTHER_WAY)

    own_ids = token_ids.reshape(1, -1)
    other_ids = swap(own_ids)
    cot_other = swap(cotangent)
    own_ids, table = fetch(own_ids, embed)
    embedded = embed_rows(own_ids, other_ids, table)
    embedded, cot_other = lax.optimization_barrier((embedded, cot_other))

    came = lax.ppermute(embedded, BOTH, GATHER_Z)
    more = lax.ppermute(embedded, BOTH, OUTER_Z_INNER_X)
    near_y = lax.ppermute(embedded, BOTH, INNER_Y)
    near_d = lax.ppermute(embedded, BOTH, INNER_XY)
    w = load(jnp.transpose(w_in, (1, 0, 2)))
    came, w = lax.optimization_barrier((came, w))
    first, other = first_way(came), other_way(came)
    sums = project(
        [embedded, near_y, near_d, came],
        [(0, 1, None), (1, 1, "y"), (2, 1, 2), (3, 2, None)],
        [(3, 1, None)],
        w,
        None,
    )
    more, sums = lax.optimization_barrier((more, sums))
    x_2 = lax.ppermute(more, BOTH, OUTER_X)
    d_2 = lax.ppermute(more, BOTH, OUTER_XY)
    first, other, more = lax.optimization_barrier((first, other, more))
    both = other_way(first)
    y_2 = lax.ppermute(more, BOTH, OUTER_Y)
    sums = project(
        [first, other, more],
        [(0, 2, 0), (1, 2, 1), (2, 1, "x")],
        [(0, 1, 0), (1, 1, 1), (2, 2, None)],
        w,
        sums,
    )
    sums = project([x_2, d_2], [], [(0, 2, "x"), (1, 2, 2)], w, sums)
    both, y_2, sums = lax.optimization_barrier((both, y_2, sums))
    inner, outer = [(0, 2, 2)], [(0, 1, 2), (1, 2, "y")]
    send = project([both, y_2], inner, outer, w, sums, "send")
    sums, send = lax.optimization_barrier((sums, send))
    keep = project([both, y_2], inner, outer, w, sums, "keep")
    got = swap(send)
    keep, got = lax.optimization_barrier((keep, got))
    mixed_own, mixed_send, grad_own = mixer(
        keep, got, jnp.transpose(taps, (1, 0, 2)), rates, residues, cotangent, cot_other
    )
    grad_other = swap(grad_own)
    mixed_other = swap(mixed_send)

    (part,) = back_project([[(1, 2), (2, 2)]], [f32], w, grad_own, None, width)
    grad_other, part = lax.optimization_barrier((grad_other, part))
    (across,) = back_project([[(1, 2), (2, 2)]], [bf16], w, None, grad_other, width, part)
    across = other_way(across)
    (other,) = back_project([[(1, 1), (2, 1)]], [bf16], w, grad_own, grad_other, width)
    other = other_way(other)
    first_2, first_1, own_2, own_1 = back_project(
        [[(2, 0)], [(1, 0)], [(2, None)], [(1, None)]], [f32] * 4, w, grad_own, grad_other, width
    )
    mixed = pair(mixed_own, mixed_other)
    across, mixed = lax.optimization_barrier((across, mixed))
    first_2, first_1 = merge(first_2, first_1, across)
    first_2, first_1 = first_way(first_2), first_way(first_1)
    sends = column(2, own_2, other, first_2)
    received = [lax.ppermute(a, BOTH, pairs) for a, pairs in zip(sends, SCATTER_Z[:2])]
    *sends, own = column(1, own_1, other, first_1)
    received += [lax.ppermute(a, BOTH, pairs) for a, pairs in zip(sends, SCATTER_Z[2:])]
    return (mixed, finish(own, received))


def solution(mesh):
    in_specs = (
        P("ctx"),
        P(None, "fsdp"),
        P("ctx", None, "fsdp"),
        P(None, None, "fsdp"),
        P(None, "fsdp"),
        P(None, "fsdp"),
        P("ctx", "fsdp"),
    )
    out_specs = (P("ctx", "fsdp"), P("ctx", "fsdp"))
    chips = mesh.shape["fsdp"] == 16 and mesh.shape["ctx"] == 2
    return jax.shard_map(
        chip_plan if chips else general_plan,
        mesh=mesh,
        in_specs=in_specs,
        out_specs=out_specs,
        check_vma=False,
    )
```

```python
import functools

import jax
import jax.numpy as jnp
from jax import lax
from jax.experimental import pallas as pl
from jax.experimental.pallas import tpu as pltpu
from jax.sharding import PartitionSpec as P

BOTH = ("fsdp", "ctx")
CHUNKS = 8
f32 = jnp.float32
bf16 = jnp.bfloat16


def from_behind(shard, axis, by):
    count = lax.axis_size(axis)
    pairs = [(i, i + by) for i in range(count) if 0 <= i + by < count]
    return lax.ppermute(shard, axis, pairs)


def pair_combine(earlier, later):
    return (earlier[0] * later[0], later[0] * earlier[1] + later[1])


def modal_states(drive, step_decay):
    tok_count = drive.shape[0]
    factors = jnp.broadcast_to(step_decay[None], (tok_count,) + step_decay.shape)
    inputs = jnp.broadcast_to(drive[:, None, :], factors.shape)
    return lax.associative_scan(pair_combine, (factors, inputs), axis=0)[1]


def short_filter(extended, taps, tok_count):
    rim_width = taps.shape[0] - 1
    filtered = taps[0] * extended[rim_width : rim_width + tok_count]
    for shift_lag in range(1, rim_width + 1):
        filtered = (
            filtered
            + taps[shift_lag] * extended[rim_width - shift_lag : rim_width - shift_lag + tok_count]
        )
    return filtered


def short_adjoint(extended, taps, tok_count):
    rim_width = taps.shape[0] - 1
    result = taps[0] * extended[:tok_count]
    for shift_lag in range(1, rim_width + 1):
        result = result + taps[shift_lag] * extended[shift_lag : shift_lag + tok_count]
    return result


def carry(block_decay, leaving, by):
    def relay_step(turn_index, incoming):
        return from_behind(block_decay * incoming + leaving, "ctx", by)

    return lax.fori_loop(0, lax.axis_size("ctx") - 1, relay_step, jnp.zeros_like(leaving))


def general_plan(token_ids, embed, w_in, taps, rates, residues, cotangent):
    tok_count = token_ids.shape[0]
    vocab_size = embed.shape[0]
    chan_width = embed.shape[1]
    rim_width = taps.shape[0] - 1
    onehot = (
        token_ids[:, None] == lax.broadcasted_iota(jnp.int32, (tok_count, vocab_size), 1)
    ).astype(bf16)
    embedded = jnp.dot(onehot, embed, preferred_element_type=f32).astype(bf16)
    features = lax.all_gather(embedded, "fsdp", axis=1, tiled=True)
    feat_width = features.shape[1]
    whole_w = lax.all_gather(w_in, "ctx", axis=0, tiled=True).reshape(feat_width, 3 * chan_width)
    projected = jnp.dot(features, whole_w, preferred_element_type=f32)
    stored = lax.optimization_barrier(projected.astype(bf16).reshape(tok_count, 3, chan_width))
    before = from_behind(stored[tok_count - rim_width :], "ctx", 1)
    extended = jnp.concatenate([before, stored], axis=0).astype(f32)
    filtered = short_filter(extended, taps, tok_count)
    query_part = filtered[:, 0]
    key_part = filtered[:, 1]
    value_part = filtered[:, 2]
    drive = key_part * value_part
    step_decay = jnp.exp(-rates)
    block_decay = jnp.exp(-rates * tok_count)
    local_states = modal_states(drive, step_decay)
    entering = carry(block_decay, local_states[tok_count - 1], 1)
    offsets = lax.broadcasted_iota(f32, (tok_count, 1, 1), 0)
    states = local_states + jnp.exp(-rates[None] * (offsets + 1.0)) * entering[None]
    long_out = jnp.sum(residues[None] * states, axis=1)
    mixed = (query_part * long_out).astype(bf16)
    incoming = cotangent.astype(f32)
    grad_long = incoming * query_part
    grad_query = incoming * long_out
    back_states = jnp.flip(modal_states(jnp.flip(grad_long, 0), step_decay), 0)
    beyond = carry(block_decay, back_states[0], -1)
    adjoint = back_states + jnp.exp(-rates[None] * (tok_count - offsets)) * beyond[None]
    grad_drive = jnp.sum(residues[None] * adjoint, axis=1)
    grad_filtered = jnp.stack([grad_query, grad_drive * value_part, grad_drive * key_part], axis=1)
    after = from_behind(grad_filtered[:rim_width], "ctx", -1)
    ext_grad = jnp.concatenate([grad_filtered, after], axis=0)
    grad_stored = short_adjoint(ext_grad, taps, tok_count).astype(bf16)
    grad_rows = grad_stored.reshape(tok_count, 3 * chan_width)
    own_rows = lax.psum_scatter(
        lax.dot_general(whole_w, grad_rows, (((1,), (1,)), ((), ())), preferred_element_type=f32),
        "fsdp",
        scatter_dimension=0,
        tiled=True,
    )
    return (mixed, own_rows.T.astype(bf16))


def device_at(z, y, x, core):
    return ((z * 2 + y) * 2 + x) * 2 + core


def everywhere(move):
    pairs = []
    for z in range(4):
        for y in range(2):
            for x in range(2):
                for core in range(2):
                    pairs.append((device_at(z, y, x, core), device_at(*move(z, y, x, core))))
    return pairs


OTHER_CORE = everywhere(lambda z, y, x, core: (z, y, x, 1 - core))


def along_z(moves):
    pairs = []
    for core in range(2):
        for (place, other), (to_place, to_other) in moves:
            z, to_z = (place, to_place) if core == 0 else (3 - place, 3 - to_place)
            for y in range(2):
                for x in range(2):
                    pairs.append(
                        (
                            device_at(z, y, x, core ^ other),
                            device_at(to_z, y, x, core ^ to_other),
                        )
                    )
    return pairs


FIRST_WAY = everywhere(lambda z, y, x, core: (z, y, 1 - x, core) if core == 0 else (z, 1 - y, x, core))
OTHER_WAY = everywhere(lambda z, y, x, core: (z, 1 - y, x, core) if core == 0 else (z, y, 1 - x, core))
def some_move(move, inner):
    def target(z, y, x, core):
        return move(z, y, x, core) if (core == z >> 1) == inner else (z, y, x, core)

    return everywhere(target)


INNER_Y = some_move(lambda z, y, x, core: (z, 1 - y, x, core), True)
INNER_XY = some_move(lambda z, y, x, core: (z, 1 - y, 1 - x, core), True)
OUTER_X = some_move(lambda z, y, x, core: (z, y, 1 - x, core), False)
OUTER_Y = some_move(lambda z, y, x, core: (z, 1 - y, x, core), False)
OUTER_XY = some_move(lambda z, y, x, core: (z, 1 - y, 1 - x, core), False)
GATHER_Z = along_z([((0, 0), (1, 0)), ((1, 0), (0, 0)), ((0, 1), (2, 0)), ((1, 1), (3, 0))])
OUTER_Z_INNER_X = along_z([((1, 1), (2, 0)), ((0, 1), (3, 0))]) + [
    pair
    for pair in everywhere(lambda z, y, x, core: (z, y, 1 - x, core))
    if (pair[0] & 1) == pair[0] >> 4
]
SCATTER_Z = (
    along_z([((0, 0), (1, 0)), ((1, 0), (0, 0)), ((2, 0), (1, 1)), ((3, 0), (0, 1))]),
    along_z([((0, 0), (1, 1)), ((1, 0), (0, 1)), ((2, 0), (1, 0)), ((3, 0), (0, 0))]),
    along_z([((0, 0), (0, 1)), ((1, 0), (1, 1)), ((2, 0), (0, 0)), ((3, 0), (1, 0))]),
    along_z([((2, 0), (0, 1)), ((3, 0), (1, 1))]),
)

IN_VMEM = pl.BlockSpec(memory_space=pltpu.VMEM)


def small_call(kernel, out_shape, operands, name, flops=0, scratch=(), limit=8):
    sizes = [o.size * o.dtype.itemsize for o in operands]
    return pl.pallas_call(
        kernel,
        in_specs=[IN_VMEM] * len(operands),
        out_specs=jax.tree.map(lambda _: IN_VMEM, out_shape),
        out_shape=out_shape,
        scratch_shapes=list(scratch),
        compiler_params=pltpu.CompilerParams(vmem_limit_bytes=limit * 1024 * 1024),
        cost_estimate=pl.CostEstimate(
            flops=flops // 64, bytes_accessed=sum(sizes) // 64, transcendentals=0
        ),
        name=name,
    )(*operands)


def here():
    spot = lax.axis_index("fsdp")
    return spot >> 2, (spot >> 1) & 1, spot & 1, lax.axis_index("ctx")


def is_inner():
    z, _, _, core = here()
    return core == (z >> 1)


def block_at(slot, way):
    z, y, x, core = here()
    along = (z & 1) if slot == 1 else 1 - (z & 1)
    far = {None: (0, 0), 0: (core, 1 - core), 1: (1 - core, core), 2: (1, 1), "x": (0, 1), "y": (1, 0)}
    far_y, far_x = far[way]
    return along * 4 + (y ^ far_y) * 2 + (x ^ far_x)


def embed_kernel(own_ref, other_ref, table_ref, out_ref):
    vocab = table_ref.shape[0]
    half = own_ref.shape[1]
    core = here()[3]
    for ref, side in ((own_ref, core), (other_ref, 1 - core)):
        across = jnp.broadcast_to(ref[...].astype(f32), (half, half)).T
        lane = lax.broadcasted_iota(jnp.int32, (half, half), 1).astype(f32)
        picks = [(across == lane + float(first)).astype(f32) for first in range(0, vocab, half)]
        rows = jnp.dot(
            jnp.concatenate(picks, axis=1).astype(bf16), table_ref[...], preferred_element_type=f32
        )
        out_ref[pl.ds(pl.multiple_of(side * half, half), half), :] = rows.astype(bf16)


def embed_rows(own_ids, other_ids, table):
    toks, width = 2 * own_ids.shape[1], table.shape[1]
    return small_call(
        embed_kernel,
        jax.ShapeDtypeStruct((toks, width), bf16),
        [own_ids, other_ids, table],
        "embed_rows",
        2 * toks * table.shape[0] * width,
    )


def fetch_kernel(ids_ref, table_ref, ids_out, table_out, sems):
    copies = [
        pltpu.make_async_copy(ids_ref, ids_out, sems.at[0]),
        pltpu.make_async_copy(table_ref, table_out, sems.at[1]),
    ]
    for copy in copies:
        copy.start()
    for copy in copies:
        copy.wait()


def in_hbm(array):
    return pltpu.with_memory_space_constraint(array, pltpu.HBM)


def in_vmem(array):
    return pltpu.with_memory_space_constraint(array, pltpu.VMEM)


def fetch(ids, table):
    out = pl.pallas_call(
        fetch_kernel,
        in_specs=[pl.BlockSpec(memory_space=pltpu.HBM)] * 2,
        out_specs=[IN_VMEM] * 2,
        out_shape=[pltpu.VMEM(ids.shape, ids.dtype), pltpu.VMEM(table.shape, bf16)],
        scratch_shapes=[pltpu.SemaphoreType.DMA((2,))],
        compiler_params=pltpu.CompilerParams(vmem_limit_bytes=2 * 1024 * 1024),
        cost_estimate=pl.CostEstimate(
            flops=0, bytes_accessed=4 * table.size, transcendentals=0
        ),
        name="fetch",
    )(in_hbm(ids), in_hbm(table))
    return [in_vmem(array) for array in out]


def load_kernel(w_ref, out_ref, sem):
    copy = pltpu.make_async_copy(w_ref, out_ref, sem)
    copy.start()
    copy.wait()


def load(w):
    out = pl.pallas_call(
        load_kernel,
        in_specs=[pl.BlockSpec(memory_space=pltpu.HBM)],
        out_specs=IN_VMEM,
        out_shape=pltpu.VMEM(w.shape, w.dtype),
        scratch_shapes=[pltpu.SemaphoreType.DMA],
        compiler_params=pltpu.CompilerParams(vmem_limit_bytes=2 * 1024 * 1024),
        cost_estimate=pl.CostEstimate(
            flops=0, bytes_accessed=2 * w.size * w.dtype.itemsize, transcendentals=0
        ),
        name="load",
    )(in_hbm(w))
    return in_vmem(out)


def project_kernel(inner, outer, count, has_base, part, w_ref, *refs):
    acts = refs[:count]
    groups, _, chans = w_ref.shape
    width = acts[0].shape[1]
    out_ref = refs[-1]
    if part is None:
        some = slice(None)
    else:
        half = chans // 2
        core = here()[3]
        side = core if part == "keep" else 1 - core
        some = pl.ds(pl.multiple_of(side * half, half), half)

    def add(entries):
        spans = [
            pl.ds(pl.multiple_of(block_at(slot, way) * width, width), width)
            for _, slot, way in entries
        ]
        for g in range(groups):
            total = refs[count][g, :, some] if has_base else None
            for (which, _, _), span in zip(entries, spans):
                term = jnp.dot(acts[which][...], w_ref[g, span, some], preferred_element_type=f32)
                total = term if total is None else total + term
            out_ref[g] = total

    pl.when(is_inner())(lambda: add(inner))
    pl.when(jnp.logical_not(is_inner()))(lambda: add(outer))


def project(acts, inner, outer, w, base, part=None):
    groups, _, chans = w.shape
    toks, width = acts[0].shape
    if part is not None:
        chans //= 2
    return small_call(
        functools.partial(project_kernel, inner, outer, len(acts), base is not None, part),
        jax.ShapeDtypeStruct((groups, toks, chans), f32),
        [w] + list(acts) + ([] if base is None else [base]),
        "project",
        2 * max(len(inner), len(outer)) * groups * width * chans * toks,
        (),
        16,
    )


def shifted(values, by):
    place = lax.broadcasted_iota(jnp.int32, values.shape, 0)
    moved = pltpu.roll(values, by % CHUNKS, 0)
    inside = place >= by if by > 0 else place < CHUNKS + by
    return jnp.where(inside, moved, 0.0)


def mixer_kernel(
    keep_ref,
    other_ref,
    taps_ref,
    rates_ref,
    residues_ref,
    cot_own_ref,
    cot_other_ref,
    mixed_own_ref,
    mixed_send_ref,
    grad_ref,
    flat,
    flat_cot,
    ext,
    filt,
    drive,
    back,
    grad_ext,
    decays,
    residues,
):
    groups, toks, chans = keep_ref.shape
    half = toks // 2
    modes = rates_ref.shape[0]
    short = taps_ref.shape[1]
    rim = short - 1
    length = toks // CHUNKS
    apart = flat.shape[1] // CHUNKS
    lanes = flat.shape[-1]
    wide = (CHUNKS, lanes)
    _, _, _, core = here()

    def spread(ref, at, values):
        for s in range(CHUNKS):
            ref[(*at, slice(s * apart, s * apart + length))] = values[s * length : (s + 1) * length]

    def row(array, at):
        return jnp.broadcast_to(array[at : at + 1, :], wide)

    def column(c, _):
        some = pl.ds(pl.multiple_of(c * lanes, lanes), lanes)
        whole = pl.ds(pl.multiple_of(core * chans + c * lanes, lanes), lanes)
        for g in range(groups):
            spread(flat, (g,), (keep_ref[g, :, some] + other_ref[g, :, some]).astype(bf16).astype(f32))
        for s in range(CHUNKS // 2):
            rows = slice(s * length, (s + 1) * length)
            own_at = pl.multiple_of((core * (CHUNKS // 2) + s) * apart, 8)
            other_at = pl.multiple_of(((1 - core) * (CHUNKS // 2) + s) * apart, 8)
            flat_cot[pl.ds(own_at, length)] = cot_own_ref[rows, whole].astype(f32)
            flat_cot[pl.ds(other_at, length)] = cot_other_ref[rows, whole].astype(f32)

        for g in range(groups):
            for k in range(length):
                ext[g, rim + k] = flat[g, pl.ds(k, CHUNKS, stride=apart), :]
            for k in range(rim):
                ext[g, k] = shifted(ext[g, length + k], 1)

        taps = [taps_ref[g, :, whole] for g in range(groups)]
        tap = [[row(taps[g], j) for g in range(groups)] for j in range(short)]

        def filter_step(k, _):
            parts = []
            for g in range(groups):
                total = tap[0][g] * ext[g, k + rim]
                for j in range(1, short):
                    total = total + tap[j][g] * ext[g, k + rim - j]
                parts.append(total)
                filt[g, k] = total
            drive[k] = parts[1] * parts[2]
            back[k] = parts[0] * flat_cot[pl.ds(k, CHUNKS, stride=apart), :]
            return _

        lax.fori_loop(0, length, filter_step, 0, unroll=16)

        rates = rates_ref[:, whole]
        decay_rows = jnp.exp(-rates)
        jump_rows = [jnp.exp(-rates * (length * n)) for n in (1, 2, 4)]
        residue_rows = residues_ref[:, whole]
        for m in range(modes):
            decays[m] = row(decay_rows, m)
            residues[m] = row(residue_rows, m)

        def long_filter(source, forward, finish):
            decay = [decays[m] for m in range(modes)]

            def place(k):
                return k if forward else length - 1 - k

            def end_step(k, states):
                value = source[place(k)]
                return tuple(decay[m] * states[m] + value for m in range(modes))

            zero = jnp.zeros(wide, f32)
            ends = lax.fori_loop(0, length, end_step, (zero,) * modes, unroll=32)
            entering = []
            sign = 1 if forward else -1
            for m in range(modes):
                carried = ends[m]
                for jump, by in zip(jump_rows, (1, 2, 4)):
                    carried = carried + row(jump, m) * shifted(carried, sign * by)
                entering.append(shifted(carried, sign))

            def out_step(k, states):
                value = source[place(k)]
                states = tuple(decay[m] * states[m] + value for m in range(modes))
                terms = [residues[m] * states[m] for m in range(modes)]
                while len(terms) > 1:
                    terms = [a + b for a, b in zip(terms[::2], terms[1::2])]
                finish(place(k), terms[0])
                return states

            lax.fori_loop(0, length, out_step, tuple(entering), unroll=16)

        def finish_forward(k, total):
            flat[0, pl.ds(k, CHUNKS, stride=apart), :] = filt[0, k] * total
            grad_ext[0, k] = flat_cot[pl.ds(k, CHUNKS, stride=apart), :] * total

        def finish_backward(k, total):
            grad_ext[1, k] = total * filt[2, k]
            grad_ext[2, k] = total * filt[1, k]

        long_filter(drive, True, finish_forward)
        for s in range(CHUNKS // 2):
            rows = slice(s * length, (s + 1) * length)
            own_at = pl.multiple_of((core * (CHUNKS // 2) + s) * apart, 8)
            other_at = pl.multiple_of(((1 - core) * (CHUNKS // 2) + s) * apart, 8)
            mixed_own_ref[rows, some] = flat[0, pl.ds(own_at, length)].astype(bf16)
            mixed_send_ref[rows, some] = flat[0, pl.ds(other_at, length)].astype(bf16)
        long_filter(back, False, finish_backward)

        for g in range(groups):
            for k in range(rim):
                grad_ext[g, length + k] = shifted(grad_ext[g, k], -1)

        def adjoint_step(k, _):
            for g in range(groups):
                total = tap[0][g] * grad_ext[g, k]
                for j in range(1, short):
                    total = total + tap[j][g] * grad_ext[g, k + j]
                flat[g, pl.ds(k, CHUNKS, stride=apart), :] = total
            return _

        lax.fori_loop(0, length, adjoint_step, 0, unroll=16)
        for g in range(groups):
            chunks = [flat[g, s * apart : s * apart + length].astype(bf16) for s in range(CHUNKS)]
            grad_ref[g, some, :] = jnp.concatenate(chunks, axis=0).T
        return _

    lax.fori_loop(0, chans // lanes, column, 0)


def mixer(keep, other, taps, rates, residues, cot_own, cot_other):
    groups, toks, chans = keep.shape
    modes = rates.shape[0]
    rim = taps.shape[1] - 1
    lanes = 128
    length = toks // CHUNKS
    return small_call(
        mixer_kernel,
        [
            jax.ShapeDtypeStruct((toks // 2, chans), bf16),
            jax.ShapeDtypeStruct((toks // 2, chans), bf16),
            jax.ShapeDtypeStruct((groups, chans, toks), bf16),
        ],
        [keep, other, taps, rates, residues, cot_own, cot_other],
        "mixer",
        12 * modes * toks * chans,
        [
            pltpu.VMEM((groups, toks + 8 * CHUNKS, lanes), f32),
            pltpu.VMEM((toks + 8 * CHUNKS, lanes), f32),
            pltpu.VMEM((groups, length + rim, CHUNKS, lanes), f32),
            pltpu.VMEM((groups, length, CHUNKS, lanes), f32),
            pltpu.VMEM((length, CHUNKS, lanes), f32),
            pltpu.VMEM((length, CHUNKS, lanes), f32),
            pltpu.VMEM((groups, length + rim, CHUNKS, lanes), f32),
            pltpu.VMEM((modes, CHUNKS, lanes), f32),
            pltpu.VMEM((modes, CHUNKS, lanes), f32),
        ],
    )


def back_kernel(outs, count, base, w_ref, *refs):
    grads, out_refs = refs[: len(count)], refs[len(count) + base :]
    groups, half, _ = grads[0].shape
    core = here()[3]
    sides = [pl.multiple_of((1 - core if other else core) * half, half) for other in count]
    for blocks, out in zip(outs, out_refs):
        width = out.shape[0] // len(blocks)
        for n, block in enumerate(blocks):
            rows = slice(n * width, (n + 1) * width)
            start = pl.multiple_of(block_at(*block) * width, width)
            total = refs[len(count)][rows] if base else None
            for g in range(groups):
                for ref, at in zip(grads, sides):
                    term = jnp.dot(
                        w_ref[g, pl.ds(start, width), pl.ds(at, half)],
                        ref[g],
                        preferred_element_type=f32,
                    )
                    total = term if total is None else total + term
            out[rows] = total.astype(out.dtype)


def back_project(outs, dtypes, w, own, other, width, base=None):
    grads = [(side, grad) for side, grad in enumerate((own, other)) if grad is not None]
    groups, half, toks = grads[0][1].shape
    extra = [] if base is None else [base]
    return small_call(
        functools.partial(back_kernel, outs, [side for side, _ in grads], len(extra)),
        [
            jax.ShapeDtypeStruct((width * len(blocks), toks), dtype)
            for blocks, dtype in zip(outs, dtypes)
        ],
        [w] + [grad for _, grad in grads] + extra,
        "back_project",
        2 * sum(len(blocks) for blocks in outs) * groups * width * half * toks * len(grads),
        (),
        16,
    )


def merge_kernel(two_ref, one_ref, got_ref, two_out, one_out):
    width = one_ref.shape[0]
    one_out[...] = (one_ref[...] + got_ref[:width].astype(f32)).astype(bf16)
    two_out[...] = (two_ref[...] + got_ref[width:].astype(f32)).astype(bf16)


def merge(two, one, got):
    shape = jax.ShapeDtypeStruct(one.shape, bf16)
    return small_call(merge_kernel, [shape, shape], [two, one, got], "merge")


def column_kernel(slot, own_ref, other_ref, first_ref, *out_refs):
    width, toks = own_ref.shape
    half = toks // 2
    total = (
        own_ref[...]
        + other_ref[(slot - 1) * width : slot * width].astype(f32)
        + first_ref[...].astype(f32)
    )
    z, _, _, core = here()
    side = (z >> 1) if slot == 2 else 1 - (z >> 1)
    low, high = total[:, :half], total[:, half:]
    send_low, send_high = out_refs[0], out_refs[1]

    @pl.when(side == 0)
    def _():
        send_low[...] = low.astype(bf16)
        send_high[...] = high.astype(bf16)

    @pl.when(side == 1)
    def _():
        send_low[...] = high.astype(bf16)
        send_high[...] = low.astype(bf16)

    if len(out_refs) == 3:
        inner = is_inner()
        out_refs[2][...] = jnp.where(inner, jnp.where(core == 0, low, high), 0.0)


def column(slot, own, other, first):
    width, toks = own.shape
    half = jax.ShapeDtypeStruct((width, toks // 2), bf16)
    kept = [jax.ShapeDtypeStruct((width, toks // 2), f32)] if slot == 1 else []
    return small_call(
        functools.partial(column_kernel, slot), [half, half] + kept, [own, other, first], "column"
    )


def finish_kernel(own_ref, a_ref, b_ref, c_ref, d_ref, out_ref):
    total = own_ref[...]
    for ref in (a_ref, b_ref, c_ref, d_ref):
        total = total + ref[...].astype(f32)
    out_ref[...] = total.T.astype(bf16)


def finish(own, received):
    shape = jax.ShapeDtypeStruct((own.shape[1], own.shape[0]), bf16)
    return small_call(finish_kernel, shape, [own] + received, "finish")


def pair_kernel(own_ref, other_ref, out_ref):
    half = own_ref.shape[1]
    core = here()[3]
    out_ref[:, pl.ds(pl.multiple_of(core * half, half), half)] = own_ref[...]
    out_ref[:, pl.ds(pl.multiple_of((1 - core) * half, half), half)] = other_ref[...]


def pair(own, other):
    shape = jax.ShapeDtypeStruct((own.shape[0], 2 * own.shape[1]), own.dtype)
    return small_call(pair_kernel, shape, [own, other], "pair")


def chip_plan(token_ids, embed, w_in, taps, rates, residues, cotangent):
    width = embed.shape[1]

    def swap(array):
        return lax.ppermute(array, BOTH, OTHER_CORE)

    def first_way(array):
        return lax.ppermute(array, BOTH, FIRST_WAY)

    def other_way(array):
        return lax.ppermute(array, BOTH, OTHER_WAY)

    own_ids = token_ids.reshape(1, -1)
    other_ids = swap(own_ids)
    cot_other = swap(cotangent)
    own_ids, table = fetch(own_ids, embed)
    embedded = embed_rows(own_ids, other_ids, table)
    embedded, cot_other = lax.optimization_barrier((embedded, cot_other))

    came = lax.ppermute(embedded, BOTH, GATHER_Z)
    more = lax.ppermute(embedded, BOTH, OUTER_Z_INNER_X)
    near_y = lax.ppermute(embedded, BOTH, INNER_Y)
    near_d = lax.ppermute(embedded, BOTH, INNER_XY)
    w = load(jnp.transpose(w_in, (1, 0, 2)))
    came, w = lax.optimization_barrier((came, w))
    first, other = first_way(came), other_way(came)
    sums = project(
        [embedded, near_y, near_d, came],
        [(0, 1, None), (1, 1, "y"), (2, 1, 2), (3, 2, None)],
        [(3, 1, None)],
        w,
        None,
    )
    more, sums = lax.optimization_barrier((more, sums))
    x_2 = lax.ppermute(more, BOTH, OUTER_X)
    d_2 = lax.ppermute(more, BOTH, OUTER_XY)
    first, other, more = lax.optimization_barrier((first, other, more))
    both = other_way(first)
    y_2 = lax.ppermute(more, BOTH, OUTER_Y)
    sums = project(
        [first, other, more],
        [(0, 2, 0), (1, 2, 1), (2, 1, "x")],
        [(0, 1, 0), (1, 1, 1), (2, 2, None)],
        w,
        sums,
    )
    sums = project([x_2], [], [(0, 2, "x")], w, sums)
    both, y_2, d_2, sums = lax.optimization_barrier((both, y_2, d_2, sums))
    acts = [both, y_2, d_2]
    inner, outer = [(0, 2, 2)], [(0, 1, 2), (1, 2, "y"), (2, 2, 2)]
    send = project(acts, inner, outer, w, sums, "send")
    sums, send = lax.optimization_barrier((sums, send))
    keep = project(acts, inner, outer, w, sums, "keep")
    got = swap(send)
    keep, got = lax.optimization_barrier((keep, got))
    mixed_own, mixed_send, grad_own = mixer(
        keep, got, jnp.transpose(taps, (1, 0, 2)), rates, residues, cotangent, cot_other
    )
    grad_other = swap(grad_own)
    mixed_other = swap(mixed_send)

    (part,) = back_project([[(1, 2), (2, 2)]], [f32], w, grad_own, None, width)
    grad_other, part = lax.optimization_barrier((grad_other, part))
    (across,) = back_project([[(1, 2), (2, 2)]], [bf16], w, None, grad_other, width, part)
    across = other_way(across)
    (other,) = back_project([[(1, 1), (2, 1)]], [bf16], w, grad_own, grad_other, width)
    other = other_way(other)
    first_2, first_1, own_2, own_1 = back_project(
        [[(2, 0)], [(1, 0)], [(2, None)], [(1, None)]], [f32] * 4, w, grad_own, grad_other, width
    )
    mixed = pair(mixed_own, mixed_other)
    across, mixed = lax.optimization_barrier((across, mixed))
    first_2, first_1 = merge(first_2, first_1, across)
    first_2, first_1 = first_way(first_2), first_way(first_1)
    sends = column(2, own_2, other, first_2)
    received = [lax.ppermute(a, BOTH, pairs) for a, pairs in zip(sends, SCATTER_Z[:2])]
    *sends, own = column(1, own_1, other, first_1)
    received += [lax.ppermute(a, BOTH, pairs) for a, pairs in zip(sends, SCATTER_Z[2:])]
    return (mixed, finish(own, received))


def solution(mesh):
    in_specs = (
        P("ctx"),
        P(None, "fsdp"),
        P("ctx", None, "fsdp"),
        P(None, None, "fsdp"),
        P(None, "fsdp"),
        P(None, "fsdp"),
        P("ctx", "fsdp"),
    )
    out_specs = (P("ctx", "fsdp"), P("ctx", "fsdp"))
    chips = mesh.shape["fsdp"] == 16 and mesh.shape["ctx"] == 2
    return jax.shard_map(
        chip_plan if chips else general_plan,
        mesh=mesh,
        in_specs=in_specs,
        out_specs=out_specs,
        check_vma=False,
    )
```

```python
import functools

import jax
import jax.numpy as jnp
from jax import lax
from jax.experimental import pallas as pl
from jax.experimental.pallas import tpu as pltpu
from jax.sharding import PartitionSpec as P

BOTH = ("fsdp", "ctx")
CHUNKS = 8
f32 = jnp.float32
bf16 = jnp.bfloat16


def from_behind(shard, axis, by):
    count = lax.axis_size(axis)
    pairs = [(i, i + by) for i in range(count) if 0 <= i + by < count]
    return lax.ppermute(shard, axis, pairs)


def pair_combine(earlier, later):
    return (earlier[0] * later[0], later[0] * earlier[1] + later[1])


def modal_states(drive, step_decay):
    tok_count = drive.shape[0]
    factors = jnp.broadcast_to(step_decay[None], (tok_count,) + step_decay.shape)
    inputs = jnp.broadcast_to(drive[:, None, :], factors.shape)
    return lax.associative_scan(pair_combine, (factors, inputs), axis=0)[1]


def short_filter(extended, taps, tok_count):
    rim_width = taps.shape[0] - 1
    filtered = taps[0] * extended[rim_width : rim_width + tok_count]
    for shift_lag in range(1, rim_width + 1):
        filtered = (
            filtered
            + taps[shift_lag] * extended[rim_width - shift_lag : rim_width - shift_lag + tok_count]
        )
    return filtered


def short_adjoint(extended, taps, tok_count):
    rim_width = taps.shape[0] - 1
    result = taps[0] * extended[:tok_count]
    for shift_lag in range(1, rim_width + 1):
        result = result + taps[shift_lag] * extended[shift_lag : shift_lag + tok_count]
    return result


def carry(block_decay, leaving, by):
    def relay_step(turn_index, incoming):
        return from_behind(block_decay * incoming + leaving, "ctx", by)

    return lax.fori_loop(0, lax.axis_size("ctx") - 1, relay_step, jnp.zeros_like(leaving))


def general_plan(token_ids, embed, w_in, taps, rates, residues, cotangent):
    tok_count = token_ids.shape[0]
    vocab_size = embed.shape[0]
    chan_width = embed.shape[1]
    rim_width = taps.shape[0] - 1
    onehot = (
        token_ids[:, None] == lax.broadcasted_iota(jnp.int32, (tok_count, vocab_size), 1)
    ).astype(bf16)
    embedded = jnp.dot(onehot, embed, preferred_element_type=f32).astype(bf16)
    features = lax.all_gather(embedded, "fsdp", axis=1, tiled=True)
    feat_width = features.shape[1]
    whole_w = lax.all_gather(w_in, "ctx", axis=0, tiled=True).reshape(feat_width, 3 * chan_width)
    projected = jnp.dot(features, whole_w, preferred_element_type=f32)
    stored = lax.optimization_barrier(projected.astype(bf16).reshape(tok_count, 3, chan_width))
    before = from_behind(stored[tok_count - rim_width :], "ctx", 1)
    extended = jnp.concatenate([before, stored], axis=0).astype(f32)
    filtered = short_filter(extended, taps, tok_count)
    query_part = filtered[:, 0]
    key_part = filtered[:, 1]
    value_part = filtered[:, 2]
    drive = key_part * value_part
    step_decay = jnp.exp(-rates)
    block_decay = jnp.exp(-rates * tok_count)
    local_states = modal_states(drive, step_decay)
    entering = carry(block_decay, local_states[tok_count - 1], 1)
    offsets = lax.broadcasted_iota(f32, (tok_count, 1, 1), 0)
    states = local_states + jnp.exp(-rates[None] * (offsets + 1.0)) * entering[None]
    long_out = jnp.sum(residues[None] * states, axis=1)
    mixed = (query_part * long_out).astype(bf16)
    incoming = cotangent.astype(f32)
    grad_long = incoming * query_part
    grad_query = incoming * long_out
    back_states = jnp.flip(modal_states(jnp.flip(grad_long, 0), step_decay), 0)
    beyond = carry(block_decay, back_states[0], -1)
    adjoint = back_states + jnp.exp(-rates[None] * (tok_count - offsets)) * beyond[None]
    grad_drive = jnp.sum(residues[None] * adjoint, axis=1)
    grad_filtered = jnp.stack([grad_query, grad_drive * value_part, grad_drive * key_part], axis=1)
    after = from_behind(grad_filtered[:rim_width], "ctx", -1)
    ext_grad = jnp.concatenate([grad_filtered, after], axis=0)
    grad_stored = short_adjoint(ext_grad, taps, tok_count).astype(bf16)
    grad_rows = grad_stored.reshape(tok_count, 3 * chan_width)
    own_rows = lax.psum_scatter(
        lax.dot_general(whole_w, grad_rows, (((1,), (1,)), ((), ())), preferred_element_type=f32),
        "fsdp",
        scatter_dimension=0,
        tiled=True,
    )
    return (mixed, own_rows.T.astype(bf16))


def device_at(z, y, x, core):
    return ((z * 2 + y) * 2 + x) * 2 + core


def everywhere(move):
    pairs = []
    for z in range(4):
        for y in range(2):
            for x in range(2):
                for core in range(2):
                    pairs.append((device_at(z, y, x, core), device_at(*move(z, y, x, core))))
    return pairs


OTHER_CORE = everywhere(lambda z, y, x, core: (z, y, x, 1 - core))


def along_z(moves):
    pairs = []
    for core in range(2):
        for (place, other), (to_place, to_other) in moves:
            z, to_z = (place, to_place) if core == 0 else (3 - place, 3 - to_place)
            for y in range(2):
                for x in range(2):
                    pairs.append(
                        (
                            device_at(z, y, x, core ^ other),
                            device_at(to_z, y, x, core ^ to_other),
                        )
                    )
    return pairs


FIRST_WAY = everywhere(lambda z, y, x, core: (z, y, 1 - x, core) if core == 0 else (z, 1 - y, x, core))
OTHER_WAY = everywhere(lambda z, y, x, core: (z, 1 - y, x, core) if core == 0 else (z, y, 1 - x, core))
def some_move(move, inner):
    def target(z, y, x, core):
        return move(z, y, x, core) if (core == z >> 1) == inner else (z, y, x, core)

    return everywhere(target)


INNER_Y = some_move(lambda z, y, x, core: (z, 1 - y, x, core), True)
INNER_XY = some_move(lambda z, y, x, core: (z, 1 - y, 1 - x, core), True)
OUTER_X = some_move(lambda z, y, x, core: (z, y, 1 - x, core), False)
OUTER_Y = some_move(lambda z, y, x, core: (z, 1 - y, x, core), False)
OUTER_XY = some_move(lambda z, y, x, core: (z, 1 - y, 1 - x, core), False)
GATHER_Z = along_z([((0, 0), (1, 0)), ((1, 0), (0, 0)), ((0, 1), (2, 0)), ((1, 1), (3, 0))])
OUTER_Z_INNER_X = along_z([((1, 1), (2, 0)), ((0, 1), (3, 0))]) + [
    pair
    for pair in everywhere(lambda z, y, x, core: (z, y, 1 - x, core))
    if (pair[0] & 1) == pair[0] >> 4
]
SCATTER_Z = (
    along_z([((0, 0), (1, 0)), ((1, 0), (0, 0)), ((2, 0), (1, 1)), ((3, 0), (0, 1))]),
    along_z([((0, 0), (1, 1)), ((1, 0), (0, 1)), ((2, 0), (1, 0)), ((3, 0), (0, 0))]),
    along_z([((0, 0), (0, 1)), ((1, 0), (1, 1)), ((2, 0), (0, 0)), ((3, 0), (1, 0))]),
    along_z([((2, 0), (0, 1)), ((3, 0), (1, 1))]),
)

IN_VMEM = pl.BlockSpec(memory_space=pltpu.VMEM)


def small_call(kernel, out_shape, operands, name, flops=0, scratch=(), limit=8):
    sizes = [o.size * o.dtype.itemsize for o in operands]
    return pl.pallas_call(
        kernel,
        in_specs=[IN_VMEM] * len(operands),
        out_specs=jax.tree.map(lambda _: IN_VMEM, out_shape),
        out_shape=out_shape,
        scratch_shapes=list(scratch),
        compiler_params=pltpu.CompilerParams(vmem_limit_bytes=limit * 1024 * 1024),
        cost_estimate=pl.CostEstimate(
            flops=flops // 64, bytes_accessed=sum(sizes) // 64, transcendentals=0
        ),
        name=name,
    )(*operands)


def here():
    spot = lax.axis_index("fsdp")
    return spot >> 2, (spot >> 1) & 1, spot & 1, lax.axis_index("ctx")


def is_inner():
    z, _, _, core = here()
    return core == (z >> 1)


def block_at(slot, way):
    z, y, x, core = here()
    along = (z & 1) if slot == 1 else 1 - (z & 1)
    far = {None: (0, 0), 0: (core, 1 - core), 1: (1 - core, core), 2: (1, 1), "x": (0, 1), "y": (1, 0)}
    far_y, far_x = far[way]
    return along * 4 + (y ^ far_y) * 2 + (x ^ far_x)


def embed_kernel(own_ref, other_ref, table_ref, out_ref):
    vocab = table_ref.shape[0]
    half = own_ref.shape[1]
    core = here()[3]
    for ref, side in ((own_ref, core), (other_ref, 1 - core)):
        across = jnp.broadcast_to(ref[...].astype(f32), (half, half)).T
        lane = lax.broadcasted_iota(jnp.int32, (half, half), 1).astype(f32)
        picks = [(across == lane + float(first)).astype(f32) for first in range(0, vocab, half)]
        rows = jnp.dot(
            jnp.concatenate(picks, axis=1).astype(bf16), table_ref[...], preferred_element_type=f32
        )
        out_ref[pl.ds(pl.multiple_of(side * half, half), half), :] = rows.astype(bf16)


def embed_rows(own_ids, other_ids, table):
    toks, width = 2 * own_ids.shape[1], table.shape[1]
    return small_call(
        embed_kernel,
        jax.ShapeDtypeStruct((toks, width), bf16),
        [own_ids, other_ids, table],
        "embed_rows",
        2 * toks * table.shape[0] * width,
    )


def fetch_kernel(ids_ref, table_ref, ids_out, table_out, sems):
    copies = [
        pltpu.make_async_copy(ids_ref, ids_out, sems.at[0]),
        pltpu.make_async_copy(table_ref, table_out, sems.at[1]),
    ]
    for copy in copies:
        copy.start()
    for copy in copies:
        copy.wait()


def in_hbm(array):
    return pltpu.with_memory_space_constraint(array, pltpu.HBM)


def in_vmem(array):
    return pltpu.with_memory_space_constraint(array, pltpu.VMEM)


def fetch(ids, table):
    out = pl.pallas_call(
        fetch_kernel,
        in_specs=[pl.BlockSpec(memory_space=pltpu.HBM)] * 2,
        out_specs=[IN_VMEM] * 2,
        out_shape=[pltpu.VMEM(ids.shape, ids.dtype), pltpu.VMEM(table.shape, bf16)],
        scratch_shapes=[pltpu.SemaphoreType.DMA((2,))],
        compiler_params=pltpu.CompilerParams(vmem_limit_bytes=2 * 1024 * 1024),
        cost_estimate=pl.CostEstimate(
            flops=0, bytes_accessed=4 * table.size, transcendentals=0
        ),
        name="fetch",
    )(in_hbm(ids), in_hbm(table))
    return [in_vmem(array) for array in out]


def load_kernel(w_ref, out_ref, sem):
    copy = pltpu.make_async_copy(w_ref, out_ref, sem)
    copy.start()
    copy.wait()


def load(w):
    out = pl.pallas_call(
        load_kernel,
        in_specs=[pl.BlockSpec(memory_space=pltpu.HBM)],
        out_specs=IN_VMEM,
        out_shape=pltpu.VMEM(w.shape, w.dtype),
        scratch_shapes=[pltpu.SemaphoreType.DMA],
        compiler_params=pltpu.CompilerParams(vmem_limit_bytes=2 * 1024 * 1024),
        cost_estimate=pl.CostEstimate(
            flops=0, bytes_accessed=2 * w.size * w.dtype.itemsize, transcendentals=0
        ),
        name="load",
    )(in_hbm(w))
    return in_vmem(out)


def project_kernel(inner, outer, count, has_base, part, w_ref, *refs):
    acts = refs[:count]
    groups, _, chans = w_ref.shape
    width = acts[0].shape[1]
    out_ref = refs[-1]
    if part is None:
        some = slice(None)
    else:
        half = chans // 2
        core = here()[3]
        side = core if part == "keep" else 1 - core
        some = pl.ds(pl.multiple_of(side * half, half), half)

    def add(entries):
        spans = [
            pl.ds(pl.multiple_of(block_at(slot, way) * width, width), width)
            for _, slot, way in entries
        ]
        for g in range(groups):
            total = refs[count][g, :, some] if has_base else None
            for (which, _, _), span in zip(entries, spans):
                term = jnp.dot(acts[which][...], w_ref[g, span, some], preferred_element_type=f32)
                total = term if total is None else total + term
            out_ref[g] = total

    pl.when(is_inner())(lambda: add(inner))
    pl.when(jnp.logical_not(is_inner()))(lambda: add(outer))


def project(acts, inner, outer, w, base, part=None):
    groups, _, chans = w.shape
    toks, width = acts[0].shape
    if part is not None:
        chans //= 2
    return small_call(
        functools.partial(project_kernel, inner, outer, len(acts), base is not None, part),
        jax.ShapeDtypeStruct((groups, toks, chans), f32),
        [w] + list(acts) + ([] if base is None else [base]),
        "project",
        2 * max(len(inner), len(outer)) * groups * width * chans * toks,
        (),
        16,
    )


def shifted(values, by):
    place = lax.broadcasted_iota(jnp.int32, values.shape, 0)
    moved = pltpu.roll(values, by % CHUNKS, 0)
    inside = place >= by if by > 0 else place < CHUNKS + by
    return jnp.where(inside, moved, 0.0)


def mixer_kernel(
    keep_ref,
    other_ref,
    taps_ref,
    rates_ref,
    residues_ref,
    cot_own_ref,
    cot_other_ref,
    mixed_own_ref,
    mixed_send_ref,
    grad_ref,
    flat,
    flat_cot,
    ext,
    filt,
    drive,
    back,
    grad_ext,
    decays,
    residues,
):
    groups, toks, chans = keep_ref.shape
    half = toks // 2
    modes = rates_ref.shape[0]
    short = taps_ref.shape[1]
    rim = short - 1
    length = toks // CHUNKS
    apart = flat.shape[1] // CHUNKS
    lanes = flat.shape[-1]
    wide = (CHUNKS, lanes)
    _, _, _, core = here()

    def spread(ref, at, values):
        for s in range(CHUNKS):
            ref[(*at, slice(s * apart, s * apart + length))] = values[s * length : (s + 1) * length]

    def row(array, at):
        return jnp.broadcast_to(array[at : at + 1, :], wide)

    def column(c, _):
        some = pl.ds(pl.multiple_of(c * lanes, lanes), lanes)
        whole = pl.ds(pl.multiple_of(core * chans + c * lanes, lanes), lanes)
        for g in range(groups):
            spread(flat, (g,), (keep_ref[g, :, some] + other_ref[g, :, some]).astype(bf16).astype(f32))
        for s in range(CHUNKS // 2):
            rows = slice(s * length, (s + 1) * length)
            own_at = pl.multiple_of((core * (CHUNKS // 2) + s) * apart, 8)
            other_at = pl.multiple_of(((1 - core) * (CHUNKS // 2) + s) * apart, 8)
            flat_cot[pl.ds(own_at, length)] = cot_own_ref[rows, whole].astype(f32)
            flat_cot[pl.ds(other_at, length)] = cot_other_ref[rows, whole].astype(f32)

        for g in range(groups):
            for k in range(length):
                ext[g, rim + k] = flat[g, pl.ds(k, CHUNKS, stride=apart), :]
            for k in range(rim):
                ext[g, k] = shifted(ext[g, length + k], 1)

        taps = [taps_ref[g, :, whole] for g in range(groups)]
        tap = [[row(taps[g], j) for g in range(groups)] for j in range(short)]

        def filter_step(k, _):
            parts = []
            for g in range(groups):
                total = tap[0][g] * ext[g, k + rim]
                for j in range(1, short):
                    total = total + tap[j][g] * ext[g, k + rim - j]
                parts.append(total)
                filt[g, k] = total
            drive[k] = parts[1] * parts[2]
            back[k] = parts[0] * flat_cot[pl.ds(k, CHUNKS, stride=apart), :]
            return _

        lax.fori_loop(0, length, filter_step, 0, unroll=16)

        rates = rates_ref[:, whole]
        decay_rows = jnp.exp(-rates)
        jump_rows = [jnp.exp(-rates * (length * n)) for n in (1, 2, 4)]
        residue_rows = residues_ref[:, whole]
        for m in range(modes):
            decays[m] = row(decay_rows, m)
            residues[m] = row(residue_rows, m)

        def long_filter(source, forward, finish):
            decay = [decays[m] for m in range(modes)]

            def place(k):
                return k if forward else length - 1 - k

            def end_step(k, states):
                value = source[place(k)]
                return tuple(decay[m] * states[m] + value for m in range(modes))

            zero = jnp.zeros(wide, f32)
            ends = lax.fori_loop(0, length, end_step, (zero,) * modes, unroll=32)
            entering = []
            sign = 1 if forward else -1
            for m in range(modes):
                carried = ends[m]
                for jump, by in zip(jump_rows, (1, 2, 4)):
                    carried = carried + row(jump, m) * shifted(carried, sign * by)
                entering.append(shifted(carried, sign))

            def out_step(k, states):
                value = source[place(k)]
                states = tuple(decay[m] * states[m] + value for m in range(modes))
                terms = [residues[m] * states[m] for m in range(modes)]
                while len(terms) > 1:
                    terms = [a + b for a, b in zip(terms[::2], terms[1::2])]
                finish(place(k), terms[0])
                return states

            lax.fori_loop(0, length, out_step, tuple(entering), unroll=16)

        def finish_forward(k, total):
            flat[0, pl.ds(k, CHUNKS, stride=apart), :] = filt[0, k] * total
            grad_ext[0, k] = flat_cot[pl.ds(k, CHUNKS, stride=apart), :] * total

        def finish_backward(k, total):
            grad_ext[1, k] = total * filt[2, k]
            grad_ext[2, k] = total * filt[1, k]

        long_filter(drive, True, finish_forward)
        for s in range(CHUNKS // 2):
            rows = slice(s * length, (s + 1) * length)
            own_at = pl.multiple_of((core * (CHUNKS // 2) + s) * apart, 8)
            other_at = pl.multiple_of(((1 - core) * (CHUNKS // 2) + s) * apart, 8)
            mixed_own_ref[rows, some] = flat[0, pl.ds(own_at, length)].astype(bf16)
            mixed_send_ref[rows, some] = flat[0, pl.ds(other_at, length)].astype(bf16)
        long_filter(back, False, finish_backward)

        for g in range(groups):
            for k in range(rim):
                grad_ext[g, length + k] = shifted(grad_ext[g, k], -1)

        def adjoint_step(k, _):
            for g in range(groups):
                total = tap[0][g] * grad_ext[g, k]
                for j in range(1, short):
                    total = total + tap[j][g] * grad_ext[g, k + j]
                flat[g, pl.ds(k, CHUNKS, stride=apart), :] = total
            return _

        lax.fori_loop(0, length, adjoint_step, 0, unroll=16)
        for g in range(groups):
            chunks = [flat[g, s * apart : s * apart + length].astype(bf16) for s in range(CHUNKS)]
            grad_ref[g, some, :] = jnp.concatenate(chunks, axis=0).T
        return _

    lax.fori_loop(0, chans // lanes, column, 0)


def mixer(keep, other, taps, rates, residues, cot_own, cot_other):
    groups, toks, chans = keep.shape
    modes = rates.shape[0]
    rim = taps.shape[1] - 1
    lanes = 128
    length = toks // CHUNKS
    return small_call(
        mixer_kernel,
        [
            jax.ShapeDtypeStruct((toks // 2, chans), bf16),
            jax.ShapeDtypeStruct((toks // 2, chans), bf16),
            jax.ShapeDtypeStruct((groups, chans, toks), bf16),
        ],
        [keep, other, taps, rates, residues, cot_own, cot_other],
        "mixer",
        12 * modes * toks * chans,
        [
            pltpu.VMEM((groups, toks + 8 * CHUNKS, lanes), f32),
            pltpu.VMEM((toks + 8 * CHUNKS, lanes), f32),
            pltpu.VMEM((groups, length + rim, CHUNKS, lanes), f32),
            pltpu.VMEM((groups, length, CHUNKS, lanes), f32),
            pltpu.VMEM((length, CHUNKS, lanes), f32),
            pltpu.VMEM((length, CHUNKS, lanes), f32),
            pltpu.VMEM((groups, length + rim, CHUNKS, lanes), f32),
            pltpu.VMEM((modes, CHUNKS, lanes), f32),
            pltpu.VMEM((modes, CHUNKS, lanes), f32),
        ],
    )


def back_kernel(outs, count, base, w_ref, *refs):
    grads, out_refs = refs[: len(count)], refs[len(count) + base :]
    groups, half, _ = grads[0].shape
    core = here()[3]
    sides = [pl.multiple_of((1 - core if other else core) * half, half) for other in count]
    for blocks, out in zip(outs, out_refs):
        width = out.shape[0] // len(blocks)
        for n, block in enumerate(blocks):
            rows = slice(n * width, (n + 1) * width)
            start = pl.multiple_of(block_at(*block) * width, width)
            total = refs[len(count)][rows] if base else None
            for g in range(groups):
                for ref, at in zip(grads, sides):
                    term = jnp.dot(
                        w_ref[g, pl.ds(start, width), pl.ds(at, half)],
                        ref[g],
                        preferred_element_type=f32,
                    )
                    total = term if total is None else total + term
            out[rows] = total.astype(out.dtype)


def back_project(outs, dtypes, w, own, other, width, base=None):
    grads = [(side, grad) for side, grad in enumerate((own, other)) if grad is not None]
    groups, half, toks = grads[0][1].shape
    extra = [] if base is None else [base]
    return small_call(
        functools.partial(back_kernel, outs, [side for side, _ in grads], len(extra)),
        [
            jax.ShapeDtypeStruct((width * len(blocks), toks), dtype)
            for blocks, dtype in zip(outs, dtypes)
        ],
        [w] + [grad for _, grad in grads] + extra,
        "back_project",
        2 * sum(len(blocks) for blocks in outs) * groups * width * half * toks * len(grads),
        (),
        16,
    )


def merge_kernel(two_ref, one_ref, got_ref, two_out, one_out):
    width = one_ref.shape[0]
    one_out[...] = (one_ref[...] + got_ref[:width].astype(f32)).astype(bf16)
    two_out[...] = (two_ref[...] + got_ref[width:].astype(f32)).astype(bf16)


def merge(two, one, got):
    shape = jax.ShapeDtypeStruct(one.shape, bf16)
    return small_call(merge_kernel, [shape, shape], [two, one, got], "merge")


def column_kernel(slot, own_ref, other_ref, first_ref, *out_refs):
    width, toks = own_ref.shape
    half = toks // 2
    total = (
        own_ref[...]
        + other_ref[(slot - 1) * width : slot * width].astype(f32)
        + first_ref[...].astype(f32)
    )
    z, _, _, core = here()
    side = (z >> 1) if slot == 2 else 1 - (z >> 1)
    low, high = total[:, :half], total[:, half:]
    send_low, send_high = out_refs[0], out_refs[1]

    @pl.when(side == 0)
    def _():
        send_low[...] = low.astype(bf16)
        send_high[...] = high.astype(bf16)

    @pl.when(side == 1)
    def _():
        send_low[...] = high.astype(bf16)
        send_high[...] = low.astype(bf16)

    if len(out_refs) == 3:
        inner = is_inner()
        out_refs[2][...] = jnp.where(inner, jnp.where(core == 0, low, high), 0.0)


def column(slot, own, other, first):
    width, toks = own.shape
    half = jax.ShapeDtypeStruct((width, toks // 2), bf16)
    kept = [jax.ShapeDtypeStruct((width, toks // 2), f32)] if slot == 1 else []
    return small_call(
        functools.partial(column_kernel, slot), [half, half] + kept, [own, other, first], "column"
    )


def finish_kernel(own_ref, a_ref, b_ref, c_ref, d_ref, out_ref):
    total = own_ref[...]
    for ref in (a_ref, b_ref, c_ref, d_ref):
        total = total + ref[...].astype(f32)
    out_ref[...] = total.T.astype(bf16)


def finish(own, received):
    shape = jax.ShapeDtypeStruct((own.shape[1], own.shape[0]), bf16)
    return small_call(finish_kernel, shape, [own] + received, "finish")


def pair_kernel(own_ref, other_ref, out_ref):
    half = own_ref.shape[1]
    core = here()[3]
    out_ref[:, pl.ds(pl.multiple_of(core * half, half), half)] = own_ref[...]
    out_ref[:, pl.ds(pl.multiple_of((1 - core) * half, half), half)] = other_ref[...]


def pair(own, other):
    shape = jax.ShapeDtypeStruct((own.shape[0], 2 * own.shape[1]), own.dtype)
    return small_call(pair_kernel, shape, [own, other], "pair")


def chip_plan(token_ids, embed, w_in, taps, rates, residues, cotangent):
    width = embed.shape[1]

    def swap(array):
        return lax.ppermute(array, BOTH, OTHER_CORE)

    def first_way(array):
        return lax.ppermute(array, BOTH, FIRST_WAY)

    def other_way(array):
        return lax.ppermute(array, BOTH, OTHER_WAY)

    own_ids = token_ids.reshape(1, -1)
    other_ids = swap(own_ids)
    cot_other = swap(cotangent)
    own_ids, table = fetch(own_ids, embed)
    embedded = embed_rows(own_ids, other_ids, table)
    embedded, cot_other = lax.optimization_barrier((embedded, cot_other))

    came = lax.ppermute(embedded, BOTH, GATHER_Z)
    more = lax.ppermute(embedded, BOTH, OUTER_Z_INNER_X)
    near_y = lax.ppermute(embedded, BOTH, INNER_Y)
    near_d = lax.ppermute(embedded, BOTH, INNER_XY)
    w = load(jnp.transpose(w_in, (1, 0, 2)))
    came, w = lax.optimization_barrier((came, w))
    first, other = first_way(came), other_way(came)
    sums = project(
        [embedded, near_y, near_d, came],
        [(0, 1, None), (1, 1, "y"), (2, 1, 2), (3, 2, None)],
        [(3, 1, None)],
        w,
        None,
    )
    more, sums = lax.optimization_barrier((more, sums))
    x_2 = lax.ppermute(more, BOTH, OUTER_X)
    d_2 = lax.ppermute(more, BOTH, OUTER_XY)
    first, other, more = lax.optimization_barrier((first, other, more))
    both = other_way(first)
    y_2 = lax.ppermute(more, BOTH, OUTER_Y)
    sums = project(
        [first, other, more],
        [(0, 2, 0), (1, 2, 1), (2, 1, "x")],
        [(0, 1, 0), (1, 1, 1), (2, 2, None)],
        w,
        sums,
    )
    sums = project([d_2], [], [(0, 2, 2)], w, sums)
    both, y_2, x_2, sums = lax.optimization_barrier((both, y_2, x_2, sums))
    acts = [both, y_2, x_2]
    inner, outer = [(0, 2, 2)], [(0, 1, 2), (1, 2, "y"), (2, 2, "x")]
    send = project(acts, inner, outer, w, sums, "send")
    sums, send = lax.optimization_barrier((sums, send))
    keep = project(acts, inner, outer, w, sums, "keep")
    got = swap(send)
    keep, got = lax.optimization_barrier((keep, got))
    mixed_own, mixed_send, grad_own = mixer(
        keep, got, jnp.transpose(taps, (1, 0, 2)), rates, residues, cotangent, cot_other
    )
    grad_other = swap(grad_own)
    mixed_other = swap(mixed_send)

    (part,) = back_project([[(1, 2), (2, 2)]], [f32], w, grad_own, None, width)
    grad_other, part = lax.optimization_barrier((grad_other, part))
    (across,) = back_project([[(1, 2), (2, 2)]], [bf16], w, None, grad_other, width, part)
    across = other_way(across)
    (other,) = back_project([[(1, 1), (2, 1)]], [bf16], w, grad_own, grad_other, width)
    other = other_way(other)
    first_2, first_1, own_2, own_1 = back_project(
        [[(2, 0)], [(1, 0)], [(2, None)], [(1, None)]], [f32] * 4, w, grad_own, grad_other, width
    )
    mixed = pair(mixed_own, mixed_other)
    across, mixed = lax.optimization_barrier((across, mixed))
    first_2, first_1 = merge(first_2, first_1, across)
    first_2, first_1 = first_way(first_2), first_way(first_1)
    sends = column(2, own_2, other, first_2)
    received = [lax.ppermute(a, BOTH, pairs) for a, pairs in zip(sends, SCATTER_Z[:2])]
    *sends, own = column(1, own_1, other, first_1)
    received += [lax.ppermute(a, BOTH, pairs) for a, pairs in zip(sends, SCATTER_Z[2:])]
    return (mixed, finish(own, received))


def solution(mesh):
    in_specs = (
        P("ctx"),
        P(None, "fsdp"),
        P("ctx", None, "fsdp"),
        P(None, None, "fsdp"),
        P(None, "fsdp"),
        P(None, "fsdp"),
        P("ctx", "fsdp"),
    )
    out_specs = (P("ctx", "fsdp"), P("ctx", "fsdp"))
    chips = mesh.shape["fsdp"] == 16 and mesh.shape["ctx"] == 2
    return jax.shard_map(
        chip_plan if chips else general_plan,
        mesh=mesh,
        in_specs=in_specs,
        out_specs=out_specs,
        check_vma=False,
    )
```

```python
import functools

import jax
import jax.numpy as jnp
from jax import lax
from jax.experimental import pallas as pl
from jax.experimental.pallas import tpu as pltpu
from jax.sharding import PartitionSpec as P

BOTH = ("fsdp", "ctx")
CHUNKS = 8
f32 = jnp.float32
bf16 = jnp.bfloat16


def from_behind(shard, axis, by):
    count = lax.axis_size(axis)
    pairs = [(i, i + by) for i in range(count) if 0 <= i + by < count]
    return lax.ppermute(shard, axis, pairs)


def pair_combine(earlier, later):
    return (earlier[0] * later[0], later[0] * earlier[1] + later[1])


def modal_states(drive, step_decay):
    tok_count = drive.shape[0]
    factors = jnp.broadcast_to(step_decay[None], (tok_count,) + step_decay.shape)
    inputs = jnp.broadcast_to(drive[:, None, :], factors.shape)
    return lax.associative_scan(pair_combine, (factors, inputs), axis=0)[1]


def short_filter(extended, taps, tok_count):
    rim_width = taps.shape[0] - 1
    filtered = taps[0] * extended[rim_width : rim_width + tok_count]
    for shift_lag in range(1, rim_width + 1):
        filtered = (
            filtered
            + taps[shift_lag] * extended[rim_width - shift_lag : rim_width - shift_lag + tok_count]
        )
    return filtered


def short_adjoint(extended, taps, tok_count):
    rim_width = taps.shape[0] - 1
    result = taps[0] * extended[:tok_count]
    for shift_lag in range(1, rim_width + 1):
        result = result + taps[shift_lag] * extended[shift_lag : shift_lag + tok_count]
    return result


def carry(block_decay, leaving, by):
    def relay_step(turn_index, incoming):
        return from_behind(block_decay * incoming + leaving, "ctx", by)

    return lax.fori_loop(0, lax.axis_size("ctx") - 1, relay_step, jnp.zeros_like(leaving))


def general_plan(token_ids, embed, w_in, taps, rates, residues, cotangent):
    tok_count = token_ids.shape[0]
    vocab_size = embed.shape[0]
    chan_width = embed.shape[1]
    rim_width = taps.shape[0] - 1
    onehot = (
        token_ids[:, None] == lax.broadcasted_iota(jnp.int32, (tok_count, vocab_size), 1)
    ).astype(bf16)
    embedded = jnp.dot(onehot, embed, preferred_element_type=f32).astype(bf16)
    features = lax.all_gather(embedded, "fsdp", axis=1, tiled=True)
    feat_width = features.shape[1]
    whole_w = lax.all_gather(w_in, "ctx", axis=0, tiled=True).reshape(feat_width, 3 * chan_width)
    projected = jnp.dot(features, whole_w, preferred_element_type=f32)
    stored = lax.optimization_barrier(projected.astype(bf16).reshape(tok_count, 3, chan_width))
    before = from_behind(stored[tok_count - rim_width :], "ctx", 1)
    extended = jnp.concatenate([before, stored], axis=0).astype(f32)
    filtered = short_filter(extended, taps, tok_count)
    query_part = filtered[:, 0]
    key_part = filtered[:, 1]
    value_part = filtered[:, 2]
    drive = key_part * value_part
    step_decay = jnp.exp(-rates)
    block_decay = jnp.exp(-rates * tok_count)
    local_states = modal_states(drive, step_decay)
    entering = carry(block_decay, local_states[tok_count - 1], 1)
    offsets = lax.broadcasted_iota(f32, (tok_count, 1, 1), 0)
    states = local_states + jnp.exp(-rates[None] * (offsets + 1.0)) * entering[None]
    long_out = jnp.sum(residues[None] * states, axis=1)
    mixed = (query_part * long_out).astype(bf16)
    incoming = cotangent.astype(f32)
    grad_long = incoming * query_part
    grad_query = incoming * long_out
    back_states = jnp.flip(modal_states(jnp.flip(grad_long, 0), step_decay), 0)
    beyond = carry(block_decay, back_states[0], -1)
    adjoint = back_states + jnp.exp(-rates[None] * (tok_count - offsets)) * beyond[None]
    grad_drive = jnp.sum(residues[None] * adjoint, axis=1)
    grad_filtered = jnp.stack([grad_query, grad_drive * value_part, grad_drive * key_part], axis=1)
    after = from_behind(grad_filtered[:rim_width], "ctx", -1)
    ext_grad = jnp.concatenate([grad_filtered, after], axis=0)
    grad_stored = short_adjoint(ext_grad, taps, tok_count).astype(bf16)
    grad_rows = grad_stored.reshape(tok_count, 3 * chan_width)
    own_rows = lax.psum_scatter(
        lax.dot_general(whole_w, grad_rows, (((1,), (1,)), ((), ())), preferred_element_type=f32),
        "fsdp",
        scatter_dimension=0,
        tiled=True,
    )
    return (mixed, own_rows.T.astype(bf16))


def device_at(z, y, x, core):
    return ((z * 2 + y) * 2 + x) * 2 + core


def everywhere(move):
    pairs = []
    for z in range(4):
        for y in range(2):
            for x in range(2):
                for core in range(2):
                    pairs.append((device_at(z, y, x, core), device_at(*move(z, y, x, core))))
    return pairs


OTHER_CORE = everywhere(lambda z, y, x, core: (z, y, x, 1 - core))


def along_z(moves):
    pairs = []
    for core in range(2):
        for (place, other), (to_place, to_other) in moves:
            z, to_z = (place, to_place) if core == 0 else (3 - place, 3 - to_place)
            for y in range(2):
                for x in range(2):
                    pairs.append(
                        (
                            device_at(z, y, x, core ^ other),
                            device_at(to_z, y, x, core ^ to_other),
                        )
                    )
    return pairs


FIRST_WAY = everywhere(lambda z, y, x, core: (z, y, 1 - x, core) if core == 0 else (z, 1 - y, x, core))
OTHER_WAY = everywhere(lambda z, y, x, core: (z, 1 - y, x, core) if core == 0 else (z, y, 1 - x, core))
def some_move(move, inner):
    def target(z, y, x, core):
        return move(z, y, x, core) if (core == z >> 1) == inner else (z, y, x, core)

    return everywhere(target)


INNER_Y = some_move(lambda z, y, x, core: (z, 1 - y, x, core), True)
INNER_XY = some_move(lambda z, y, x, core: (z, 1 - y, 1 - x, core), True)
OUTER_X = some_move(lambda z, y, x, core: (z, y, 1 - x, core), False)
OUTER_Y = some_move(lambda z, y, x, core: (z, 1 - y, x, core), False)
OUTER_XY = some_move(lambda z, y, x, core: (z, 1 - y, 1 - x, core), False)
GATHER_Z = along_z([((0, 0), (1, 0)), ((1, 0), (0, 0)), ((0, 1), (2, 0)), ((1, 1), (3, 0))])
OUTER_Z_INNER_X = along_z([((1, 1), (2, 0)), ((0, 1), (3, 0))]) + [
    pair
    for pair in everywhere(lambda z, y, x, core: (z, y, 1 - x, core))
    if (pair[0] & 1) == pair[0] >> 4
]
SCATTER_Z = (
    along_z([((0, 0), (1, 0)), ((1, 0), (0, 0)), ((2, 0), (1, 1)), ((3, 0), (0, 1))]),
    along_z([((0, 0), (1, 1)), ((1, 0), (0, 1)), ((2, 0), (1, 0)), ((3, 0), (0, 0))]),
    along_z([((0, 0), (0, 1)), ((1, 0), (1, 1)), ((2, 0), (0, 0)), ((3, 0), (1, 0))]),
    along_z([((2, 0), (0, 1)), ((3, 0), (1, 1))]),
)

IN_VMEM = pl.BlockSpec(memory_space=pltpu.VMEM)


def small_call(kernel, out_shape, operands, name, flops=0, scratch=(), limit=8):
    sizes = [o.size * o.dtype.itemsize for o in operands]
    return pl.pallas_call(
        kernel,
        in_specs=[IN_VMEM] * len(operands),
        out_specs=jax.tree.map(lambda _: IN_VMEM, out_shape),
        out_shape=out_shape,
        scratch_shapes=list(scratch),
        compiler_params=pltpu.CompilerParams(vmem_limit_bytes=limit * 1024 * 1024),
        cost_estimate=pl.CostEstimate(
            flops=flops // 64, bytes_accessed=sum(sizes) // 64, transcendentals=0
        ),
        name=name,
    )(*operands)


def here():
    spot = lax.axis_index("fsdp")
    return spot >> 2, (spot >> 1) & 1, spot & 1, lax.axis_index("ctx")


def is_inner():
    z, _, _, core = here()
    return core == (z >> 1)


def block_at(slot, way):
    z, y, x, core = here()
    along = (z & 1) if slot == 1 else 1 - (z & 1)
    far = {None: (0, 0), 0: (core, 1 - core), 1: (1 - core, core), 2: (1, 1), "x": (0, 1), "y": (1, 0)}
    far_y, far_x = far[way]
    return along * 4 + (y ^ far_y) * 2 + (x ^ far_x)


def embed_kernel(own_ref, other_ref, table_ref, out_ref):
    vocab = table_ref.shape[0]
    half = own_ref.shape[1]
    core = here()[3]
    for ref, side in ((own_ref, core), (other_ref, 1 - core)):
        across = jnp.broadcast_to(ref[...].astype(f32), (half, half)).T
        lane = lax.broadcasted_iota(jnp.int32, (half, half), 1).astype(f32)
        picks = [(across == lane + float(first)).astype(f32) for first in range(0, vocab, half)]
        rows = jnp.dot(
            jnp.concatenate(picks, axis=1).astype(bf16), table_ref[...], preferred_element_type=f32
        )
        out_ref[pl.ds(pl.multiple_of(side * half, half), half), :] = rows.astype(bf16)


def embed_rows(own_ids, other_ids, table):
    toks, width = 2 * own_ids.shape[1], table.shape[1]
    return small_call(
        embed_kernel,
        jax.ShapeDtypeStruct((toks, width), bf16),
        [own_ids, other_ids, table],
        "embed_rows",
        2 * toks * table.shape[0] * width,
    )


def fetch_kernel(ids_ref, table_ref, ids_out, table_out, sems):
    copies = [
        pltpu.make_async_copy(ids_ref, ids_out, sems.at[0]),
        pltpu.make_async_copy(table_ref, table_out, sems.at[1]),
    ]
    for copy in copies:
        copy.start()
    for copy in copies:
        copy.wait()


def in_hbm(array):
    return pltpu.with_memory_space_constraint(array, pltpu.HBM)


def in_vmem(array):
    return pltpu.with_memory_space_constraint(array, pltpu.VMEM)


def fetch(ids, table):
    out = pl.pallas_call(
        fetch_kernel,
        in_specs=[pl.BlockSpec(memory_space=pltpu.HBM)] * 2,
        out_specs=[IN_VMEM] * 2,
        out_shape=[pltpu.VMEM(ids.shape, ids.dtype), pltpu.VMEM(table.shape, bf16)],
        scratch_shapes=[pltpu.SemaphoreType.DMA((2,))],
        compiler_params=pltpu.CompilerParams(vmem_limit_bytes=2 * 1024 * 1024),
        cost_estimate=pl.CostEstimate(
            flops=0, bytes_accessed=4 * table.size, transcendentals=0
        ),
        name="fetch",
    )(in_hbm(ids), in_hbm(table))
    return [in_vmem(array) for array in out]


def load_kernel(w_ref, out_ref, sem):
    copy = pltpu.make_async_copy(w_ref, out_ref, sem)
    copy.start()
    copy.wait()


def load(w):
    out = pl.pallas_call(
        load_kernel,
        in_specs=[pl.BlockSpec(memory_space=pltpu.HBM)],
        out_specs=IN_VMEM,
        out_shape=pltpu.VMEM(w.shape, w.dtype),
        scratch_shapes=[pltpu.SemaphoreType.DMA],
        compiler_params=pltpu.CompilerParams(vmem_limit_bytes=2 * 1024 * 1024),
        cost_estimate=pl.CostEstimate(
            flops=0, bytes_accessed=2 * w.size * w.dtype.itemsize, transcendentals=0
        ),
        name="load",
    )(in_hbm(w))
    return in_vmem(out)


def project_kernel(inner, outer, count, has_base, part, w_ref, *refs):
    acts = refs[:count]
    groups, _, chans = w_ref.shape
    width = acts[0].shape[1]
    out_ref = refs[-1]
    if part is None:
        some = slice(None)
    else:
        half = chans // 2
        core = here()[3]
        side = core if part == "keep" else 1 - core
        some = pl.ds(pl.multiple_of(side * half, half), half)

    def add(entries):
        spans = [
            pl.ds(pl.multiple_of(block_at(slot, way) * width, width), width)
            for _, slot, way in entries
        ]
        for g in range(groups):
            total = refs[count][g, :, some] if has_base else None
            for (which, _, _), span in zip(entries, spans):
                term = jnp.dot(acts[which][...], w_ref[g, span, some], preferred_element_type=f32)
                total = term if total is None else total + term
            out_ref[g] = total

    pl.when(is_inner())(lambda: add(inner))
    pl.when(jnp.logical_not(is_inner()))(lambda: add(outer))


def project(acts, inner, outer, w, base, part=None):
    groups, _, chans = w.shape
    toks, width = acts[0].shape
    if part is not None:
        chans //= 2
    return small_call(
        functools.partial(project_kernel, inner, outer, len(acts), base is not None, part),
        jax.ShapeDtypeStruct((groups, toks, chans), f32),
        [w] + list(acts) + ([] if base is None else [base]),
        "project",
        2 * max(len(inner), len(outer)) * groups * width * chans * toks,
        (),
        16,
    )


def shifted(values, by):
    place = lax.broadcasted_iota(jnp.int32, values.shape, 0)
    moved = pltpu.roll(values, by % CHUNKS, 0)
    inside = place >= by if by > 0 else place < CHUNKS + by
    return jnp.where(inside, moved, 0.0)


def mixer_kernel(
    keep_ref,
    other_ref,
    taps_ref,
    rates_ref,
    residues_ref,
    cot_own_ref,
    cot_other_ref,
    mixed_own_ref,
    mixed_send_ref,
    grad_ref,
    flat,
    flat_cot,
    ext,
    filt,
    drive,
    back,
    grad_ext,
    decays,
    residues,
):
    groups, toks, chans = keep_ref.shape
    half = toks // 2
    modes = rates_ref.shape[0]
    short = taps_ref.shape[1]
    rim = short - 1
    length = toks // CHUNKS
    apart = flat.shape[1] // CHUNKS
    lanes = flat.shape[-1]
    wide = (CHUNKS, lanes)
    _, _, _, core = here()

    def spread(ref, at, values):
        for s in range(CHUNKS):
            ref[(*at, slice(s * apart, s * apart + length))] = values[s * length : (s + 1) * length]

    def row(array, at):
        return jnp.broadcast_to(array[at : at + 1, :], wide)

    def column(c, _):
        some = pl.ds(pl.multiple_of(c * lanes, lanes), lanes)
        whole = pl.ds(pl.multiple_of(core * chans + c * lanes, lanes), lanes)
        for g in range(groups):
            spread(flat, (g,), (keep_ref[g, :, some] + other_ref[g, :, some]).astype(bf16).astype(f32))
        for s in range(CHUNKS // 2):
            rows = slice(s * length, (s + 1) * length)
            own_at = pl.multiple_of((core * (CHUNKS // 2) + s) * apart, 8)
            other_at = pl.multiple_of(((1 - core) * (CHUNKS // 2) + s) * apart, 8)
            flat_cot[pl.ds(own_at, length)] = cot_own_ref[rows, whole].astype(f32)
            flat_cot[pl.ds(other_at, length)] = cot_other_ref[rows, whole].astype(f32)

        for g in range(groups):
            for k in range(length):
                ext[g, rim + k] = flat[g, pl.ds(k, CHUNKS, stride=apart), :]
            for k in range(rim):
                ext[g, k] = shifted(ext[g, length + k], 1)

        taps = [taps_ref[g, :, whole] for g in range(groups)]
        tap = [[row(taps[g], j) for g in range(groups)] for j in range(short)]

        def filter_step(k, _):
            parts = []
            for g in range(groups):
                total = tap[0][g] * ext[g, k + rim]
                for j in range(1, short):
                    total = total + tap[j][g] * ext[g, k + rim - j]
                parts.append(total)
                filt[g, k] = total
            drive[k] = parts[1] * parts[2]
            back[k] = parts[0] * flat_cot[pl.ds(k, CHUNKS, stride=apart), :]
            return _

        lax.fori_loop(0, length, filter_step, 0, unroll=16)

        rates = rates_ref[:, whole]
        decay_rows = jnp.exp(-rates)
        jump_rows = [jnp.exp(-rates * (length * n)) for n in (1, 2, 4)]
        residue_rows = residues_ref[:, whole]
        for m in range(modes):
            decays[m] = row(decay_rows, m)
            residues[m] = row(residue_rows, m)

        def long_filter(source, forward, finish):
            decay = [decays[m] for m in range(modes)]

            def place(k):
                return k if forward else length - 1 - k

            def end_step(k, states):
                value = source[place(k)]
                return tuple(decay[m] * states[m] + value for m in range(modes))

            zero = jnp.zeros(wide, f32)
            ends = lax.fori_loop(0, length, end_step, (zero,) * modes, unroll=32)
            entering = []
            sign = 1 if forward else -1
            for m in range(modes):
                carried = ends[m]
                for jump, by in zip(jump_rows, (1, 2, 4)):
                    carried = carried + row(jump, m) * shifted(carried, sign * by)
                entering.append(shifted(carried, sign))

            def out_step(k, states):
                value = source[place(k)]
                states = tuple(decay[m] * states[m] + value for m in range(modes))
                terms = [residues[m] * states[m] for m in range(modes)]
                while len(terms) > 1:
                    terms = [a + b for a, b in zip(terms[::2], terms[1::2])]
                finish(place(k), terms[0])
                return states

            lax.fori_loop(0, length, out_step, tuple(entering), unroll=16)

        def finish_forward(k, total):
            flat[0, pl.ds(k, CHUNKS, stride=apart), :] = filt[0, k] * total
            grad_ext[0, k] = flat_cot[pl.ds(k, CHUNKS, stride=apart), :] * total

        def finish_backward(k, total):
            grad_ext[1, k] = total * filt[2, k]
            grad_ext[2, k] = total * filt[1, k]

        long_filter(drive, True, finish_forward)
        for s in range(CHUNKS // 2):
            rows = slice(s * length, (s + 1) * length)
            own_at = pl.multiple_of((core * (CHUNKS // 2) + s) * apart, 8)
            other_at = pl.multiple_of(((1 - core) * (CHUNKS // 2) + s) * apart, 8)
            mixed_own_ref[rows, some] = flat[0, pl.ds(own_at, length)].astype(bf16)
            mixed_send_ref[rows, some] = flat[0, pl.ds(other_at, length)].astype(bf16)
        long_filter(back, False, finish_backward)

        for g in range(groups):
            for k in range(rim):
                grad_ext[g, length + k] = shifted(grad_ext[g, k], -1)

        def adjoint_step(k, _):
            for g in range(groups):
                total = tap[0][g] * grad_ext[g, k]
                for j in range(1, short):
                    total = total + tap[j][g] * grad_ext[g, k + j]
                flat[g, pl.ds(k, CHUNKS, stride=apart), :] = total
            return _

        lax.fori_loop(0, length, adjoint_step, 0, unroll=16)
        for g in range(groups):
            chunks = [flat[g, s * apart : s * apart + length].astype(bf16) for s in range(CHUNKS)]
            grad_ref[g, some, :] = jnp.concatenate(chunks, axis=0).T
        return _

    lax.fori_loop(0, chans // lanes, column, 0)


def mixer(keep, other, taps, rates, residues, cot_own, cot_other):
    groups, toks, chans = keep.shape
    modes = rates.shape[0]
    rim = taps.shape[1] - 1
    lanes = 128
    length = toks // CHUNKS
    return small_call(
        mixer_kernel,
        [
            jax.ShapeDtypeStruct((toks // 2, chans), bf16),
            jax.ShapeDtypeStruct((toks // 2, chans), bf16),
            jax.ShapeDtypeStruct((groups, chans, toks), bf16),
        ],
        [keep, other, taps, rates, residues, cot_own, cot_other],
        "mixer",
        12 * modes * toks * chans,
        [
            pltpu.VMEM((groups, toks + 8 * CHUNKS, lanes), f32),
            pltpu.VMEM((toks + 8 * CHUNKS, lanes), f32),
            pltpu.VMEM((groups, length + rim, CHUNKS, lanes), f32),
            pltpu.VMEM((groups, length, CHUNKS, lanes), f32),
            pltpu.VMEM((length, CHUNKS, lanes), f32),
            pltpu.VMEM((length, CHUNKS, lanes), f32),
            pltpu.VMEM((groups, length + rim, CHUNKS, lanes), f32),
            pltpu.VMEM((modes, CHUNKS, lanes), f32),
            pltpu.VMEM((modes, CHUNKS, lanes), f32),
        ],
    )


def back_kernel(outs, count, base, w_ref, *refs):
    grads, out_refs = refs[: len(count)], refs[len(count) + base :]
    groups, half, _ = grads[0].shape
    core = here()[3]
    sides = [pl.multiple_of((1 - core if other else core) * half, half) for other in count]
    for blocks, out in zip(outs, out_refs):
        width = out.shape[0] // len(blocks)
        for n, block in enumerate(blocks):
            rows = slice(n * width, (n + 1) * width)
            start = pl.multiple_of(block_at(*block) * width, width)
            total = refs[len(count)][rows] if base else None
            for g in range(groups):
                for ref, at in zip(grads, sides):
                    term = jnp.dot(
                        w_ref[g, pl.ds(start, width), pl.ds(at, half)],
                        ref[g],
                        preferred_element_type=f32,
                    )
                    total = term if total is None else total + term
            out[rows] = total.astype(out.dtype)


def back_project(outs, dtypes, w, own, other, width, base=None):
    grads = [(side, grad) for side, grad in enumerate((own, other)) if grad is not None]
    groups, half, toks = grads[0][1].shape
    extra = [] if base is None else [base]
    return small_call(
        functools.partial(back_kernel, outs, [side for side, _ in grads], len(extra)),
        [
            jax.ShapeDtypeStruct((width * len(blocks), toks), dtype)
            for blocks, dtype in zip(outs, dtypes)
        ],
        [w] + [grad for _, grad in grads] + extra,
        "back_project",
        2 * sum(len(blocks) for blocks in outs) * groups * width * half * toks * len(grads),
        (),
        16,
    )


def merge_kernel(two_ref, one_ref, got_ref, two_out, one_out):
    width = one_ref.shape[0]
    one_out[...] = (one_ref[...] + got_ref[:width].astype(f32)).astype(bf16)
    two_out[...] = (two_ref[...] + got_ref[width:].astype(f32)).astype(bf16)


def merge(two, one, got):
    shape = jax.ShapeDtypeStruct(one.shape, bf16)
    return small_call(merge_kernel, [shape, shape], [two, one, got], "merge")


def column_kernel(slot, own_ref, other_ref, first_ref, *out_refs):
    width, toks = own_ref.shape
    half = toks // 2
    total = (
        own_ref[...]
        + other_ref[(slot - 1) * width : slot * width].astype(f32)
        + first_ref[...].astype(f32)
    )
    z, _, _, core = here()
    side = (z >> 1) if slot == 2 else 1 - (z >> 1)
    low, high = total[:, :half], total[:, half:]
    send_low, send_high = out_refs[0], out_refs[1]

    @pl.when(side == 0)
    def _():
        send_low[...] = low.astype(bf16)
        send_high[...] = high.astype(bf16)

    @pl.when(side == 1)
    def _():
        send_low[...] = high.astype(bf16)
        send_high[...] = low.astype(bf16)

    if len(out_refs) == 3:
        inner = is_inner()
        out_refs[2][...] = jnp.where(inner, jnp.where(core == 0, low, high), 0.0)


def column(slot, own, other, first):
    width, toks = own.shape
    half = jax.ShapeDtypeStruct((width, toks // 2), bf16)
    kept = [jax.ShapeDtypeStruct((width, toks // 2), f32)] if slot == 1 else []
    return small_call(
        functools.partial(column_kernel, slot), [half, half] + kept, [own, other, first], "column"
    )


def finish_kernel(own_ref, a_ref, b_ref, c_ref, d_ref, out_ref):
    total = own_ref[...]
    for ref in (a_ref, b_ref, c_ref, d_ref):
        total = total + ref[...].astype(f32)
    out_ref[...] = total.T.astype(bf16)


def finish(own, received):
    shape = jax.ShapeDtypeStruct((own.shape[1], own.shape[0]), bf16)
    return small_call(finish_kernel, shape, [own] + received, "finish")


def pair_kernel(own_ref, other_ref, out_ref):
    half = own_ref.shape[1]
    core = here()[3]
    out_ref[:, pl.ds(pl.multiple_of(core * half, half), half)] = own_ref[...]
    out_ref[:, pl.ds(pl.multiple_of((1 - core) * half, half), half)] = other_ref[...]


def pair(own, other):
    shape = jax.ShapeDtypeStruct((own.shape[0], 2 * own.shape[1]), own.dtype)
    return small_call(pair_kernel, shape, [own, other], "pair")


def chip_plan(token_ids, embed, w_in, taps, rates, residues, cotangent):
    width = embed.shape[1]

    def swap(array):
        return lax.ppermute(array, BOTH, OTHER_CORE)

    def first_way(array):
        return lax.ppermute(array, BOTH, FIRST_WAY)

    def other_way(array):
        return lax.ppermute(array, BOTH, OTHER_WAY)

    own_ids = token_ids.reshape(1, -1)
    other_ids = swap(own_ids)
    cot_other = swap(cotangent)
    own_ids, table = fetch(own_ids, embed)
    embedded = embed_rows(own_ids, other_ids, table)
    embedded, cot_other = lax.optimization_barrier((embedded, cot_other))

    came = lax.ppermute(embedded, BOTH, GATHER_Z)
    more = lax.ppermute(embedded, BOTH, OUTER_Z_INNER_X)
    near_y = lax.ppermute(embedded, BOTH, INNER_Y)
    near_d = lax.ppermute(embedded, BOTH, INNER_XY)
    w = load(jnp.transpose(w_in, (1, 0, 2)))
    came, w = lax.optimization_barrier((came, w))
    first, other = first_way(came), other_way(came)
    sums = project(
        [embedded, near_y, near_d, came],
        [(0, 1, None), (1, 1, "y"), (2, 1, 2), (3, 2, None)],
        [(3, 1, None)],
        w,
        None,
    )
    more, sums = lax.optimization_barrier((more, sums))
    x_2 = lax.ppermute(more, BOTH, OUTER_X)
    d_2 = lax.ppermute(more, BOTH, OUTER_XY)
    first, other, more = lax.optimization_barrier((first, other, more))
    both = other_way(first)
    y_2 = lax.ppermute(more, BOTH, OUTER_Y)
    sums = project(
        [first, other, more],
        [(0, 2, 0), (1, 2, 1), (2, 1, "x")],
        [(0, 1, 0), (1, 1, 1), (2, 2, None)],
        w,
        sums,
    )
    sums = project([d_2], [], [(0, 2, 2)], w, sums)
    both, x_2, sums = lax.optimization_barrier((both, x_2, sums))
    sums = project([both, x_2], [(0, 2, 2)], [(0, 1, 2), (1, 2, "x")], w, sums)
    y_2, sums = lax.optimization_barrier((y_2, sums))
    send = project([y_2], [], [(0, 2, "y")], w, sums, "send")
    sums, send = lax.optimization_barrier((sums, send))
    keep = project([y_2], [], [(0, 2, "y")], w, sums, "keep")
    got = swap(send)
    keep, got = lax.optimization_barrier((keep, got))
    mixed_own, mixed_send, grad_own = mixer(
        keep, got, jnp.transpose(taps, (1, 0, 2)), rates, residues, cotangent, cot_other
    )
    grad_other = swap(grad_own)
    mixed_other = swap(mixed_send)

    (part,) = back_project([[(1, 2), (2, 2)]], [f32], w, grad_own, None, width)
    grad_other, part = lax.optimization_barrier((grad_other, part))
    (across,) = back_project([[(1, 2), (2, 2)]], [bf16], w, None, grad_other, width, part)
    across = other_way(across)
    (other,) = back_project([[(1, 1), (2, 1)]], [bf16], w, grad_own, grad_other, width)
    other = other_way(other)
    first_2, first_1, own_2, own_1 = back_project(
        [[(2, 0)], [(1, 0)], [(2, None)], [(1, None)]], [f32] * 4, w, grad_own, grad_other, width
    )
    mixed = pair(mixed_own, mixed_other)
    across, mixed = lax.optimization_barrier((across, mixed))
    first_2, first_1 = merge(first_2, first_1, across)
    first_2, first_1 = first_way(first_2), first_way(first_1)
    sends = column(2, own_2, other, first_2)
    received = [lax.ppermute(a, BOTH, pairs) for a, pairs in zip(sends, SCATTER_Z[:2])]
    *sends, own = column(1, own_1, other, first_1)
    received += [lax.ppermute(a, BOTH, pairs) for a, pairs in zip(sends, SCATTER_Z[2:])]
    return (mixed, finish(own, received))


def solution(mesh):
    in_specs = (
        P("ctx"),
        P(None, "fsdp"),
        P("ctx", None, "fsdp"),
        P(None, None, "fsdp"),
        P(None, "fsdp"),
        P(None, "fsdp"),
        P("ctx", "fsdp"),
    )
    out_specs = (P("ctx", "fsdp"), P("ctx", "fsdp"))
    chips = mesh.shape["fsdp"] == 16 and mesh.shape["ctx"] == 2
    return jax.shard_map(
        chip_plan if chips else general_plan,
        mesh=mesh,
        in_specs=in_specs,
        out_specs=out_specs,
        check_vma=False,
    )
```

```python
import functools

import jax
import jax.numpy as jnp
from jax import lax
from jax.experimental import pallas as pl
from jax.experimental.pallas import tpu as pltpu
from jax.sharding import PartitionSpec as P

BOTH = ("fsdp", "ctx")
CHUNKS = 8
f32 = jnp.float32
bf16 = jnp.bfloat16


def from_behind(shard, axis, by):
    count = lax.axis_size(axis)
    pairs = [(i, i + by) for i in range(count) if 0 <= i + by < count]
    return lax.ppermute(shard, axis, pairs)


def pair_combine(earlier, later):
    return (earlier[0] * later[0], later[0] * earlier[1] + later[1])


def modal_states(drive, step_decay):
    tok_count = drive.shape[0]
    factors = jnp.broadcast_to(step_decay[None], (tok_count,) + step_decay.shape)
    inputs = jnp.broadcast_to(drive[:, None, :], factors.shape)
    return lax.associative_scan(pair_combine, (factors, inputs), axis=0)[1]


def short_filter(extended, taps, tok_count):
    rim_width = taps.shape[0] - 1
    filtered = taps[0] * extended[rim_width : rim_width + tok_count]
    for shift_lag in range(1, rim_width + 1):
        filtered = (
            filtered
            + taps[shift_lag] * extended[rim_width - shift_lag : rim_width - shift_lag + tok_count]
        )
    return filtered


def short_adjoint(extended, taps, tok_count):
    rim_width = taps.shape[0] - 1
    result = taps[0] * extended[:tok_count]
    for shift_lag in range(1, rim_width + 1):
        result = result + taps[shift_lag] * extended[shift_lag : shift_lag + tok_count]
    return result


def carry(block_decay, leaving, by):
    def relay_step(turn_index, incoming):
        return from_behind(block_decay * incoming + leaving, "ctx", by)

    return lax.fori_loop(0, lax.axis_size("ctx") - 1, relay_step, jnp.zeros_like(leaving))


def general_plan(token_ids, embed, w_in, taps, rates, residues, cotangent):
    tok_count = token_ids.shape[0]
    vocab_size = embed.shape[0]
    chan_width = embed.shape[1]
    rim_width = taps.shape[0] - 1
    onehot = (
        token_ids[:, None] == lax.broadcasted_iota(jnp.int32, (tok_count, vocab_size), 1)
    ).astype(bf16)
    embedded = jnp.dot(onehot, embed, preferred_element_type=f32).astype(bf16)
    features = lax.all_gather(embedded, "fsdp", axis=1, tiled=True)
    feat_width = features.shape[1]
    whole_w = lax.all_gather(w_in, "ctx", axis=0, tiled=True).reshape(feat_width, 3 * chan_width)
    projected = jnp.dot(features, whole_w, preferred_element_type=f32)
    stored = lax.optimization_barrier(projected.astype(bf16).reshape(tok_count, 3, chan_width))
    before = from_behind(stored[tok_count - rim_width :], "ctx", 1)
    extended = jnp.concatenate([before, stored], axis=0).astype(f32)
    filtered = short_filter(extended, taps, tok_count)
    query_part = filtered[:, 0]
    key_part = filtered[:, 1]
    value_part = filtered[:, 2]
    drive = key_part * value_part
    step_decay = jnp.exp(-rates)
    block_decay = jnp.exp(-rates * tok_count)
    local_states = modal_states(drive, step_decay)
    entering = carry(block_decay, local_states[tok_count - 1], 1)
    offsets = lax.broadcasted_iota(f32, (tok_count, 1, 1), 0)
    states = local_states + jnp.exp(-rates[None] * (offsets + 1.0)) * entering[None]
    long_out = jnp.sum(residues[None] * states, axis=1)
    mixed = (query_part * long_out).astype(bf16)
    incoming = cotangent.astype(f32)
    grad_long = incoming * query_part
    grad_query = incoming * long_out
    back_states = jnp.flip(modal_states(jnp.flip(grad_long, 0), step_decay), 0)
    beyond = carry(block_decay, back_states[0], -1)
    adjoint = back_states + jnp.exp(-rates[None] * (tok_count - offsets)) * beyond[None]
    grad_drive = jnp.sum(residues[None] * adjoint, axis=1)
    grad_filtered = jnp.stack([grad_query, grad_drive * value_part, grad_drive * key_part], axis=1)
    after = from_behind(grad_filtered[:rim_width], "ctx", -1)
    ext_grad = jnp.concatenate([grad_filtered, after], axis=0)
    grad_stored = short_adjoint(ext_grad, taps, tok_count).astype(bf16)
    grad_rows = grad_stored.reshape(tok_count, 3 * chan_width)
    own_rows = lax.psum_scatter(
        lax.dot_general(whole_w, grad_rows, (((1,), (1,)), ((), ())), preferred_element_type=f32),
        "fsdp",
        scatter_dimension=0,
        tiled=True,
    )
    return (mixed, own_rows.T.astype(bf16))


def device_at(z, y, x, core):
    return ((z * 2 + y) * 2 + x) * 2 + core


def everywhere(move):
    pairs = []
    for z in range(4):
        for y in range(2):
            for x in range(2):
                for core in range(2):
                    pairs.append((device_at(z, y, x, core), device_at(*move(z, y, x, core))))
    return pairs


OTHER_CORE = everywhere(lambda z, y, x, core: (z, y, x, 1 - core))


def along_z(moves):
    pairs = []
    for core in range(2):
        for (place, other), (to_place, to_other) in moves:
            z, to_z = (place, to_place) if core == 0 else (3 - place, 3 - to_place)
            for y in range(2):
                for x in range(2):
                    pairs.append(
                        (
                            device_at(z, y, x, core ^ other),
                            device_at(to_z, y, x, core ^ to_other),
                        )
                    )
    return pairs


FIRST_WAY = everywhere(lambda z, y, x, core: (z, y, 1 - x, core) if core == 0 else (z, 1 - y, x, core))
OTHER_WAY = everywhere(lambda z, y, x, core: (z, 1 - y, x, core) if core == 0 else (z, y, 1 - x, core))
def some_move(move, inner):
    def target(z, y, x, core):
        return move(z, y, x, core) if (core == z >> 1) == inner else (z, y, x, core)

    return everywhere(target)


INNER_Y = some_move(lambda z, y, x, core: (z, 1 - y, x, core), True)
INNER_XY = some_move(lambda z, y, x, core: (z, 1 - y, 1 - x, core), True)
OUTER_X = some_move(lambda z, y, x, core: (z, y, 1 - x, core), False)
OUTER_Y = some_move(lambda z, y, x, core: (z, 1 - y, x, core), False)
OUTER_XY = some_move(lambda z, y, x, core: (z, 1 - y, 1 - x, core), False)
GATHER_Z = along_z([((0, 0), (1, 0)), ((1, 0), (0, 0)), ((0, 1), (2, 0)), ((1, 1), (3, 0))])
OUTER_Z_INNER_X = along_z([((1, 1), (2, 0)), ((0, 1), (3, 0))]) + [
    pair
    for pair in everywhere(lambda z, y, x, core: (z, y, 1 - x, core))
    if (pair[0] & 1) == pair[0] >> 4
]
SCATTER_Z = (
    along_z([((0, 0), (1, 0)), ((1, 0), (0, 0)), ((2, 0), (1, 1)), ((3, 0), (0, 1))]),
    along_z([((0, 0), (1, 1)), ((1, 0), (0, 1)), ((2, 0), (1, 0)), ((3, 0), (0, 0))]),
    along_z([((0, 0), (0, 1)), ((1, 0), (1, 1)), ((2, 0), (0, 0)), ((3, 0), (1, 0))]),
    along_z([((2, 0), (0, 1)), ((3, 0), (1, 1))]),
)

IN_VMEM = pl.BlockSpec(memory_space=pltpu.VMEM)


def small_call(kernel, out_shape, operands, name, flops=0, scratch=(), limit=8):
    sizes = [o.size * o.dtype.itemsize for o in operands]
    return pl.pallas_call(
        kernel,
        in_specs=[IN_VMEM] * len(operands),
        out_specs=jax.tree.map(lambda _: IN_VMEM, out_shape),
        out_shape=out_shape,
        scratch_shapes=list(scratch),
        compiler_params=pltpu.CompilerParams(vmem_limit_bytes=limit * 1024 * 1024),
        cost_estimate=pl.CostEstimate(
            flops=flops // 64, bytes_accessed=sum(sizes) // 64, transcendentals=0
        ),
        name=name,
    )(*operands)


def here():
    spot = lax.axis_index("fsdp")
    return spot >> 2, (spot >> 1) & 1, spot & 1, lax.axis_index("ctx")


def is_inner():
    z, _, _, core = here()
    return core == (z >> 1)


def block_at(slot, way):
    z, y, x, core = here()
    along = (z & 1) if slot == 1 else 1 - (z & 1)
    far = {None: (0, 0), 0: (core, 1 - core), 1: (1 - core, core), 2: (1, 1), "x": (0, 1), "y": (1, 0)}
    far_y, far_x = far[way]
    return along * 4 + (y ^ far_y) * 2 + (x ^ far_x)


def embed_kernel(own_ref, other_ref, table_ref, out_ref):
    vocab = table_ref.shape[0]
    half = own_ref.shape[1]
    core = here()[3]
    for ref, side in ((own_ref, core), (other_ref, 1 - core)):
        across = jnp.broadcast_to(ref[...].astype(f32), (half, half)).T
        lane = lax.broadcasted_iota(jnp.int32, (half, half), 1).astype(f32)
        picks = [(across == lane + float(first)).astype(f32) for first in range(0, vocab, half)]
        rows = jnp.dot(
            jnp.concatenate(picks, axis=1).astype(bf16), table_ref[...], preferred_element_type=f32
        )
        out_ref[pl.ds(pl.multiple_of(side * half, half), half), :] = rows.astype(bf16)


def embed_rows(own_ids, other_ids, table):
    toks, width = 2 * own_ids.shape[1], table.shape[1]
    return small_call(
        embed_kernel,
        jax.ShapeDtypeStruct((toks, width), bf16),
        [own_ids, other_ids, table],
        "embed_rows",
        2 * toks * table.shape[0] * width,
    )


def fetch_kernel(ids_ref, table_ref, ids_out, table_out, sems):
    copies = [
        pltpu.make_async_copy(ids_ref, ids_out, sems.at[0]),
        pltpu.make_async_copy(table_ref, table_out, sems.at[1]),
    ]
    for copy in copies:
        copy.start()
    for copy in copies:
        copy.wait()


def in_hbm(array):
    return pltpu.with_memory_space_constraint(array, pltpu.HBM)


def in_vmem(array):
    return pltpu.with_memory_space_constraint(array, pltpu.VMEM)


def fetch(ids, table):
    out = pl.pallas_call(
        fetch_kernel,
        in_specs=[pl.BlockSpec(memory_space=pltpu.HBM)] * 2,
        out_specs=[IN_VMEM] * 2,
        out_shape=[pltpu.VMEM(ids.shape, ids.dtype), pltpu.VMEM(table.shape, bf16)],
        scratch_shapes=[pltpu.SemaphoreType.DMA((2,))],
        compiler_params=pltpu.CompilerParams(vmem_limit_bytes=2 * 1024 * 1024),
        cost_estimate=pl.CostEstimate(
            flops=0, bytes_accessed=4 * table.size, transcendentals=0
        ),
        name="fetch",
    )(in_hbm(ids), in_hbm(table))
    return [in_vmem(array) for array in out]


def load_kernel(w_ref, out_ref, sem):
    copy = pltpu.make_async_copy(w_ref, out_ref, sem)
    copy.start()
    copy.wait()


def load(w):
    out = pl.pallas_call(
        load_kernel,
        in_specs=[pl.BlockSpec(memory_space=pltpu.HBM)],
        out_specs=IN_VMEM,
        out_shape=pltpu.VMEM(w.shape, w.dtype),
        scratch_shapes=[pltpu.SemaphoreType.DMA],
        compiler_params=pltpu.CompilerParams(vmem_limit_bytes=2 * 1024 * 1024),
        cost_estimate=pl.CostEstimate(
            flops=0, bytes_accessed=2 * w.size * w.dtype.itemsize, transcendentals=0
        ),
        name="load",
    )(in_hbm(w))
    return in_vmem(out)


def project_kernel(inner, outer, count, has_base, part, w_ref, *refs):
    acts = refs[:count]
    groups, _, chans = w_ref.shape
    width = acts[0].shape[1]
    out_ref = refs[-1]
    if part is None:
        some = slice(None)
    else:
        half = chans // 2
        core = here()[3]
        side = core if part == "keep" else 1 - core
        some = pl.ds(pl.multiple_of(side * half, half), half)

    def add(entries):
        spans = [
            pl.ds(pl.multiple_of(block_at(slot, way) * width, width), width)
            for _, slot, way in entries
        ]
        for g in range(groups):
            total = refs[count][g, :, some] if has_base else None
            for (which, _, _), span in zip(entries, spans):
                term = jnp.dot(acts[which][...], w_ref[g, span, some], preferred_element_type=f32)
                total = term if total is None else total + term
            out_ref[g] = total

    pl.when(is_inner())(lambda: add(inner))
    pl.when(jnp.logical_not(is_inner()))(lambda: add(outer))


def project(acts, inner, outer, w, base, part=None):
    groups, _, chans = w.shape
    toks, width = acts[0].shape
    if part is not None:
        chans //= 2
    return small_call(
        functools.partial(project_kernel, inner, outer, len(acts), base is not None, part),
        jax.ShapeDtypeStruct((groups, toks, chans), f32),
        [w] + list(acts) + ([] if base is None else [base]),
        "project",
        2 * max(len(inner), len(outer)) * groups * width * chans * toks,
        (),
        16,
    )


def shifted(values, by):
    place = lax.broadcasted_iota(jnp.int32, values.shape, 0)
    moved = pltpu.roll(values, by % CHUNKS, 0)
    inside = place >= by if by > 0 else place < CHUNKS + by
    return jnp.where(inside, moved, 0.0)


def mixer_kernel(
    keep_ref,
    other_ref,
    taps_ref,
    rates_ref,
    residues_ref,
    cot_own_ref,
    cot_other_ref,
    mixed_own_ref,
    mixed_send_ref,
    grad_ref,
    flat,
    flat_cot,
    ext,
    filt,
    drive,
    back,
    grad_ext,
    decays,
    residues,
):
    groups, toks, chans = keep_ref.shape
    half = toks // 2
    modes = rates_ref.shape[0]
    short = taps_ref.shape[1]
    rim = short - 1
    length = toks // CHUNKS
    apart = flat.shape[1] // CHUNKS
    lanes = flat.shape[-1]
    wide = (CHUNKS, lanes)
    _, _, _, core = here()

    def spread(ref, at, values):
        for s in range(CHUNKS):
            ref[(*at, slice(s * apart, s * apart + length))] = values[s * length : (s + 1) * length]

    def row(array, at):
        return jnp.broadcast_to(array[at : at + 1, :], wide)

    def column(c, _):
        some = pl.ds(pl.multiple_of(c * lanes, lanes), lanes)
        whole = pl.ds(pl.multiple_of(core * chans + c * lanes, lanes), lanes)
        for g in range(groups):
            spread(flat, (g,), (keep_ref[g, :, some] + other_ref[g, :, some]).astype(bf16).astype(f32))
        for s in range(CHUNKS // 2):
            rows = slice(s * length, (s + 1) * length)
            own_at = pl.multiple_of((core * (CHUNKS // 2) + s) * apart, 8)
            other_at = pl.multiple_of(((1 - core) * (CHUNKS // 2) + s) * apart, 8)
            flat_cot[pl.ds(own_at, length)] = cot_own_ref[rows, whole].astype(f32)
            flat_cot[pl.ds(other_at, length)] = cot_other_ref[rows, whole].astype(f32)

        for g in range(groups):
            for k in range(length):
                ext[g, rim + k] = flat[g, pl.ds(k, CHUNKS, stride=apart), :]
            for k in range(rim):
                ext[g, k] = shifted(ext[g, length + k], 1)

        taps = [taps_ref[g, :, whole] for g in range(groups)]
        tap = [[row(taps[g], j) for g in range(groups)] for j in range(short)]

        def filter_step(k, _):
            parts = []
            for g in range(groups):
                total = tap[0][g] * ext[g, k + rim]
                for j in range(1, short):
                    total = total + tap[j][g] * ext[g, k + rim - j]
                parts.append(total)
                filt[g, k] = total
            drive[k] = parts[1] * parts[2]
            back[k] = parts[0] * flat_cot[pl.ds(k, CHUNKS, stride=apart), :]
            return _

        lax.fori_loop(0, length, filter_step, 0, unroll=16)

        rates = rates_ref[:, whole]
        decay_rows = jnp.exp(-rates)
        jump_rows = [jnp.exp(-rates * (length * n)) for n in (1, 2, 4)]
        residue_rows = residues_ref[:, whole]
        for m in range(modes):
            decays[m] = row(decay_rows, m)
            residues[m] = row(residue_rows, m)

        def long_filter(source, forward, finish):
            decay = [decays[m] for m in range(modes)]

            def place(k):
                return k if forward else length - 1 - k

            def end_step(k, states):
                value = source[place(k)]
                return tuple(decay[m] * states[m] + value for m in range(modes))

            zero = jnp.zeros(wide, f32)
            ends = lax.fori_loop(0, length, end_step, (zero,) * modes, unroll=32)
            entering = []
            sign = 1 if forward else -1
            for m in range(modes):
                carried = ends[m]
                for jump, by in zip(jump_rows, (1, 2, 4)):
                    carried = carried + row(jump, m) * shifted(carried, sign * by)
                entering.append(shifted(carried, sign))

            def out_step(k, states):
                value = source[place(k)]
                states = tuple(decay[m] * states[m] + value for m in range(modes))
                terms = [residues[m] * states[m] for m in range(modes)]
                while len(terms) > 1:
                    terms = [a + b for a, b in zip(terms[::2], terms[1::2])]
                finish(place(k), terms[0])
                return states

            lax.fori_loop(0, length, out_step, tuple(entering), unroll=16)

        def finish_forward(k, total):
            flat[0, pl.ds(k, CHUNKS, stride=apart), :] = filt[0, k] * total
            grad_ext[0, k] = flat_cot[pl.ds(k, CHUNKS, stride=apart), :] * total

        def finish_backward(k, total):
            grad_ext[1, k] = total * filt[2, k]
            grad_ext[2, k] = total * filt[1, k]

        long_filter(drive, True, finish_forward)
        for s in range(CHUNKS // 2):
            rows = slice(s * length, (s + 1) * length)
            own_at = pl.multiple_of((core * (CHUNKS // 2) + s) * apart, 8)
            other_at = pl.multiple_of(((1 - core) * (CHUNKS // 2) + s) * apart, 8)
            mixed_own_ref[rows, some] = flat[0, pl.ds(own_at, length)].astype(bf16)
            mixed_send_ref[rows, some] = flat[0, pl.ds(other_at, length)].astype(bf16)
        long_filter(back, False, finish_backward)

        for g in range(groups):
            for k in range(rim):
                grad_ext[g, length + k] = shifted(grad_ext[g, k], -1)

        def adjoint_step(k, _):
            for g in range(groups):
                total = tap[0][g] * grad_ext[g, k]
                for j in range(1, short):
                    total = total + tap[j][g] * grad_ext[g, k + j]
                flat[g, pl.ds(k, CHUNKS, stride=apart), :] = total
            return _

        lax.fori_loop(0, length, adjoint_step, 0, unroll=16)
        for g in range(groups):
            chunks = [flat[g, s * apart : s * apart + length].astype(bf16) for s in range(CHUNKS)]
            grad_ref[g, some, :] = jnp.concatenate(chunks, axis=0).T
        return _

    lax.fori_loop(0, chans // lanes, column, 0)


def mixer(keep, other, taps, rates, residues, cot_own, cot_other):
    groups, toks, chans = keep.shape
    modes = rates.shape[0]
    rim = taps.shape[1] - 1
    lanes = 128
    length = toks // CHUNKS
    return small_call(
        mixer_kernel,
        [
            jax.ShapeDtypeStruct((toks // 2, chans), bf16),
            jax.ShapeDtypeStruct((toks // 2, chans), bf16),
            jax.ShapeDtypeStruct((groups, chans, toks), bf16),
        ],
        [keep, other, taps, rates, residues, cot_own, cot_other],
        "mixer",
        12 * modes * toks * chans,
        [
            pltpu.VMEM((groups, toks + 8 * CHUNKS, lanes), f32),
            pltpu.VMEM((toks + 8 * CHUNKS, lanes), f32),
            pltpu.VMEM((groups, length + rim, CHUNKS, lanes), f32),
            pltpu.VMEM((groups, length, CHUNKS, lanes), f32),
            pltpu.VMEM((length, CHUNKS, lanes), f32),
            pltpu.VMEM((length, CHUNKS, lanes), f32),
            pltpu.VMEM((groups, length + rim, CHUNKS, lanes), f32),
            pltpu.VMEM((modes, CHUNKS, lanes), f32),
            pltpu.VMEM((modes, CHUNKS, lanes), f32),
        ],
    )


def back_kernel(outs, count, base, w_ref, *refs):
    grads, out_refs = refs[: len(count)], refs[len(count) + base :]
    groups, half, _ = grads[0].shape
    core = here()[3]
    sides = [pl.multiple_of((1 - core if other else core) * half, half) for other in count]
    for blocks, out in zip(outs, out_refs):
        width = out.shape[0] // len(blocks)
        for n, block in enumerate(blocks):
            rows = slice(n * width, (n + 1) * width)
            start = pl.multiple_of(block_at(*block) * width, width)
            total = refs[len(count)][rows] if base else None
            for g in range(groups):
                for ref, at in zip(grads, sides):
                    term = jnp.dot(
                        w_ref[g, pl.ds(start, width), pl.ds(at, half)],
                        ref[g],
                        preferred_element_type=f32,
                    )
                    total = term if total is None else total + term
            out[rows] = total.astype(out.dtype)


def back_project(outs, dtypes, w, own, other, width, base=None):
    grads = [(side, grad) for side, grad in enumerate((own, other)) if grad is not None]
    groups, half, toks = grads[0][1].shape
    extra = [] if base is None else [base]
    return small_call(
        functools.partial(back_kernel, outs, [side for side, _ in grads], len(extra)),
        [
            jax.ShapeDtypeStruct((width * len(blocks), toks), dtype)
            for blocks, dtype in zip(outs, dtypes)
        ],
        [w] + [grad for _, grad in grads] + extra,
        "back_project",
        2 * sum(len(blocks) for blocks in outs) * groups * width * half * toks * len(grads),
        (),
        16,
    )


def merge_kernel(two_ref, one_ref, got_ref, two_out, one_out):
    width = one_ref.shape[0]
    one_out[...] = (one_ref[...] + got_ref[:width].astype(f32)).astype(bf16)
    two_out[...] = (two_ref[...] + got_ref[width:].astype(f32)).astype(bf16)


def merge(two, one, got):
    shape = jax.ShapeDtypeStruct(one.shape, bf16)
    return small_call(merge_kernel, [shape, shape], [two, one, got], "merge")


def column_kernel(slot, own_ref, other_ref, first_ref, *out_refs):
    width, toks = own_ref.shape
    half = toks // 2
    total = (
        own_ref[...]
        + other_ref[(slot - 1) * width : slot * width].astype(f32)
        + first_ref[...].astype(f32)
    )
    z, _, _, core = here()
    side = (z >> 1) if slot == 2 else 1 - (z >> 1)
    low, high = total[:, :half], total[:, half:]
    send_low, send_high = out_refs[0], out_refs[1]

    @pl.when(side == 0)
    def _():
        send_low[...] = low.astype(bf16)
        send_high[...] = high.astype(bf16)

    @pl.when(side == 1)
    def _():
        send_low[...] = high.astype(bf16)
        send_high[...] = low.astype(bf16)

    if len(out_refs) == 3:
        inner = is_inner()
        out_refs[2][...] = jnp.where(inner, jnp.where(core == 0, low, high), 0.0)


def column(slot, own, other, first):
    width, toks = own.shape
    half = jax.ShapeDtypeStruct((width, toks // 2), bf16)
    kept = [jax.ShapeDtypeStruct((width, toks // 2), f32)] if slot == 1 else []
    return small_call(
        functools.partial(column_kernel, slot), [half, half] + kept, [own, other, first], "column"
    )


def finish_kernel(own_ref, a_ref, b_ref, out_ref):
    total = own_ref[...]
    for ref in (a_ref, b_ref):
        total = total + ref[...].astype(f32)
    out_ref[...] = total.T.astype(bf16)


def finish(own, received):
    shape = jax.ShapeDtypeStruct((own.shape[1], own.shape[0]), bf16)
    return small_call(finish_kernel, shape, [own] + received, "finish")


def presum_kernel(own_ref, a_ref, b_ref, out_ref):
    out_ref[...] = own_ref[...] + a_ref[...].astype(f32) + b_ref[...].astype(f32)


def presum(own, received):
    shape = jax.ShapeDtypeStruct(own.shape, f32)
    return small_call(presum_kernel, shape, [own] + received, "presum")


def pair_kernel(own_ref, other_ref, out_ref):
    half = own_ref.shape[1]
    core = here()[3]
    out_ref[:, pl.ds(pl.multiple_of(core * half, half), half)] = own_ref[...]
    out_ref[:, pl.ds(pl.multiple_of((1 - core) * half, half), half)] = other_ref[...]


def pair(own, other):
    shape = jax.ShapeDtypeStruct((own.shape[0], 2 * own.shape[1]), own.dtype)
    return small_call(pair_kernel, shape, [own, other], "pair")


def chip_plan(token_ids, embed, w_in, taps, rates, residues, cotangent):
    width = embed.shape[1]

    def swap(array):
        return lax.ppermute(array, BOTH, OTHER_CORE)

    def first_way(array):
        return lax.ppermute(array, BOTH, FIRST_WAY)

    def other_way(array):
        return lax.ppermute(array, BOTH, OTHER_WAY)

    own_ids = token_ids.reshape(1, -1)
    other_ids = swap(own_ids)
    cot_other = swap(cotangent)
    own_ids, table = fetch(own_ids, embed)
    embedded = embed_rows(own_ids, other_ids, table)
    embedded, cot_other = lax.optimization_barrier((embedded, cot_other))

    came = lax.ppermute(embedded, BOTH, GATHER_Z)
    more = lax.ppermute(embedded, BOTH, OUTER_Z_INNER_X)
    near_y = lax.ppermute(embedded, BOTH, INNER_Y)
    near_d = lax.ppermute(embedded, BOTH, INNER_XY)
    w = load(jnp.transpose(w_in, (1, 0, 2)))
    came, w = lax.optimization_barrier((came, w))
    first, other = first_way(came), other_way(came)
    sums = project(
        [embedded, near_y, near_d, came],
        [(0, 1, None), (1, 1, "y"), (2, 1, 2), (3, 2, None)],
        [(3, 1, None)],
        w,
        None,
    )
    more, sums = lax.optimization_barrier((more, sums))
    x_2 = lax.ppermute(more, BOTH, OUTER_X)
    d_2 = lax.ppermute(more, BOTH, OUTER_XY)
    first, other, more = lax.optimization_barrier((first, other, more))
    both = other_way(first)
    y_2 = lax.ppermute(more, BOTH, OUTER_Y)
    sums = project(
        [first, other, more],
        [(0, 2, 0), (1, 2, 1), (2, 1, "x")],
        [(0, 1, 0), (1, 1, 1), (2, 2, None)],
        w,
        sums,
    )
    sums = project([d_2], [], [(0, 2, 2)], w, sums)
    both, x_2, sums = lax.optimization_barrier((both, x_2, sums))
    sums = project([both, x_2], [(0, 2, 2)], [(0, 1, 2), (1, 2, "x")], w, sums)
    y_2, sums = lax.optimization_barrier((y_2, sums))
    send = project([y_2], [], [(0, 2, "y")], w, sums, "send")
    sums, send = lax.optimization_barrier((sums, send))
    keep = project([y_2], [], [(0, 2, "y")], w, sums, "keep")
    got = swap(send)
    keep, got = lax.optimization_barrier((keep, got))
    mixed_own, mixed_send, grad_own = mixer(
        keep, got, jnp.transpose(taps, (1, 0, 2)), rates, residues, cotangent, cot_other
    )
    grad_other = swap(grad_own)
    mixed_other = swap(mixed_send)

    (part,) = back_project([[(1, 2), (2, 2)]], [f32], w, grad_own, None, width)
    grad_other, part = lax.optimization_barrier((grad_other, part))
    (across,) = back_project([[(1, 2), (2, 2)]], [bf16], w, None, grad_other, width, part)
    across = other_way(across)
    (other,) = back_project([[(1, 1), (2, 1)]], [bf16], w, grad_own, grad_other, width)
    other = other_way(other)
    first_2, first_1, own_2, own_1 = back_project(
        [[(2, 0)], [(1, 0)], [(2, None)], [(1, None)]], [f32] * 4, w, grad_own, grad_other, width
    )
    mixed = pair(mixed_own, mixed_other)
    across, mixed = lax.optimization_barrier((across, mixed))
    first_2, first_1 = merge(first_2, first_1, across)
    first_2, first_1 = first_way(first_2), first_way(first_1)
    sends = column(2, own_2, other, first_2)
    received = [lax.ppermute(a, BOTH, pairs) for a, pairs in zip(sends, SCATTER_Z[:2])]
    *sends, own = column(1, own_1, other, first_1)
    received += [lax.ppermute(a, BOTH, pairs) for a, pairs in zip(sends, SCATTER_Z[2:])]
    return (mixed, finish(presum(own, received[2:]), received[:2]))


def solution(mesh):
    in_specs = (
        P("ctx"),
        P(None, "fsdp"),
        P("ctx", None, "fsdp"),
        P(None, None, "fsdp"),
        P(None, "fsdp"),
        P(None, "fsdp"),
        P("ctx", "fsdp"),
    )
    out_specs = (P("ctx", "fsdp"), P("ctx", "fsdp"))
    chips = mesh.shape["fsdp"] == 16 and mesh.shape["ctx"] == 2
    return jax.shard_map(
        chip_plan if chips else general_plan,
        mesh=mesh,
        in_specs=in_specs,
        out_specs=out_specs,
        check_vma=False,
    )
```
